32 devices in a mesh: group: 2 (over y), dp: 8 (over z, x), tensor: 2 (over core).
Axes of the slice: x: 2, y: 2, z: 4, core: 2. Of those that a mesh axis runs over, the one named last changes fastest.
Arguments:
- tokens: bfloat16 [12288, 2048], P(('group', 'dp')), may hold values from -6 to 6
- doc_lengths: int32 [16, 3], P(('group', 'dp')), may hold values from 1 to 480, 768 in all within a row
- cotangent: bfloat16 [12288, 2048], P(('group', 'dp')), may hold values from -6 to 6
- inner_in: float32 [2, 2048, 2, 5120], P('group', 'dp', 'tensor')
- inner_out: float32 [2, 2, 5120, 2048], P('group', 'tensor', None, 'dp')
- inner_shared: float32 [2, 2048, 267], P('group', ('dp', 'tensor'))
- first_in: float32 [2, 2048, 2, 5120], P('group', 'dp', 'tensor')
- first_out: float32 [2, 2, 5120, 2048], P('group', 'tensor', None, 'dp')
- first_shared: float32 [2, 2048, 267], P('group', ('dp', 'tensor'))
- second_in: float32 [2, 2048, 2, 5120], P('group', 'dp', 'tensor')
- second_out: float32 [2, 2, 5120, 2048], P('group', 'tensor', None, 'dp')
- second_shared: float32 [2, 2048, 267], P('group', ('dp', 'tensor'))
- outer_in: float32 [2048, 2, 5120], P('dp', 'tensor')
- outer_out: float32 [2, 5120, 2048], P('tensor', None, 'dp')
- outer_shared: float32 [2048, 267], P(('dp', 'tensor'))
- momentum_in: float32 [2048, 2, 5120], P('dp', 'tensor')
- momentum_out: float32 [2, 5120, 2048], P('tensor', None, 'dp')
- momentum_shared: float32 [2048, 267], P(('dp', 'tensor'))
Outputs:
- block_out: bfloat16 [12288, 2048], P(('group', 'dp'))
- tokens_grad: bfloat16 [12288, 2048], P(('group', 'dp'))
- clip_factors: float32 [16], replicated
- new_first_in: float32 [2, 2048, 2, 5120], P('group', 'dp', 'tensor')
- new_first_out: float32 [2, 2, 5120, 2048], P('group', 'tensor', None, 'dp')
- new_first_shared: float32 [2, 2048, 267], P('group', ('dp', 'tensor'))
- new_second_in: float32 [2, 2048, 2, 5120], P('group', 'dp', 'tensor')
- new_second_out: float32 [2, 2, 5120, 2048], P('group', 'tensor', None, 'dp')
- new_second_shared: float32 [2, 2048, 267], P('group', ('dp', 'tensor'))
- mean_delta_in: float32 [2048, 2, 5120], P('dp', 'tensor')
- mean_delta_out: float32 [2, 5120, 2048], P('tensor', None, 'dp')
- mean_delta_shared: float32 [2048, 267], P(('dp', 'tensor'))
- new_momentum_in: float32 [2048, 2, 5120], P('dp', 'tensor')
- new_momentum_out: float32 [2, 5120, 2048], P('tensor', None, 'dp')
- new_momentum_shared: float32 [2048, 267], P(('dp', 'tensor'))
- new_outer_in: float32 [2048, 2, 5120], P('dp', 'tensor')
- new_outer_out: float32 [2, 5120, 2048], P('tensor', None, 'dp')
- new_outer_shared: float32 [2048, 267], P(('dp', 'tensor'))
- copy_in: bfloat16 [2048, 2, 5120], P('dp', 'tensor')
- copy_out: bfloat16 [2, 5120, 2048], P('tensor', None, 'dp')
- copy_shared: bfloat16 [2048, 267], P(('dp', 'tensor'))
The draws below stay inside these ranges and needn't reach their ends.
Inputs may be any that keep to these rules, and one draw needn't show every extreme that they name: `doc_lengths`: each row holds the lengths, in order, of the documents packed into one sequence slot; a row sums to 768.
All inputs are finite; a program needn't handle non-finite values.
Results may differ from the reference program's by a relative error of at most 0.024.
Values may be sent and summed in bfloat16 or wider, within the bound.
No kernel may reach another device: no remote copies, remote signals or barrier semaphores. Data moves between devices by JAX's collectives and lax.ppermute only.
A program may use at most 320 MiB of HBM per device.

```python
import math
import jax
import jax.numpy as jnp
import numpy as np
from jax import lax

D = 2048
HEADS = 16
HD = 128
FF = 8192
TOK_DEV = 768
BLOCK = 256
DOCS = 3
STEP = 10
MOST = 480
SPLITS = 2
GROUPS = 2
SEQS = 16
TOKENS = 12288
GROUP_TOKENS = 6144
LOCAL_COLS = 5120
SHARED_COLS = 267
N_DP = 8


def head_spread(key):
    return jnp.exp(jax.random.uniform(jax.random.fold_in(key, 101), (HEADS,), minval=math.log(0.6), maxval=math.log(2.0)))


def in_scales(key):
    query_cols = D // SPLITS
    columns = jnp.arange(LOCAL_COLS)
    split_ids = jnp.arange(SPLITS)
    head_of = split_ids[:, None] * (HEADS // SPLITS) + jnp.minimum(columns, query_cols - 1)[None, :] // HD
    factor = jnp.sum(jnp.where(head_of[:, :, None] == jnp.arange(HEADS)[None, None, :], head_spread(key)[None, None, :], 0.0), axis=2)
    return jnp.where(columns[None, :] < query_cols, factor, 1.0) / math.sqrt(D)


def out_scales():
    columns = jnp.arange(LOCAL_COLS)
    row_scale = jnp.where(columns < D // SPLITS, 4.0 / math.sqrt(D), 1.0 / math.sqrt(FF))
    return jnp.broadcast_to(row_scale[None, :, None], (SPLITS, LOCAL_COLS, 1))


def shared_scale():
    columns = jnp.arange(SHARED_COLS)
    gains = (columns == 2 * HD) | (columns == 2 * HD + 2)
    return jnp.where(columns < 2 * HD, 1.0 / math.sqrt(D), jnp.where(gains, 0.1, 0.3))


def shared_center():
    columns = jnp.arange(SHARED_COLS)
    return jnp.where((columns == 2 * HD) | (columns == 2 * HD + 2), 1.0, 0.0)


def shared_vector(matrix_val, vector_val):
    return jnp.where(jnp.arange(SHARED_COLS) < 2 * HD, matrix_val, vector_val)


def base_in(key):
    return jax.random.normal(jax.random.fold_in(key, 102), (D, SPLITS, LOCAL_COLS)) * in_scales(key)[None, :, :]


def base_out(key):
    return jax.random.normal(jax.random.fold_in(key, 103), (SPLITS, LOCAL_COLS, D)) * out_scales()


def base_shared(key):
    return jax.random.normal(jax.random.fold_in(key, 104), (D, SHARED_COLS)) * shared_scale()[None, :] + shared_center()[None, :]


def first_moment(key, shape, size):
    return jax.random.normal(key, shape) * size / 9.0


def second_moment(key, shape, size):
    factor = jnp.exp(jax.random.uniform(key, shape, minval=0.0, maxval=math.log(4.0)))
    return factor * size * size * (0.05 / 0.95)


def grad_big():
    return 0.3 * math.sqrt(GROUP_TOKENS)


def grad_shared():
    return shared_vector(0.3 * math.sqrt(GROUP_TOKENS), 1.0 * math.sqrt(GROUP_TOKENS))[None, None, :]


def draw_outer_in(key, part):
    return base_in(key)


def draw_outer_out(key, part):
    return base_out(key)


def draw_outer_shared(key, part):
    return base_shared(key)


def draw_inner_in(key, part):
    base_field = base_in(key)
    key = jax.random.fold_in(key, 1)
    return base_field[None] + jax.random.normal(key, (GROUPS, D, SPLITS, LOCAL_COLS)) * 0.01


def draw_inner_out(key, part):
    base_field = base_out(key)
    key = jax.random.fold_in(key, 2)
    return base_field[None] + jax.random.normal(key, (GROUPS, SPLITS, LOCAL_COLS, D)) * 0.01


def draw_inner_shared(key, part):
    base_field = base_shared(key)
    key = jax.random.fold_in(key, 3)
    return base_field[None] + jax.random.normal(key, (GROUPS, D, SHARED_COLS)) * shared_vector(0.01, 0.1)[None, None, :]


def draw_first_in(key, part):
    key = jax.random.fold_in(key, 4)
    return first_moment(key, (GROUPS, D, SPLITS, LOCAL_COLS), grad_big())


def draw_first_out(key, part):
    key = jax.random.fold_in(key, 5)
    return first_moment(key, (GROUPS, SPLITS, LOCAL_COLS, D), grad_big())


def draw_first_shared(key, part):
    key = jax.random.fold_in(key, 6)
    return first_moment(key, (GROUPS, D, SHARED_COLS), grad_shared())


def draw_second_in(key, part):
    key = jax.random.fold_in(key, 7)
    return second_moment(key, (GROUPS, D, SPLITS, LOCAL_COLS), grad_big())


def draw_second_out(key, part):
    key = jax.random.fold_in(key, 8)
    return second_moment(key, (GROUPS, SPLITS, LOCAL_COLS, D), grad_big())


def draw_second_shared(key, part):
    key = jax.random.fold_in(key, 9)
    return second_moment(key, (GROUPS, D, SHARED_COLS), grad_shared())


def draw_momentum_in(key, part):
    key = jax.random.fold_in(key, 10)
    return jax.random.normal(key, (D, SPLITS, LOCAL_COLS)) * 0.02


def draw_momentum_out(key, part):
    key = jax.random.fold_in(key, 11)
    return jax.random.normal(key, (SPLITS, LOCAL_COLS, D)) * 0.02


def draw_momentum_shared(key, part):
    key = jax.random.fold_in(key, 12)
    return jax.random.normal(key, (D, SHARED_COLS)) * shared_vector(0.02, 0.2)[None, :]


def steps_of(stream_key, extent, shards, least, high):
    gain, own = 1.0, jax.random.fold_in(stream_key, 6)
    for position, blocks in shards:
        draws = jnp.exp(jax.random.uniform(jax.random.fold_in(own, position), (blocks,), jnp.float32, least / len(shards), high / len(shards)))
        gain = gain * jnp.repeat(draws, extent[position] // blocks).reshape([-1 if axis == position else 1 for axis in range(len(extent))])
    return gain


def length_profile(amount, total, most, slope):
    loads = [(1 << 20) // math.isqrt(grade ** slope) + 1 for grade in range(2, amount + 1)]
    spare, holding = total - most - (amount - 1), [1] * (amount - 1)
    while spare > 0:
        free = [i for i in range(amount - 1) if holding[i] < most]
        whole, left = sum([loads[i] for i in free]), spare
        for i in free:
            more = min(most - holding[i], max(1, left * loads[i] // whole), spare)
            holding[i] = holding[i] + more
            spare = spare - more
    return np.array([most] + holding)


def uneven(key, count, total, bound, lean):
    if count == 2:
        one = jax.random.randint(key, (), max(1, total - bound), min(bound, total - 1) + 1)
        return jnp.stack([one, total - one])
    sizes = jnp.asarray(length_profile(count, total, bound, lean), jnp.int32)
    pairs = (count - 1) // 2
    giver, receiver = sizes[1:1 + 2 * pairs:2], sizes[2:2 + 2 * pairs:2]
    room = jnp.minimum(giver - 1, bound - receiver)
    shifted = jax.random.randint(jax.random.fold_in(key, 1), (pairs,), 0, 1 << 20) % (room + 1)
    sizes = sizes.at[1:1 + 2 * pairs:2].set(giver - shifted).at[2:2 + 2 * pairs:2].set(receiver + shifted)
    return sizes[jax.random.permutation(jax.random.fold_in(key, 2), count)]


def noise(own_key, dims, deviation, bound, pieces=(), kind=jnp.bfloat16):
    drawn = deviation * jax.random.normal(own_key, dims, jnp.float32)
    if pieces:
        drawn = drawn * steps_of(own_key, dims, pieces, -0.22, 0.18)
    return jnp.clip(drawn, -bound, bound).astype(kind)


def setup_inputs(seed: int = 0) -> dict:
    arg_keys = jax.random.split(jax.random.key(seed), 19)
    return {
        "tokens": noise(arg_keys[0], (TOKENS, D), 1.0, 6.0, ((0, 16),)),
        "doc_lengths": jax.vmap(lambda own: uneven(own, DOCS, TOK_DEV, MOST, 0))(jax.random.split(arg_keys[1], SEQS)).reshape((SEQS, DOCS)).astype(jnp.int32),
        "cotangent": noise(arg_keys[2], (TOKENS, D), 1.0, 6.0, ((0, 16),)),
        "inner_in": draw_inner_in(jax.random.fold_in(arg_keys[18], 71), 0),
        "inner_out": draw_inner_out(jax.random.fold_in(arg_keys[18], 71), 0),
        "inner_shared": draw_inner_shared(jax.random.fold_in(arg_keys[18], 71), 0),
        "first_in": draw_first_in(jax.random.fold_in(arg_keys[18], 71), 0),
        "first_out": draw_first_out(jax.random.fold_in(arg_keys[18], 71), 0),
        "first_shared": draw_first_shared(jax.random.fold_in(arg_keys[18], 71), 0),
        "second_in": draw_second_in(jax.random.fold_in(arg_keys[18], 71), 0),
        "second_out": draw_second_out(jax.random.fold_in(arg_keys[18], 71), 0),
        "second_shared": draw_second_shared(jax.random.fold_in(arg_keys[18], 71), 0),
        "outer_in": draw_outer_in(jax.random.fold_in(arg_keys[18], 71), 0),
        "outer_out": draw_outer_out(jax.random.fold_in(arg_keys[18], 71), 0),
        "outer_shared": draw_outer_shared(jax.random.fold_in(arg_keys[18], 71), 0),
        "momentum_in": draw_momentum_in(jax.random.fold_in(arg_keys[18], 71), 0),
        "momentum_out": draw_momentum_out(jax.random.fold_in(arg_keys[18], 71), 0),
        "momentum_shared": draw_momentum_shared(jax.random.fold_in(arg_keys[18], 71), 0),
    }


norm_eps = 1e-05
masked_fill = -1e+30
beta_one = 0.9
beta_two = 0.95
adam_eps = 1e-08
rate_matrix = 0.02
rate_vector = 0.2
weight_decay = 0.1
outer_beta = 0.9
outer_rate = 0.7
clip_limit = 5.0

@jax.custom_vjp
def low(v):
    return lax.optimization_barrier(v.astype(jnp.bfloat16)).astype(jnp.float32)

@jax.custom_vjp
def low_back(v):
    return v

def low_keep(v):
    return (low(v), None)

def low_pass(kept, grad):
    return (grad,)

def back_keep(v):
    return (v, None)

def back_low(kept, grad):
    return (low(grad),)
low.defvjp(low_keep, low_pass)
low_back.defvjp(back_keep, back_low)

def product(left_side, right_side):
    return jnp.dot(left_side, right_side, precision=lax.Precision.HIGHEST, preferred_element_type=jnp.float32)

def layer_norm(inputs, gain_vec, bias_vec):
    centered = inputs - lax.optimization_barrier(jnp.mean(inputs, axis=-1, keepdims=True))
    inv_std = lax.rsqrt(lax.optimization_barrier(jnp.mean(centered * centered, axis=-1, keepdims=True)) + norm_eps)
    return centered * inv_std * gain_vec + bias_vec

def visible_pairs(lengths, token_count):
    doc_ends = jnp.cumsum(lengths).astype(jnp.int32)
    doc_starts = (doc_ends - lengths).astype(jnp.int32)
    places = jnp.arange(token_count, dtype=jnp.int32)
    doc_ids = lax.optimization_barrier(jnp.sum((places[:, None] >= doc_ends[None, :]).astype(jnp.int32), axis=1)).astype(jnp.int32)
    owners = doc_ids[:, None] == jnp.arange(lengths.shape[0], dtype=jnp.int32)[None, :]
    doc_begin = lax.optimization_barrier(jnp.sum(jnp.where(owners, doc_starts[None, :], 0), axis=1)).astype(jnp.int32)
    blocks = ((places - doc_begin) // BLOCK).astype(jnp.int32)
    return (doc_ids[:, None] == doc_ids[None, :]) & (blocks[None, :] <= blocks[:, None])

def lookup(table_vals, indices):
    return lax.optimization_barrier(jnp.sum(jnp.where(indices[..., None] == jnp.arange(HEADS, dtype=jnp.int32), table_vals, 0.0), axis=-1))

def block_forward(weights, token_rows, lengths):
    w_query, w_up, w_attn, w_down, w_keyval, gain_one, bias_one, gain_two, bias_two, bias_query, bias_out, bias_down, bias_up = weights
    token_count = token_rows.shape[0]
    normed = low(layer_norm(token_rows, gain_one, bias_one))
    queries = low(low_back(product(normed, w_query) + bias_query))
    key_value = low(low_back(product(normed, w_keyval)))
    key_rows = key_value[:, :HD]
    values = key_value[:, HD:]
    visible = visible_pairs(lengths, token_count)
    query_heads = queries.reshape(token_count, HEADS, HD).transpose(1, 0, 2)

    def one_head(head_rows):
        scores = low_back(product(head_rows, key_rows.T) * HD ** (-0.5))
        masked = jnp.where(visible, scores, masked_fill)
        row_top = lax.optimization_barrier(jnp.max(masked, axis=1, keepdims=True))
        log_total = row_top + jnp.log(lax.optimization_barrier(jnp.sum(jnp.exp(masked - row_top), axis=1, keepdims=True)))
        attn_probs = low(jnp.exp(masked - log_total))
        return (product(attn_probs, values), jnp.max(masked))
    mixed_rows, peak_vals = lax.map(jax.checkpoint(one_head), query_heads)
    attended = low(low_back(mixed_rows.transpose(1, 0, 2).reshape(token_count, D)))
    middle = token_rows + low_back(product(attended, w_attn) + bias_out)
    normed_two = low(layer_norm(middle, gain_two, bias_two))
    pre_act = low_back(product(normed_two, w_up) + bias_up)
    hidden = low(jax.nn.gelu(pre_act, approximate=True))
    return (middle + low_back(product(hidden, w_down) + bias_down), peak_vals)

def group_forward(token_rows, weights, lengths):
    rounded = tuple((low(entry) for entry in weights[:5])) + tuple(weights[5:])

    def one_slot(running, slot_item):
        slot_out, slot_peaks = block_forward(rounded, slot_item[0], slot_item[1])
        return (running, (slot_out, slot_peaks))
    running, (slot_outs, slot_peaks) = lax.scan(jax.checkpoint(one_slot), jnp.zeros((), jnp.float32), (token_rows, lengths))
    return (slot_outs, slot_peaks)

def unpack(group_in, group_out, group_shared):
    query_cols = D // SPLITS
    vec_base = 2 * HD
    w_query = group_in[:, :, :query_cols].reshape(D, D)
    w_up = group_in[:, :, query_cols:].reshape(D, FF)
    w_attn = group_out[:, :query_cols, :].reshape(D, D)
    w_down = group_out[:, query_cols:, :].reshape(FF, D)
    w_keyval = group_shared[:, :vec_base]
    vectors = tuple((group_shared[:, vec_base + column] for column in range(7)))
    bias_up = group_shared[:, vec_base + 7:].T.reshape(FF)
    return (w_query, w_up, w_attn, w_down, w_keyval) + vectors + (bias_up,)

def pack(gradients):
    query_cols = D // SPLITS
    grad_in = jnp.concatenate([gradients[0].reshape(D, SPLITS, query_cols), gradients[1].reshape(D, SPLITS, FF // SPLITS)], axis=2)
    grad_out = jnp.concatenate([gradients[2].reshape(SPLITS, query_cols, D), gradients[3].reshape(SPLITS, FF // SPLITS, D)], axis=1)
    vector_grads = jnp.stack(list(gradients[5:12]), axis=1)
    grad_shared = jnp.concatenate([gradients[4], vector_grads, gradients[12].reshape(FF // D, D).T], axis=1)
    return (grad_in, grad_out, grad_shared)

def adam_step(gradient, weight, moment_one, moment_two, step_rate, step_decay):
    new_one = beta_one * moment_one + (1.0 - beta_one) * gradient
    new_two = beta_two * moment_two + (1.0 - beta_two) * gradient * gradient
    direction = new_one / (1.0 - beta_one ** STEP) / (jnp.sqrt(new_two / (1.0 - beta_two ** STEP)) + adam_eps)
    return (new_one, new_two, weight - step_rate * (direction + step_decay * weight))

def reference(tokens, doc_lengths, cotangent, inner_in, inner_out, inner_shared, first_in, first_out, first_shared, second_in, second_out, second_shared, outer_in, outer_out, outer_shared, momentum_in, momentum_out, momentum_shared):
    slot_tokens = N_DP * TOK_DEV
    column_ids = jnp.arange(SHARED_COLS, dtype=jnp.int32)
    rate_cols = jnp.where(column_ids < 2 * HD, rate_matrix, rate_vector)
    decay_cols = jnp.where(column_ids < 2 * HD, weight_decay, 0.0)
    out_list, grad_list, peak_list = ([], [], [])
    firsts = ([], [], [])
    seconds = ([], [], [])
    delta_sums = [jnp.zeros_like(outer_in), jnp.zeros_like(outer_out), jnp.zeros_like(outer_shared)]
    outers = (outer_in, outer_out, outer_shared)
    for group_id in range(GROUPS):
        token_rows = tokens[group_id * slot_tokens:(group_id + 1) * slot_tokens].astype(jnp.float32).reshape(N_DP, TOK_DEV, D)
        cot_rows = cotangent[group_id * slot_tokens:(group_id + 1) * slot_tokens].astype(jnp.float32).reshape(N_DP, TOK_DEV, D)
        lengths = doc_lengths[group_id * N_DP:(group_id + 1) * N_DP]
        weights = unpack(inner_in[group_id], inner_out[group_id], inner_shared[group_id])

        def forward_group(token_arg, *weight_args):
            return group_forward(token_arg, weight_args, lengths)
        slot_outs, pull_back, peak_vals = jax.vjp(forward_group, token_rows, *weights, has_aux=True)
        gradients = pull_back(cot_rows)
        out_list.append(slot_outs.reshape(slot_tokens, D))
        grad_list.append(gradients[0].reshape(slot_tokens, D))
        peak_list.append(lax.optimization_barrier(jnp.max(peak_vals, axis=0)))
        packed = pack(gradients[1:])
        inners = (inner_in[group_id], inner_out[group_id], inner_shared[group_id])
        ones = (first_in[group_id], first_out[group_id], first_shared[group_id])
        twos = (second_in[group_id], second_out[group_id], second_shared[group_id])
        rates = (rate_matrix, rate_matrix, rate_cols)
        decays = (weight_decay, weight_decay, decay_cols)
        for kind in range(3):
            new_one, new_two, stepped = adam_step(packed[kind], inners[kind], ones[kind], twos[kind], rates[kind], decays[kind])
            firsts[kind].append(new_one)
            seconds[kind].append(new_two)
            delta_sums[kind] = delta_sums[kind] + (outers[kind] - stepped)
    peak_all = lax.optimization_barrier(jnp.max(jnp.stack(peak_list, axis=0), axis=0))
    clip_vec = clip_limit / jnp.maximum(peak_all, clip_limit)
    query_cols = D // SPLITS
    local_ids = jnp.arange(LOCAL_COLS, dtype=jnp.int32)
    split_ids = jnp.arange(SPLITS, dtype=jnp.int32)
    head_of = split_ids[:, None] * (HEADS // SPLITS) + jnp.minimum(local_ids, query_cols - 1)[None, :] // HD
    factor_in = jnp.where(local_ids[None, :] < query_cols, lookup(clip_vec, head_of), 1.0)
    row_ids = jnp.arange(D, dtype=jnp.int32)
    factor_shared = jnp.where(column_ids[None, :] == 2 * HD + 4, lookup(clip_vec, row_ids // HD)[:, None], 1.0)
    factors = (factor_in[None, :, :], 1.0, factor_shared)
    moments = (momentum_in, momentum_out, momentum_shared)
    means, velocities, new_outers = ([], [], [])
    for kind in range(3):
        mean_delta = delta_sums[kind] / GROUPS
        velocity = outer_beta * moments[kind] + mean_delta
        means.append(mean_delta)
        velocities.append(velocity)
        new_outers.append((outers[kind] - outer_rate * (mean_delta + outer_beta * velocity)) * factors[kind])
    block_out = jnp.concatenate(out_list, axis=0).astype(jnp.bfloat16)
    tokens_grad = jnp.concatenate(grad_list, axis=0).astype(jnp.bfloat16)
    return (block_out, tokens_grad, clip_vec, jnp.stack(firsts[0], axis=0), jnp.stack(firsts[1], axis=0), jnp.stack(firsts[2], axis=0), jnp.stack(seconds[0], axis=0), jnp.stack(seconds[1], axis=0), jnp.stack(seconds[2], axis=0), means[0], means[1], means[2], velocities[0], velocities[1], velocities[2], new_outers[0], new_outers[1], new_outers[2], new_outers[0].astype(jnp.bfloat16), new_outers[1].astype(jnp.bfloat16), new_outers[2].astype(jnp.bfloat16))
```

```python
import jax
import jax.numpy as jnp
from jax import lax
from jax.experimental import pallas as pl
from jax.experimental.pallas import tpu as pltpu
from jax.sharding import PartitionSpec as P

HEADS = 16
HD = 128
FF = 8192
BLOCK = 256
STEP = 10

norm_eps = 1e-05
hidden_score = -1e30
shown_score = 3e38
beta_one = 0.9
beta_two = 0.95
adam_eps = 1e-08
rate_matrix = 0.02
rate_vector = 0.2
weight_decay = 0.1
outer_beta = 0.9
outer_rate = 0.7
clip_limit = 5.0
score_scale = HD ** (-0.5)
log2_e = 1.4426950408889634
correct_one = 1.0 / (1.0 - beta_one**STEP)
correct_two = 1.0 / (1.0 - beta_two**STEP)

f32 = jnp.float32
bf16 = jnp.bfloat16
ROWS = 128
LANES = 128
VMEM_LIMIT = 40 * 1024 * 1024


def shape(dims, dtype):
    return jax.ShapeDtypeStruct(dims, dtype)


def call(body, out_shape, grid, in_specs, out_specs, args, *, ids=(), scratch=(), aliases=None,
         flops=0, name=None):
    outs = out_shape if isinstance(out_shape, (list, tuple)) else [out_shape]
    moved = sum(a.size * a.dtype.itemsize for a in args)
    moved += sum(o.size * o.dtype.itemsize for o in outs)
    return pl.pallas_call(
        body,
        out_shape=out_shape,
        grid_spec=pltpu.PrefetchScalarGridSpec(
            num_scalar_prefetch=len(ids),
            grid=grid,
            in_specs=in_specs,
            out_specs=out_specs,
            scratch_shapes=list(scratch),
        ),
        input_output_aliases=aliases or {},
        compiler_params=pltpu.CompilerParams(vmem_limit_bytes=VMEM_LIMIT),
        cost_estimate=pl.CostEstimate(flops=flops, bytes_accessed=moved, transcendentals=0),
        name=name,
    )(*ids, *args)


def pick_blocks(array, block_ids, width, count, stacked):
    rows = array.shape[0]
    if width % LANES:
        taken = jnp.take(array.reshape(rows, -1, width), block_ids, axis=1)
        return taken.transpose(1, 0, 2) if stacked else taken.reshape(rows, count * width)

    def body(ids_ref, in_ref, out_ref):
        if stacked:
            out_ref[0] = in_ref[...]
        else:
            out_ref[...] = in_ref[...]

    if stacked:
        out, spec = shape((count, rows, width), array.dtype), pl.BlockSpec(
            (1, rows, width), lambda j, ids: (j, 0, 0)
        )
    else:
        out, spec = shape((rows, count * width), array.dtype), pl.BlockSpec(
            (rows, width), lambda j, ids: (0, j)
        )
    return call(
        body, out, (count,), [pl.BlockSpec((rows, width), lambda j, ids: (0, ids[j]))], spec,
        [array], ids=[block_ids], name="pick_blocks",
    )


def columns_of(block_id, width):
    return pl.ds(pl.multiple_of(block_id * width, width), width)


def placing(array, ids, count):
    part = array.shape[1] // count
    if part % LANES == 0:
        return array, count, part
    return pick_blocks(array, ids, part, count, False), 0, part


def put_back(array, ids, count):
    part = array.shape[1] // count
    if part % LANES == 0:
        return array
    back = jnp.sum(
        jnp.where(ids[None, :] == jnp.arange(count)[:, None], jnp.arange(count)[None, :], 0), axis=1
    ).astype(jnp.int32)
    return pick_blocks(array, back, part, count, False)


def norm_stats(rows):
    mean = jnp.mean(rows, axis=-1, keepdims=True)
    centered = rows - mean
    inv = lax.rsqrt(jnp.mean(centered * centered, axis=-1, keepdims=True) + norm_eps)
    return centered * inv, inv


def row_spec(cols, rows=ROWS):
    return pl.BlockSpec((rows, cols), lambda i, *ids: (i, 0))


def whole_spec(rows, cols):
    return pl.BlockSpec((rows, cols), lambda i, *ids: (0, 0))


def first_norm(tokens, ids, gain, bias, count):
    total, width = tokens.shape
    tokens, moved, part = placing(tokens, ids, count)

    def body(ids_ref, x_ref, g_ref, c_ref, x_out, n_out):
        for o in range(moved):
            x_out[:, o * part : (o + 1) * part] = x_ref[:, columns_of(ids_ref[o], part)]
        if not moved:
            x_out[...] = x_ref[...]
        unit, _ = norm_stats(x_out[...].astype(f32))
        n_out[...] = (unit * g_ref[...] + c_ref[...]).astype(bf16)

    return call(
        body,
        [shape((total, width), bf16)] * 2,
        (total // ROWS,),
        [row_spec(width), whole_spec(1, width), whole_spec(1, width)],
        [row_spec(width)] * 2,
        [tokens, gain, bias],
        ids=[ids],
        name="first_norm",
    )


def cotangent_order(cotangent, ids, count):
    total, width = cotangent.shape
    cotangent, moved, part = placing(cotangent, ids, count)

    def body(ids_ref, c_ref, c_out, sum_out):
        for o in range(moved):
            c_out[:, o * part : (o + 1) * part] = c_ref[:, columns_of(ids_ref[o], part)]
        if not moved:
            c_out[...] = c_ref[...]
        add_rows(sum_out, c_out[...].astype(f32))

    return call(
        body,
        [shape((total, width), bf16), shape((1, width), f32)],
        (total // ROWS,),
        [row_spec(width)],
        [row_spec(width), whole_spec(1, width)],
        [cotangent],
        ids=[ids],
        name="cotangent_order",
    )


def add_rows(sum_ref, values):
    @pl.when(pl.program_id(0) == 0)
    def _():
        sum_ref[...] = jnp.zeros_like(sum_ref)

    sum_ref[...] += jnp.sum(values, axis=0, keepdims=True)


def middle_norm(x_rel, part_own, part_other, bias_out, gain, bias):
    total, width = x_rel.shape

    def body(x_ref, a_ref, b_ref, bo_ref, g_ref, c_ref, h_out, n_out):
        mid = x_ref[...].astype(f32) + (
            a_ref[...].astype(f32) + b_ref[...].astype(f32)
        ) + bo_ref[...]
        h_out[...] = mid
        unit, _ = norm_stats(mid)
        n_out[...] = (unit * g_ref[...] + c_ref[...]).astype(bf16)

    return call(
        body,
        [shape((total, width), f32), shape((total, width), bf16)],
        (total // ROWS,),
        [row_spec(width)] * 3 + [whole_spec(1, width)] * 3,
        [row_spec(width)] * 2,
        [x_rel, part_own, part_other, bias_out, gain, bias],
        name="middle_norm",
    )


def block_result(middle, part_own, part_other, bias_down, ids, count):
    total, width = middle.shape
    part = width // count

    def body(ids_ref, h_ref, a_ref, b_ref, b2_ref, out_ref):
        value = (
            h_ref[...] + (a_ref[...].astype(f32) + b_ref[...].astype(f32)) + b2_ref[...]
        ).astype(bf16)
        if part % LANES:
            out_ref[...] = value
        else:
            for o in range(count):
                out_ref[:, columns_of(ids_ref[o], part)] = value[:, o * part : (o + 1) * part]

    result = call(
        body,
        shape((total, width), bf16),
        (total // ROWS,),
        [row_spec(width)] * 3 + [whole_spec(1, width)],
        row_spec(width),
        [middle, part_own, part_other, bias_down],
        ids=[ids],
        name="block_result",
    )
    return put_back(result, ids, count)


def middle_backward(middle, part_own, part_other, cot_rel, gain):
    total, width = middle.shape

    def body(h_ref, a_ref, b_ref, dy_ref, g_ref, dh_out, low_out, gg_out, gc_out, gbo_out):
        unit, inv = norm_stats(h_ref[...])
        grad = a_ref[...].astype(f32) + b_ref[...].astype(f32)
        scaled = grad * g_ref[...]
        dh = dy_ref[...].astype(f32) + inv * (
            scaled
            - jnp.mean(scaled, axis=-1, keepdims=True)
            - unit * jnp.mean(scaled * unit, axis=-1, keepdims=True)
        )
        dh_out[...] = dh
        low = dh.astype(bf16)
        low_out[...] = low
        add_rows(gg_out, grad * unit)
        add_rows(gc_out, grad)
        add_rows(gbo_out, low.astype(f32))

    vec = shape((1, width), f32)
    return call(
        body,
        [shape((total, width), f32), shape((total, width), bf16), vec, vec, vec],
        (total // ROWS,),
        [row_spec(width)] * 4 + [whole_spec(1, width)],
        [row_spec(width)] * 2 + [whole_spec(1, width)] * 3,
        [middle, part_own, part_other, cot_rel, gain],
        name="middle_backward",
    )


def first_backward(x_rel, part_own, part_other, keyval_grad, w_keyval_t, dh, gain, ids, count):
    total, width = x_rel.shape
    part = width // count
    kv = keyval_grad.shape[1]

    def body(ids_ref, x_ref, a_ref, b_ref, kv_ref, w_ref, dh_ref, g_ref, t_out, gg_out, gc_out):
        unit, inv = norm_stats(x_ref[...].astype(f32))
        grad = (a_ref[...].astype(f32) + b_ref[...].astype(f32)) + jnp.dot(
            kv_ref[...], w_ref[...], preferred_element_type=f32
        )
        scaled = grad * g_ref[...]
        value = dh_ref[...] + inv * (
            scaled
            - jnp.mean(scaled, axis=-1, keepdims=True)
            - unit * jnp.mean(scaled * unit, axis=-1, keepdims=True)
        )
        low = value.astype(bf16)
        if part % LANES:
            t_out[...] = low
        else:
            for o in range(count):
                t_out[:, columns_of(ids_ref[o], part)] = low[:, o * part : (o + 1) * part]
        add_rows(gg_out, grad * unit)
        add_rows(gc_out, grad)

    vec = shape((1, width), f32)
    result, gain_grad, bias_grad = call(
        body,
        [shape((total, width), bf16), vec, vec],
        (total // ROWS,),
        [row_spec(width)] * 3
        + [row_spec(kv), whole_spec(kv, width), row_spec(width), whole_spec(1, width)],
        [row_spec(width)] + [whole_spec(1, width)] * 2,
        [x_rel, part_own, part_other, keyval_grad, w_keyval_t, dh, gain],
        ids=[ids],
        flops=2 * total * width * kv,
        name="first_backward",
    )
    return put_back(result, ids, count), gain_grad, bias_grad


TILE = 256


def score_limits(lengths, token_count):
    doc_ends = jnp.cumsum(lengths)
    doc_starts = doc_ends - lengths
    places = jnp.arange(token_count, dtype=jnp.int32)
    doc_ids = jnp.sum((places[:, None] >= doc_ends[None, :]).astype(jnp.int32), axis=1)
    owners = doc_ids[:, None] == jnp.arange(lengths.shape[0], dtype=jnp.int32)[None, :]
    doc_begin = jnp.sum(jnp.where(owners, doc_starts[None, :], 0), axis=1)
    blocks = (places - doc_begin) // BLOCK
    seen = (doc_ids[:, None] == doc_ids[None, :]) & (blocks[None, :] <= blocks[:, None])
    seen_t = (doc_ids[None, :] == doc_ids[:, None]) & (blocks[:, None] <= blocks[None, :])
    pick = lambda s: jnp.where(s, shown_score, hidden_score).astype(f32)
    return pick(seen), pick(seen_t)


def attention_forward(queries, key_value, limits, heads):
    total = queries.shape[0]
    tiles = total // TILE
    c = score_scale * log2_e

    def body(q_ref, kv_ref, lim_ref, o_ref, lse_ref, top_ref):
        tile, head = pl.program_id(0), pl.program_id(1)
        k = kv_ref[:, :HD]
        v = kv_ref[:, HD:]
        s = lax.dot_general(
            q_ref[...], k, (((1,), (1,)), ((), ())), preferred_element_type=f32
        )
        s = jnp.minimum(s, lim_ref[...])
        m = jnp.max(s, axis=1, keepdims=True)
        p = jnp.exp2((s - m) * c)
        l = jnp.sum(p, axis=1, keepdims=True)
        o = jnp.dot(p.astype(bf16), v, preferred_element_type=f32)
        o_ref[...] = (o / l).astype(bf16)
        lane = lax.broadcasted_iota(jnp.int32, (TILE, LANES), 1)
        lse = m * c + jnp.log2(l)
        lse_ref[...] = jnp.where(lane == head, lse, lse_ref[...])

        @pl.when((tile == 0) & (head == 0))
        def _():
            top_ref[...] = jnp.full_like(top_ref, hidden_score)

        row = lax.broadcasted_iota(jnp.int32, (heads, LANES), 0)
        best = jnp.max(m, axis=0, keepdims=True) * score_scale
        top_ref[...] = jnp.where(row == head, jnp.maximum(top_ref[...], best), top_ref[...])

    return call(
        body,
        [shape((total, heads * HD), bf16), shape((total, LANES), f32), shape((heads, LANES), f32)],
        (tiles, heads),
        [
            pl.BlockSpec((TILE, HD), lambda i, h: (i, h)),
            pl.BlockSpec((total, 2 * HD), lambda i, h: (0, 0)),
            pl.BlockSpec((TILE, total), lambda i, h: (i, 0)),
        ],
        [
            pl.BlockSpec((TILE, HD), lambda i, h: (i, h)),
            pl.BlockSpec((TILE, LANES), lambda i, h: (i, 0)),
            pl.BlockSpec((heads, LANES), lambda i, h: (0, 0)),
        ],
        [queries, key_value, limits],
        flops=8 * total * total * HD * heads,
        name="attention_forward",
    )


def attention_backward(queries, grad_att, key_value, limits_t, lse_t, dot_t, heads):
    total = queries.shape[0]
    tiles = total // TILE
    c = score_scale * log2_e

    def body(q_ref, da_ref, kv_ref, lim_ref, lse_ref, dot_ref, dq_ref, dkv_ref):
        tile, head = pl.program_id(0), pl.program_id(1)
        k = kv_ref[:, :HD]
        v = kv_ref[:, HD:]
        q = q_ref[...]
        da = da_ref[...]
        nt = (((1,), (1,)), ((), ()))
        s = lax.dot_general(k, q, nt, preferred_element_type=f32)
        s = jnp.minimum(s, lim_ref[...])
        p = jnp.exp2(s * c - lse_ref[pl.ds(head, 1), :])
        dp = lax.dot_general(v, da, nt, preferred_element_type=f32)
        ds = (p * (dp - dot_ref[pl.ds(head, 1), :])).astype(bf16)
        dq = lax.dot_general(ds, k, (((0,), (0,)), ((), ())), preferred_element_type=f32)
        dq_ref[...] = (dq * score_scale).astype(bf16)

        @pl.when((tile == 0) & (head == 0))
        def _():
            dkv_ref[...] = jnp.zeros_like(dkv_ref)

        dkv_ref[:, :HD] += jnp.dot(ds, q, preferred_element_type=f32) * score_scale
        dkv_ref[:, HD:] += jnp.dot(p.astype(bf16), da, preferred_element_type=f32)

    return call(
        body,
        [shape((total, heads * HD), bf16), shape((total, 2 * HD), f32)],
        (tiles, heads),
        [
            pl.BlockSpec((TILE, HD), lambda i, h: (i, h)),
            pl.BlockSpec((TILE, HD), lambda i, h: (i, h)),
            pl.BlockSpec((total, 2 * HD), lambda i, h: (0, 0)),
            pl.BlockSpec((total, TILE), lambda i, h: (0, i)),
            pl.BlockSpec((heads, TILE), lambda i, h: (0, i)),
            pl.BlockSpec((heads, TILE), lambda i, h: (0, i)),
        ],
        [
            pl.BlockSpec((TILE, HD), lambda i, h: (i, h)),
            pl.BlockSpec((total, 2 * HD), lambda i, h: (0, 0)),
        ],
        [queries, grad_att, key_value, limits_t, lse_t, dot_t],
        flops=20 * total * total * HD * heads,
        name="attention_backward",
    )


def adam_values(gradient, weight, one, two, rate, decay):
    new_one = beta_one * one + (1.0 - beta_one) * gradient
    new_two = beta_two * two + (1.0 - beta_two) * gradient * gradient
    direction = (new_one * correct_one) / (jnp.sqrt(new_two * correct_two) + adam_eps)
    return new_one, new_two, weight - rate * (direction + decay * weight)


def to_tiles(flat, tiles_ref):
    for j in range(8):
        tiles_ref[:, j, :] = flat[:, j * LANES : (j + 1) * LANES]


def adam_in(gradient, weight, one, two, outer, start, full):
    rows, cols = gradient.shape
    step = 64
    base = start // 1024
    tall = pl.BlockSpec((step, 8, LANES), lambda i, j: (i, base + j, 0))
    flat = pl.BlockSpec((step, 1024), lambda i, j: (i, j))
    args = [gradient, weight, one, two, outer]
    specs = [flat] + [tall] * 4
    aliases = {}
    if full is not None:
        aliases = {5: 0, 6: 1}
        args += list(full)
        specs += [pl.BlockSpec(memory_space=pl.ANY)] * 2

    def body(g_ref, w_ref, one_ref, two_ref, out_ref, *rest):
        one_out, two_out, delta_out, grad_tiles, delta_tiles = rest[-5:]
        to_tiles(g_ref[...].astype(f32), grad_tiles)
        new_one, new_two, stepped = adam_values(
            grad_tiles[...], w_ref[...], one_ref[...], two_ref[...], rate_matrix, weight_decay
        )
        one_out[...] = new_one
        two_out[...] = new_two
        delta_tiles[...] = out_ref[...] - stepped
        for j in range(8):
            delta_out[:, j * LANES : (j + 1) * LANES] = delta_tiles[:, j, :].astype(bf16)

    whole = shape(weight.shape, f32)
    return call(
        body,
        [whole, whole, shape((rows, cols), bf16)],
        (rows // step, cols // 1024),
        specs,
        [tall, tall, flat],
        args,
        scratch=[pltpu.VMEM((step, 8, LANES), f32)] * 2,
        aliases=aliases,
        name="adam_in",
    )


def adam_out(gradient, weight, one, two, outer, start, full):
    rows, cols = gradient.shape
    step = 512
    base = start // step
    tall = pl.BlockSpec((step, cols), lambda i: (base + i, 0))
    flat = pl.BlockSpec((step, cols), lambda i: (i, 0))
    args = [gradient, weight, one, two, outer]
    specs = [flat] + [tall] * 4
    aliases = {}
    if full is not None:
        aliases = {5: 0, 6: 1}
        args += list(full)
        specs += [pl.BlockSpec(memory_space=pl.ANY)] * 2

    def body(g_ref, w_ref, one_ref, two_ref, out_ref, *rest):
        one_out, two_out, delta_out = rest[-3:]
        new_one, new_two, stepped = adam_values(
            g_ref[...].astype(f32), w_ref[...], one_ref[...], two_ref[...], rate_matrix,
            weight_decay,
        )
        one_out[...] = new_one
        two_out[...] = new_two
        delta_out[...] = (out_ref[...] - stepped).astype(bf16)

    whole = shape(weight.shape, f32)
    return call(
        body,
        [whole, whole, shape((rows, cols), bf16)],
        (rows // step,),
        specs,
        [tall, tall, flat],
        args,
        aliases=aliases,
        name="adam_out",
    )


def outer_values(mean, momentum, outer):
    velocity = outer_beta * momentum + mean
    return velocity, outer - outer_rate * (mean + outer_beta * velocity)


def outer_in(own, other, momentum, outer, factor, start, full):
    rows, cols = own.shape
    step = 64
    base = start // 1024
    tall = pl.BlockSpec((step, 8, LANES), lambda i, j: (i, base + j, 0))
    flat = pl.BlockSpec((step, 1024), lambda i, j: (i, j))
    wide = pl.BlockSpec((step, 1024), lambda i, j: (i, base + j))
    args = [own, other, momentum, outer]
    specs = [flat, flat, tall, tall]
    if factor is not None:
        args.append(factor)
        specs.append(pl.BlockSpec((8, LANES), lambda i, j: (0, 0)))
    aliases = {}
    if full is not None:
        aliases = {len(args) + k: k for k in range(4)}
        args += list(full)
        specs += [pl.BlockSpec(memory_space=pl.ANY)] * 4

    def body(own_ref, other_ref, mom_ref, out_ref, *rest):
        mean_out, vel_out, new_out, copy_out, mean_tiles, new_tiles = rest[-6:]
        to_tiles((own_ref[...].astype(f32) + other_ref[...].astype(f32)) * 0.5, mean_tiles)
        mean = mean_tiles[...]
        velocity, fresh = outer_values(mean, mom_ref[...], out_ref[...])
        if factor is not None:
            fresh = fresh * rest[0][...][None]
        mean_out[...] = mean
        vel_out[...] = velocity
        new_out[...] = fresh
        new_tiles[...] = fresh
        for j in range(8):
            copy_out[:, j * LANES : (j + 1) * LANES] = new_tiles[:, j, :].astype(bf16)

    whole = shape(outer.shape, f32)
    return call(
        body,
        [whole, whole, whole, shape((rows, outer.shape[1] * LANES), bf16)],
        (rows // step, cols // 1024),
        specs,
        [tall, tall, tall, wide],
        args,
        scratch=[pltpu.VMEM((step, 8, LANES), f32)] * 2,
        aliases=aliases,
        name="outer_in",
    )


def outer_out(own, other, momentum, outer, start, full):
    rows, cols = own.shape
    step = 512
    base = start // step
    tall = pl.BlockSpec((step, cols), lambda i: (base + i, 0))
    flat = pl.BlockSpec((step, cols), lambda i: (i, 0))
    args = [own, other, momentum, outer]
    specs = [flat, flat, tall, tall]
    aliases = {}
    if full is not None:
        aliases = {4 + k: k for k in range(4)}
        args += list(full)
        specs += [pl.BlockSpec(memory_space=pl.ANY)] * 4

    def body(own_ref, other_ref, mom_ref, out_ref, *rest):
        mean_out, vel_out, new_out, copy_out = rest[-4:]
        mean = (own_ref[...].astype(f32) + other_ref[...].astype(f32)) * 0.5
        velocity, fresh = outer_values(mean, mom_ref[...], out_ref[...])
        mean_out[...] = mean
        vel_out[...] = velocity
        new_out[...] = fresh
        copy_out[...] = fresh.astype(bf16)

    whole = shape(outer.shape, f32)
    return call(
        body,
        [whole, whole, whole, shape(outer.shape, bf16)],
        (rows // step,),
        specs,
        [tall] * 4,
        args,
        aliases=aliases,
        name="outer_out",
    )


class Lane:
    def __init__(self, pairs, window):
        self.pairs, self.window, self.landed = pairs, window, []

    def send(self, block):
        if len(self.landed) >= self.window:
            block, _ = lax.optimization_barrier((block, self.landed[-self.window]))
        arrived = lax.ppermute(block, "dp", self.pairs)
        self.landed.append(arrived)
        return arrived


def halves(block):
    cut = -(-(block.shape[0] // 2) // 16) * 16
    return block[:cut], block[cut:]


def gather_steps(block, up, down, count):
    far = count // 2
    held = {0: block}
    from_below, from_above = block, block
    for k in range(1, far):
        from_below = up.send(from_below)
        from_above = down.send(from_above)
        held[count - k], held[k] = from_below, from_above
        yield
    top_half = up.send(halves(from_below)[0])
    low_half = down.send(halves(from_above)[1])
    held[far] = (top_half, low_half)
    yield
    return held


def scatter_steps(part, up, down, count, low):
    far = count // 2
    first = part(far)
    top, bottom = halves(first.astype(low))
    rise, fall = up.send(top), down.send(bottom)
    yield
    for k in range(1, far):
        ahead, behind = part(far - k), part(far + k)
        if k == 1:
            a, b = halves(ahead)
            c, d = halves(behind)
            ahead = jnp.concatenate([a + rise.astype(f32), b], axis=0)
            behind = jnp.concatenate([c, d + fall.astype(f32)], axis=0)
        else:
            ahead = ahead + rise.astype(f32)
            behind = behind + fall.astype(f32)
        rise, fall = up.send(ahead.astype(low)), down.send(behind.astype(low))
        yield
    return part(0) + (rise.astype(f32) + fall.astype(f32))


def together(*generators):
    results = [None] * len(generators)
    live = list(enumerate(generators))
    while live:
        still = []
        for place, generator in live:
            try:
                next(generator)
                still.append((place, generator))
            except StopIteration as stop:
                results[place] = stop.value
        live = still
    return results


def joined(held, count, axis):
    pieces = []
    for o in range(count):
        if isinstance(held[o], tuple):
            if axis == 0:
                pieces += list(held[o])
            else:
                pieces.append(jnp.concatenate(held[o], axis=0))
        else:
            pieces.append(held[o])
    return jnp.concatenate(pieces, axis=axis)


def local(
    tokens,
    doc_lengths,
    cotangent,
    inner_in,
    inner_out,
    inner_shared,
    first_in,
    first_out,
    first_shared,
    second_in,
    second_out,
    second_shared,
    outer_in_w,
    outer_out_w,
    outer_shared,
    momentum_in,
    momentum_out,
    momentum_shared,
):
    splits = lax.axis_size("tensor")
    count = lax.axis_size("dp")
    split = lax.axis_index("tensor")
    place = lax.axis_index("dp")
    total, width = tokens.shape
    part = width // count
    local_cols = inner_in.shape[3]
    shared_cols = inner_shared.shape[2]
    heads = HEADS // splits
    qcols = heads * HD
    hidden = local_cols - qcols
    vec = 2 * HD
    own_cols = part // splits

    order = [2 * p if p < count // 2 else 2 * (count - 1 - p) + 1 for p in range(count)]
    position = jnp.where(place % 2 == 0, place // 2, count - 1 - place // 2)
    offsets = (position + jnp.arange(count, dtype=jnp.int32)) % count
    ids = jnp.where(
        offsets < count // 2, 2 * offsets, 2 * (count - 1 - offsets) + 1
    ).astype(jnp.int32)
    up = Lane([(order[p], order[(p + 1) % count]) for p in range(count)], 2)
    down = Lane([(order[p], order[(p - 1) % count]) for p in range(count)], 2)
    swap_tensor = [(i, (i + 1) % splits) for i in range(splits)]
    swap_group = [(0, 1), (1, 0)]

    def across(value):
        return lax.ppermute(value, "tensor", swap_tensor)

    def tall(array):
        return array.reshape(part, local_cols // LANES, LANES)

    w_in = tall(inner_in)
    w_out = inner_out.reshape(local_cols, part)
    shared_rows = lax.all_gather(inner_shared[0], ("dp", "tensor"), axis=0, tiled=True)

    half = hidden // 2
    spans = [(0, qcols), (qcols, half), (qcols + half, half)]
    low_in = inner_in.reshape(part, local_cols).astype(bf16)
    low_out = w_out.astype(bf16)
    in_blocks = [low_in[:, s : s + c] for s, c in spans]
    out_blocks = [low_out[s : s + c] for s, c in spans]

    held_q, held_o = together(
        gather_steps(in_blocks[0], up, down, count), gather_steps(out_blocks[0], up, down, count)
    )
    w_query, w_attn = joined(held_q, count, 0), joined(held_o, count, 1)
    held_a, held_b = together(
        gather_steps(in_blocks[1], up, down, count), gather_steps(in_blocks[2], up, down, count)
    )
    w_up = [joined(held_a, count, 0), joined(held_b, count, 0)]
    held_a, held_b = together(
        gather_steps(out_blocks[1], up, down, count), gather_steps(out_blocks[2], up, down, count)
    )
    w_down = [joined(held_a, count, 1), joined(held_b, count, 1)]

    shared_t = shared_rows.T
    shared_rel = pick_blocks(shared_t, ids, part, count, False)
    w_keyval_t = shared_rel[:vec].astype(bf16)
    gain_one, bias_one, gain_two, bias_two = (shared_rel[vec + k : vec + k + 1] for k in range(4))
    bias_out, bias_down = shared_rel[vec + 5 : vec + 6], shared_rel[vec + 6 : vec + 7]
    bias_query = lax.dynamic_slice_in_dim(shared_t[vec + 4], split * qcols, qcols)
    bias_up = lax.dynamic_slice_in_dim(shared_t[vec + 7 :].reshape(FF), split * hidden, hidden)

    nt = (((1,), (1,)), ((), ()))
    tn = (((0,), (0,)), ((), ()))

    def mm(a, b, dims=(((1,), (0,)), ((), ()))):
        return lax.dot_general(a, b, dims, preferred_element_type=f32)

    x_rel, normed = first_norm(tokens, ids, gain_one, bias_one, count)
    cot_rel, grad_bias_down = cotangent_order(cotangent, ids, count)
    limits, limits_t = score_limits(doc_lengths[0], total)
    key_value = mm(normed, w_keyval_t, nt).astype(bf16)
    queries = (mm(normed, w_query) + bias_query).astype(bf16)
    attended, log_totals, tops = attention_forward(queries, key_value, limits, heads)
    attn_part = mm(attended, w_attn).astype(bf16)
    middle, normed_two = middle_norm(
        x_rel, attn_part, across(attn_part), bias_out, gain_two, bias_two
    )

    peers = across(tops)
    peak = jnp.where(
        split == 0, jnp.concatenate([tops, peers]), jnp.concatenate([peers, tops])
    )
    peak = jnp.maximum(peak, lax.ppermute(peak, "group", swap_group))
    shift = 1
    while shift < count:
        peak = jnp.maximum(
            peak, lax.ppermute(peak, "dp", [(i, (i + shift) % count) for i in range(count)])
        )
        shift *= 2
    clip_rows = clip_limit / jnp.maximum(peak, clip_limit)

    pre, acts, pulls = [], [], []
    for k in range(2):
        u = mm(normed_two, w_up[k]) + bias_up[k * half : (k + 1) * half]
        value, pull = jax.vjp(lambda v: jax.nn.gelu(v, approximate=True), u)
        acts.append(value.astype(bf16))
        pulls.append(pull)
    down_part = (mm(acts[0], w_down[0]) + mm(acts[1], w_down[1])).astype(bf16)

    def block(array, o):
        return array[:, o * part : (o + 1) * part]

    red_down = together(
        *[
            scatter_steps(lambda o, k=k: mm(acts[k], block(cot_rel, o), tn), up, down, count, bf16)
            for k in range(2)
        ]
    )
    block_out = block_result(middle, down_part, across(down_part), bias_down, ids, count)

    grad_pre = []
    for k in range(2):
        dz = mm(cot_rel, w_down[k], nt)
        grad_pre.append(pulls[k](dz)[0].astype(bf16))
    grad_bias_up = jnp.concatenate([jnp.sum(g.astype(f32), axis=0) for g in grad_pre])
    two_part = (mm(grad_pre[0], w_up[0], nt) + mm(grad_pre[1], w_up[1], nt)).astype(bf16)
    red_up = together(
        *[
            scatter_steps(
                lambda o, k=k: mm(block(normed_two, o), grad_pre[k], tn), up, down, count, bf16
            )
            for k in range(2)
        ]
    )
    dh, dh_low, grad_gain_two, grad_bias_two, grad_bias_out = middle_backward(
        middle, two_part, across(two_part), cot_rel, gain_two
    )
    grad_att = mm(dh_low, w_attn, nt).astype(bf16)
    (red_attn,) = together(
        scatter_steps(lambda o: mm(attended, block(dh_low, o), tn), up, down, count, bf16)
    )
    dots = jnp.sum(
        (grad_att.astype(f32) * attended.astype(f32)).reshape(total, heads, HD), axis=2
    )
    grad_queries, kv_part = attention_backward(
        queries, grad_att, key_value, limits_t, log_totals.T[:heads], dots.T, heads
    )
    one_part = mm(grad_queries, w_query, nt).astype(bf16)
    (red_query,) = together(
        scatter_steps(lambda o: mm(block(normed, o), grad_queries, tn), up, down, count, bf16)
    )
    kv_low = (kv_part + across(kv_part)).astype(bf16)
    grad_keyval_t = mm(kv_low, normed, tn)
    tokens_grad, grad_gain_one, grad_bias_one = first_backward(
        x_rel, one_part, across(one_part), kv_low, w_keyval_t, dh, gain_one, ids, count
    )

    grad_bias_query = jnp.sum(grad_queries.astype(f32), axis=0)
    spread = jnp.concatenate(
        [
            lax.dynamic_update_slice_in_dim(
                jnp.zeros((width,), f32), grad_bias_query, split * qcols, 0
            ),
            lax.dynamic_update_slice_in_dim(
                jnp.zeros((FF,), f32), grad_bias_up, split * hidden, 0
            ),
        ]
    ).reshape(1 + FF // width, width)
    spread = spread + across(spread)
    near = jnp.concatenate(
        [grad_keyval_t, grad_gain_one, grad_bias_one, grad_gain_two, grad_bias_two, grad_bias_out,
         grad_bias_down],
        axis=0,
    )
    picks = jnp.arange(count, dtype=jnp.int32) * splits + split
    near = pick_blocks(near, picks, own_cols, count, True)
    spread = pick_blocks(spread, ids * splits + split, own_cols, count, True)
    pieces = jnp.concatenate(
        [near[:, : vec + 4], spread[:, :1], near[:, vec + 4 :], spread[:, 1:]], axis=1
    )
    (red_shared,) = together(scatter_steps(lambda o: pieces[o], up, down, count, f32))

    one_in, two_in = tall(first_in), tall(second_in)
    one_out, two_out = (a.reshape(local_cols, part) for a in (first_out, second_out))
    base_in, mom_in = tall(outer_in_w), tall(momentum_in)
    base_out, mom_out = (a.reshape(local_cols, part) for a in (outer_out_w, momentum_out))
    clip_own = lax.dynamic_slice_in_dim(clip_rows, split * heads, heads)

    def swap(value):
        return lax.ppermute(value, "group", swap_group)

    full_in = full_out = new_in = new_out = None
    for k in (0, 1):
        s = spans[1 + k][0]
        *full_out, delta = adam_out(red_down[k], w_out, one_out, two_out, base_out, s, full_out)
        new_out = outer_out(delta, swap(delta), mom_out, base_out, s, new_out)
    for k in (0, 1):
        s = spans[1 + k][0]
        *full_in, delta = adam_in(red_up[k], w_in, one_in, two_in, base_in, s, full_in)
        new_in = outer_in(delta, swap(delta), mom_in, base_in, None, s, new_in)
    *full_out, delta = adam_out(red_attn, w_out, one_out, two_out, base_out, 0, full_out)
    new_out = outer_out(delta, swap(delta), mom_out, base_out, 0, new_out)
    *full_in, delta = adam_in(red_query, w_in, one_in, two_in, base_in, 0, full_in)
    new_in = outer_in(delta, swap(delta), mom_in, base_in, clip_own, 0, new_in)

    ids_col = jnp.arange(shared_cols, dtype=jnp.int32)[:, None]
    one_sh, two_sh, stepped = adam_values(
        red_shared,
        inner_shared[0].T,
        first_shared[0].T,
        second_shared[0].T,
        jnp.where(ids_col < vec, rate_matrix, rate_vector),
        jnp.where(ids_col < vec, weight_decay, 0.0),
    )
    base_sh = outer_shared.T
    delta = (base_sh - stepped).astype(bf16)
    mean_sh = (delta.astype(f32) + swap(delta).astype(f32)) * 0.5
    vel_sh, fresh_sh = outer_values(mean_sh, momentum_shared.T, base_sh)
    row_ids = (place * splits + split) * own_cols + jnp.arange(own_cols, dtype=jnp.int32)
    clip_vec = clip_rows[:, 0]
    row_clip = jnp.sum(
        jnp.where((row_ids // HD)[None, :] == jnp.arange(HEADS)[:, None], clip_vec[:, None], 0.0),
        axis=0,
    )
    fresh_sh = fresh_sh * jnp.where(ids_col == vec + 4, row_clip[None, :], 1.0)

    shape_in, shape_out = (part, 1, local_cols), (1, local_cols, part)
    mean_in, vel_in, fresh_in, copy_in = new_in
    mean_out, vel_out, fresh_out, copy_out = new_out
    return (
        block_out,
        tokens_grad,
        clip_vec,
        full_in[0].reshape((1,) + shape_in),
        full_out[0].reshape((1,) + shape_out),
        one_sh.T[None],
        full_in[1].reshape((1,) + shape_in),
        full_out[1].reshape((1,) + shape_out),
        two_sh.T[None],
        mean_in.reshape(shape_in),
        mean_out.reshape(shape_out),
        mean_sh.T,
        vel_in.reshape(shape_in),
        vel_out.reshape(shape_out),
        vel_sh.T,
        fresh_in.reshape(shape_in),
        fresh_out.reshape(shape_out),
        fresh_sh.T,
        copy_in.reshape(shape_in),
        copy_out.reshape(shape_out),
        fresh_sh.T.astype(bf16),
    )


def solution(mesh):
    rows = P(("group", "dp"), None)
    inner = [P("group", "dp", "tensor", None), P("group", "tensor", None, "dp"),
             P("group", ("dp", "tensor"), None)]
    outer = [P("dp", "tensor", None), P("tensor", None, "dp"), P(("dp", "tensor"), None)]
    in_specs = tuple([rows] * 3 + inner * 3 + outer * 2)
    out_specs = tuple([rows] * 2 + [P()] + inner * 2 + outer * 4)
    return jax.shard_map(local, mesh=mesh, in_specs=in_specs, out_specs=out_specs, check_vma=False)
```

```python
import jax
import jax.numpy as jnp
from jax import lax
from jax.experimental import pallas as pl
from jax.experimental.pallas import tpu as pltpu
from jax.sharding import PartitionSpec as P

HEADS = 16
HD = 128
FF = 8192
BLOCK = 256
STEP = 10

norm_eps = 1e-05
hidden_score = -1e30
shown_score = 3e38
beta_one = 0.9
beta_two = 0.95
adam_eps = 1e-08
rate_matrix = 0.02
rate_vector = 0.2
weight_decay = 0.1
outer_beta = 0.9
outer_rate = 0.7
clip_limit = 5.0
score_scale = HD ** (-0.5)
log2_e = 1.4426950408889634
correct_one = 1.0 / (1.0 - beta_one**STEP)
correct_two = 1.0 / (1.0 - beta_two**STEP)

f32 = jnp.float32
bf16 = jnp.bfloat16
ROWS = 128
LANES = 128
VMEM_LIMIT = 40 * 1024 * 1024


def shape(dims, dtype):
    return jax.ShapeDtypeStruct(dims, dtype)


def call(body, out_shape, grid, in_specs, out_specs, args, *, ids=(), scratch=(), aliases=None,
         flops=0, name=None):
    outs = out_shape if isinstance(out_shape, (list, tuple)) else [out_shape]
    moved = sum(a.size * a.dtype.itemsize for a in args)
    moved += sum(o.size * o.dtype.itemsize for o in outs)
    return pl.pallas_call(
        body,
        out_shape=out_shape,
        grid_spec=pltpu.PrefetchScalarGridSpec(
            num_scalar_prefetch=len(ids),
            grid=grid,
            in_specs=in_specs,
            out_specs=out_specs,
            scratch_shapes=list(scratch),
        ),
        input_output_aliases={len(ids) + k: v for k, v in (aliases or {}).items()},
        compiler_params=pltpu.CompilerParams(vmem_limit_bytes=VMEM_LIMIT),
        cost_estimate=pl.CostEstimate(flops=flops, bytes_accessed=moved, transcendentals=0),
        name=name,
    )(*ids, *args)


def pick_blocks(array, block_ids, width, count, stacked):
    rows = array.shape[0]
    if width % LANES:
        taken = jnp.take(array.reshape(rows, -1, width), block_ids, axis=1)
        return taken.transpose(1, 0, 2) if stacked else taken.reshape(rows, count * width)

    def body(ids_ref, in_ref, out_ref):
        if stacked:
            out_ref[0] = in_ref[...]
        else:
            out_ref[...] = in_ref[...]

    if stacked:
        out, spec = shape((count, rows, width), array.dtype), pl.BlockSpec(
            (1, rows, width), lambda j, ids: (j, 0, 0)
        )
    else:
        out, spec = shape((rows, count * width), array.dtype), pl.BlockSpec(
            (rows, width), lambda j, ids: (0, j)
        )
    return call(
        body, out, (count,), [pl.BlockSpec((rows, width), lambda j, ids: (0, ids[j]))], spec,
        [array], ids=[block_ids], name="pick_blocks",
    )


def columns_of(block_id, width):
    return pl.ds(pl.multiple_of(block_id * width, width), width)


def placing(array, ids, count):
    part = array.shape[1] // count
    if part % LANES == 0:
        return array, count, part
    return pick_blocks(array, ids, part, count, False), 0, part


def put_back(array, ids, count):
    part = array.shape[1] // count
    if part % LANES == 0:
        return array
    back = jnp.sum(
        jnp.where(ids[None, :] == jnp.arange(count)[:, None], jnp.arange(count)[None, :], 0), axis=1
    ).astype(jnp.int32)
    return pick_blocks(array, back, part, count, False)


def norm_stats(rows):
    mean = jnp.mean(rows, axis=-1, keepdims=True)
    centered = rows - mean
    inv = lax.rsqrt(jnp.mean(centered * centered, axis=-1, keepdims=True) + norm_eps)
    return centered * inv, inv


def row_spec(cols, rows=ROWS):
    return pl.BlockSpec((rows, cols), lambda i, *ids: (i, 0))


def turned_spec(cols, blocks):
    return pl.BlockSpec(
        (ROWS, cols), lambda i, ids, split: ((i + split[0] * (blocks // 2)) % blocks, 0)
    )


def whole_spec(rows, cols):
    return pl.BlockSpec((rows, cols), lambda i, *ids: (0, 0))


def first_norm(tokens, ids, split, gain, bias, count):
    total, width = tokens.shape
    tokens, moved, part = placing(tokens, ids, count)

    def body(ids_ref, split_ref, x_ref, g_ref, c_ref, x_out, n_out):
        for o in range(moved):
            x_out[:, o * part : (o + 1) * part] = x_ref[:, columns_of(ids_ref[o], part)]
        if not moved:
            x_out[...] = x_ref[...]
        unit, _ = norm_stats(x_out[...].astype(f32))
        n_out[...] = (unit * g_ref[...] + c_ref[...]).astype(bf16)

    return call(
        body,
        [shape((total, width), bf16)] * 2,
        (total // ROWS,),
        [turned_spec(width, total // ROWS), whole_spec(1, width), whole_spec(1, width)],
        [row_spec(width)] * 2,
        [tokens, gain, bias],
        ids=[ids, split],
        name="first_norm",
    )


def first_spec(cols, blocks):
    return pl.BlockSpec((ROWS, cols), lambda i, *ids: (jnp.minimum(i, blocks - 1), 0))


def swapped(values):
    half = values.shape[1] // 2
    return jnp.concatenate([values[:, half:], values[:, :half]], axis=1)


def cotangent_order(cotangent, ids, split, count):
    total, width = cotangent.shape
    cotangent, moved, part = placing(cotangent, ids, count)
    mine = total // ROWS // 2

    def body(ids_ref, split_ref, c_ref, c_out, pair_out, sum_out):
        for o in range(moved):
            c_out[:, o * part : (o + 1) * part] = c_ref[:, columns_of(ids_ref[o], part)]
        if not moved:
            c_out[...] = c_ref[...]

        @pl.when(pl.program_id(0) < mine)
        def _():
            pair_out[...] = swapped(c_out[...])
            add_rows(sum_out, c_out[...].astype(f32))

    return call(
        body,
        [shape((total, width), bf16), shape((total // 2, width), bf16), shape((1, width), f32)],
        (total // ROWS,),
        [turned_spec(width, total // ROWS)],
        [row_spec(width), first_spec(width, mine), whole_spec(1, width)],
        [cotangent],
        ids=[ids, split],
        name="cotangent_order",
    )


def add_rows(sum_ref, values):
    @pl.when(pl.program_id(0) == 0)
    def _():
        sum_ref[...] = jnp.zeros_like(sum_ref)

    sum_ref[...] += jnp.sum(values, axis=0, keepdims=True)


def middle_norm(x_rel, part_own, part_other, bias_out, gain, bias):
    total, width = part_other.shape

    def body(x_ref, a_ref, b_ref, bo_ref, g_ref, c_ref, h_out, n_out, pair_out):
        mid = x_ref[...].astype(f32) + (
            a_ref[...].astype(f32) + b_ref[...].astype(f32)
        ) + bo_ref[...]
        h_out[...] = mid
        unit, _ = norm_stats(mid)
        low = (unit * g_ref[...] + c_ref[...]).astype(bf16)
        n_out[...] = low
        pair_out[...] = swapped(low)

    return call(
        body,
        [shape((total, width), f32)] + [shape((total, width), bf16)] * 2,
        (total // ROWS,),
        [row_spec(width)] * 3 + [whole_spec(1, width)] * 3,
        [row_spec(width)] * 3,
        [x_rel, part_own, part_other, bias_out, gain, bias],
        name="middle_norm",
    )


def block_result(middle, part_own, part_other, part_pair, bias_down, ids, count):
    total, width = middle.shape
    part = width // count

    def body(ids_ref, h_ref, a_ref, b_ref, p_ref, b2_ref, out_ref):
        value = a_ref[...].astype(f32) + b_ref[...].astype(f32)
        value = h_ref[...] + (value + swapped(p_ref[...]).astype(f32)) + b2_ref[...]
        value = value.astype(bf16)
        if part % LANES:
            out_ref[...] = value
        else:
            for o in range(count):
                out_ref[:, columns_of(ids_ref[o], part)] = value[:, o * part : (o + 1) * part]

    result = call(
        body,
        shape((total, width), bf16),
        (total // ROWS,),
        [row_spec(width)] * 4 + [whole_spec(1, width)],
        row_spec(width),
        [middle, part_own, part_other, part_pair, bias_down],
        ids=[ids],
        name="block_result",
    )
    return put_back(result, ids, count)


def middle_backward(middle, part_own, part_other, part_pair, cot_rel, gain):
    total, width = middle.shape

    def body(h_ref, a_ref, b_ref, p_ref, dy_ref, g_ref, dh_out, low_out, gg_out, gc_out, gbo_out):
        unit, inv = norm_stats(h_ref[...])
        grad = a_ref[...].astype(f32) + b_ref[...].astype(f32)
        grad = grad + swapped(p_ref[...]).astype(f32)
        scaled = grad * g_ref[...]
        dh = dy_ref[...].astype(f32) + inv * (
            scaled
            - jnp.mean(scaled, axis=-1, keepdims=True)
            - unit * jnp.mean(scaled * unit, axis=-1, keepdims=True)
        )
        dh_out[...] = dh
        low = dh.astype(bf16)
        low_out[...] = low
        add_rows(gg_out, grad * unit)
        add_rows(gc_out, grad)
        add_rows(gbo_out, low.astype(f32))

    vec = shape((1, width), f32)
    return call(
        body,
        [shape((total, width), f32), shape((total, width), bf16), vec, vec, vec],
        (total // ROWS,),
        [row_spec(width)] * 5 + [whole_spec(1, width)],
        [row_spec(width)] * 2 + [whole_spec(1, width)] * 3,
        [middle, part_own, part_other, part_pair, cot_rel, gain],
        name="middle_backward",
    )


def first_backward(x_rel, part_own, part_other, keyval_grad, w_keyval_t, dh, gain, ids, count):
    total, width = dh.shape
    part = width // count
    kv = keyval_grad.shape[1]

    def body(ids_ref, x_ref, a_ref, b_ref, kv_ref, w_ref, dh_ref, g_ref, t_out, gg_out, gc_out):
        unit, inv = norm_stats(x_ref[...].astype(f32))
        grad = (a_ref[...].astype(f32) + b_ref[...].astype(f32)) + jnp.dot(
            kv_ref[...], w_ref[...], preferred_element_type=f32
        )
        scaled = grad * g_ref[...]
        value = dh_ref[...] + inv * (
            scaled
            - jnp.mean(scaled, axis=-1, keepdims=True)
            - unit * jnp.mean(scaled * unit, axis=-1, keepdims=True)
        )
        low = value.astype(bf16)
        if part % LANES:
            t_out[...] = low
        else:
            for o in range(count):
                t_out[:, columns_of(ids_ref[o], part)] = low[:, o * part : (o + 1) * part]
        add_rows(gg_out, grad * unit)
        add_rows(gc_out, grad)

    vec = shape((1, width), f32)
    result, gain_grad, bias_grad = call(
        body,
        [shape((total, width), bf16), vec, vec],
        (total // ROWS,),
        [row_spec(width)] * 3
        + [row_spec(kv), whole_spec(kv, width), row_spec(width), whole_spec(1, width)],
        [row_spec(width)] + [whole_spec(1, width)] * 2,
        [x_rel, part_own, part_other, keyval_grad, w_keyval_t, dh, gain],
        ids=[ids],
        flops=2 * total * width * kv,
        name="first_backward",
    )
    return put_back(result, ids, count), gain_grad, bias_grad


TILE = 256


def score_limits(lengths, token_count, first_place):
    doc_ends = jnp.cumsum(lengths)
    doc_starts = doc_ends - lengths
    places = (jnp.arange(token_count, dtype=jnp.int32) + first_place) % token_count
    doc_ids = jnp.sum((places[:, None] >= doc_ends[None, :]).astype(jnp.int32), axis=1)
    owners = doc_ids[:, None] == jnp.arange(lengths.shape[0], dtype=jnp.int32)[None, :]
    doc_begin = jnp.sum(jnp.where(owners, doc_starts[None, :], 0), axis=1)
    blocks = (places - doc_begin) // BLOCK
    seen = (doc_ids[:, None] == doc_ids[None, :]) & (blocks[None, :] <= blocks[:, None])
    seen_t = (doc_ids[None, :] == doc_ids[:, None]) & (blocks[:, None] <= blocks[None, :])
    pick = lambda s: jnp.where(s, shown_score, hidden_score).astype(f32)
    return pick(seen), pick(seen_t)


def attention_forward(queries, key_value, limits, heads):
    total = queries.shape[0]
    tiles = total // TILE
    c = score_scale * log2_e

    def body(q_ref, kv_ref, lim_ref, o_ref, lse_ref, top_ref):
        tile, head = pl.program_id(0), pl.program_id(1)
        k = kv_ref[:, :HD]
        v = kv_ref[:, HD:]
        s = lax.dot_general(
            q_ref[...], k, (((1,), (1,)), ((), ())), preferred_element_type=f32
        )
        s = jnp.minimum(s, lim_ref[...])
        m = jnp.max(s, axis=1, keepdims=True)
        p = jnp.exp2((s - m) * c)
        l = jnp.sum(p, axis=1, keepdims=True)
        o = jnp.dot(p.astype(bf16), v, preferred_element_type=f32)
        o_ref[...] = (o / l).astype(bf16)
        lane = lax.broadcasted_iota(jnp.int32, (TILE, LANES), 1)
        lse = m * c + jnp.log2(l)
        lse_ref[...] = jnp.where(lane == head, lse, lse_ref[...])

        @pl.when((tile == 0) & (head == 0))
        def _():
            top_ref[...] = jnp.full_like(top_ref, hidden_score)

        row = lax.broadcasted_iota(jnp.int32, (heads, LANES), 0)
        best = jnp.max(m, axis=0, keepdims=True) * score_scale
        top_ref[...] = jnp.where(row == head, jnp.maximum(top_ref[...], best), top_ref[...])

    return call(
        body,
        [shape((total, heads * HD), bf16), shape((total, LANES), f32), shape((heads, LANES), f32)],
        (tiles, heads),
        [
            pl.BlockSpec((TILE, HD), lambda i, h: (i, h)),
            pl.BlockSpec((total, 2 * HD), lambda i, h: (0, 0)),
            pl.BlockSpec((TILE, total), lambda i, h: (i, 0)),
        ],
        [
            pl.BlockSpec((TILE, HD), lambda i, h: (i, h)),
            pl.BlockSpec((TILE, LANES), lambda i, h: (i, 0)),
            pl.BlockSpec((heads, LANES), lambda i, h: (0, 0)),
        ],
        [queries, key_value, limits],
        flops=8 * total * total * HD * heads,
        name="attention_forward",
    )


def attention_backward(queries, grad_att, key_value, limits_t, lse_t, dot_t, heads):
    total = queries.shape[0]
    tiles = total // TILE
    c = score_scale * log2_e

    def body(q_ref, da_ref, kv_ref, lim_ref, lse_ref, dot_ref, dq_ref, dkv_ref):
        tile, head = pl.program_id(0), pl.program_id(1)
        k = kv_ref[:, :HD]
        v = kv_ref[:, HD:]
        q = q_ref[...]
        da = da_ref[...]
        nt = (((1,), (1,)), ((), ()))
        s = lax.dot_general(k, q, nt, preferred_element_type=f32)
        s = jnp.minimum(s, lim_ref[...])
        p = jnp.exp2(s * c - lse_ref[pl.ds(head, 1), :])
        dp = lax.dot_general(v, da, nt, preferred_element_type=f32)
        ds = (p * (dp - dot_ref[pl.ds(head, 1), :])).astype(bf16)
        dq = lax.dot_general(ds, k, (((0,), (0,)), ((), ())), preferred_element_type=f32)
        dq_ref[...] = (dq * score_scale).astype(bf16)

        @pl.when((tile == 0) & (head == 0))
        def _():
            dkv_ref[...] = jnp.zeros_like(dkv_ref)

        dkv_ref[:, :HD] += jnp.dot(ds, q, preferred_element_type=f32) * score_scale
        dkv_ref[:, HD:] += jnp.dot(p.astype(bf16), da, preferred_element_type=f32)

    return call(
        body,
        [shape((total, heads * HD), bf16), shape((total, 2 * HD), f32)],
        (tiles, heads),
        [
            pl.BlockSpec((TILE, HD), lambda i, h: (i, h)),
            pl.BlockSpec((TILE, HD), lambda i, h: (i, h)),
            pl.BlockSpec((total, 2 * HD), lambda i, h: (0, 0)),
            pl.BlockSpec((total, TILE), lambda i, h: (0, i)),
            pl.BlockSpec((heads, TILE), lambda i, h: (0, i)),
            pl.BlockSpec((heads, TILE), lambda i, h: (0, i)),
        ],
        [
            pl.BlockSpec((TILE, HD), lambda i, h: (i, h)),
            pl.BlockSpec((total, 2 * HD), lambda i, h: (0, 0)),
        ],
        [queries, grad_att, key_value, limits_t, lse_t, dot_t],
        flops=20 * total * total * HD * heads,
        name="attention_backward",
    )


def adam_values(gradient, weight, one, two, rate, decay):
    new_one = beta_one * one + (1.0 - beta_one) * gradient
    new_two = beta_two * two + (1.0 - beta_two) * gradient * gradient
    direction = (new_one * correct_one) / (jnp.sqrt(new_two * correct_two) + adam_eps)
    return new_one, new_two, weight - rate * (direction + decay * weight)


def to_tiles(flat, tiles_ref):
    for j in range(8):
        tiles_ref[:, j, :] = flat[:, j * LANES : (j + 1) * LANES]


def adam_in(gradient, weight, one, two, outer, start, full):
    rows, cols = gradient.shape
    step = 64
    base = (start // 1024).reshape(1)
    tall = pl.BlockSpec((step, 8, LANES), lambda i, j, b: (i, b[0] + j, 0))
    flat = pl.BlockSpec((step, 1024), lambda i, j, b: (i, j))
    args = [gradient, weight, one, two, outer]
    specs = [flat] + [tall] * 4
    aliases = {}
    if full is not None:
        aliases = {5: 0, 6: 1}
        args += list(full)
        specs += [pl.BlockSpec(memory_space=pl.ANY)] * 2

    def body(_, g_ref, w_ref, one_ref, two_ref, out_ref, *rest):
        one_out, two_out, delta_out, grad_tiles, delta_tiles = rest[-5:]
        to_tiles(g_ref[...].astype(f32), grad_tiles)
        new_one, new_two, stepped = adam_values(
            grad_tiles[...], w_ref[...], one_ref[...], two_ref[...], rate_matrix, weight_decay
        )
        one_out[...] = new_one
        two_out[...] = new_two
        delta_tiles[...] = out_ref[...] - stepped
        for j in range(8):
            delta_out[:, j * LANES : (j + 1) * LANES] = delta_tiles[:, j, :].astype(bf16)

    whole = shape(weight.shape, f32)
    return call(
        body,
        [whole, whole, shape((rows, cols), bf16)],
        (rows // step, cols // 1024),
        specs,
        [tall, tall, flat],
        args,
        ids=[base],
        scratch=[pltpu.VMEM((step, 8, LANES), f32)] * 2,
        aliases=aliases,
        name="adam_in",
    )


def adam_out(gradient, weight, one, two, outer, start, full):
    rows, cols = gradient.shape
    step = 512
    base = (start // step).reshape(1)
    tall = pl.BlockSpec((step, cols), lambda i, b: (b[0] + i, 0))
    flat = pl.BlockSpec((step, cols), lambda i, b: (i, 0))
    args = [gradient, weight, one, two, outer]
    specs = [flat] + [tall] * 4
    aliases = {}
    if full is not None:
        aliases = {5: 0, 6: 1}
        args += list(full)
        specs += [pl.BlockSpec(memory_space=pl.ANY)] * 2

    def body(_, g_ref, w_ref, one_ref, two_ref, out_ref, *rest):
        one_out, two_out, delta_out = rest[-3:]
        new_one, new_two, stepped = adam_values(
            g_ref[...].astype(f32), w_ref[...], one_ref[...], two_ref[...], rate_matrix,
            weight_decay,
        )
        one_out[...] = new_one
        two_out[...] = new_two
        delta_out[...] = (out_ref[...] - stepped).astype(bf16)

    whole = shape(weight.shape, f32)
    return call(
        body,
        [whole, whole, shape((rows, cols), bf16)],
        (rows // step,),
        specs,
        [tall, tall, flat],
        args,
        ids=[base],
        aliases=aliases,
        name="adam_out",
    )


def outer_values(mean, momentum, outer):
    velocity = outer_beta * momentum + mean
    return velocity, outer - outer_rate * (mean + outer_beta * velocity)


def outer_in(own, other, momentum, outer, factor, start, full):
    rows, cols = own.shape
    step = 64
    base = (start // 1024).reshape(1)
    tall = pl.BlockSpec((step, 8, LANES), lambda i, j, b: (i, b[0] + j, 0))
    flat = pl.BlockSpec((step, 1024), lambda i, j, b: (i, j))
    wide = pl.BlockSpec((step, 1024), lambda i, j, b: (i, b[0] + j))
    args = [own, other, momentum, outer]
    specs = [flat, flat, tall, tall]
    if factor is not None:
        args.append(factor)
        specs.append(pl.BlockSpec((8, LANES), lambda i, j, b: (0, 0)))
    aliases = {}
    if full is not None:
        aliases = {len(args) + k: k for k in range(4)}
        args += list(full)
        specs += [pl.BlockSpec(memory_space=pl.ANY)] * 4

    def body(_, own_ref, other_ref, mom_ref, out_ref, *rest):
        mean_out, vel_out, new_out, copy_out, mean_tiles, new_tiles = rest[-6:]
        to_tiles((own_ref[...].astype(f32) + other_ref[...].astype(f32)) * 0.5, mean_tiles)
        mean = mean_tiles[...]
        velocity, fresh = outer_values(mean, mom_ref[...], out_ref[...])
        if factor is not None:
            fresh = fresh * rest[0][...][None]
        mean_out[...] = mean
        vel_out[...] = velocity
        new_out[...] = fresh
        new_tiles[...] = fresh
        for j in range(8):
            copy_out[:, j * LANES : (j + 1) * LANES] = new_tiles[:, j, :].astype(bf16)

    whole = shape(outer.shape, f32)
    return call(
        body,
        [whole, whole, whole, shape((rows, outer.shape[1] * LANES), bf16)],
        (rows // step, cols // 1024),
        specs,
        [tall, tall, tall, wide],
        args,
        ids=[base],
        scratch=[pltpu.VMEM((step, 8, LANES), f32)] * 2,
        aliases=aliases,
        name="outer_in",
    )


def outer_out(own, other, momentum, outer, start, full):
    rows, cols = own.shape
    step = 512
    base = (start // step).reshape(1)
    tall = pl.BlockSpec((step, cols), lambda i, b: (b[0] + i, 0))
    flat = pl.BlockSpec((step, cols), lambda i, b: (i, 0))
    args = [own, other, momentum, outer]
    specs = [flat, flat, tall, tall]
    aliases = {}
    if full is not None:
        aliases = {4 + k: k for k in range(4)}
        args += list(full)
        specs += [pl.BlockSpec(memory_space=pl.ANY)] * 4

    def body(_, own_ref, other_ref, mom_ref, out_ref, *rest):
        mean_out, vel_out, new_out, copy_out = rest[-4:]
        mean = (own_ref[...].astype(f32) + other_ref[...].astype(f32)) * 0.5
        velocity, fresh = outer_values(mean, mom_ref[...], out_ref[...])
        mean_out[...] = mean
        vel_out[...] = velocity
        new_out[...] = fresh
        copy_out[...] = fresh.astype(bf16)

    whole = shape(outer.shape, f32)
    return call(
        body,
        [whole, whole, whole, shape(outer.shape, bf16)],
        (rows // step,),
        specs,
        [tall] * 4,
        args,
        ids=[base],
        aliases=aliases,
        name="outer_out",
    )


class Lane:
    def __init__(self, mask, count, window):
        self.pairs = [(i, i ^ mask) for i in range(count)]
        self.window, self.landed = window, []

    def send(self, block):
        if len(self.landed) >= self.window:
            block, _ = lax.optimization_barrier((block, self.landed[-self.window]))
        arrived = self.at_once(block)
        self.landed.append(arrived)
        return arrived

    def at_once(self, block):
        return lax.ppermute(block, "dp", self.pairs)


def gather_cube(mine, other, lanes, axis):
    held = {0: mine}
    for level, lane in enumerate(lanes):
        bit = 1 << (len(lanes) - 1 - level)
        for o in list(held):
            held[o | bit] = lane.send(other if level == 0 else held[o])
    return jnp.concatenate([held[o] for o in sorted(held)], axis=axis)


def reduce_cube(part, lanes):
    levels = len(lanes)
    landed = {}

    def value(o):
        total = part(o)
        for block in landed.pop(o, []):
            total = total + block.astype(f32)
        return total

    def turned(o):
        return sum(((o >> b) & 1) << (levels - 1 - b) for b in range(levels))

    for level in range(levels):
        bit = 1 << level
        here = [o for o in range(1 << levels) if o & bit and o % bit == 0]
        for o in sorted(here, key=turned, reverse=True):
            arrived = lanes[levels - 1 - level].send(value(o).astype(bf16))
            landed.setdefault(o ^ bit, []).append(arrived)
    from_pair = landed[0].pop()
    return value(0), from_pair


def local(
    tokens,
    doc_lengths,
    cotangent,
    inner_in,
    inner_out,
    inner_shared,
    first_in,
    first_out,
    first_shared,
    second_in,
    second_out,
    second_shared,
    outer_in_w,
    outer_out_w,
    outer_shared,
    momentum_in,
    momentum_out,
    momentum_shared,
):
    splits = lax.axis_size("tensor")
    count = lax.axis_size("dp")
    split = lax.axis_index("tensor")
    place = lax.axis_index("dp")
    total, width = tokens.shape
    part = width // count
    local_cols = inner_in.shape[3]
    shared_cols = inner_shared.shape[2]
    heads = HEADS // splits
    qcols = heads * HD
    hidden = local_cols - qcols
    vec = 2 * HD
    own_cols = part // splits
    mine = total // 2

    levels = count.bit_length() - 1
    masks = ([2, 6, 1] + [1 << b for b in range(3, levels)])[:levels]
    flips = [0] * count
    for o in range(count):
        for level in range(levels):
            if o >> (levels - 1 - level) & 1:
                flips[o] ^= masks[level]
    ids = (place ^ jnp.array(flips, jnp.int32)).astype(jnp.int32)
    side = ((place >> 1) ^ (place >> 2)) & 1
    lanes = [Lane(mask, count, 3) for mask in masks]
    pair = lanes[0]
    swap_tensor = [(i, (i + 1) % splits) for i in range(splits)]
    swap_group = [(0, 1), (1, 0)]
    split_id = split.astype(jnp.int32).reshape(1)

    def across(value):
        return lax.ppermute(value, "tensor", swap_tensor)

    def tall(array):
        return array.reshape(part, local_cols // LANES, LANES)

    w_in = tall(inner_in)
    w_out = inner_out.reshape(local_cols, part)
    shared_rows = lax.all_gather(inner_shared[0], ("dp", "tensor"), axis=0, tiled=True)

    half = hidden // 2
    flat_in = inner_in.reshape(part, local_cols)

    def sides(low, high):
        return (
            jnp.where(side == 0, low, high).astype(bf16),
            jnp.where(side == 0, high, low).astype(bf16),
        )

    block_q = flat_in[:, :qcols].astype(bf16)
    block_o = w_out[:qcols].astype(bf16)
    w_query = gather_cube(block_q, block_q, lanes, 0)
    w_attn = gather_cube(block_o, block_o, lanes, 1)
    w_up = gather_cube(
        *sides(flat_in[:, qcols : qcols + half], flat_in[:, qcols + half :]), lanes, 0
    )
    w_down = gather_cube(*sides(w_out[qcols : qcols + half], w_out[qcols + half :]), lanes, 1)

    shared_t = shared_rows.T
    shared_rel = pick_blocks(shared_t, ids, part, count, False)
    w_keyval_t = shared_rel[:vec].astype(bf16)
    gain_one, bias_one, gain_two, bias_two = (shared_rel[vec + k : vec + k + 1] for k in range(4))
    bias_out, bias_down = shared_rel[vec + 5 : vec + 6], shared_rel[vec + 6 : vec + 7]
    bias_query = lax.dynamic_slice_in_dim(shared_t[vec + 4], split * qcols, qcols)
    bias_up = lax.dynamic_slice_in_dim(
        shared_t[vec + 7 :].reshape(FF), split * hidden + side * half, half
    )

    nt = (((1,), (1,)), ((), ()))
    tn = (((0,), (0,)), ((), ()))

    def mm(a, b, dims=(((1,), (0,)), ((), ()))):
        return lax.dot_general(a, b, dims, preferred_element_type=f32)

    def block(array, o):
        return array[:, o * part : (o + 1) * part]

    def spread_rows(own, to_pair):
        theirs = pair.at_once(to_pair)
        return jnp.concatenate([own, across(own), theirs, across(theirs)], axis=0)

    def sum_rows(partial):
        other = across(partial[mine : 2 * mine])
        pair_rows = partial[2 * mine : 3 * mine].astype(f32) + across(
            partial[3 * mine :]
        ).astype(f32)
        return other, pair.at_once(pair_rows.astype(bf16))

    def both_rows(rows):
        other = across(rows)
        whole = jnp.zeros((total, width), rows.dtype)
        whole = lax.dynamic_update_slice_in_dim(whole, rows, split * mine, 0)
        return lax.dynamic_update_slice_in_dim(whole, other, (1 - split) * mine, 0)

    cot_own, cot_pair, grad_bias_down = cotangent_order(cotangent, ids, split_id, count)
    cot_theirs = pair.at_once(cot_pair)
    cot_all = jnp.concatenate([cot_own, cot_theirs, across(cot_theirs)], axis=0)
    x_rel, normed = first_norm(tokens, ids, split_id, gain_one, bias_one, count)
    limits, limits_t = score_limits(doc_lengths[0], total, split * mine)
    key_value = mm(normed, w_keyval_t, nt).astype(bf16)
    queries = (mm(normed, w_query) + bias_query).astype(bf16)
    attended, log_totals, tops = attention_forward(queries, key_value, limits, heads)
    attn_part = mm(attended, w_attn).astype(bf16)
    middle, normed_two, normed_pair = middle_norm(
        x_rel, attn_part, across(attn_part[mine:]), bias_out, gain_two, bias_two
    )
    normed_all = spread_rows(normed_two, normed_pair)

    peers = across(tops)
    peak = jnp.where(
        split == 0, jnp.concatenate([tops, peers]), jnp.concatenate([peers, tops])
    )
    peak = jnp.maximum(peak, lax.ppermute(peak, "group", swap_group))
    for lane in lanes:
        peak = jnp.maximum(peak, lane.at_once(peak))
    clip_rows = clip_limit / jnp.maximum(peak, clip_limit)

    pre_act = mm(normed_all, w_up) + bias_up
    act_value, act_pull = jax.vjp(lambda v: jax.nn.gelu(v, approximate=True), pre_act)
    acts = act_value.astype(bf16)
    red_down = reduce_cube(lambda o: mm(acts, block(cot_all, o), tn), lanes)
    down_part = mm(acts, w_down).astype(bf16)
    down_other, down_pair = sum_rows(down_part)
    block_out = both_rows(
        block_result(middle, down_part, down_other, down_pair, bias_down, ids, count)
    )

    grad_pre = act_pull(mm(cot_all, w_down, nt))[0].astype(bf16)
    grad_bias_up = jnp.sum(grad_pre.astype(f32), axis=0)
    red_up = reduce_cube(lambda o: mm(block(normed_all, o), grad_pre, tn), lanes)
    two_part = mm(grad_pre, w_up, nt).astype(bf16)
    two_other, two_pair = sum_rows(two_part)
    dh, dh_mine, grad_gain_two, grad_bias_two, grad_bias_out = middle_backward(
        middle, two_part, two_other, two_pair, cot_own, gain_two
    )
    dh_low = jnp.concatenate([dh_mine, across(dh_mine)], axis=0)
    grad_att = mm(dh_low, w_attn, nt).astype(bf16)
    attn_mine, attn_pair = reduce_cube(lambda o: mm(attended, block(dh_low, o), tn), lanes)
    dots = jnp.sum(
        (grad_att.astype(f32) * attended.astype(f32)).reshape(total, heads, HD), axis=2
    )
    grad_queries, kv_part = attention_backward(
        queries, grad_att, key_value, limits_t, log_totals.T[:heads], dots.T, heads
    )
    query_mine, query_pair = reduce_cube(lambda o: mm(block(normed, o), grad_queries, tn), lanes)
    one_part = mm(grad_queries, w_query, nt).astype(bf16)
    kv_low = (kv_part[:mine] + across(kv_part[mine:])).astype(bf16)
    grad_keyval_t = mm(kv_low, normed[:mine], tn)
    grad_mine, grad_gain_one, grad_bias_one = first_backward(
        x_rel, one_part, across(one_part[mine:]), kv_low, w_keyval_t, dh, gain_one, ids, count
    )
    tokens_grad = both_rows(grad_mine)

    grad_bias_query = jnp.sum(grad_queries.astype(f32), axis=0)
    spread = jnp.concatenate(
        [
            lax.dynamic_update_slice_in_dim(
                jnp.zeros((width,), f32), grad_bias_query, split * qcols, 0
            ),
            lax.dynamic_update_slice_in_dim(
                jnp.zeros((FF,), f32), grad_bias_up, split * hidden + side * half, 0
            ),
        ]
    ).reshape(1 + FF // width, width)
    near = jnp.concatenate(
        [grad_keyval_t, grad_gain_one, grad_bias_one, grad_gain_two, grad_bias_two, grad_bias_out,
         grad_bias_down],
        axis=0,
    )
    steps = jnp.arange(count, dtype=jnp.int32)

    def pieces(core):
        a = pick_blocks(near, steps * splits + core, own_cols, count, True)
        b = pick_blocks(spread, ids * splits + core, own_cols, count, True)
        return jnp.concatenate([a[:, : vec + 4], b[:, :1], a[:, vec + 4 :], b[:, 1:]], axis=1)

    red_shared = pieces(split) + across(pieces(1 - split))
    for lane in reversed(lanes):
        red_shared = red_shared.reshape((-1, 2) + red_shared.shape[1:])
        red_shared = red_shared[:, 0] + lane.at_once(red_shared[:, 1])
    red_shared = red_shared[0]

    one_in, two_in = tall(first_in), tall(second_in)
    one_out, two_out = (a.reshape(local_cols, part) for a in (first_out, second_out))
    base_in, mom_in = tall(outer_in_w), tall(momentum_in)
    base_out, mom_out = (a.reshape(local_cols, part) for a in (outer_out_w, momentum_out))
    clip_own = lax.dynamic_slice_in_dim(clip_rows, split * heads, heads)

    def swap(value):
        return lax.ppermute(value, "group", swap_group)

    starts = [qcols + side * half, qcols + (1 - side) * half]
    zero = jnp.zeros((), jnp.int32)
    full_in = full_out = new_in = new_out = None
    for s, gradient in zip(starts, red_down):
        *full_out, delta = adam_out(gradient, w_out, one_out, two_out, base_out, s, full_out)
        new_out = outer_out(delta, swap(delta), mom_out, base_out, s, new_out)
    for s, gradient in zip(starts, red_up):
        *full_in, delta = adam_in(gradient, w_in, one_in, two_in, base_in, s, full_in)
        new_in = outer_in(delta, swap(delta), mom_in, base_in, None, s, new_in)
    red_attn = attn_mine + attn_pair.astype(f32)
    *full_out, delta = adam_out(red_attn, w_out, one_out, two_out, base_out, zero, full_out)
    new_out = outer_out(delta, swap(delta), mom_out, base_out, zero, new_out)
    red_query = query_mine + query_pair.astype(f32)
    *full_in, delta = adam_in(red_query, w_in, one_in, two_in, base_in, zero, full_in)
    new_in = outer_in(delta, swap(delta), mom_in, base_in, clip_own, zero, new_in)

    ids_col = jnp.arange(shared_cols, dtype=jnp.int32)[:, None]
    one_sh, two_sh, stepped = adam_values(
        red_shared,
        inner_shared[0].T,
        first_shared[0].T,
        second_shared[0].T,
        jnp.where(ids_col < vec, rate_matrix, rate_vector),
        jnp.where(ids_col < vec, weight_decay, 0.0),
    )
    base_sh = outer_shared.T
    delta = (base_sh - stepped).astype(bf16)
    mean_sh = (delta.astype(f32) + swap(delta).astype(f32)) * 0.5
    vel_sh, fresh_sh = outer_values(mean_sh, momentum_shared.T, base_sh)
    row_ids = (place * splits + split) * own_cols + jnp.arange(own_cols, dtype=jnp.int32)
    clip_vec = clip_rows[:, 0]
    row_clip = jnp.sum(
        jnp.where((row_ids // HD)[None, :] == jnp.arange(HEADS)[:, None], clip_vec[:, None], 0.0),
        axis=0,
    )
    fresh_sh = fresh_sh * jnp.where(ids_col == vec + 4, row_clip[None, :], 1.0)

    shape_in, shape_out = (part, 1, local_cols), (1, local_cols, part)
    mean_in, vel_in, fresh_in, copy_in = new_in
    mean_out, vel_out, fresh_out, copy_out = new_out
    return (
        block_out,
        tokens_grad,
        clip_vec,
        full_in[0].reshape((1,) + shape_in),
        full_out[0].reshape((1,) + shape_out),
        one_sh.T[None],
        full_in[1].reshape((1,) + shape_in),
        full_out[1].reshape((1,) + shape_out),
        two_sh.T[None],
        mean_in.reshape(shape_in),
        mean_out.reshape(shape_out),
        mean_sh.T,
        vel_in.reshape(shape_in),
        vel_out.reshape(shape_out),
        vel_sh.T,
        fresh_in.reshape(shape_in),
        fresh_out.reshape(shape_out),
        fresh_sh.T,
        copy_in.reshape(shape_in),
        copy_out.reshape(shape_out),
        fresh_sh.T.astype(bf16),
    )


def solution(mesh):
    rows = P(("group", "dp"), None)
    inner = [P("group", "dp", "tensor", None), P("group", "tensor", None, "dp"),
             P("group", ("dp", "tensor"), None)]
    outer = [P("dp", "tensor", None), P("tensor", None, "dp"), P(("dp", "tensor"), None)]
    in_specs = tuple([rows] * 3 + inner * 3 + outer * 2)
    out_specs = tuple([rows] * 2 + [P()] + inner * 2 + outer * 4)
    return jax.shard_map(local, mesh=mesh, in_specs=in_specs, out_specs=out_specs, check_vma=False)
```

```python
import jax
import jax.numpy as jnp
from jax import lax
from jax.experimental import pallas as pl
from jax.experimental.pallas import tpu as pltpu
from jax.sharding import PartitionSpec as P

HEADS = 16
HD = 128
FF = 8192
BLOCK = 256
STEP = 10

norm_eps = 1e-05
hidden_score = -1e30
shown_score = 3e38
beta_one = 0.9
beta_two = 0.95
adam_eps = 1e-08
rate_matrix = 0.02
rate_vector = 0.2
weight_decay = 0.1
outer_beta = 0.9
outer_rate = 0.7
clip_limit = 5.0
score_scale = HD ** (-0.5)
log2_e = 1.4426950408889634
correct_one = 1.0 / (1.0 - beta_one**STEP)
correct_two = 1.0 / (1.0 - beta_two**STEP)

f32 = jnp.float32
bf16 = jnp.bfloat16
ROWS = 128
LANES = 128
VMEM_LIMIT = 40 * 1024 * 1024
VMEM_MOST = 58 * 1024 * 1024


def shape(dims, dtype):
    return jax.ShapeDtypeStruct(dims, dtype)


def call(body, out_shape, grid, in_specs, out_specs, args, *, ids=(), scratch=(), aliases=None,
         flops=0, name=None, vmem=VMEM_LIMIT):
    outs = out_shape if isinstance(out_shape, (list, tuple)) else [out_shape]
    moved = sum(a.size * a.dtype.itemsize for a in args)
    moved += sum(o.size * o.dtype.itemsize for o in outs)
    return pl.pallas_call(
        body,
        out_shape=out_shape,
        grid_spec=pltpu.PrefetchScalarGridSpec(
            num_scalar_prefetch=len(ids),
            grid=grid,
            in_specs=in_specs,
            out_specs=out_specs,
            scratch_shapes=list(scratch),
        ),
        input_output_aliases={len(ids) + k: v for k, v in (aliases or {}).items()},
        compiler_params=pltpu.CompilerParams(vmem_limit_bytes=vmem),
        cost_estimate=pl.CostEstimate(flops=flops, bytes_accessed=moved, transcendentals=0),
        name=name,
    )(*ids, *args)


def pick_blocks(array, block_ids, width, count, stacked):
    rows = array.shape[0]
    if width % LANES:
        taken = jnp.take(array.reshape(rows, -1, width), block_ids, axis=1)
        return taken.transpose(1, 0, 2) if stacked else taken.reshape(rows, count * width)

    def body(ids_ref, in_ref, out_ref):
        if stacked:
            out_ref[0] = in_ref[...]
        else:
            out_ref[...] = in_ref[...]

    if stacked:
        out, spec = shape((count, rows, width), array.dtype), pl.BlockSpec(
            (1, rows, width), lambda j, ids: (j, 0, 0)
        )
    else:
        out, spec = shape((rows, count * width), array.dtype), pl.BlockSpec(
            (rows, width), lambda j, ids: (0, j)
        )
    return call(
        body, out, (count,), [pl.BlockSpec((rows, width), lambda j, ids: (0, ids[j]))], spec,
        [array], ids=[block_ids], name="pick_blocks",
    )


def columns_of(block_id, width):
    return pl.ds(pl.multiple_of(block_id * width, width), width)


def placing(array, ids, count):
    part = array.shape[1] // count
    if part % LANES == 0:
        return array, count, part
    return pick_blocks(array, ids, part, count, False), 0, part


def put_back(array, ids, count):
    part = array.shape[1] // count
    if part % LANES == 0:
        return array
    back = jnp.sum(
        jnp.where(ids[None, :] == jnp.arange(count)[:, None], jnp.arange(count)[None, :], 0), axis=1
    ).astype(jnp.int32)
    return pick_blocks(array, back, part, count, False)


def norm_stats(rows):
    mean = jnp.mean(rows, axis=-1, keepdims=True)
    centered = rows - mean
    inv = lax.rsqrt(jnp.mean(centered * centered, axis=-1, keepdims=True) + norm_eps)
    return centered * inv, inv


def row_spec(cols, rows=ROWS):
    return pl.BlockSpec((rows, cols), lambda i, *ids: (i, 0))


def turned_spec(cols, blocks):
    return pl.BlockSpec(
        (ROWS, cols), lambda i, ids, split: ((i + split[0] * (blocks // 2)) % blocks, 0)
    )


def whole_spec(rows, cols):
    return pl.BlockSpec((rows, cols), lambda i, *ids: (0, 0))


def first_norm(tokens, ids, split, gain, bias, count):
    total, width = tokens.shape
    tokens, moved, part = placing(tokens, ids, count)

    def body(ids_ref, split_ref, x_ref, g_ref, c_ref, x_out, n_out):
        for o in range(moved):
            x_out[:, o * part : (o + 1) * part] = x_ref[:, columns_of(ids_ref[o], part)]
        if not moved:
            x_out[...] = x_ref[...]
        unit, _ = norm_stats(x_out[...].astype(f32))
        n_out[...] = (unit * g_ref[...] + c_ref[...]).astype(bf16)

    return call(
        body,
        [shape((total, width), bf16)] * 2,
        (total // ROWS,),
        [turned_spec(width, total // ROWS), whole_spec(1, width), whole_spec(1, width)],
        [row_spec(width)] * 2,
        [tokens, gain, bias],
        ids=[ids, split],
        name="first_norm",
    )


def first_spec(cols, blocks):
    return pl.BlockSpec((ROWS, cols), lambda i, *ids: (jnp.minimum(i, blocks - 1), 0))


def swapped(values, part):
    if part % LANES:
        return values
    blocks = [values[:, o : o + part] for o in range(0, values.shape[1], part)]
    return jnp.concatenate([blocks[o ^ 1] for o in range(len(blocks))], axis=1)


def swap_small(values, part):
    if part % LANES == 0:
        return values
    parted = values.reshape(values.shape[0], -1, 2, part)
    return parted[:, :, ::-1].reshape(values.shape)


def cotangent_order(cotangent, ids, split, count):
    total, width = cotangent.shape
    cotangent, moved, part = placing(cotangent, ids, count)
    mine = total // ROWS // 2

    def body(ids_ref, split_ref, c_ref, c_out, pair_out, sum_out):
        for o in range(moved):
            c_out[:, o * part : (o + 1) * part] = c_ref[:, columns_of(ids_ref[o], part)]
        if not moved:
            c_out[...] = c_ref[...]

        @pl.when(pl.program_id(0) < mine)
        def _():
            pair_out[...] = swapped(c_out[...], part)
            add_rows(sum_out, c_out[...].astype(f32))

    return call(
        body,
        [shape((total, width), bf16), shape((total // 2, width), bf16), shape((1, width), f32)],
        (total // ROWS,),
        [turned_spec(width, total // ROWS)],
        [row_spec(width), first_spec(width, mine), whole_spec(1, width)],
        [cotangent],
        ids=[ids, split],
        name="cotangent_order",
    )


def add_rows(sum_ref, values):
    @pl.when(pl.program_id(0) == 0)
    def _():
        sum_ref[...] = jnp.zeros_like(sum_ref)

    sum_ref[...] += jnp.sum(values, axis=0, keepdims=True)


def middle_norm(x_rel, part_own, part_other, bias_out, gain, bias, part):
    total, width = part_other.shape

    def body(x_ref, a_ref, b_ref, bo_ref, g_ref, c_ref, h_out, n_out, pair_out):
        mid = x_ref[...].astype(f32) + (
            a_ref[...].astype(f32) + b_ref[...].astype(f32)
        ) + bo_ref[...]
        h_out[...] = mid
        unit, _ = norm_stats(mid)
        low = (unit * g_ref[...] + c_ref[...]).astype(bf16)
        n_out[...] = low
        pair_out[...] = swapped(low, part)

    return call(
        body,
        [shape((total, width), f32)] + [shape((total, width), bf16)] * 2,
        (total // ROWS,),
        [row_spec(width)] * 3 + [whole_spec(1, width)] * 3,
        [row_spec(width)] * 3,
        [x_rel, part_own, part_other, bias_out, gain, bias],
        name="middle_norm",
    )


def block_result(middle, part_own, part_other, part_pair, bias_down, ids, count):
    total, width = middle.shape
    part = width // count

    def body(ids_ref, h_ref, a_ref, b_ref, p_ref, b2_ref, out_ref):
        value = a_ref[...].astype(f32) + b_ref[...].astype(f32)
        value = h_ref[...] + (value + swapped(p_ref[...], part).astype(f32)) + b2_ref[...]
        value = value.astype(bf16)
        if part % LANES:
            out_ref[...] = value
        else:
            for o in range(count):
                out_ref[:, columns_of(ids_ref[o], part)] = value[:, o * part : (o + 1) * part]

    result = call(
        body,
        shape((total, width), bf16),
        (total // ROWS,),
        [row_spec(width)] * 4 + [whole_spec(1, width)],
        row_spec(width),
        [middle, part_own, part_other, part_pair, bias_down],
        ids=[ids],
        name="block_result",
    )
    return put_back(result, ids, count)


def middle_backward(middle, part_own, part_other, part_pair, cot_rel, gain, part):
    total, width = middle.shape

    def body(h_ref, a_ref, b_ref, p_ref, dy_ref, g_ref, dh_out, low_out, gg_out, gc_out, gbo_out):
        unit, inv = norm_stats(h_ref[...])
        grad = a_ref[...].astype(f32) + b_ref[...].astype(f32)
        grad = grad + swapped(p_ref[...], part).astype(f32)
        scaled = grad * g_ref[...]
        dh = dy_ref[...].astype(f32) + inv * (
            scaled
            - jnp.mean(scaled, axis=-1, keepdims=True)
            - unit * jnp.mean(scaled * unit, axis=-1, keepdims=True)
        )
        dh_out[...] = dh
        low = dh.astype(bf16)
        low_out[...] = low
        add_rows(gg_out, grad * unit)
        add_rows(gc_out, grad)
        add_rows(gbo_out, low.astype(f32))

    vec = shape((1, width), f32)
    return call(
        body,
        [shape((total, width), f32), shape((total, width), bf16), vec, vec, vec],
        (total // ROWS,),
        [row_spec(width)] * 5 + [whole_spec(1, width)],
        [row_spec(width)] * 2 + [whole_spec(1, width)] * 3,
        [middle, part_own, part_other, part_pair, cot_rel, gain],
        name="middle_backward",
    )


def first_backward(x_rel, part_own, part_other, keyval_grad, w_keyval_t, dh, gain, ids, count):
    total, width = dh.shape
    part = width // count
    kv = keyval_grad.shape[1]

    def body(ids_ref, x_ref, a_ref, b_ref, kv_ref, w_ref, dh_ref, g_ref, t_out, gg_out, gc_out):
        unit, inv = norm_stats(x_ref[...].astype(f32))
        grad = (a_ref[...].astype(f32) + b_ref[...].astype(f32)) + jnp.dot(
            kv_ref[...], w_ref[...], preferred_element_type=f32
        )
        scaled = grad * g_ref[...]
        value = dh_ref[...] + inv * (
            scaled
            - jnp.mean(scaled, axis=-1, keepdims=True)
            - unit * jnp.mean(scaled * unit, axis=-1, keepdims=True)
        )
        low = value.astype(bf16)
        if part % LANES:
            t_out[...] = low
        else:
            for o in range(count):
                t_out[:, columns_of(ids_ref[o], part)] = low[:, o * part : (o + 1) * part]
        add_rows(gg_out, grad * unit)
        add_rows(gc_out, grad)

    vec = shape((1, width), f32)
    result, gain_grad, bias_grad = call(
        body,
        [shape((total, width), bf16), vec, vec],
        (total // ROWS,),
        [row_spec(width)] * 3
        + [row_spec(kv), whole_spec(kv, width), row_spec(width), whole_spec(1, width)],
        [row_spec(width)] + [whole_spec(1, width)] * 2,
        [x_rel, part_own, part_other, keyval_grad, w_keyval_t, dh, gain],
        ids=[ids],
        flops=2 * total * width * kv,
        name="first_backward",
    )
    return put_back(result, ids, count), gain_grad, bias_grad


TILE = 256


def score_limits(lengths, token_count, first_place):
    doc_ends = jnp.cumsum(lengths)
    doc_starts = doc_ends - lengths
    places = (jnp.arange(token_count, dtype=jnp.int32) + first_place) % token_count
    doc_ids = jnp.sum((places[:, None] >= doc_ends[None, :]).astype(jnp.int32), axis=1)
    owners = doc_ids[:, None] == jnp.arange(lengths.shape[0], dtype=jnp.int32)[None, :]
    doc_begin = jnp.sum(jnp.where(owners, doc_starts[None, :], 0), axis=1)
    blocks = (places - doc_begin) // BLOCK
    seen = (doc_ids[:, None] == doc_ids[None, :]) & (blocks[None, :] <= blocks[:, None])
    seen_t = (doc_ids[None, :] == doc_ids[:, None]) & (blocks[:, None] <= blocks[None, :])
    pick = lambda s: jnp.where(s, shown_score, hidden_score).astype(f32)
    return pick(seen), pick(seen_t)


def attention_forward(queries, key_value, limits, heads):
    total = queries.shape[0]
    tiles = total // TILE
    c = score_scale * log2_e

    def body(q_ref, kv_ref, lim_ref, o_ref, lse_ref, top_ref):
        tile, head = pl.program_id(0), pl.program_id(1)
        k = kv_ref[:, :HD]
        v = kv_ref[:, HD:]
        s = lax.dot_general(
            q_ref[...], k, (((1,), (1,)), ((), ())), preferred_element_type=f32
        )
        s = jnp.minimum(s, lim_ref[...])
        m = jnp.max(s, axis=1, keepdims=True)
        p = jnp.exp2((s - m) * c)
        l = jnp.sum(p, axis=1, keepdims=True)
        o = jnp.dot(p.astype(bf16), v, preferred_element_type=f32)
        o_ref[...] = (o / l).astype(bf16)
        lane = lax.broadcasted_iota(jnp.int32, (TILE, LANES), 1)
        lse = m * c + jnp.log2(l)
        lse_ref[...] = jnp.where(lane == head, lse, lse_ref[...])

        @pl.when((tile == 0) & (head == 0))
        def _():
            top_ref[...] = jnp.full_like(top_ref, hidden_score)

        row = lax.broadcasted_iota(jnp.int32, (heads, LANES), 0)
        best = jnp.max(m, axis=0, keepdims=True) * score_scale
        top_ref[...] = jnp.where(row == head, jnp.maximum(top_ref[...], best), top_ref[...])

    return call(
        body,
        [shape((total, heads * HD), bf16), shape((total, LANES), f32), shape((heads, LANES), f32)],
        (tiles, heads),
        [
            pl.BlockSpec((TILE, HD), lambda i, h: (i, h)),
            pl.BlockSpec((total, 2 * HD), lambda i, h: (0, 0)),
            pl.BlockSpec((TILE, total), lambda i, h: (i, 0)),
        ],
        [
            pl.BlockSpec((TILE, HD), lambda i, h: (i, h)),
            pl.BlockSpec((TILE, LANES), lambda i, h: (i, 0)),
            pl.BlockSpec((heads, LANES), lambda i, h: (0, 0)),
        ],
        [queries, key_value, limits],
        flops=8 * total * total * HD * heads,
        name="attention_forward",
    )


def attention_backward(queries, grad_att, key_value, limits_t, lse_t, dot_t, heads):
    total = queries.shape[0]
    tiles = total // TILE
    c = score_scale * log2_e

    def body(q_ref, da_ref, kv_ref, lim_ref, lse_ref, dot_ref, dq_ref, dkv_ref):
        tile, head = pl.program_id(0), pl.program_id(1)
        k = kv_ref[:, :HD]
        v = kv_ref[:, HD:]
        q = q_ref[...]
        da = da_ref[...]
        nt = (((1,), (1,)), ((), ()))
        s = lax.dot_general(k, q, nt, preferred_element_type=f32)
        s = jnp.minimum(s, lim_ref[...])
        p = jnp.exp2(s * c - lse_ref[pl.ds(head, 1), :])
        dp = lax.dot_general(v, da, nt, preferred_element_type=f32)
        ds = (p * (dp - dot_ref[pl.ds(head, 1), :])).astype(bf16)
        dq = lax.dot_general(ds, k, (((0,), (0,)), ((), ())), preferred_element_type=f32)
        dq_ref[...] = (dq * score_scale).astype(bf16)

        @pl.when((tile == 0) & (head == 0))
        def _():
            dkv_ref[...] = jnp.zeros_like(dkv_ref)

        dkv_ref[:, :HD] += jnp.dot(ds, q, preferred_element_type=f32) * score_scale
        dkv_ref[:, HD:] += jnp.dot(p.astype(bf16), da, preferred_element_type=f32)

    return call(
        body,
        [shape((total, heads * HD), bf16), shape((total, 2 * HD), f32)],
        (tiles, heads),
        [
            pl.BlockSpec((TILE, HD), lambda i, h: (i, h)),
            pl.BlockSpec((TILE, HD), lambda i, h: (i, h)),
            pl.BlockSpec((total, 2 * HD), lambda i, h: (0, 0)),
            pl.BlockSpec((total, TILE), lambda i, h: (0, i)),
            pl.BlockSpec((heads, TILE), lambda i, h: (0, i)),
            pl.BlockSpec((heads, TILE), lambda i, h: (0, i)),
        ],
        [
            pl.BlockSpec((TILE, HD), lambda i, h: (i, h)),
            pl.BlockSpec((total, 2 * HD), lambda i, h: (0, 0)),
        ],
        [queries, grad_att, key_value, limits_t, lse_t, dot_t],
        flops=20 * total * total * HD * heads,
        name="attention_backward",
    )


def adam_values(gradient, weight, one, two, rate, decay):
    new_one = beta_one * one + (1.0 - beta_one) * gradient
    new_two = beta_two * two + (1.0 - beta_two) * gradient * gradient
    direction = (new_one * correct_one) / (jnp.sqrt(new_two * correct_two) + adam_eps)
    return new_one, new_two, weight - rate * (direction + decay * weight)


def to_tiles(flat, tiles_ref):
    for j in range(8):
        tiles_ref[:, j, :] = flat[:, j * LANES : (j + 1) * LANES]


def adam_in(gradient, weight, one, two, outer, start, full):
    rows, cols = gradient.shape
    step = 64
    base = (start // 1024).reshape(1)
    tall = pl.BlockSpec((step, 8, LANES), lambda i, j, b: (i, b[0] + j, 0))
    flat = pl.BlockSpec((step, 1024), lambda i, j, b: (i, j))
    args = [gradient, weight, one, two, outer]
    specs = [flat] + [tall] * 4
    aliases = {}
    if full is not None:
        aliases = {5: 0, 6: 1}
        args += list(full)
        specs += [pl.BlockSpec(memory_space=pl.ANY)] * 2

    def body(_, g_ref, w_ref, one_ref, two_ref, out_ref, *rest):
        one_out, two_out, delta_out, grad_tiles, delta_tiles = rest[-5:]
        to_tiles(g_ref[...].astype(f32), grad_tiles)
        new_one, new_two, stepped = adam_values(
            grad_tiles[...], w_ref[...], one_ref[...], two_ref[...], rate_matrix, weight_decay
        )
        one_out[...] = new_one
        two_out[...] = new_two
        delta_tiles[...] = out_ref[...] - stepped
        for j in range(8):
            delta_out[:, j * LANES : (j + 1) * LANES] = delta_tiles[:, j, :].astype(bf16)

    whole = shape(weight.shape, f32)
    return call(
        body,
        [whole, whole, shape((rows, cols), bf16)],
        (rows // step, cols // 1024),
        specs,
        [tall, tall, flat],
        args,
        ids=[base],
        scratch=[pltpu.VMEM((step, 8, LANES), f32)] * 2,
        aliases=aliases,
        name="adam_in",
        vmem=VMEM_MOST,
    )


def adam_out(gradient, weight, one, two, outer, start, full):
    rows, cols = gradient.shape
    step = 512
    base = (start // step).reshape(1)
    tall = pl.BlockSpec((step, cols), lambda i, b: (b[0] + i, 0))
    flat = pl.BlockSpec((step, cols), lambda i, b: (i, 0))
    args = [gradient, weight, one, two, outer]
    specs = [flat] + [tall] * 4
    aliases = {}
    if full is not None:
        aliases = {5: 0, 6: 1}
        args += list(full)
        specs += [pl.BlockSpec(memory_space=pl.ANY)] * 2

    def body(_, g_ref, w_ref, one_ref, two_ref, out_ref, *rest):
        one_out, two_out, delta_out = rest[-3:]
        new_one, new_two, stepped = adam_values(
            g_ref[...].astype(f32), w_ref[...], one_ref[...], two_ref[...], rate_matrix,
            weight_decay,
        )
        one_out[...] = new_one
        two_out[...] = new_two
        delta_out[...] = (out_ref[...] - stepped).astype(bf16)

    whole = shape(weight.shape, f32)
    return call(
        body,
        [whole, whole, shape((rows, cols), bf16)],
        (rows // step,),
        specs,
        [tall, tall, flat],
        args,
        ids=[base],
        aliases=aliases,
        name="adam_out",
        vmem=VMEM_MOST,
    )


def outer_values(mean, momentum, outer):
    velocity = outer_beta * momentum + mean
    return velocity, outer - outer_rate * (mean + outer_beta * velocity)


def outer_in(own, other, momentum, outer, factor, start, full):
    rows, cols = own.shape
    step = 64
    base = (start // 1024).reshape(1)
    tall = pl.BlockSpec((step, 8, LANES), lambda i, j, b: (i, b[0] + j, 0))
    flat = pl.BlockSpec((step, 1024), lambda i, j, b: (i, j))
    wide = pl.BlockSpec((step, 1024), lambda i, j, b: (i, b[0] + j))
    args = [own, other, momentum, outer]
    specs = [flat, flat, tall, tall]
    if factor is not None:
        args.append(factor)
        specs.append(pl.BlockSpec((8, LANES), lambda i, j, b: (0, 0)))
    aliases = {}
    if full is not None:
        aliases = {len(args) + k: k for k in range(4)}
        args += list(full)
        specs += [pl.BlockSpec(memory_space=pl.ANY)] * 4

    def body(_, own_ref, other_ref, mom_ref, out_ref, *rest):
        mean_out, vel_out, new_out, copy_out, mean_tiles, new_tiles = rest[-6:]
        to_tiles((own_ref[...].astype(f32) + other_ref[...].astype(f32)) * 0.5, mean_tiles)
        mean = mean_tiles[...]
        velocity, fresh = outer_values(mean, mom_ref[...], out_ref[...])
        if factor is not None:
            fresh = fresh * rest[0][...][None]
        mean_out[...] = mean
        vel_out[...] = velocity
        new_out[...] = fresh
        new_tiles[...] = fresh
        for j in range(8):
            copy_out[:, j * LANES : (j + 1) * LANES] = new_tiles[:, j, :].astype(bf16)

    whole = shape(outer.shape, f32)
    return call(
        body,
        [whole, whole, whole, shape((rows, outer.shape[1] * LANES), bf16)],
        (rows // step, cols // 1024),
        specs,
        [tall, tall, tall, wide],
        args,
        ids=[base],
        scratch=[pltpu.VMEM((step, 8, LANES), f32)] * 2,
        aliases=aliases,
        name="outer_in",
        vmem=VMEM_MOST,
    )


def outer_out(own, other, momentum, outer, start, full):
    rows, cols = own.shape
    step = 512
    base = (start // step).reshape(1)
    tall = pl.BlockSpec((step, cols), lambda i, b: (b[0] + i, 0))
    flat = pl.BlockSpec((step, cols), lambda i, b: (i, 0))
    args = [own, other, momentum, outer]
    specs = [flat, flat, tall, tall]
    aliases = {}
    if full is not None:
        aliases = {4 + k: k for k in range(4)}
        args += list(full)
        specs += [pl.BlockSpec(memory_space=pl.ANY)] * 4

    def body(_, own_ref, other_ref, mom_ref, out_ref, *rest):
        mean_out, vel_out, new_out, copy_out = rest[-4:]
        mean = (own_ref[...].astype(f32) + other_ref[...].astype(f32)) * 0.5
        velocity, fresh = outer_values(mean, mom_ref[...], out_ref[...])
        mean_out[...] = mean
        vel_out[...] = velocity
        new_out[...] = fresh
        copy_out[...] = fresh.astype(bf16)

    whole = shape(outer.shape, f32)
    return call(
        body,
        [whole, whole, whole, shape(outer.shape, bf16)],
        (rows // step,),
        specs,
        [tall] * 4,
        args,
        ids=[base],
        aliases=aliases,
        name="outer_out",
        vmem=VMEM_MOST,
    )


class Lane:
    def __init__(self, mask, count, window):
        self.pairs = [(i, i ^ mask) for i in range(count)]
        self.window, self.landed = window, []

    def send(self, block):
        if len(self.landed) >= self.window:
            block, _ = lax.optimization_barrier((block, self.landed[-self.window]))
        arrived = self.at_once(block)
        self.landed.append(arrived)
        return arrived

    def at_once(self, block):
        return lax.ppermute(block, "dp", self.pairs)


def after(value, *earlier):
    return lax.optimization_barrier((value, *earlier))[0]


class Gathered:
    def __init__(self, mine, other, lanes, axis):
        self.lanes, self.axis = lanes, axis
        arrived = lanes[0].send(other)
        self.held = {0: jnp.concatenate([mine, arrived], axis=axis)}

    def send(self, level, o):
        self.held[o + (1 << level)] = self.lanes[level].send(self.held[o])

    def rest(self):
        for level in range(1, len(self.lanes)):
            for o in range(0, 1 << level, 2):
                if o + (1 << level) not in self.held:
                    self.send(level, o)

    def whole(self):
        return jnp.concatenate([self.held[o] for o in sorted(self.held)], axis=self.axis)


class Reduced:
    def __init__(self, part, lanes, axis, size):
        self.part, self.lanes, self.axis, self.size = part, lanes, axis, size
        self.landed = {}

    def pair_sum(self, o):
        total = self.part(o, 2)
        for block in self.landed.pop(o, []):
            total = total + block.astype(f32)
        return total

    def send(self, level, o):
        value = self.pair_sum(o).astype(bf16)
        arrived = self.lanes[level].send(value)
        self.landed.setdefault(o - (1 << level), []).append(arrived)
        return value

    def level(self, level):
        return [
            self.send(level, o)
            for o in reversed(range(1 << level, 2 << level, 2))
        ]

    def finish(self):
        values = []
        for o in (1, 0):
            total = self.part(o, 1)
            for block in self.landed[0]:
                total = total + lax.slice_in_dim(
                    block, o * self.size, (o + 1) * self.size, axis=self.axis
                ).astype(f32)
            values.append(total)
        return values[1], self.lanes[0].send(values[0].astype(bf16))


def local(
    tokens,
    doc_lengths,
    cotangent,
    inner_in,
    inner_out,
    inner_shared,
    first_in,
    first_out,
    first_shared,
    second_in,
    second_out,
    second_shared,
    outer_in_w,
    outer_out_w,
    outer_shared,
    momentum_in,
    momentum_out,
    momentum_shared,
):
    splits = lax.axis_size("tensor")
    count = lax.axis_size("dp")
    split = lax.axis_index("tensor")
    place = lax.axis_index("dp")
    total, width = tokens.shape
    part = width // count
    local_cols = inner_in.shape[3]
    shared_cols = inner_shared.shape[2]
    heads = HEADS // splits
    qcols = heads * HD
    hidden = local_cols - qcols
    vec = 2 * HD
    own_cols = part // splits
    mine = total // 2

    levels = count.bit_length() - 1
    masks = ([2, 6, 1] + [1 << b for b in range(3, levels)])[:levels]
    flips = [0] * count
    for o in range(count):
        for level in range(levels):
            if o >> level & 1:
                flips[o] ^= masks[level]
    ids = (place ^ jnp.array(flips, jnp.int32)).astype(jnp.int32)
    side = ((place >> 1) ^ (place >> 2)) & 1
    windows = [2, 1, 2] + [2] * levels
    lanes = [Lane(mask, count, window) for mask, window in zip(masks, windows)]
    pair = lanes[0]
    swap_tensor = [(i, (i + 1) % splits) for i in range(splits)]
    swap_group = [(0, 1), (1, 0)]
    split_id = split.astype(jnp.int32).reshape(1)

    def across(value):
        return lax.ppermute(value, "tensor", swap_tensor)

    def tall(array):
        return array.reshape(part, local_cols // LANES, LANES)

    w_in = tall(inner_in)
    w_out = inner_out.reshape(local_cols, part)
    shared_rows = lax.all_gather(inner_shared[0], ("dp", "tensor"), axis=0, tiled=True)

    half = hidden // 2
    flat_in = inner_in.reshape(part, local_cols)

    def sides(low, high):
        return (
            jnp.where(side == 0, low, high).astype(bf16),
            jnp.where(side == 0, high, low).astype(bf16),
        )

    block_q = flat_in[:, :qcols].astype(bf16)
    block_o = w_out[:qcols].astype(bf16)
    up_sides = sides(flat_in[:, qcols : qcols + half], flat_in[:, qcols + half :])
    down_sides = sides(w_out[qcols : qcols + half], w_out[qcols + half :])
    got_query = Gathered(block_q, block_q, lanes, 0)
    got_attn = Gathered(block_o, block_o, lanes, 1)
    got_up = Gathered(*up_sides, lanes, 0)
    got_down = Gathered(*down_sides, lanes, 1)
    weights = [got_query, got_attn, got_up, got_down]
    if levels == 3:
        order = [(0, 1, 0), (0, 2, 0), (1, 1, 0), (1, 2, 0), (0, 2, 2), (2, 1, 0), (2, 2, 0),
                 (1, 2, 2), (3, 1, 0), (3, 2, 0), (2, 2, 2), (3, 2, 2)]
        for which, level, o in order:
            weights[which].send(level, o)
    for weight in weights:
        weight.rest()
    w_query, w_attn, w_up, w_down = (weight.whole() for weight in weights)

    shared_t = shared_rows.T
    shared_rel = pick_blocks(shared_t, ids, part, count, False)
    w_keyval_t = shared_rel[:vec].astype(bf16)
    gain_one, bias_one, gain_two, bias_two = (shared_rel[vec + k : vec + k + 1] for k in range(4))
    bias_out, bias_down = shared_rel[vec + 5 : vec + 6], shared_rel[vec + 6 : vec + 7]
    bias_query = lax.dynamic_slice_in_dim(shared_t[vec + 4], split * qcols, qcols)
    bias_up = lax.dynamic_slice_in_dim(
        shared_t[vec + 7 :].reshape(FF), split * hidden + side * half, half
    )

    nt = (((1,), (1,)), ((), ()))
    tn = (((0,), (0,)), ((), ()))

    def mm(a, b, dims=(((1,), (0,)), ((), ()))):
        return lax.dot_general(a, b, dims, preferred_element_type=f32)

    def block(array, o, blocks):
        return array[:, o * part : (o + blocks) * part]

    def sum_rows(give, keep):
        other = across(give)
        theirs = keep[mine:].astype(f32) + other[mine:].astype(f32)
        theirs = pair.at_once(swap_small(theirs.astype(bf16), part))
        return other, theirs

    def both_rows(rows):
        other = across(rows)
        whole = jnp.zeros((total, width), rows.dtype)
        whole = lax.dynamic_update_slice_in_dim(whole, rows, split * mine, 0)
        return lax.dynamic_update_slice_in_dim(whole, other, (1 - split) * mine, 0)

    cot_own, cot_pair, grad_bias_down = cotangent_order(cotangent, ids, split_id, count)
    cot_theirs = pair.at_once(swap_small(cot_pair, part))
    cot_all = jnp.concatenate(
        [cot_own[:mine], cot_theirs, cot_own[mine:], across(cot_theirs)], axis=0
    )
    x_rel, normed = first_norm(tokens, ids, split_id, gain_one, bias_one, count)
    limits, limits_t = score_limits(doc_lengths[0], total, split * mine)
    key_value = mm(normed, w_keyval_t, nt).astype(bf16)
    queries = (mm(normed, w_query) + bias_query).astype(bf16)
    attended, log_totals, tops = attention_forward(queries, key_value, limits, heads)
    attn_give = mm(attended[mine:], w_attn).astype(bf16)
    attn_keep = mm(attended[:mine], w_attn).astype(bf16)
    middle, normed_two, normed_pair = middle_norm(
        x_rel, attn_keep, across(attn_give), bias_out, gain_two, bias_two, part
    )
    normed_first = jnp.concatenate(
        [normed_two, pair.at_once(swap_small(normed_pair, part))], axis=0
    )
    normed_all = jnp.concatenate([normed_first, across(normed_first)], axis=0)

    all_tops = lax.all_gather(tops, ("group", "dp", "tensor"), axis=0)
    all_tops = jnp.max(all_tops.reshape((-1, splits * heads, LANES)), axis=0)
    clip_rows = clip_limit / jnp.maximum(all_tops, clip_limit)

    pre_act = mm(normed_all, w_up) + bias_up
    act_value, act_pull = jax.vjp(lambda v: jax.nn.gelu(v, approximate=True), pre_act)
    acts = act_value.astype(bf16)
    sum_down = Reduced(lambda o, b: mm(acts, block(cot_all, o, b), tn), lanes, 1, part)
    top = levels - 1
    sent_down = sum_down.level(top)

    grad_pre = act_pull(mm(cot_all, after(w_down, *sent_down), nt))[0].astype(bf16)
    grad_bias_up = jnp.sum(grad_pre.astype(f32), axis=0)
    sum_up = Reduced(lambda o, b: mm(block(normed_all, o, b), grad_pre, tn), lanes, 0, part)
    sent_up = sum_up.level(top)
    for level in range(top - 1, 0, -1):
        sent_down = sum_down.level(level)
    w_up_late = after(w_up, *sent_up, *sent_down)
    two_give = mm(grad_pre[2 * mine :], w_up_late, nt).astype(bf16)
    two_keep = mm(grad_pre[: 2 * mine], w_up_late, nt).astype(bf16)
    two_other, two_pair = sum_rows(two_give, two_keep)
    dh, dh_mine, grad_gain_two, grad_bias_two, grad_bias_out = middle_backward(
        middle, two_keep, two_other, two_pair, cot_own, gain_two, part
    )
    dh_low = jnp.concatenate([dh_mine, across(dh_mine)], axis=0)
    red_down = sum_down.finish()

    acts_late = after(acts, two_give, two_keep)
    down_give = mm(acts_late[2 * mine :], w_down).astype(bf16)
    down_keep = mm(acts_late[: 2 * mine], w_down).astype(bf16)
    down_other, down_pair = sum_rows(down_give, down_keep)
    block_out = both_rows(
        block_result(middle, down_keep, down_other, down_pair, bias_down, ids, count)
    )

    grad_att = mm(dh_low, w_attn, nt).astype(bf16)
    sum_attn = Reduced(lambda o, b: mm(attended, block(dh_low, o, b), tn), lanes, 1, part)
    sent_attn = sum_attn.level(top)
    for level in range(top - 1, 0, -1):
        sum_up.level(level)
    dots = jnp.sum(
        (grad_att.astype(f32) * attended.astype(f32)).reshape(total, heads, HD), axis=2
    )
    grad_queries, kv_part = attention_backward(
        queries, after(grad_att, *sent_attn), key_value, limits_t, log_totals.T[:heads], dots.T,
        heads,
    )
    sum_query = Reduced(lambda o, b: mm(block(normed, o, b), grad_queries, tn), lanes, 0, part)
    sent_query = sum_query.level(top)
    w_query_late = after(w_query, *sent_query)
    one_give = mm(grad_queries[mine:], w_query_late, nt).astype(bf16)
    one_keep = mm(grad_queries[:mine], w_query_late, nt).astype(bf16)
    kv_low = (kv_part[:mine] + across(kv_part[mine:])).astype(bf16)
    grad_keyval_t = mm(kv_low, normed[:mine], tn)
    red_up = sum_up.finish()
    for level in range(top - 1, 0, -1):
        sum_attn.level(level)
    for level in range(top - 1, 0, -1):
        sum_query.level(level)
    attn_mine, attn_pair = sum_attn.finish()
    query_mine, query_pair = sum_query.finish()
    grad_mine, grad_gain_one, grad_bias_one = first_backward(
        x_rel, one_keep, across(one_give), kv_low, w_keyval_t, dh, gain_one, ids, count
    )
    tokens_grad = both_rows(grad_mine)

    grad_bias_query = jnp.sum(grad_queries.astype(f32), axis=0)
    spread = jnp.concatenate(
        [
            lax.dynamic_update_slice_in_dim(
                jnp.zeros((width,), f32), grad_bias_query, split * qcols, 0
            ),
            lax.dynamic_update_slice_in_dim(
                jnp.zeros((FF,), f32), grad_bias_up, split * hidden + side * half, 0
            ),
        ]
    ).reshape(1 + FF // width, width)
    near = jnp.concatenate(
        [grad_keyval_t, grad_gain_one, grad_bias_one, grad_gain_two, grad_bias_two, grad_bias_out,
         grad_bias_down],
        axis=0,
    )
    steps = jnp.arange(count, dtype=jnp.int32)

    def pieces(core):
        a = pick_blocks(near, steps * splits + core, own_cols, count, True)
        b = pick_blocks(spread, ids * splits + core, own_cols, count, True)
        return jnp.concatenate([a[:, : vec + 4], b[:, :1], a[:, vec + 4 :], b[:, 1:]], axis=1)

    red_shared = pieces(split) + across(pieces(1 - split))
    for lane in reversed(lanes):
        keep = red_shared.shape[0] // 2
        red_shared = red_shared[:keep] + lane.at_once(red_shared[keep:])
    red_shared = red_shared[0]

    one_in, two_in = tall(first_in), tall(second_in)
    one_out, two_out = (a.reshape(local_cols, part) for a in (first_out, second_out))
    base_in, mom_in = tall(outer_in_w), tall(momentum_in)
    base_out, mom_out = (a.reshape(local_cols, part) for a in (outer_out_w, momentum_out))
    clip_own = lax.dynamic_slice_in_dim(clip_rows, split * heads, heads)

    def swap(value):
        return lax.ppermute(value, "group", swap_group)

    starts = [qcols + side * half, qcols + (1 - side) * half]
    zero = jnp.zeros((), jnp.int32)
    full_in = full_out = new_in = new_out = None
    for s, gradient in zip(starts, red_down):
        *full_out, delta = adam_out(gradient, w_out, one_out, two_out, base_out, s, full_out)
        new_out = outer_out(delta, swap(delta), mom_out, base_out, s, new_out)
    for s, gradient in zip(starts, red_up):
        *full_in, delta = adam_in(gradient, w_in, one_in, two_in, base_in, s, full_in)
        new_in = outer_in(delta, swap(delta), mom_in, base_in, None, s, new_in)
    red_attn = attn_mine + attn_pair.astype(f32)
    *full_out, delta = adam_out(red_attn, w_out, one_out, two_out, base_out, zero, full_out)
    new_out = outer_out(delta, swap(delta), mom_out, base_out, zero, new_out)
    red_query = query_mine + query_pair.astype(f32)
    *full_in, delta = adam_in(red_query, w_in, one_in, two_in, base_in, zero, full_in)
    new_in = outer_in(delta, swap(delta), mom_in, base_in, clip_own, zero, new_in)

    ids_col = jnp.arange(shared_cols, dtype=jnp.int32)[:, None]
    one_sh, two_sh, stepped = adam_values(
        red_shared,
        inner_shared[0].T,
        first_shared[0].T,
        second_shared[0].T,
        jnp.where(ids_col < vec, rate_matrix, rate_vector),
        jnp.where(ids_col < vec, weight_decay, 0.0),
    )
    base_sh = outer_shared.T
    delta = (base_sh - stepped).astype(bf16)
    mean_sh = (delta.astype(f32) + swap(delta).astype(f32)) * 0.5
    vel_sh, fresh_sh = outer_values(mean_sh, momentum_shared.T, base_sh)
    row_ids = (place * splits + split) * own_cols + jnp.arange(own_cols, dtype=jnp.int32)
    clip_vec = clip_rows[:, 0]
    row_clip = jnp.sum(
        jnp.where((row_ids // HD)[None, :] == jnp.arange(HEADS)[:, None], clip_vec[:, None], 0.0),
        axis=0,
    )
    fresh_sh = fresh_sh * jnp.where(ids_col == vec + 4, row_clip[None, :], 1.0)

    shape_in, shape_out = (part, 1, local_cols), (1, local_cols, part)
    mean_in, vel_in, fresh_in, copy_in = new_in
    mean_out, vel_out, fresh_out, copy_out = new_out
    return (
        block_out,
        tokens_grad,
        clip_vec,
        full_in[0].reshape((1,) + shape_in),
        full_out[0].reshape((1,) + shape_out),
        one_sh.T[None],
        full_in[1].reshape((1,) + shape_in),
        full_out[1].reshape((1,) + shape_out),
        two_sh.T[None],
        mean_in.reshape(shape_in),
        mean_out.reshape(shape_out),
        mean_sh.T,
        vel_in.reshape(shape_in),
        vel_out.reshape(shape_out),
        vel_sh.T,
        fresh_in.reshape(shape_in),
        fresh_out.reshape(shape_out),
        fresh_sh.T,
        copy_in.reshape(shape_in),
        copy_out.reshape(shape_out),
        fresh_sh.T.astype(bf16),
    )


def solution(mesh):
    rows = P(("group", "dp"), None)
    inner = [P("group", "dp", "tensor", None), P("group", "tensor", None, "dp"),
             P("group", ("dp", "tensor"), None)]
    outer = [P("dp", "tensor", None), P("tensor", None, "dp"), P(("dp", "tensor"), None)]
    in_specs = tuple([rows] * 3 + inner * 3 + outer * 2)
    out_specs = tuple([rows] * 2 + [P()] + inner * 2 + outer * 4)
    return jax.shard_map(local, mesh=mesh, in_specs=in_specs, out_specs=out_specs, check_vma=False)
```

```python
import jax
import jax.numpy as jnp
from jax import lax
from jax.experimental import pallas as pl
from jax.experimental.pallas import tpu as pltpu
from jax.sharding import PartitionSpec as P

HEADS = 16
HD = 128
FF = 8192
BLOCK = 256
STEP = 10

norm_eps = 1e-05
hidden_score = -1e30
shown_score = 3e38
beta_one = 0.9
beta_two = 0.95
adam_eps = 1e-08
rate_matrix = 0.02
rate_vector = 0.2
weight_decay = 0.1
outer_beta = 0.9
outer_rate = 0.7
clip_limit = 5.0
score_scale = HD ** (-0.5)
log2_e = 1.4426950408889634
correct_one = 1.0 / (1.0 - beta_one**STEP)
correct_two = 1.0 / (1.0 - beta_two**STEP)

f32 = jnp.float32
bf16 = jnp.bfloat16
ROWS = 128
LANES = 128
VMEM_LIMIT = 40 * 1024 * 1024
VMEM_MOST = 58 * 1024 * 1024


def shape(dims, dtype):
    return jax.ShapeDtypeStruct(dims, dtype)


def call(body, out_shape, grid, in_specs, out_specs, args, *, ids=(), scratch=(), aliases=None,
         flops=0, name=None, vmem=VMEM_LIMIT):
    outs = out_shape if isinstance(out_shape, (list, tuple)) else [out_shape]
    moved = sum(a.size * a.dtype.itemsize for a in args)
    moved += sum(o.size * o.dtype.itemsize for o in outs)
    return pl.pallas_call(
        body,
        out_shape=out_shape,
        grid_spec=pltpu.PrefetchScalarGridSpec(
            num_scalar_prefetch=len(ids),
            grid=grid,
            in_specs=in_specs,
            out_specs=out_specs,
            scratch_shapes=list(scratch),
        ),
        input_output_aliases={len(ids) + k: v for k, v in (aliases or {}).items()},
        compiler_params=pltpu.CompilerParams(vmem_limit_bytes=vmem),
        cost_estimate=pl.CostEstimate(flops=flops, bytes_accessed=moved, transcendentals=0),
        name=name,
    )(*ids, *args)


def pick_blocks(array, block_ids, width, count, stacked):
    rows = array.shape[0]
    if width % LANES:
        taken = jnp.take(array.reshape(rows, -1, width), block_ids, axis=1)
        return taken.transpose(1, 0, 2) if stacked else taken.reshape(rows, count * width)

    def body(ids_ref, in_ref, out_ref):
        if stacked:
            out_ref[0] = in_ref[...]
        else:
            out_ref[...] = in_ref[...]

    if stacked:
        out, spec = shape((count, rows, width), array.dtype), pl.BlockSpec(
            (1, rows, width), lambda j, ids: (j, 0, 0)
        )
    else:
        out, spec = shape((rows, count * width), array.dtype), pl.BlockSpec(
            (rows, width), lambda j, ids: (0, j)
        )
    return call(
        body, out, (count,), [pl.BlockSpec((rows, width), lambda j, ids: (0, ids[j]))], spec,
        [array], ids=[block_ids], name="pick_blocks",
    )


def columns_of(block_id, width):
    return pl.ds(pl.multiple_of(block_id * width, width), width)


def placing(array, ids, count):
    part = array.shape[1] // count
    if part % LANES == 0:
        return array, count, part
    return pick_blocks(array, ids, part, count, False), 0, part


def put_back(array, ids, count):
    part = array.shape[1] // count
    if part % LANES == 0:
        return array
    back = jnp.sum(
        jnp.where(ids[None, :] == jnp.arange(count)[:, None], jnp.arange(count)[None, :], 0), axis=1
    ).astype(jnp.int32)
    return pick_blocks(array, back, part, count, False)


def norm_stats(rows):
    mean = jnp.mean(rows, axis=-1, keepdims=True)
    centered = rows - mean
    inv = lax.rsqrt(jnp.mean(centered * centered, axis=-1, keepdims=True) + norm_eps)
    return centered * inv, inv


def row_spec(cols, rows=ROWS):
    return pl.BlockSpec((rows, cols), lambda i, *ids: (i, 0))


def turned_spec(cols, blocks):
    return pl.BlockSpec(
        (ROWS, cols), lambda i, ids, split: ((i + split[0] * (blocks // 2)) % blocks, 0)
    )


def whole_spec(rows, cols):
    return pl.BlockSpec((rows, cols), lambda i, *ids: (0, 0))


def first_norm(tokens, ids, split, gain, bias, count):
    total, width = tokens.shape
    tokens, moved, part = placing(tokens, ids, count)

    def body(ids_ref, split_ref, x_ref, g_ref, c_ref, x_out, n_out):
        for o in range(moved):
            x_out[:, o * part : (o + 1) * part] = x_ref[:, columns_of(ids_ref[o], part)]
        if not moved:
            x_out[...] = x_ref[...]
        unit, _ = norm_stats(x_out[...].astype(f32))
        n_out[...] = (unit * g_ref[...] + c_ref[...]).astype(bf16)

    return call(
        body,
        [shape((total, width), bf16)] * 2,
        (total // ROWS,),
        [turned_spec(width, total // ROWS), whole_spec(1, width), whole_spec(1, width)],
        [row_spec(width)] * 2,
        [tokens, gain, bias],
        ids=[ids, split],
        name="first_norm",
    )


def first_spec(cols, blocks):
    return pl.BlockSpec((ROWS, cols), lambda i, *ids: (jnp.minimum(i, blocks - 1), 0))


def swapped(values, part):
    if part % LANES:
        return values
    blocks = [values[:, o : o + part] for o in range(0, values.shape[1], part)]
    return jnp.concatenate([blocks[pair_of(o)] for o in range(len(blocks))], axis=1)


def pair_of(o):
    return o if o & 2 else o ^ 1


def swap_small(values, part):
    if part % LANES == 0:
        return values
    blocks = [values[:, o : o + part] for o in range(0, values.shape[1], part)]
    return jnp.concatenate([blocks[pair_of(o)] for o in range(len(blocks))], axis=1)


def cotangent_order(cotangent, ids, split, count):
    total, width = cotangent.shape
    cotangent, moved, part = placing(cotangent, ids, count)
    mine = total // ROWS // 2

    def body(ids_ref, split_ref, c_ref, c_out, pair_out, sum_out):
        for o in range(moved):
            c_out[:, o * part : (o + 1) * part] = c_ref[:, columns_of(ids_ref[o], part)]
        if not moved:
            c_out[...] = c_ref[...]

        @pl.when(pl.program_id(0) < mine)
        def _():
            pair_out[...] = swapped(c_out[...], part)
            add_rows(sum_out, c_out[...].astype(f32))

    return call(
        body,
        [shape((total, width), bf16), shape((total // 2, width), bf16), shape((1, width), f32)],
        (total // ROWS,),
        [turned_spec(width, total // ROWS)],
        [row_spec(width), first_spec(width, mine), whole_spec(1, width)],
        [cotangent],
        ids=[ids, split],
        name="cotangent_order",
    )


def add_rows(sum_ref, values):
    @pl.when(pl.program_id(0) == 0)
    def _():
        sum_ref[...] = jnp.zeros_like(sum_ref)

    sum_ref[...] += jnp.sum(values, axis=0, keepdims=True)


def middle_norm(x_rel, part_own, part_other, bias_out, gain, bias, part):
    total, width = part_other.shape

    def body(x_ref, a_ref, b_ref, bo_ref, g_ref, c_ref, h_out, n_out, pair_out):
        mid = x_ref[...].astype(f32) + (
            a_ref[...].astype(f32) + b_ref[...].astype(f32)
        ) + bo_ref[...]
        h_out[...] = mid
        unit, _ = norm_stats(mid)
        low = (unit * g_ref[...] + c_ref[...]).astype(bf16)
        n_out[...] = low
        pair_out[...] = swapped(low, part)

    return call(
        body,
        [shape((total, width), f32)] + [shape((total, width), bf16)] * 2,
        (total // ROWS,),
        [row_spec(width)] * 3 + [whole_spec(1, width)] * 3,
        [row_spec(width)] * 3,
        [x_rel, part_own, part_other, bias_out, gain, bias],
        name="middle_norm",
    )


def block_result(middle, part_own, part_other, part_pair, bias_down, ids, count):
    total, width = middle.shape
    part = width // count

    def body(ids_ref, h_ref, a_ref, b_ref, p_ref, b2_ref, out_ref):
        value = a_ref[...].astype(f32) + b_ref[...].astype(f32)
        value = h_ref[...] + (value + swapped(p_ref[...], part).astype(f32)) + b2_ref[...]
        value = value.astype(bf16)
        if part % LANES:
            out_ref[...] = value
        else:
            for o in range(count):
                out_ref[:, columns_of(ids_ref[o], part)] = value[:, o * part : (o + 1) * part]

    result = call(
        body,
        shape((total, width), bf16),
        (total // ROWS,),
        [row_spec(width)] * 4 + [whole_spec(1, width)],
        row_spec(width),
        [middle, part_own, part_other, part_pair, bias_down],
        ids=[ids],
        name="block_result",
    )
    return put_back(result, ids, count)


def middle_backward(middle, part_own, part_other, part_pair, cot_rel, gain, part):
    total, width = middle.shape

    def body(h_ref, a_ref, b_ref, p_ref, dy_ref, g_ref, dh_out, low_out, gg_out, gc_out, gbo_out):
        unit, inv = norm_stats(h_ref[...])
        grad = a_ref[...].astype(f32) + b_ref[...].astype(f32)
        grad = grad + swapped(p_ref[...], part).astype(f32)
        scaled = grad * g_ref[...]
        dh = dy_ref[...].astype(f32) + inv * (
            scaled
            - jnp.mean(scaled, axis=-1, keepdims=True)
            - unit * jnp.mean(scaled * unit, axis=-1, keepdims=True)
        )
        dh_out[...] = dh
        low = dh.astype(bf16)
        low_out[...] = low
        add_rows(gg_out, grad * unit)
        add_rows(gc_out, grad)
        add_rows(gbo_out, low.astype(f32))

    vec = shape((1, width), f32)
    return call(
        body,
        [shape((total, width), f32), shape((total, width), bf16), vec, vec, vec],
        (total // ROWS,),
        [row_spec(width)] * 5 + [whole_spec(1, width)],
        [row_spec(width)] * 2 + [whole_spec(1, width)] * 3,
        [middle, part_own, part_other, part_pair, cot_rel, gain],
        name="middle_backward",
    )


def first_backward(x_rel, part_own, part_other, keyval_grad, w_keyval_t, dh, gain, ids, count):
    total, width = dh.shape
    part = width // count
    kv = keyval_grad.shape[1]

    def body(ids_ref, x_ref, a_ref, b_ref, kv_ref, w_ref, dh_ref, g_ref, t_out, gg_out, gc_out):
        unit, inv = norm_stats(x_ref[...].astype(f32))
        grad = (a_ref[...].astype(f32) + b_ref[...].astype(f32)) + jnp.dot(
            kv_ref[...], w_ref[...], preferred_element_type=f32
        )
        scaled = grad * g_ref[...]
        value = dh_ref[...] + inv * (
            scaled
            - jnp.mean(scaled, axis=-1, keepdims=True)
            - unit * jnp.mean(scaled * unit, axis=-1, keepdims=True)
        )
        low = value.astype(bf16)
        if part % LANES:
            t_out[...] = low
        else:
            for o in range(count):
                t_out[:, columns_of(ids_ref[o], part)] = low[:, o * part : (o + 1) * part]
        add_rows(gg_out, grad * unit)
        add_rows(gc_out, grad)

    vec = shape((1, width), f32)
    result, gain_grad, bias_grad = call(
        body,
        [shape((total, width), bf16), vec, vec],
        (total // ROWS,),
        [row_spec(width)] * 3
        + [row_spec(kv), whole_spec(kv, width), row_spec(width), whole_spec(1, width)],
        [row_spec(width)] + [whole_spec(1, width)] * 2,
        [x_rel, part_own, part_other, keyval_grad, w_keyval_t, dh, gain],
        ids=[ids],
        flops=2 * total * width * kv,
        name="first_backward",
    )
    return put_back(result, ids, count), gain_grad, bias_grad


TILE = 256


def score_limits(lengths, token_count, first_place):
    doc_ends = jnp.cumsum(lengths)
    doc_starts = doc_ends - lengths
    places = (jnp.arange(token_count, dtype=jnp.int32) + first_place) % token_count
    doc_ids = jnp.sum((places[:, None] >= doc_ends[None, :]).astype(jnp.int32), axis=1)
    owners = doc_ids[:, None] == jnp.arange(lengths.shape[0], dtype=jnp.int32)[None, :]
    doc_begin = jnp.sum(jnp.where(owners, doc_starts[None, :], 0), axis=1)
    blocks = (places - doc_begin) // BLOCK
    seen = (doc_ids[:, None] == doc_ids[None, :]) & (blocks[None, :] <= blocks[:, None])
    seen_t = (doc_ids[None, :] == doc_ids[:, None]) & (blocks[:, None] <= blocks[None, :])
    pick = lambda s: jnp.where(s, shown_score, hidden_score).astype(f32)
    return pick(seen), pick(seen_t)


def attention_forward(queries, key_value, limits, heads):
    total = queries.shape[0]
    tiles = total // TILE
    c = score_scale * log2_e

    def body(q_ref, kv_ref, lim_ref, o_ref, lse_ref, top_ref):
        tile, head = pl.program_id(0), pl.program_id(1)
        k = kv_ref[:, :HD]
        v = kv_ref[:, HD:]
        s = lax.dot_general(
            q_ref[...], k, (((1,), (1,)), ((), ())), preferred_element_type=f32
        )
        s = jnp.minimum(s, lim_ref[...])
        m = jnp.max(s, axis=1, keepdims=True)
        p = jnp.exp2((s - m) * c)
        l = jnp.sum(p, axis=1, keepdims=True)
        o = jnp.dot(p.astype(bf16), v, preferred_element_type=f32)
        o_ref[...] = (o / l).astype(bf16)
        lane = lax.broadcasted_iota(jnp.int32, (TILE, LANES), 1)
        lse = m * c + jnp.log2(l)
        lse_ref[...] = jnp.where(lane == head, lse, lse_ref[...])

        @pl.when((tile == 0) & (head == 0))
        def _():
            top_ref[...] = jnp.full_like(top_ref, hidden_score)

        row = lax.broadcasted_iota(jnp.int32, (heads, LANES), 0)
        best = jnp.max(m, axis=0, keepdims=True) * score_scale
        top_ref[...] = jnp.where(row == head, jnp.maximum(top_ref[...], best), top_ref[...])

    return call(
        body,
        [shape((total, heads * HD), bf16), shape((total, LANES), f32), shape((heads, LANES), f32)],
        (tiles, heads),
        [
            pl.BlockSpec((TILE, HD), lambda i, h: (i, h)),
            pl.BlockSpec((total, 2 * HD), lambda i, h: (0, 0)),
            pl.BlockSpec((TILE, total), lambda i, h: (i, 0)),
        ],
        [
            pl.BlockSpec((TILE, HD), lambda i, h: (i, h)),
            pl.BlockSpec((TILE, LANES), lambda i, h: (i, 0)),
            pl.BlockSpec((heads, LANES), lambda i, h: (0, 0)),
        ],
        [queries, key_value, limits],
        flops=8 * total * total * HD * heads,
        name="attention_forward",
    )


def attention_backward(queries, grad_att, key_value, limits_t, lse_t, dot_t, heads):
    total = queries.shape[0]
    tiles = total // TILE
    c = score_scale * log2_e

    def body(q_ref, da_ref, kv_ref, lim_ref, lse_ref, dot_ref, dq_ref, dkv_ref):
        tile, head = pl.program_id(0), pl.program_id(1)
        k = kv_ref[:, :HD]
        v = kv_ref[:, HD:]
        q = q_ref[...]
        da = da_ref[...]
        nt = (((1,), (1,)), ((), ()))
        s = lax.dot_general(k, q, nt, preferred_element_type=f32)
        s = jnp.minimum(s, lim_ref[...])
        p = jnp.exp2(s * c - lse_ref[pl.ds(head, 1), :])
        dp = lax.dot_general(v, da, nt, preferred_element_type=f32)
        ds = (p * (dp - dot_ref[pl.ds(head, 1), :])).astype(bf16)
        dq = lax.dot_general(ds, k, (((0,), (0,)), ((), ())), preferred_element_type=f32)
        dq_ref[...] = (dq * score_scale).astype(bf16)

        @pl.when((tile == 0) & (head == 0))
        def _():
            dkv_ref[...] = jnp.zeros_like(dkv_ref)

        dkv_ref[:, :HD] += jnp.dot(ds, q, preferred_element_type=f32) * score_scale
        dkv_ref[:, HD:] += jnp.dot(p.astype(bf16), da, preferred_element_type=f32)

    return call(
        body,
        [shape((total, heads * HD), bf16), shape((total, 2 * HD), f32)],
        (tiles, heads),
        [
            pl.BlockSpec((TILE, HD), lambda i, h: (i, h)),
            pl.BlockSpec((TILE, HD), lambda i, h: (i, h)),
            pl.BlockSpec((total, 2 * HD), lambda i, h: (0, 0)),
            pl.BlockSpec((total, TILE), lambda i, h: (0, i)),
            pl.BlockSpec((heads, TILE), lambda i, h: (0, i)),
            pl.BlockSpec((heads, TILE), lambda i, h: (0, i)),
        ],
        [
            pl.BlockSpec((TILE, HD), lambda i, h: (i, h)),
            pl.BlockSpec((total, 2 * HD), lambda i, h: (0, 0)),
        ],
        [queries, grad_att, key_value, limits_t, lse_t, dot_t],
        flops=20 * total * total * HD * heads,
        name="attention_backward",
    )


def adam_values(gradient, weight, one, two, rate, decay):
    new_one = beta_one * one + (1.0 - beta_one) * gradient
    new_two = beta_two * two + (1.0 - beta_two) * gradient * gradient
    direction = (new_one * correct_one) / (jnp.sqrt(new_two * correct_two) + adam_eps)
    return new_one, new_two, weight - rate * (direction + decay * weight)


def to_tiles(flat, tiles_ref):
    for j in range(8):
        tiles_ref[:, j, :] = flat[:, j * LANES : (j + 1) * LANES]


def adam_in(gradient, weight, one, two, outer, start, full):
    rows, cols = gradient.shape
    step = 64
    base = (start // 1024).reshape(1)
    tall = pl.BlockSpec((step, 8, LANES), lambda i, j, b: (i, b[0] + j, 0))
    flat = pl.BlockSpec((step, 1024), lambda i, j, b: (i, j))
    args = [gradient, weight, one, two, outer]
    specs = [flat] + [tall] * 4
    aliases = {}
    if full is not None:
        aliases = {5: 0, 6: 1}
        args += list(full)
        specs += [pl.BlockSpec(memory_space=pl.ANY)] * 2

    def body(_, g_ref, w_ref, one_ref, two_ref, out_ref, *rest):
        one_out, two_out, delta_out, grad_tiles, delta_tiles = rest[-5:]
        to_tiles(g_ref[...].astype(f32), grad_tiles)
        new_one, new_two, stepped = adam_values(
            grad_tiles[...], w_ref[...], one_ref[...], two_ref[...], rate_matrix, weight_decay
        )
        one_out[...] = new_one
        two_out[...] = new_two
        delta_tiles[...] = out_ref[...] - stepped
        for j in range(8):
            delta_out[:, j * LANES : (j + 1) * LANES] = delta_tiles[:, j, :].astype(bf16)

    whole = shape(weight.shape, f32)
    return call(
        body,
        [whole, whole, shape((rows, cols), bf16)],
        (rows // step, cols // 1024),
        specs,
        [tall, tall, flat],
        args,
        ids=[base],
        scratch=[pltpu.VMEM((step, 8, LANES), f32)] * 2,
        aliases=aliases,
        name="adam_in",
        vmem=VMEM_MOST,
    )


def adam_out(gradient, weight, one, two, outer, start, full):
    rows, cols = gradient.shape
    step = 512
    base = (start // step).reshape(1)
    tall = pl.BlockSpec((step, cols), lambda i, b: (b[0] + i, 0))
    flat = pl.BlockSpec((step, cols), lambda i, b: (i, 0))
    args = [gradient, weight, one, two, outer]
    specs = [flat] + [tall] * 4
    aliases = {}
    if full is not None:
        aliases = {5: 0, 6: 1}
        args += list(full)
        specs += [pl.BlockSpec(memory_space=pl.ANY)] * 2

    def body(_, g_ref, w_ref, one_ref, two_ref, out_ref, *rest):
        one_out, two_out, delta_out = rest[-3:]
        new_one, new_two, stepped = adam_values(
            g_ref[...].astype(f32), w_ref[...], one_ref[...], two_ref[...], rate_matrix,
            weight_decay,
        )
        one_out[...] = new_one
        two_out[...] = new_two
        delta_out[...] = (out_ref[...] - stepped).astype(bf16)

    whole = shape(weight.shape, f32)
    return call(
        body,
        [whole, whole, shape((rows, cols), bf16)],
        (rows // step,),
        specs,
        [tall, tall, flat],
        args,
        ids=[base],
        aliases=aliases,
        name="adam_out",
        vmem=VMEM_MOST,
    )


def outer_values(mean, momentum, outer):
    velocity = outer_beta * momentum + mean
    return velocity, outer - outer_rate * (mean + outer_beta * velocity)


def outer_in(own, other, momentum, outer, factor, start, full):
    rows, cols = own.shape
    step = 64
    base = (start // 1024).reshape(1)
    tall = pl.BlockSpec((step, 8, LANES), lambda i, j, b: (i, b[0] + j, 0))
    flat = pl.BlockSpec((step, 1024), lambda i, j, b: (i, j))
    wide = pl.BlockSpec((step, 1024), lambda i, j, b: (i, b[0] + j))
    args = [own, other, momentum, outer]
    specs = [flat, flat, tall, tall]
    if factor is not None:
        args.append(factor)
        specs.append(pl.BlockSpec((8, LANES), lambda i, j, b: (0, 0)))
    aliases = {}
    if full is not None:
        aliases = {len(args) + k: k for k in range(4)}
        args += list(full)
        specs += [pl.BlockSpec(memory_space=pl.ANY)] * 4

    def body(_, own_ref, other_ref, mom_ref, out_ref, *rest):
        mean_out, vel_out, new_out, copy_out, mean_tiles, new_tiles = rest[-6:]
        to_tiles((own_ref[...].astype(f32) + other_ref[...].astype(f32)) * 0.5, mean_tiles)
        mean = mean_tiles[...]
        velocity, fresh = outer_values(mean, mom_ref[...], out_ref[...])
        if factor is not None:
            fresh = fresh * rest[0][...][None]
        mean_out[...] = mean
        vel_out[...] = velocity
        new_out[...] = fresh
        new_tiles[...] = fresh
        for j in range(8):
            copy_out[:, j * LANES : (j + 1) * LANES] = new_tiles[:, j, :].astype(bf16)

    whole = shape(outer.shape, f32)
    return call(
        body,
        [whole, whole, whole, shape((rows, outer.shape[1] * LANES), bf16)],
        (rows // step, cols // 1024),
        specs,
        [tall, tall, tall, wide],
        args,
        ids=[base],
        scratch=[pltpu.VMEM((step, 8, LANES), f32)] * 2,
        aliases=aliases,
        name="outer_in",
        vmem=VMEM_MOST,
    )


def outer_out(own, other, momentum, outer, start, full):
    rows, cols = own.shape
    step = 512
    base = (start // step).reshape(1)
    tall = pl.BlockSpec((step, cols), lambda i, b: (b[0] + i, 0))
    flat = pl.BlockSpec((step, cols), lambda i, b: (i, 0))
    args = [own, other, momentum, outer]
    specs = [flat, flat, tall, tall]
    aliases = {}
    if full is not None:
        aliases = {4 + k: k for k in range(4)}
        args += list(full)
        specs += [pl.BlockSpec(memory_space=pl.ANY)] * 4

    def body(_, own_ref, other_ref, mom_ref, out_ref, *rest):
        mean_out, vel_out, new_out, copy_out = rest[-4:]
        mean = (own_ref[...].astype(f32) + other_ref[...].astype(f32)) * 0.5
        velocity, fresh = outer_values(mean, mom_ref[...], out_ref[...])
        mean_out[...] = mean
        vel_out[...] = velocity
        new_out[...] = fresh
        copy_out[...] = fresh.astype(bf16)

    whole = shape(outer.shape, f32)
    return call(
        body,
        [whole, whole, whole, shape(outer.shape, bf16)],
        (rows // step,),
        specs,
        [tall] * 4,
        args,
        ids=[base],
        aliases=aliases,
        name="outer_out",
        vmem=VMEM_MOST,
    )


class Lane:
    def __init__(self, window):
        self.window, self.landed = window, []

    def send(self, block, pairs):
        if len(self.landed) >= self.window:
            block, _ = lax.optimization_barrier((block, self.landed[-self.window]))
        arrived = lax.ppermute(block, "dp", pairs)
        self.landed.append(arrived)
        return arrived


class Links:
    def __init__(self, count):
        self.levels = count.bit_length() - 1
        self.far = ([1] + [1 << b for b in range(3, self.levels)])[: self.levels - 2]
        places = range(count)
        middle = [i for i in places if (i >> 1 ^ i >> 2) & 1]
        outer = [i for i in places if i not in middle]
        self.pair = [(i, i ^ 2) for i in places]
        self.inward = [(i, i ^ 2) for i in outer]
        self.outward = [(i, i ^ 2) for i in middle]
        self.between = [(i, i ^ 6) for i in middle]
        self.beside = [[(i, i ^ mask) for i in places] for mask in self.far]
        self.mirror = [(i, i ^ 6) for i in places]
        self.side_lane, self.middle_lane = Lane(2), Lane(1)
        self.far_lanes = [Lane(2) for _ in self.far]

    def flips(self, across):
        masks = [2, across] + self.far
        table = []
        for o in range(1 << self.levels):
            flip = 0
            for level, mask in enumerate(masks):
                if o >> level & 1:
                    flip ^= mask
            table.append(flip)
        return table

    def to_side(self, block, pairs):
        return self.side_lane.send(block, pairs)

    def to_middle(self, block):
        return self.middle_lane.send(block, self.between)

    def to_far(self, block, level):
        return self.far_lanes[level - 2].send(block, self.beside[level - 2])

    def to_pair(self, block):
        return lax.ppermute(block, "dp", self.pair)


def after(value, *earlier):
    return lax.optimization_barrier((value, *earlier))[0]


class Gathered:
    def __init__(self, links, axis, mine, other=None):
        self.links, self.axis, self.mine, self.other = links, axis, mine, other
        self.held = {}

    def join(self, *blocks):
        return jnp.concatenate(blocks, axis=self.axis)

    def near(self):
        give = self.mine if self.other is None else self.other
        self.held[0] = self.join(self.mine, self.links.to_side(give, self.links.pair))

    def inward(self):
        if self.other is not None:
            self.passed = self.links.to_side(self.mine, self.links.inward)

    def middle(self):
        if self.other is None:
            self.relay = self.direct = self.links.to_middle(self.held[0])
        else:
            self.relay = self.links.to_middle(self.join(self.other, self.passed))
            self.direct = self.links.to_middle(self.held[0])

    def outward(self):
        self.held[2] = self.direct + self.links.to_side(self.relay, self.links.outward)

    def far(self, level, o):
        self.held[o + (1 << level)] = self.links.to_far(self.held[o], level)

    def whole(self):
        for level in range(2, self.links.levels):
            for o in range(0, 1 << level, 2):
                if o + (1 << level) not in self.held:
                    self.far(level, o)
        return self.join(*[self.held[o] for o in sorted(self.held)])


class Reduced:
    def __init__(self, links, axis, size, halved, part):
        self.links, self.axis, self.size, self.halved, self.part = links, axis, size, halved, part
        self.landed = {}

    def pair_sum(self, o):
        total = self.part(o, 2)
        for block in self.landed.pop(o, []):
            total = total + block.astype(f32)
        return total.astype(bf16)

    def one(self, block, o):
        return lax.slice_in_dim(
            block, o * self.size, (o + 1) * self.size, axis=self.axis
        ).astype(f32)

    def far(self):
        sent = []
        for level in range(self.links.levels - 1, 1, -1):
            for o in reversed(range(1 << level, 2 << level, 2)):
                sent.append(self.pair_sum(o))
                arrived = self.links.to_far(sent[-1], level)
                self.landed.setdefault(o - (1 << level), []).append(arrived)
        return sent

    def inward(self):
        self.ahead = self.pair_sum(2)
        self.passed = self.links.to_side(self.ahead, self.links.inward)
        return self.ahead

    def middle(self):
        if self.halved:
            self.direct = self.links.to_middle(self.ahead)
            self.relay = self.links.to_middle(self.passed)
        else:
            self.direct = self.links.to_middle(self.ahead + self.passed)

    def finish(self):
        values = []
        for o in (1, 0):
            total = self.part(o, 1)
            for block in self.landed[0] + [self.direct]:
                total = total + self.one(block, o)
            values.append(total)
        theirs = self.links.to_side(values[0].astype(bf16), self.links.pair).astype(f32)
        if not self.halved:
            return values[1] + theirs, None
        passed = self.links.to_side(self.one(self.relay, 1).astype(bf16), self.links.outward)
        return values[1] + passed.astype(f32), theirs + self.one(self.relay, 0)


def local(
    tokens,
    doc_lengths,
    cotangent,
    inner_in,
    inner_out,
    inner_shared,
    first_in,
    first_out,
    first_shared,
    second_in,
    second_out,
    second_shared,
    outer_in_w,
    outer_out_w,
    outer_shared,
    momentum_in,
    momentum_out,
    momentum_shared,
):
    splits = lax.axis_size("tensor")
    count = lax.axis_size("dp")
    split = lax.axis_index("tensor")
    place = lax.axis_index("dp")
    total, width = tokens.shape
    part = width // count
    local_cols = inner_in.shape[3]
    shared_cols = inner_shared.shape[2]
    heads = HEADS // splits
    qcols = heads * HD
    hidden = local_cols - qcols
    vec = 2 * HD
    own_cols = part // splits
    mine = total // 2

    links = Links(count)
    levels = links.levels
    side = ((place >> 1) ^ (place >> 2)) & 1
    from_outer, from_middle = (jnp.array(links.flips(m), jnp.int32) for m in (4, 6))
    ids = (place ^ jnp.where(side == 0, from_outer, from_middle)).astype(jnp.int32)
    swap_tensor = [(i, (i + 1) % splits) for i in range(splits)]
    swap_group = [(0, 1), (1, 0)]
    split_id = split.astype(jnp.int32).reshape(1)

    def across(value):
        return lax.ppermute(value, "tensor", swap_tensor)

    def tall(array):
        return array.reshape(part, local_cols // LANES, LANES)

    w_in = tall(inner_in)
    w_out = inner_out.reshape(local_cols, part)
    shared_rows = lax.all_gather(inner_shared[0], ("dp", "tensor"), axis=0, tiled=True)

    half = hidden // 2
    flat_in = inner_in.reshape(part, local_cols)

    def sides(low, high):
        return (
            jnp.where(side == 0, low, high).astype(bf16),
            jnp.where(side == 0, high, low).astype(bf16),
        )

    block_q = flat_in[:, :qcols].astype(bf16)
    block_o = w_out[:qcols].astype(bf16)
    up_sides = sides(flat_in[:, qcols : qcols + half], flat_in[:, qcols + half :])
    down_sides = sides(w_out[qcols : qcols + half], w_out[qcols + half :])
    got_query = Gathered(links, 0, block_q)
    got_attn = Gathered(links, 1, block_o)
    got_up = Gathered(links, 0, *up_sides)
    got_down = Gathered(links, 1, *down_sides)
    got_query.near()
    got_attn.near()
    got_up.near()
    got_up.inward()
    got_query.middle()
    got_query.outward()
    got_attn.middle()
    got_attn.outward()
    got_up.middle()
    got_down.near()
    got_down.inward()
    got_up.outward()
    got_down.middle()
    got_down.outward()
    if levels == 3:
        for weight, o in [(got_query, 0), (got_attn, 0), (got_query, 2), (got_attn, 2),
                          (got_up, 0), (got_down, 0), (got_up, 2), (got_down, 2)]:
            weight.far(2, o)
    w_query, w_attn, w_up, w_down = (
        weight.whole() for weight in (got_query, got_attn, got_up, got_down)
    )

    shared_t = shared_rows.T
    shared_rel = pick_blocks(shared_t, ids, part, count, False)
    w_keyval_t = shared_rel[:vec].astype(bf16)
    gain_one, bias_one, gain_two, bias_two = (shared_rel[vec + k : vec + k + 1] for k in range(4))
    bias_out, bias_down = shared_rel[vec + 5 : vec + 6], shared_rel[vec + 6 : vec + 7]
    bias_query = lax.dynamic_slice_in_dim(shared_t[vec + 4], split * qcols, qcols)
    bias_up = lax.dynamic_slice_in_dim(
        shared_t[vec + 7 :].reshape(FF), split * hidden + side * half, half
    )

    nt = (((1,), (1,)), ((), ()))
    tn = (((0,), (0,)), ((), ()))

    def mm(a, b, dims=(((1,), (0,)), ((), ()))):
        return lax.dot_general(a, b, dims, preferred_element_type=f32)

    def block(array, o, blocks):
        return array[:, o * part : (o + blocks) * part]

    def sum_rows(give, keep):
        other = across(give)
        theirs = keep[mine:].astype(f32) + other[mine:].astype(f32)
        theirs = links.to_pair(swap_small(theirs.astype(bf16), part))
        return other, theirs

    def both_rows(rows):
        other = across(rows)
        whole = jnp.zeros((total, width), rows.dtype)
        whole = lax.dynamic_update_slice_in_dim(whole, rows, split * mine, 0)
        return lax.dynamic_update_slice_in_dim(whole, other, (1 - split) * mine, 0)

    cot_own, cot_pair, grad_bias_down = cotangent_order(cotangent, ids, split_id, count)
    cot_theirs = links.to_pair(swap_small(cot_pair, part))
    cot_all = jnp.concatenate(
        [cot_own[:mine], cot_theirs, cot_own[mine:], across(cot_theirs)], axis=0
    )
    x_rel, normed = first_norm(tokens, ids, split_id, gain_one, bias_one, count)
    limits, limits_t = score_limits(doc_lengths[0], total, split * mine)
    key_value = mm(normed, w_keyval_t, nt).astype(bf16)
    queries = (mm(normed, w_query) + bias_query).astype(bf16)
    attended, log_totals, tops = attention_forward(queries, key_value, limits, heads)
    attn_give = mm(attended[mine:], w_attn).astype(bf16)
    attn_keep = mm(attended[:mine], w_attn).astype(bf16)
    middle, normed_two, normed_pair = middle_norm(
        x_rel, attn_keep, across(attn_give), bias_out, gain_two, bias_two, part
    )
    normed_first = jnp.concatenate(
        [normed_two, links.to_pair(swap_small(normed_pair, part))], axis=0
    )
    normed_all = jnp.concatenate([normed_first, across(normed_first)], axis=0)

    tops = after(tops, normed_first)
    peers = across(tops)
    peak = jnp.where(
        split == 0, jnp.concatenate([tops, peers]), jnp.concatenate([peers, tops])
    )
    peak = jnp.maximum(peak, lax.ppermute(peak, "group", swap_group))
    for pairs in [links.pair, links.mirror] + links.beside:
        peak = jnp.maximum(peak, lax.ppermute(peak, "dp", pairs))
    clip_rows = clip_limit / jnp.maximum(peak, clip_limit)

    pre_act = mm(normed_all, w_up) + bias_up
    act_value, act_pull = jax.vjp(lambda v: jax.nn.gelu(v, approximate=True), pre_act)
    acts = act_value.astype(bf16)
    sum_down = Reduced(
        links, 1, part, True, lambda o, b: mm(acts, block(cot_all, o, b), tn)
    )
    sent_down = sum_down.far()

    grad_pre = act_pull(mm(cot_all, after(w_down, *sent_down), nt))[0].astype(bf16)
    grad_bias_up = jnp.sum(grad_pre.astype(f32), axis=0)
    sum_up = Reduced(
        links, 0, part, True, lambda o, b: mm(block(normed_all, o, b), grad_pre, tn)
    )
    sent_up = sum_up.far()
    w_up_late = after(w_up, *sent_up, sum_down.inward())
    sum_down.middle()
    two_give = mm(grad_pre[2 * mine :], w_up_late, nt).astype(bf16)
    two_keep = mm(grad_pre[: 2 * mine], w_up_late, nt).astype(bf16)
    two_other, two_pair = sum_rows(two_give, two_keep)
    dh, dh_mine, grad_gain_two, grad_bias_two, grad_bias_out = middle_backward(
        middle, two_keep, two_other, two_pair, cot_own, gain_two, part
    )
    dh_low = jnp.concatenate([dh_mine, across(dh_mine)], axis=0)
    red_down = sum_down.finish()

    acts_late = after(acts, two_give, two_keep)
    down_give = mm(acts_late[2 * mine :], w_down).astype(bf16)
    down_keep = mm(acts_late[: 2 * mine], w_down).astype(bf16)
    down_other, down_pair = sum_rows(down_give, down_keep)
    block_out = both_rows(
        block_result(middle, down_keep, down_other, down_pair, bias_down, ids, count)
    )

    grad_att = mm(dh_low, w_attn, nt).astype(bf16)
    sum_attn = Reduced(
        links, 1, part, False, lambda o, b: mm(attended, block(dh_low, o, b), tn)
    )
    sent_attn = sum_attn.far()
    sum_up.inward()
    sum_up.middle()
    dots = jnp.sum(
        (grad_att.astype(f32) * attended.astype(f32)).reshape(total, heads, HD), axis=2
    )
    grad_queries, kv_part = attention_backward(
        queries, after(grad_att, *sent_attn), key_value, limits_t, log_totals.T[:heads], dots.T,
        heads,
    )
    sum_query = Reduced(
        links, 0, part, False, lambda o, b: mm(block(normed, o, b), grad_queries, tn)
    )
    w_query_late = after(w_query, *sum_query.far())
    one_give = mm(grad_queries[mine:], w_query_late, nt).astype(bf16)
    one_keep = mm(grad_queries[:mine], w_query_late, nt).astype(bf16)
    kv_low = (kv_part[:mine] + across(kv_part[mine:])).astype(bf16)
    grad_keyval_t = mm(kv_low, normed[:mine], tn)
    red_up = sum_up.finish()
    sum_attn.inward()
    sum_attn.middle()
    sum_query.inward()
    sum_query.middle()
    red_attn, _ = sum_attn.finish()
    red_query, _ = sum_query.finish()
    grad_mine, grad_gain_one, grad_bias_one = first_backward(
        x_rel, one_keep, across(one_give), kv_low, w_keyval_t, dh, gain_one, ids, count
    )
    tokens_grad = both_rows(grad_mine)

    grad_bias_query = jnp.sum(grad_queries.astype(f32), axis=0)
    spread = jnp.concatenate(
        [
            lax.dynamic_update_slice_in_dim(
                jnp.zeros((width,), f32), grad_bias_query, split * qcols, 0
            ),
            lax.dynamic_update_slice_in_dim(
                jnp.zeros((FF,), f32), grad_bias_up, split * hidden + side * half, 0
            ),
        ]
    ).reshape(1 + FF // width, width)
    near = jnp.concatenate(
        [grad_keyval_t, grad_gain_one, grad_bias_one, grad_gain_two, grad_bias_two, grad_bias_out,
         grad_bias_down],
        axis=0,
    )
    steps = jnp.arange(count, dtype=jnp.int32)
    turned = jnp.where((side == 0) & ((steps & 2) != 0), steps ^ 1, steps)
    mirrored = (place ^ from_middle).astype(jnp.int32)

    def pieces(core):
        a = pick_blocks(near, turned * splits + core, own_cols, count, True)
        b = pick_blocks(spread, mirrored * splits + core, own_cols, count, True)
        return jnp.concatenate([a[:, : vec + 4], b[:, :1], a[:, vec + 4 :], b[:, 1:]], axis=1)

    red_shared = pieces(split) + across(pieces(1 - split))
    for pairs in reversed([links.pair, links.mirror] + links.beside):
        keep = red_shared.shape[0] // 2
        red_shared = red_shared[:keep] + lax.ppermute(red_shared[keep:], "dp", pairs)
    red_shared = red_shared[0]

    one_in, two_in = tall(first_in), tall(second_in)
    one_out, two_out = (a.reshape(local_cols, part) for a in (first_out, second_out))
    base_in, mom_in = tall(outer_in_w), tall(momentum_in)
    base_out, mom_out = (a.reshape(local_cols, part) for a in (outer_out_w, momentum_out))
    clip_own = lax.dynamic_slice_in_dim(clip_rows, split * heads, heads)

    def swap(value):
        return lax.ppermute(value, "group", swap_group)

    starts = [qcols + side * half, qcols + (1 - side) * half]
    zero = jnp.zeros((), jnp.int32)
    full_in = full_out = new_in = new_out = None
    for s, gradient in zip(starts, red_down):
        *full_out, delta = adam_out(gradient, w_out, one_out, two_out, base_out, s, full_out)
        new_out = outer_out(delta, swap(delta), mom_out, base_out, s, new_out)
    for s, gradient in zip(starts, red_up):
        *full_in, delta = adam_in(gradient, w_in, one_in, two_in, base_in, s, full_in)
        new_in = outer_in(delta, swap(delta), mom_in, base_in, None, s, new_in)
    *full_out, delta = adam_out(red_attn, w_out, one_out, two_out, base_out, zero, full_out)
    new_out = outer_out(delta, swap(delta), mom_out, base_out, zero, new_out)
    *full_in, delta = adam_in(red_query, w_in, one_in, two_in, base_in, zero, full_in)
    new_in = outer_in(delta, swap(delta), mom_in, base_in, clip_own, zero, new_in)

    ids_col = jnp.arange(shared_cols, dtype=jnp.int32)[:, None]
    one_sh, two_sh, stepped = adam_values(
        red_shared,
        inner_shared[0].T,
        first_shared[0].T,
        second_shared[0].T,
        jnp.where(ids_col < vec, rate_matrix, rate_vector),
        jnp.where(ids_col < vec, weight_decay, 0.0),
    )
    base_sh = outer_shared.T
    delta = (base_sh - stepped).astype(bf16)
    mean_sh = (delta.astype(f32) + swap(delta).astype(f32)) * 0.5
    vel_sh, fresh_sh = outer_values(mean_sh, momentum_shared.T, base_sh)
    row_ids = (place * splits + split) * own_cols + jnp.arange(own_cols, dtype=jnp.int32)
    clip_vec = clip_rows[:, 0]
    row_clip = jnp.sum(
        jnp.where((row_ids // HD)[None, :] == jnp.arange(HEADS)[:, None], clip_vec[:, None], 0.0),
        axis=0,
    )
    fresh_sh = fresh_sh * jnp.where(ids_col == vec + 4, row_clip[None, :], 1.0)

    shape_in, shape_out = (part, 1, local_cols), (1, local_cols, part)
    mean_in, vel_in, fresh_in, copy_in = new_in
    mean_out, vel_out, fresh_out, copy_out = new_out
    return (
        block_out,
        tokens_grad,
        clip_vec,
        full_in[0].reshape((1,) + shape_in),
        full_out[0].reshape((1,) + shape_out),
        one_sh.T[None],
        full_in[1].reshape((1,) + shape_in),
        full_out[1].reshape((1,) + shape_out),
        two_sh.T[None],
        mean_in.reshape(shape_in),
        mean_out.reshape(shape_out),
        mean_sh.T,
        vel_in.reshape(shape_in),
        vel_out.reshape(shape_out),
        vel_sh.T,
        fresh_in.reshape(shape_in),
        fresh_out.reshape(shape_out),
        fresh_sh.T,
        copy_in.reshape(shape_in),
        copy_out.reshape(shape_out),
        fresh_sh.T.astype(bf16),
    )


def solution(mesh):
    rows = P(("group", "dp"), None)
    inner = [P("group", "dp", "tensor", None), P("group", "tensor", None, "dp"),
             P("group", ("dp", "tensor"), None)]
    outer = [P("dp", "tensor", None), P("tensor", None, "dp"), P(("dp", "tensor"), None)]
    in_specs = tuple([rows] * 3 + inner * 3 + outer * 2)
    out_specs = tuple([rows] * 2 + [P()] + inner * 2 + outer * 4)
    return jax.shard_map(local, mesh=mesh, in_specs=in_specs, out_specs=out_specs, check_vma=False)
```

```python
import jax
import jax.numpy as jnp
from jax import lax
from jax.experimental import pallas as pl
from jax.experimental.pallas import tpu as pltpu
from jax.sharding import PartitionSpec as P

HEADS = 16
HD = 128
FF = 8192
BLOCK = 256
STEP = 10

norm_eps = 1e-05
hidden_score = -1e30
shown_score = 3e38
beta_one = 0.9
beta_two = 0.95
adam_eps = 1e-08
rate_matrix = 0.02
rate_vector = 0.2
weight_decay = 0.1
outer_beta = 0.9
outer_rate = 0.7
clip_limit = 5.0
score_scale = HD ** (-0.5)
log2_e = 1.4426950408889634
correct_one = 1.0 / (1.0 - beta_one**STEP)
correct_two = 1.0 / (1.0 - beta_two**STEP)

f32 = jnp.float32
bf16 = jnp.bfloat16
ROWS = 128
LANES = 128
VMEM_LIMIT = 40 * 1024 * 1024
VMEM_MOST = 58 * 1024 * 1024


def shape(dims, dtype):
    return jax.ShapeDtypeStruct(dims, dtype)


def call(body, out_shape, grid, in_specs, out_specs, args, *, ids=(), scratch=(), aliases=None,
         flops=0, name=None, vmem=VMEM_LIMIT):
    outs = out_shape if isinstance(out_shape, (list, tuple)) else [out_shape]
    moved = sum(a.size * a.dtype.itemsize for a in args)
    moved += sum(o.size * o.dtype.itemsize for o in outs)
    return pl.pallas_call(
        body,
        out_shape=out_shape,
        grid_spec=pltpu.PrefetchScalarGridSpec(
            num_scalar_prefetch=len(ids),
            grid=grid,
            in_specs=in_specs,
            out_specs=out_specs,
            scratch_shapes=list(scratch),
        ),
        input_output_aliases={len(ids) + k: v for k, v in (aliases or {}).items()},
        compiler_params=pltpu.CompilerParams(vmem_limit_bytes=vmem),
        cost_estimate=pl.CostEstimate(flops=flops, bytes_accessed=moved, transcendentals=0),
        name=name,
    )(*ids, *args)


def pick_blocks(array, block_ids, width, count, stacked):
    rows = array.shape[0]
    if width % LANES:
        taken = jnp.take(array.reshape(rows, -1, width), block_ids, axis=1)
        return taken.transpose(1, 0, 2) if stacked else taken.reshape(rows, count * width)

    def body(ids_ref, in_ref, out_ref):
        if stacked:
            out_ref[0] = in_ref[...]
        else:
            out_ref[...] = in_ref[...]

    if stacked:
        out, spec = shape((count, rows, width), array.dtype), pl.BlockSpec(
            (1, rows, width), lambda j, ids: (j, 0, 0)
        )
    else:
        out, spec = shape((rows, count * width), array.dtype), pl.BlockSpec(
            (rows, width), lambda j, ids: (0, j)
        )
    return call(
        body, out, (count,), [pl.BlockSpec((rows, width), lambda j, ids: (0, ids[j]))], spec,
        [array], ids=[block_ids], name="pick_blocks",
    )


def columns_of(block_id, width):
    return pl.ds(pl.multiple_of(block_id * width, width), width)


def placing(array, ids, count):
    part = array.shape[1] // count
    if part % LANES == 0:
        return array, count, part
    return pick_blocks(array, ids, part, count, False), 0, part


def put_back(array, ids, count):
    part = array.shape[1] // count
    if part % LANES == 0:
        return array
    back = jnp.sum(
        jnp.where(ids[None, :] == jnp.arange(count)[:, None], jnp.arange(count)[None, :], 0), axis=1
    ).astype(jnp.int32)
    return pick_blocks(array, back, part, count, False)


def norm_stats(rows):
    mean = jnp.mean(rows, axis=-1, keepdims=True)
    centered = rows - mean
    inv = lax.rsqrt(jnp.mean(centered * centered, axis=-1, keepdims=True) + norm_eps)
    return centered * inv, inv


def row_spec(cols, rows=ROWS):
    return pl.BlockSpec((rows, cols), lambda i, *ids: (i, 0))


def turned_spec(cols, blocks):
    return pl.BlockSpec(
        (ROWS, cols), lambda i, ids, split: ((i + split[0] * (blocks // 2)) % blocks, 0)
    )


def whole_spec(rows, cols):
    return pl.BlockSpec((rows, cols), lambda i, *ids: (0, 0))


def first_norm(tokens, ids, split, gain, bias, count):
    total, width = tokens.shape
    tokens, moved, part = placing(tokens, ids, count)

    def body(ids_ref, split_ref, x_ref, g_ref, c_ref, x_out, n_out):
        for o in range(moved):
            x_out[:, o * part : (o + 1) * part] = x_ref[:, columns_of(ids_ref[o], part)]
        if not moved:
            x_out[...] = x_ref[...]
        unit, _ = norm_stats(x_out[...].astype(f32))
        n_out[...] = (unit * g_ref[...] + c_ref[...]).astype(bf16)

    return call(
        body,
        [shape((total, width), bf16)] * 2,
        (total // ROWS,),
        [turned_spec(width, total // ROWS), whole_spec(1, width), whole_spec(1, width)],
        [row_spec(width)] * 2,
        [tokens, gain, bias],
        ids=[ids, split],
        name="first_norm",
    )


def first_spec(cols, blocks):
    return pl.BlockSpec((ROWS, cols), lambda i, *ids: (jnp.minimum(i, blocks - 1), 0))


def swapped(values, part):
    if part % LANES:
        return values
    blocks = [values[:, o : o + part] for o in range(0, values.shape[1], part)]
    return jnp.concatenate([blocks[pair_of(o)] for o in range(len(blocks))], axis=1)


def pair_of(o):
    return o if o & 2 else o ^ 1


def swap_small(values, part):
    if part % LANES == 0:
        return values
    blocks = [values[:, o : o + part] for o in range(0, values.shape[1], part)]
    return jnp.concatenate([blocks[pair_of(o)] for o in range(len(blocks))], axis=1)


def cotangent_order(cotangent, ids, split, count):
    total, width = cotangent.shape
    cotangent, moved, part = placing(cotangent, ids, count)
    mine = total // ROWS // 2

    def body(ids_ref, split_ref, c_ref, c_out, pair_out, sum_out):
        for o in range(moved):
            c_out[:, o * part : (o + 1) * part] = c_ref[:, columns_of(ids_ref[o], part)]
        if not moved:
            c_out[...] = c_ref[...]

        @pl.when(pl.program_id(0) < mine)
        def _():
            pair_out[...] = swapped(c_out[...], part)
            add_rows(sum_out, c_out[...].astype(f32))

    return call(
        body,
        [shape((total, width), bf16), shape((total // 2, width), bf16), shape((1, width), f32)],
        (total // ROWS,),
        [turned_spec(width, total // ROWS)],
        [row_spec(width), first_spec(width, mine), whole_spec(1, width)],
        [cotangent],
        ids=[ids, split],
        name="cotangent_order",
    )


def add_rows(sum_ref, values):
    @pl.when(pl.program_id(0) == 0)
    def _():
        sum_ref[...] = jnp.zeros_like(sum_ref)

    sum_ref[...] += jnp.sum(values, axis=0, keepdims=True)


def middle_norm(x_rel, part_own, part_other, bias_out, gain, bias, part):
    total, width = part_other.shape

    def body(x_ref, a_ref, b_ref, bo_ref, g_ref, c_ref, h_out, n_out, pair_out):
        mid = x_ref[...].astype(f32) + (
            a_ref[...].astype(f32) + b_ref[...].astype(f32)
        ) + bo_ref[...]
        h_out[...] = mid
        unit, _ = norm_stats(mid)
        low = (unit * g_ref[...] + c_ref[...]).astype(bf16)
        n_out[...] = low
        pair_out[...] = swapped(low, part)

    return call(
        body,
        [shape((total, width), f32)] + [shape((total, width), bf16)] * 2,
        (total // ROWS,),
        [row_spec(width)] * 3 + [whole_spec(1, width)] * 3,
        [row_spec(width)] * 3,
        [x_rel, part_own, part_other, bias_out, gain, bias],
        name="middle_norm",
    )


def block_result(middle, part_own, part_other, part_pair, bias_down, ids, count):
    total, width = middle.shape
    part = width // count

    def body(ids_ref, h_ref, a_ref, b_ref, p_ref, b2_ref, out_ref):
        value = a_ref[...].astype(f32) + b_ref[...].astype(f32)
        value = h_ref[...] + (value + swapped(p_ref[...], part).astype(f32)) + b2_ref[...]
        value = value.astype(bf16)
        if part % LANES:
            out_ref[...] = value
        else:
            for o in range(count):
                out_ref[:, columns_of(ids_ref[o], part)] = value[:, o * part : (o + 1) * part]

    result = call(
        body,
        shape((total, width), bf16),
        (total // ROWS,),
        [row_spec(width)] * 4 + [whole_spec(1, width)],
        row_spec(width),
        [middle, part_own, part_other, part_pair, bias_down],
        ids=[ids],
        name="block_result",
    )
    return put_back(result, ids, count)


def middle_backward(middle, part_own, part_other, part_pair, cot_rel, gain, part):
    total, width = middle.shape

    def body(h_ref, a_ref, b_ref, p_ref, dy_ref, g_ref, dh_out, low_out, gg_out, gc_out, gbo_out):
        unit, inv = norm_stats(h_ref[...])
        grad = a_ref[...].astype(f32) + b_ref[...].astype(f32)
        grad = grad + swapped(p_ref[...], part).astype(f32)
        scaled = grad * g_ref[...]
        dh = dy_ref[...].astype(f32) + inv * (
            scaled
            - jnp.mean(scaled, axis=-1, keepdims=True)
            - unit * jnp.mean(scaled * unit, axis=-1, keepdims=True)
        )
        dh_out[...] = dh
        low = dh.astype(bf16)
        low_out[...] = low
        add_rows(gg_out, grad * unit)
        add_rows(gc_out, grad)
        add_rows(gbo_out, low.astype(f32))

    vec = shape((1, width), f32)
    return call(
        body,
        [shape((total, width), f32), shape((total, width), bf16), vec, vec, vec],
        (total // ROWS,),
        [row_spec(width)] * 5 + [whole_spec(1, width)],
        [row_spec(width)] * 2 + [whole_spec(1, width)] * 3,
        [middle, part_own, part_other, part_pair, cot_rel, gain],
        name="middle_backward",
    )


def first_backward(x_rel, part_own, part_other, keyval_grad, w_keyval_t, dh, gain, ids, count):
    total, width = dh.shape
    part = width // count
    kv = keyval_grad.shape[1]

    def body(ids_ref, x_ref, a_ref, b_ref, kv_ref, w_ref, dh_ref, g_ref, t_out, gg_out, gc_out):
        unit, inv = norm_stats(x_ref[...].astype(f32))
        grad = (a_ref[...].astype(f32) + b_ref[...].astype(f32)) + jnp.dot(
            kv_ref[...], w_ref[...], preferred_element_type=f32
        )
        scaled = grad * g_ref[...]
        value = dh_ref[...] + inv * (
            scaled
            - jnp.mean(scaled, axis=-1, keepdims=True)
            - unit * jnp.mean(scaled * unit, axis=-1, keepdims=True)
        )
        low = value.astype(bf16)
        if part % LANES:
            t_out[...] = low
        else:
            for o in range(count):
                t_out[:, columns_of(ids_ref[o], part)] = low[:, o * part : (o + 1) * part]
        add_rows(gg_out, grad * unit)
        add_rows(gc_out, grad)

    vec = shape((1, width), f32)
    result, gain_grad, bias_grad = call(
        body,
        [shape((total, width), bf16), vec, vec],
        (total // ROWS,),
        [row_spec(width)] * 3
        + [row_spec(kv), whole_spec(kv, width), row_spec(width), whole_spec(1, width)],
        [row_spec(width)] + [whole_spec(1, width)] * 2,
        [x_rel, part_own, part_other, keyval_grad, w_keyval_t, dh, gain],
        ids=[ids],
        flops=2 * total * width * kv,
        name="first_backward",
    )
    return put_back(result, ids, count), gain_grad, bias_grad


TILE = 256


def score_limits(lengths, token_count, first_place):
    doc_ends = jnp.cumsum(lengths)
    doc_starts = doc_ends - lengths
    places = (jnp.arange(token_count, dtype=jnp.int32) + first_place) % token_count
    doc_ids = jnp.sum((places[:, None] >= doc_ends[None, :]).astype(jnp.int32), axis=1)
    owners = doc_ids[:, None] == jnp.arange(lengths.shape[0], dtype=jnp.int32)[None, :]
    doc_begin = jnp.sum(jnp.where(owners, doc_starts[None, :], 0), axis=1)
    blocks = (places - doc_begin) // BLOCK
    seen = (doc_ids[:, None] == doc_ids[None, :]) & (blocks[None, :] <= blocks[:, None])
    seen_t = (doc_ids[None, :] == doc_ids[:, None]) & (blocks[:, None] <= blocks[None, :])
    pick = lambda s: jnp.where(s, shown_score, hidden_score).astype(f32)
    return pick(seen), pick(seen_t)


def attention_forward(queries, key_value, limits, heads):
    total = queries.shape[0]
    tiles = total // TILE
    c = score_scale * log2_e

    def body(q_ref, kv_ref, lim_ref, o_ref, lse_ref, top_ref):
        tile, head = pl.program_id(0), pl.program_id(1)
        k = kv_ref[:, :HD]
        v = kv_ref[:, HD:]
        s = lax.dot_general(
            q_ref[...], k, (((1,), (1,)), ((), ())), preferred_element_type=f32
        )
        s = jnp.minimum(s, lim_ref[...])
        m = jnp.max(s, axis=1, keepdims=True)
        p = jnp.exp2((s - m) * c)
        l = jnp.sum(p, axis=1, keepdims=True)
        o = jnp.dot(p.astype(bf16), v, preferred_element_type=f32)
        o_ref[...] = (o / l).astype(bf16)
        lane = lax.broadcasted_iota(jnp.int32, (TILE, LANES), 1)
        lse = m * c + jnp.log2(l)
        lse_ref[...] = jnp.where(lane == head, lse, lse_ref[...])

        @pl.when((tile == 0) & (head == 0))
        def _():
            top_ref[...] = jnp.full_like(top_ref, hidden_score)

        row = lax.broadcasted_iota(jnp.int32, (heads, LANES), 0)
        best = jnp.max(m, axis=0, keepdims=True) * score_scale
        top_ref[...] = jnp.where(row == head, jnp.maximum(top_ref[...], best), top_ref[...])

    return call(
        body,
        [shape((total, heads * HD), bf16), shape((total, LANES), f32), shape((heads, LANES), f32)],
        (tiles, heads),
        [
            pl.BlockSpec((TILE, HD), lambda i, h: (i, h)),
            pl.BlockSpec((total, 2 * HD), lambda i, h: (0, 0)),
            pl.BlockSpec((TILE, total), lambda i, h: (i, 0)),
        ],
        [
            pl.BlockSpec((TILE, HD), lambda i, h: (i, h)),
            pl.BlockSpec((TILE, LANES), lambda i, h: (i, 0)),
            pl.BlockSpec((heads, LANES), lambda i, h: (0, 0)),
        ],
        [queries, key_value, limits],
        flops=8 * total * total * HD * heads,
        name="attention_forward",
    )


def attention_backward(queries, grad_att, key_value, limits_t, lse_t, dot_t, heads):
    total = queries.shape[0]
    tiles = total // TILE
    c = score_scale * log2_e

    def body(q_ref, da_ref, kv_ref, lim_ref, lse_ref, dot_ref, dq_ref, dkv_ref):
        tile, head = pl.program_id(0), pl.program_id(1)
        k = kv_ref[:, :HD]
        v = kv_ref[:, HD:]
        q = q_ref[...]
        da = da_ref[...]
        nt = (((1,), (1,)), ((), ()))
        s = lax.dot_general(k, q, nt, preferred_element_type=f32)
        s = jnp.minimum(s, lim_ref[...])
        p = jnp.exp2(s * c - lse_ref[pl.ds(head, 1), :])
        dp = lax.dot_general(v, da, nt, preferred_element_type=f32)
        ds = (p * (dp - dot_ref[pl.ds(head, 1), :])).astype(bf16)
        dq = lax.dot_general(ds, k, (((0,), (0,)), ((), ())), preferred_element_type=f32)
        dq_ref[...] = (dq * score_scale).astype(bf16)

        @pl.when((tile == 0) & (head == 0))
        def _():
            dkv_ref[...] = jnp.zeros_like(dkv_ref)

        dkv_ref[:, :HD] += jnp.dot(ds, q, preferred_element_type=f32) * score_scale
        dkv_ref[:, HD:] += jnp.dot(p.astype(bf16), da, preferred_element_type=f32)

    return call(
        body,
        [shape((total, heads * HD), bf16), shape((total, 2 * HD), f32)],
        (tiles, heads),
        [
            pl.BlockSpec((TILE, HD), lambda i, h: (i, h)),
            pl.BlockSpec((TILE, HD), lambda i, h: (i, h)),
            pl.BlockSpec((total, 2 * HD), lambda i, h: (0, 0)),
            pl.BlockSpec((total, TILE), lambda i, h: (0, i)),
            pl.BlockSpec((heads, TILE), lambda i, h: (0, i)),
            pl.BlockSpec((heads, TILE), lambda i, h: (0, i)),
        ],
        [
            pl.BlockSpec((TILE, HD), lambda i, h: (i, h)),
            pl.BlockSpec((total, 2 * HD), lambda i, h: (0, 0)),
        ],
        [queries, grad_att, key_value, limits_t, lse_t, dot_t],
        flops=20 * total * total * HD * heads,
        name="attention_backward",
    )


def adam_values(gradient, weight, one, two, rate, decay):
    new_one = beta_one * one + (1.0 - beta_one) * gradient
    new_two = beta_two * two + (1.0 - beta_two) * gradient * gradient
    direction = (new_one * correct_one) / (jnp.sqrt(new_two * correct_two) + adam_eps)
    return new_one, new_two, weight - rate * (direction + decay * weight)


def to_tiles(flat, tiles_ref):
    for j in range(8):
        tiles_ref[:, j, :] = flat[:, j * LANES : (j + 1) * LANES]


def adam_in(gradient, weight, one, two, outer, start, full):
    rows, cols = gradient.shape
    step = 64
    base = (start // 1024).reshape(1)
    tall = pl.BlockSpec((step, 8, LANES), lambda i, j, b: (i, b[0] + j, 0))
    flat = pl.BlockSpec((step, 1024), lambda i, j, b: (i, j))
    args = [gradient, weight, one, two, outer]
    specs = [flat] + [tall] * 4
    aliases = {}
    if full is not None:
        aliases = {5: 0, 6: 1}
        args += list(full)
        specs += [pl.BlockSpec(memory_space=pl.ANY)] * 2

    def body(_, g_ref, w_ref, one_ref, two_ref, out_ref, *rest):
        one_out, two_out, delta_out, grad_tiles, delta_tiles = rest[-5:]
        to_tiles(g_ref[...].astype(f32), grad_tiles)
        new_one, new_two, stepped = adam_values(
            grad_tiles[...], w_ref[...], one_ref[...], two_ref[...], rate_matrix, weight_decay
        )
        one_out[...] = new_one
        two_out[...] = new_two
        delta_tiles[...] = out_ref[...] - stepped
        for j in range(8):
            delta_out[:, j * LANES : (j + 1) * LANES] = delta_tiles[:, j, :].astype(bf16)

    whole = shape(weight.shape, f32)
    return call(
        body,
        [whole, whole, shape((rows, cols), bf16)],
        (rows // step, cols // 1024),
        specs,
        [tall, tall, flat],
        args,
        ids=[base],
        scratch=[pltpu.VMEM((step, 8, LANES), f32)] * 2,
        aliases=aliases,
        name="adam_in",
        vmem=VMEM_MOST,
    )


def adam_out(gradient, weight, one, two, outer, start, full):
    rows, cols = gradient.shape
    step = 512
    base = (start // step).reshape(1)
    tall = pl.BlockSpec((step, cols), lambda i, b: (b[0] + i, 0))
    flat = pl.BlockSpec((step, cols), lambda i, b: (i, 0))
    args = [gradient, weight, one, two, outer]
    specs = [flat] + [tall] * 4
    aliases = {}
    if full is not None:
        aliases = {5: 0, 6: 1}
        args += list(full)
        specs += [pl.BlockSpec(memory_space=pl.ANY)] * 2

    def body(_, g_ref, w_ref, one_ref, two_ref, out_ref, *rest):
        one_out, two_out, delta_out = rest[-3:]
        new_one, new_two, stepped = adam_values(
            g_ref[...].astype(f32), w_ref[...], one_ref[...], two_ref[...], rate_matrix,
            weight_decay,
        )
        one_out[...] = new_one
        two_out[...] = new_two
        delta_out[...] = (out_ref[...] - stepped).astype(bf16)

    whole = shape(weight.shape, f32)
    return call(
        body,
        [whole, whole, shape((rows, cols), bf16)],
        (rows // step,),
        specs,
        [tall, tall, flat],
        args,
        ids=[base],
        aliases=aliases,
        name="adam_out",
        vmem=VMEM_MOST,
    )


def outer_values(mean, momentum, outer):
    velocity = outer_beta * momentum + mean
    return velocity, outer - outer_rate * (mean + outer_beta * velocity)


def outer_in(both, momentum, outer, factor, start, full):
    _, rows, cols = both.shape
    step = 64
    base = (start // 1024).reshape(1)
    tall = pl.BlockSpec((step, 8, LANES), lambda i, j, b: (i, b[0] + j, 0))
    flat = pl.BlockSpec((2, step, 1024), lambda i, j, b: (0, i, j))
    wide = pl.BlockSpec((step, 1024), lambda i, j, b: (i, b[0] + j))
    args = [both, momentum, outer]
    specs = [flat, tall, tall]
    if factor is not None:
        args.append(factor)
        specs.append(pl.BlockSpec((8, LANES), lambda i, j, b: (0, 0)))
    aliases = {}
    if full is not None:
        aliases = {len(args) + k: k for k in range(4)}
        args += list(full)
        specs += [pl.BlockSpec(memory_space=pl.ANY)] * 4

    def body(_, both_ref, mom_ref, out_ref, *rest):
        mean_out, vel_out, new_out, copy_out, mean_tiles, new_tiles = rest[-6:]
        to_tiles((both_ref[0].astype(f32) + both_ref[1].astype(f32)) * 0.5, mean_tiles)
        mean = mean_tiles[...]
        velocity, fresh = outer_values(mean, mom_ref[...], out_ref[...])
        if factor is not None:
            fresh = fresh * rest[0][...][None]
        mean_out[...] = mean
        vel_out[...] = velocity
        new_out[...] = fresh
        new_tiles[...] = fresh
        for j in range(8):
            copy_out[:, j * LANES : (j + 1) * LANES] = new_tiles[:, j, :].astype(bf16)

    whole = shape(outer.shape, f32)
    return call(
        body,
        [whole, whole, whole, shape((rows, outer.shape[1] * LANES), bf16)],
        (rows // step, cols // 1024),
        specs,
        [tall, tall, tall, wide],
        args,
        ids=[base],
        scratch=[pltpu.VMEM((step, 8, LANES), f32)] * 2,
        aliases=aliases,
        name="outer_in",
        vmem=VMEM_MOST,
    )


def outer_out(both, momentum, outer, start, full):
    _, rows, cols = both.shape
    step = 512
    base = (start // step).reshape(1)
    tall = pl.BlockSpec((step, cols), lambda i, b: (b[0] + i, 0))
    flat = pl.BlockSpec((2, step, cols), lambda i, b: (0, i, 0))
    args = [both, momentum, outer]
    specs = [flat, tall, tall]
    aliases = {}
    if full is not None:
        aliases = {3 + k: k for k in range(4)}
        args += list(full)
        specs += [pl.BlockSpec(memory_space=pl.ANY)] * 4

    def body(_, both_ref, mom_ref, out_ref, *rest):
        mean_out, vel_out, new_out, copy_out = rest[-4:]
        mean = (both_ref[0].astype(f32) + both_ref[1].astype(f32)) * 0.5
        velocity, fresh = outer_values(mean, mom_ref[...], out_ref[...])
        mean_out[...] = mean
        vel_out[...] = velocity
        new_out[...] = fresh
        copy_out[...] = fresh.astype(bf16)

    whole = shape(outer.shape, f32)
    return call(
        body,
        [whole, whole, whole, shape(outer.shape, bf16)],
        (rows // step,),
        specs,
        [tall] * 4,
        args,
        ids=[base],
        aliases=aliases,
        name="outer_out",
        vmem=VMEM_MOST,
    )


class Wire:
    def __init__(self, window):
        self.window, self.landed = window, []

    def send(self, block, axis, pairs):
        if len(self.landed) >= self.window:
            block, _ = lax.optimization_barrier((block, self.landed[-self.window]))
        arrived = lax.ppermute(block, axis, pairs)
        self.landed.append(arrived)
        return arrived


class Links:
    def __init__(self, count, splits, window):
        self.levels = count.bit_length() - 1
        self.far = ([1] + [1 << b for b in range(3, self.levels)])[: self.levels - 2]
        places = range(count)
        middle = [i for i in places if (i >> 1 ^ i >> 2) & 1]
        outer = [i for i in places if i not in middle]
        self.pair = [(i, i ^ 2) for i in places]
        self.inward = [(i, i ^ 2) for i in outer]
        self.outward = [(i, i ^ 2) for i in middle]
        self.between = [(i, i ^ 6) for i in middle]
        self.beside = [[(i, i ^ mask) for i in places] for mask in self.far]
        self.mirror = [(i, i ^ 6) for i in places]
        self.cores = [(i, (i + 1) % splits) for i in range(splits)]
        self.wire = Wire(window)

    def flips(self, across):
        masks = [2, across] + self.far
        table = []
        for o in range(1 << self.levels):
            flip = 0
            for level, mask in enumerate(masks):
                if o >> level & 1:
                    flip ^= mask
            table.append(flip)
        return table

    def to_side(self, block, pairs):
        return self.wire.send(block, "dp", pairs)

    def to_middle(self, block):
        return self.wire.send(block, "dp", self.between)

    def to_far(self, block, level):
        return self.wire.send(block, "dp", self.beside[level - 2])

    def to_pair(self, block):
        return self.wire.send(block, "dp", self.pair)

    def across(self, block):
        return self.wire.send(block, "tensor", self.cores)


def after(value, *earlier):
    return lax.optimization_barrier((value, *earlier))[0]


class Gathered:
    def __init__(self, links, axis, mine, other=None):
        self.links, self.axis, self.mine, self.other = links, axis, mine, other
        self.held = {}

    def join(self, *blocks):
        return jnp.concatenate(blocks, axis=self.axis)

    def near(self):
        give = self.mine if self.other is None else self.other
        self.held[0] = self.join(self.mine, self.links.to_side(give, self.links.pair))

    def inward(self):
        if self.other is not None:
            self.passed = self.links.to_side(self.mine, self.links.inward)

    def middle(self):
        if self.other is None:
            self.relay = self.direct = self.links.to_middle(self.held[0])
        else:
            self.relay = self.links.to_middle(self.join(self.other, self.passed))

    def middle_rest(self):
        self.direct = self.links.to_middle(self.held[0])

    def outward(self):
        self.relayed = self.links.to_side(self.relay, self.links.outward)

    def join_far(self):
        self.held[2] = self.direct + self.relayed

    def far(self, level, o):
        self.held[o + (1 << level)] = self.links.to_far(self.held[o], level)

    def whole(self):
        for level in range(2, self.links.levels):
            for o in range(0, 1 << level, 2):
                if o + (1 << level) not in self.held:
                    self.far(level, o)
        return self.join(*[self.held[o] for o in sorted(self.held)])


class Reduced:
    def __init__(self, links, axis, size, halved, part):
        self.links, self.axis, self.size, self.halved, self.part = links, axis, size, halved, part
        self.landed = {}

    def pair_sum(self, o):
        total = self.part(o, 2)
        for block in self.landed.pop(o, []):
            total = total + block.astype(f32)
        return total.astype(bf16)

    def one(self, block, o):
        return lax.slice_in_dim(
            block, o * self.size, (o + 1) * self.size, axis=self.axis
        ).astype(f32)

    def far(self):
        sent = []
        for level in range(self.links.levels - 1, 1, -1):
            for o in reversed(range(1 << level, 2 << level, 2)):
                sent.append(self.pair_sum(o))
                arrived = self.links.to_far(sent[-1], level)
                self.landed.setdefault(o - (1 << level), []).append(arrived)
        return sent

    def inward(self):
        self.ahead = self.pair_sum(2)
        self.passed = self.links.to_side(self.ahead, self.links.inward)
        return self.ahead

    def middle(self):
        self.direct = self.links.to_middle(
            self.ahead if self.halved else self.ahead + self.passed
        )

    def middle_rest(self):
        self.relay = self.links.to_middle(self.passed)

    def single(self, o):
        total = self.part(o, 1)
        for block in self.landed[0] + [self.direct]:
            total = total + self.one(block, o)
        return total

    def near(self):
        value = self.single(1).astype(bf16)
        self.theirs = self.links.to_side(value, self.links.pair).astype(f32)
        return value

    def outward(self):
        value = self.one(self.relay, 1).astype(bf16)
        self.last = self.links.to_side(value, self.links.outward).astype(f32)

    def result(self):
        if not self.halved:
            return self.single(0) + self.theirs, None
        return self.single(0) + self.last, self.theirs + self.one(self.relay, 0)


def local(
    tokens,
    doc_lengths,
    cotangent,
    inner_in,
    inner_out,
    inner_shared,
    first_in,
    first_out,
    first_shared,
    second_in,
    second_out,
    second_shared,
    outer_in_w,
    outer_out_w,
    outer_shared,
    momentum_in,
    momentum_out,
    momentum_shared,
):
    splits = lax.axis_size("tensor")
    count = lax.axis_size("dp")
    split = lax.axis_index("tensor")
    place = lax.axis_index("dp")
    total, width = tokens.shape
    part = width // count
    local_cols = inner_in.shape[3]
    shared_cols = inner_shared.shape[2]
    heads = HEADS // splits
    qcols = heads * HD
    hidden = local_cols - qcols
    vec = 2 * HD
    own_cols = part // splits
    mine = total // 2

    links = Links(count, splits, 4)
    across = links.across
    levels = links.levels
    side = ((place >> 1) ^ (place >> 2)) & 1
    from_outer, from_middle = (jnp.array(links.flips(m), jnp.int32) for m in (4, 6))
    ids = (place ^ jnp.where(side == 0, from_outer, from_middle)).astype(jnp.int32)
    swap_group = [(0, 1), (1, 0)]
    split_id = split.astype(jnp.int32).reshape(1)

    def tall(array):
        return array.reshape(part, local_cols // LANES, LANES)

    w_in = tall(inner_in)
    w_out = inner_out.reshape(local_cols, part)
    shared_rows = lax.all_gather(inner_shared[0], ("dp", "tensor"), axis=0, tiled=True)

    half = hidden // 2
    flat_in = inner_in.reshape(part, local_cols)

    def sides(low, high):
        return (
            jnp.where(side == 0, low, high).astype(bf16),
            jnp.where(side == 0, high, low).astype(bf16),
        )

    block_q = flat_in[:, :qcols].astype(bf16)
    block_o = w_out[:qcols].astype(bf16)
    up_sides = sides(flat_in[:, qcols : qcols + half], flat_in[:, qcols + half :])
    down_sides = sides(w_out[qcols : qcols + half], w_out[qcols + half :])
    got_query = Gathered(links, 0, block_q)
    got_attn = Gathered(links, 1, block_o)
    got_up = Gathered(links, 0, *up_sides)
    got_down = Gathered(links, 1, *down_sides)
    shared_t = shared_rows.T
    shared_rel = pick_blocks(shared_t, ids, part, count, False)
    w_keyval_t = shared_rel[:vec].astype(bf16)
    gain_one, bias_one, gain_two, bias_two = (shared_rel[vec + k : vec + k + 1] for k in range(4))
    bias_out, bias_down = shared_rel[vec + 5 : vec + 6], shared_rel[vec + 6 : vec + 7]
    bias_query = lax.dynamic_slice_in_dim(shared_t[vec + 4], split * qcols, qcols)
    bias_up = lax.dynamic_slice_in_dim(
        shared_t[vec + 7 :].reshape(FF), split * hidden + side * half, half
    )

    nt = (((1,), (1,)), ((), ()))
    tn = (((0,), (0,)), ((), ()))

    def mm(a, b, dims=(((1,), (0,)), ((), ()))):
        return lax.dot_general(a, b, dims, preferred_element_type=f32)

    def block(array, o, blocks):
        return array[:, o * part : (o + blocks) * part]

    def pair_rows(keep, other):
        theirs = keep[mine:].astype(f32) + other[mine:].astype(f32)
        return links.to_pair(swap_small(theirs.astype(bf16), part))

    def both_rows(rows):
        return lax.all_gather(rows, "tensor", axis=0, tiled=True)

    cot_own, cot_pair, grad_bias_down = cotangent_order(cotangent, ids, split_id, count)
    got_query.near()
    got_attn.near()
    got_query.middle()
    if levels == 3:
        got_query.far(2, 0)
    got_up.near()
    got_up.inward()
    got_attn.middle()
    if levels == 3:
        got_attn.far(2, 0)
    got_query.outward()
    got_query.join_far()
    if levels == 3:
        got_query.far(2, 2)
    got_attn.outward()
    got_attn.join_far()
    got_up.middle()
    got_down.near()
    w_query = got_query.whole()
    w_attn = got_attn.whole()
    got_down.inward()
    if levels == 3:
        got_up.far(2, 0)
    cot_theirs = links.to_pair(swap_small(cot_pair, part))

    x_rel, normed = first_norm(tokens, ids, split_id, gain_one, bias_one, count)
    limits, limits_t = score_limits(doc_lengths[0], total, split * mine)
    key_value = mm(normed, w_keyval_t, nt).astype(bf16)
    queries = (mm(normed, w_query) + bias_query).astype(bf16)
    attended, log_totals, tops = attention_forward(queries, key_value, limits, heads)
    attn_give = mm(attended[mine:], w_attn).astype(bf16)
    attn_keep = mm(attended[:mine], w_attn).astype(bf16)
    got_up.outward()
    attn_other = across(attn_give)
    got_up.middle_rest()
    got_up.join_far()
    middle, normed_two, normed_pair = middle_norm(
        x_rel, attn_keep, attn_other, bias_out, gain_two, bias_two, part
    )
    normed_theirs = links.to_pair(swap_small(normed_pair, part))
    if levels == 3:
        got_down.far(2, 0)
    got_down.middle()
    normed_first = jnp.concatenate([normed_two, normed_theirs], axis=0)
    normed_all = jnp.concatenate([normed_first, across(normed_first)], axis=0)
    cot_all = jnp.concatenate(
        [cot_own[:mine], cot_theirs, cot_own[mine:], across(cot_theirs)], axis=0
    )
    w_up = got_up.whole()
    peers = across(tops)
    peak = jnp.where(
        split == 0, jnp.concatenate([tops, peers]), jnp.concatenate([peers, tops])
    )
    got_down.middle_rest()
    peak = jnp.maximum(peak, links.wire.send(peak, "group", swap_group))
    got_down.outward()
    got_down.join_far()
    for pairs in [links.pair, links.mirror]:
        peak = jnp.maximum(peak, links.to_side(peak, pairs))
    w_down = got_down.whole()
    for pairs in links.beside:
        peak = jnp.maximum(peak, links.to_side(peak, pairs))
    clip_rows = clip_limit / jnp.maximum(peak, clip_limit)

    pre_act = mm(normed_all, w_up) + bias_up
    act_value, act_pull = jax.vjp(lambda v: jax.nn.gelu(v, approximate=True), pre_act)
    acts = act_value.astype(bf16)
    sum_down = Reduced(
        links, 1, part, True, lambda o, b: mm(acts, block(cot_all, o, b), tn)
    )
    sent_down = sum_down.far()

    grad_pre = act_pull(mm(cot_all, after(w_down, *sent_down), nt))[0].astype(bf16)
    grad_bias_up = jnp.sum(grad_pre.astype(f32), axis=0)
    sum_up = Reduced(
        links, 0, part, True, lambda o, b: mm(block(normed_all, o, b), grad_pre, tn)
    )
    sent_up = sum_up.far()
    w_up_late = after(w_up, *sent_up, sum_down.inward())
    sum_down.middle()
    two_give = mm(grad_pre[2 * mine :], w_up_late, nt).astype(bf16)
    two_keep = mm(grad_pre[: 2 * mine], w_up_late, nt).astype(bf16)
    two_other = across(two_give)
    sum_down.middle_rest()
    two_pair = pair_rows(two_keep, two_other)

    acts_late = after(acts, two_give, two_keep)
    down_give = mm(acts_late[2 * mine :], w_down).astype(bf16)
    down_keep = mm(acts_late[: 2 * mine], w_down).astype(bf16)

    dh, dh_mine, grad_gain_two, grad_bias_two, grad_bias_out = middle_backward(
        middle, two_keep, two_other, two_pair, cot_own, gain_two, part
    )
    sum_down.near()
    sum_down.outward()
    dh_low = jnp.concatenate([dh_mine, across(dh_mine)], axis=0)
    down_other = across(down_give)
    sum_up.inward()
    sum_up.middle()
    down_pair = pair_rows(down_keep, down_other)
    block_out = both_rows(
        block_result(middle, down_keep, down_other, down_pair, bias_down, ids, count)
    )

    grad_att = mm(dh_low, w_attn, nt).astype(bf16)
    sum_attn = Reduced(
        links, 1, part, False, lambda o, b: mm(attended, block(dh_low, o, b), tn)
    )
    sent_attn = sum_attn.far()
    sum_up.middle_rest()
    dots = jnp.sum(
        (grad_att.astype(f32) * attended.astype(f32)).reshape(total, heads, HD), axis=2
    )
    grad_queries, kv_part = attention_backward(
        queries, after(grad_att, *sent_attn), key_value, limits_t, log_totals.T[:heads], dots.T,
        heads,
    )
    sum_query = Reduced(
        links, 0, part, False, lambda o, b: mm(block(normed, o, b), grad_queries, tn)
    )
    w_query_late = after(w_query, *sum_query.far())
    one_give = mm(grad_queries[mine:], w_query_late, nt).astype(bf16)
    one_keep = mm(grad_queries[:mine], w_query_late, nt).astype(bf16)
    one_other = across(one_give)
    kv_low = (kv_part[:mine] + across(kv_part[mine:])).astype(bf16)
    grad_keyval_t = mm(kv_low, normed[:mine], tn)
    sum_up.near()
    sum_up.outward()
    sum_attn.inward()
    sum_attn.middle()
    sum_query.inward()
    grad_mine, grad_gain_one, grad_bias_one = first_backward(
        x_rel, one_keep, one_other, kv_low, w_keyval_t, dh, gain_one, ids, count
    )
    tokens_grad = both_rows(grad_mine)

    grad_bias_query = jnp.sum(grad_queries.astype(f32), axis=0)
    spread = jnp.concatenate(
        [
            lax.dynamic_update_slice_in_dim(
                jnp.zeros((width,), f32), grad_bias_query, split * qcols, 0
            ),
            lax.dynamic_update_slice_in_dim(
                jnp.zeros((FF,), f32), grad_bias_up, split * hidden + side * half, 0
            ),
        ]
    ).reshape(1 + FF // width, width)
    near = jnp.concatenate(
        [grad_keyval_t, grad_gain_one, grad_bias_one, grad_gain_two, grad_bias_two, grad_bias_out,
         grad_bias_down],
        axis=0,
    )
    steps = jnp.arange(count, dtype=jnp.int32)
    turned = jnp.where((side == 0) & ((steps & 2) != 0), steps ^ 1, steps)
    mirrored = (place ^ from_middle).astype(jnp.int32)

    def pieces(core):
        a = pick_blocks(near, turned * splits + core, own_cols, count, True)
        b = pick_blocks(spread, mirrored * splits + core, own_cols, count, True)
        return jnp.concatenate([a[:, : vec + 4], b[:, :1], a[:, vec + 4 :], b[:, 1:]], axis=1)

    red_shared = pieces(split) + across(pieces(1 - split))
    sum_query.middle()
    sum_attn.near()
    for pairs in reversed([links.pair, links.mirror] + links.beside):
        keep = red_shared.shape[0] // 2
        red_shared = red_shared[:keep] + links.to_side(red_shared[keep:], pairs)
    red_shared = red_shared[0]
    sum_query.near()
    red_down, red_up = sum_down.result(), sum_up.result()
    red_attn, red_query = sum_attn.result()[0], sum_query.result()[0]

    one_in, two_in = tall(first_in), tall(second_in)
    one_out, two_out = (a.reshape(local_cols, part) for a in (first_out, second_out))
    base_in, mom_in = tall(outer_in_w), tall(momentum_in)
    base_out, mom_out = (a.reshape(local_cols, part) for a in (outer_out_w, momentum_out))
    clip_own = lax.dynamic_slice_in_dim(clip_rows, split * heads, heads)

    starts = [qcols + side * half, qcols + (1 - side) * half]
    zero = jnp.zeros((), jnp.int32)
    gathered = []

    def groups(delta):
        both = lax.all_gather(after(delta, *gathered[-1:]), "group", axis=0)
        gathered.append(both)
        return both

    full_in = full_out = new_in = new_out = None
    for s, gradient in zip(starts, red_down):
        *full_out, delta = adam_out(gradient, w_out, one_out, two_out, base_out, s, full_out)
        new_out = outer_out(groups(delta), mom_out, base_out, s, new_out)
    for s, gradient in zip(starts, red_up):
        *full_in, delta = adam_in(gradient, w_in, one_in, two_in, base_in, s, full_in)
        new_in = outer_in(groups(delta), mom_in, base_in, None, s, new_in)
    *full_out, delta = adam_out(red_attn, w_out, one_out, two_out, base_out, zero, full_out)
    new_out = outer_out(groups(delta), mom_out, base_out, zero, new_out)
    *full_in, delta = adam_in(red_query, w_in, one_in, two_in, base_in, zero, full_in)
    both = jnp.stack([delta, lax.ppermute(delta, "group", swap_group)])
    new_in = outer_in(both, mom_in, base_in, clip_own, zero, new_in)

    ids_col = jnp.arange(shared_cols, dtype=jnp.int32)[:, None]
    one_sh, two_sh, stepped = adam_values(
        red_shared,
        inner_shared[0].T,
        first_shared[0].T,
        second_shared[0].T,
        jnp.where(ids_col < vec, rate_matrix, rate_vector),
        jnp.where(ids_col < vec, weight_decay, 0.0),
    )
    base_sh = outer_shared.T
    delta = (base_sh - stepped).astype(bf16)
    mean_sh = (delta.astype(f32) + lax.ppermute(delta, "group", swap_group).astype(f32)) * 0.5
    vel_sh, fresh_sh = outer_values(mean_sh, momentum_shared.T, base_sh)
    row_ids = (place * splits + split) * own_cols + jnp.arange(own_cols, dtype=jnp.int32)
    clip_vec = clip_rows[:, 0]
    row_clip = jnp.sum(
        jnp.where((row_ids // HD)[None, :] == jnp.arange(HEADS)[:, None], clip_vec[:, None], 0.0),
        axis=0,
    )
    fresh_sh = fresh_sh * jnp.where(ids_col == vec + 4, row_clip[None, :], 1.0)

    shape_in, shape_out = (part, 1, local_cols), (1, local_cols, part)
    mean_in, vel_in, fresh_in, copy_in = new_in
    mean_out, vel_out, fresh_out, copy_out = new_out
    return (
        block_out,
        tokens_grad,
        clip_vec,
        full_in[0].reshape((1,) + shape_in),
        full_out[0].reshape((1,) + shape_out),
        one_sh.T[None],
        full_in[1].reshape((1,) + shape_in),
        full_out[1].reshape((1,) + shape_out),
        two_sh.T[None],
        mean_in.reshape(shape_in),
        mean_out.reshape(shape_out),
        mean_sh.T,
        vel_in.reshape(shape_in),
        vel_out.reshape(shape_out),
        vel_sh.T,
        fresh_in.reshape(shape_in),
        fresh_out.reshape(shape_out),
        fresh_sh.T,
        copy_in.reshape(shape_in),
        copy_out.reshape(shape_out),
        fresh_sh.T.astype(bf16),
    )


def solution(mesh):
    rows = P(("group", "dp"), None)
    inner = [P("group", "dp", "tensor", None), P("group", "tensor", None, "dp"),
             P("group", ("dp", "tensor"), None)]
    outer = [P("dp", "tensor", None), P("tensor", None, "dp"), P(("dp", "tensor"), None)]
    in_specs = tuple([rows] * 3 + inner * 3 + outer * 2)
    out_specs = tuple([rows] * 2 + [P()] + inner * 2 + outer * 4)
    return jax.shard_map(local, mesh=mesh, in_specs=in_specs, out_specs=out_specs, check_vma=False)
```

```python
import jax
import jax.numpy as jnp
from jax import lax
from jax.experimental import pallas as pl
from jax.experimental.pallas import tpu as pltpu
from jax.sharding import PartitionSpec as P

HEADS = 16
HD = 128
FF = 8192
BLOCK = 256
STEP = 10

norm_eps = 1e-05
hidden_score = -1e30
shown_score = 3e38
beta_one = 0.9
beta_two = 0.95
adam_eps = 1e-08
rate_matrix = 0.02
rate_vector = 0.2
weight_decay = 0.1
outer_beta = 0.9
outer_rate = 0.7
clip_limit = 5.0
score_scale = HD ** (-0.5)
log2_e = 1.4426950408889634
correct_one = 1.0 / (1.0 - beta_one**STEP)
correct_two = 1.0 / (1.0 - beta_two**STEP)

f32 = jnp.float32
bf16 = jnp.bfloat16
ROWS = 128
LANES = 128
VMEM_LIMIT = 40 * 1024 * 1024
VMEM_MOST = 58 * 1024 * 1024


def shape(dims, dtype):
    return jax.ShapeDtypeStruct(dims, dtype)


def call(body, out_shape, grid, in_specs, out_specs, args, *, ids=(), scratch=(), aliases=None,
         flops=0, name=None, vmem=VMEM_LIMIT):
    outs = out_shape if isinstance(out_shape, (list, tuple)) else [out_shape]
    moved = sum(a.size * a.dtype.itemsize for a in args)
    moved += sum(o.size * o.dtype.itemsize for o in outs)
    return pl.pallas_call(
        body,
        out_shape=out_shape,
        grid_spec=pltpu.PrefetchScalarGridSpec(
            num_scalar_prefetch=len(ids),
            grid=grid,
            in_specs=in_specs,
            out_specs=out_specs,
            scratch_shapes=list(scratch),
        ),
        input_output_aliases={len(ids) + k: v for k, v in (aliases or {}).items()},
        compiler_params=pltpu.CompilerParams(vmem_limit_bytes=vmem),
        cost_estimate=pl.CostEstimate(flops=flops, bytes_accessed=moved, transcendentals=0),
        name=name,
    )(*ids, *args)


def pick_blocks(array, block_ids, width, count, stacked):
    rows = array.shape[0]
    if width % LANES:
        taken = jnp.take(array.reshape(rows, -1, width), block_ids, axis=1)
        return taken.transpose(1, 0, 2) if stacked else taken.reshape(rows, count * width)

    def body(ids_ref, in_ref, out_ref):
        if stacked:
            out_ref[0] = in_ref[...]
        else:
            out_ref[...] = in_ref[...]

    if stacked:
        out, spec = shape((count, rows, width), array.dtype), pl.BlockSpec(
            (1, rows, width), lambda j, ids: (j, 0, 0)
        )
    else:
        out, spec = shape((rows, count * width), array.dtype), pl.BlockSpec(
            (rows, width), lambda j, ids: (0, j)
        )
    return call(
        body, out, (count,), [pl.BlockSpec((rows, width), lambda j, ids: (0, ids[j]))], spec,
        [array], ids=[block_ids], name="pick_blocks",
    )


def columns_of(block_id, width):
    return pl.ds(pl.multiple_of(block_id * width, width), width)


def placing(array, ids, count):
    part = array.shape[1] // count
    if part % LANES == 0:
        return array, count, part
    return pick_blocks(array, ids, part, count, False), 0, part


def put_back(array, ids, count):
    part = array.shape[1] // count
    if part % LANES == 0:
        return array
    back = jnp.sum(
        jnp.where(ids[None, :] == jnp.arange(count)[:, None], jnp.arange(count)[None, :], 0), axis=1
    ).astype(jnp.int32)
    return pick_blocks(array, back, part, count, False)


def norm_stats(rows):
    mean = jnp.mean(rows, axis=-1, keepdims=True)
    centered = rows - mean
    inv = lax.rsqrt(jnp.mean(centered * centered, axis=-1, keepdims=True) + norm_eps)
    return centered * inv, inv


def row_spec(cols, rows=ROWS):
    return pl.BlockSpec((rows, cols), lambda i, *ids: (i, 0))


def turned_spec(cols, blocks):
    return pl.BlockSpec(
        (ROWS, cols), lambda i, ids, split: ((i + split[0] * (blocks // 2)) % blocks, 0)
    )


def whole_spec(rows, cols):
    return pl.BlockSpec((rows, cols), lambda i, *ids: (0, 0))


def first_norm(tokens, ids, split, gain, bias, count):
    total, width = tokens.shape
    tokens, moved, part = placing(tokens, ids, count)

    def body(ids_ref, split_ref, x_ref, g_ref, c_ref, x_out, n_out):
        for o in range(moved):
            x_out[:, o * part : (o + 1) * part] = x_ref[:, columns_of(ids_ref[o], part)]
        if not moved:
            x_out[...] = x_ref[...]
        unit, _ = norm_stats(x_out[...].astype(f32))
        n_out[...] = (unit * g_ref[...] + c_ref[...]).astype(bf16)

    return call(
        body,
        [shape((total, width), bf16)] * 2,
        (total // ROWS,),
        [turned_spec(width, total // ROWS), whole_spec(1, width), whole_spec(1, width)],
        [row_spec(width)] * 2,
        [tokens, gain, bias],
        ids=[ids, split],
        name="first_norm",
    )


def first_spec(cols, blocks):
    return pl.BlockSpec((ROWS, cols), lambda i, *ids: (jnp.minimum(i, blocks - 1), 0))


def swapped(values, part):
    if part % LANES:
        return values
    blocks = [values[:, o : o + part] for o in range(0, values.shape[1], part)]
    return jnp.concatenate([blocks[pair_of(o)] for o in range(len(blocks))], axis=1)


def pair_of(o):
    return o if o & 2 else o ^ 1


def swap_small(values, part):
    if part % LANES == 0:
        return values
    blocks = [values[:, o : o + part] for o in range(0, values.shape[1], part)]
    return jnp.concatenate([blocks[pair_of(o)] for o in range(len(blocks))], axis=1)


def cotangent_order(cotangent, ids, split, count):
    total, width = cotangent.shape
    cotangent, moved, part = placing(cotangent, ids, count)
    mine = total // ROWS // 2

    def body(ids_ref, split_ref, c_ref, c_out, pair_out, sum_out):
        for o in range(moved):
            c_out[:, o * part : (o + 1) * part] = c_ref[:, columns_of(ids_ref[o], part)]
        if not moved:
            c_out[...] = c_ref[...]
        pair_out[...] = swapped(c_out[...], part)
        add_rows(sum_out, c_out[...].astype(f32))

    return call(
        body,
        [shape((total // 2, width), bf16)] * 2 + [shape((1, width), f32)],
        (mine,),
        [turned_spec(width, total // ROWS)],
        [row_spec(width)] * 2 + [whole_spec(1, width)],
        [cotangent],
        ids=[ids, split],
        name="cotangent_order",
    )


def order_rows(array, block_ids, height, count):
    cols = array.shape[1]

    def body(ids_ref, in_ref, out_ref):
        out_ref[...] = in_ref[...]

    return call(
        body,
        shape((count * height, cols), array.dtype),
        (count,),
        [pl.BlockSpec((height, cols), lambda j, ids: (ids[j], 0))],
        pl.BlockSpec((height, cols), lambda j, ids: (j, 0)),
        [array],
        ids=[block_ids],
        name="order_rows",
    )


def hidden_units(rows, weight, bias, hidden_grad):
    total, depth = rows.shape
    cols = weight.shape[1]
    high, wide, sub = 256, 1024, 256
    curve, cube = (2.0 / 3.141592653589793) ** 0.5, 0.044715

    def body(n_ref, w_ref, b_ref, dz_ref, z_out, du_out, sum_out):
        first = pl.program_id(1) == 0
        for c in range(0, wide, sub):
            at = slice(c, c + sub)
            u = jnp.dot(n_ref[...], w_ref[:, at], preferred_element_type=f32) + b_ref[:, at]
            square = u * u
            t = jnp.tanh(curve * u * (1.0 + cube * square))
            z_out[:, at] = (0.5 * u * (1.0 + t)).astype(bf16)
            slope = 0.5 * (1.0 + t) + (0.5 * curve) * u * (1.0 - t * t) * (
                1.0 + (3.0 * cube) * square
            )
            du = (slope * dz_ref[:, at].astype(f32)).astype(bf16)
            du_out[:, at] = du
            total_du = jnp.sum(du.astype(f32), axis=0, keepdims=True)
            sum_out[:, at] = jnp.where(first, total_du, sum_out[:, at] + total_du)

    tile = pl.BlockSpec((high, wide), lambda j, i: (i, j))
    line = pl.BlockSpec((1, wide), lambda j, i: (0, j))
    return call(
        body,
        [shape((total, cols), bf16)] * 2 + [shape((1, cols), f32)],
        (cols // wide, total // high),
        [
            pl.BlockSpec((high, depth), lambda j, i: (i, 0)),
            pl.BlockSpec((depth, wide), lambda j, i: (0, j)),
            line,
            tile,
        ],
        [tile, tile, line],
        [rows, weight, bias, hidden_grad],
        flops=2 * total * depth * cols,
        name="hidden_units",
    )


def add_rows(sum_ref, values):
    @pl.when(pl.program_id(0) == 0)
    def _():
        sum_ref[...] = jnp.zeros_like(sum_ref)

    sum_ref[...] += jnp.sum(values, axis=0, keepdims=True)


def middle_norm(x_rel, part_own, part_other, bias_out, gain, bias, part):
    total, width = part_other.shape

    def body(x_ref, a_ref, b_ref, bo_ref, g_ref, c_ref, h_out, n_out, pair_out):
        mid = x_ref[...].astype(f32) + (
            a_ref[...].astype(f32) + b_ref[...].astype(f32)
        ) + bo_ref[...]
        h_out[...] = mid
        unit, _ = norm_stats(mid)
        low = (unit * g_ref[...] + c_ref[...]).astype(bf16)
        n_out[...] = low
        pair_out[...] = swapped(low, part)

    return call(
        body,
        [shape((total, width), f32)] + [shape((total, width), bf16)] * 2,
        (total // ROWS,),
        [row_spec(width)] * 3 + [whole_spec(1, width)] * 3,
        [row_spec(width)] * 3,
        [x_rel, part_own, part_other, bias_out, gain, bias],
        name="middle_norm",
    )


def block_result(middle, part_own, part_pair, bias_down, ids, count):
    total, width = middle.shape
    part = width // count

    def body(ids_ref, h_ref, a_ref, p_ref, b2_ref, out_ref):
        value = a_ref[...].astype(f32) + swapped(p_ref[...], part).astype(f32)
        value = (h_ref[...] + value + b2_ref[...]).astype(bf16)
        if part % LANES:
            out_ref[...] = value
        else:
            for o in range(count):
                out_ref[:, columns_of(ids_ref[o], part)] = value[:, o * part : (o + 1) * part]

    result = call(
        body,
        shape((total, width), bf16),
        (total // ROWS,),
        [row_spec(width)] * 3 + [whole_spec(1, width)],
        row_spec(width),
        [middle, part_own, part_pair, bias_down],
        ids=[ids],
        name="block_result",
    )
    return put_back(result, ids, count)


def middle_backward(middle, part_own, part_other, part_pair, cot_rel, gain, part):
    total, width = middle.shape

    def body(h_ref, a_ref, b_ref, p_ref, dy_ref, g_ref, dh_out, low_out, gg_out, gc_out, gbo_out):
        unit, inv = norm_stats(h_ref[...])
        grad = a_ref[...].astype(f32) + b_ref[...].astype(f32)
        grad = grad + swapped(p_ref[...], part).astype(f32)
        scaled = grad * g_ref[...]
        dh = dy_ref[...].astype(f32) + inv * (
            scaled
            - jnp.mean(scaled, axis=-1, keepdims=True)
            - unit * jnp.mean(scaled * unit, axis=-1, keepdims=True)
        )
        dh_out[...] = dh
        low = dh.astype(bf16)
        low_out[...] = low
        add_rows(gg_out, grad * unit)
        add_rows(gc_out, grad)
        add_rows(gbo_out, low.astype(f32))

    vec = shape((1, width), f32)
    return call(
        body,
        [shape((total, width), f32), shape((total, width), bf16), vec, vec, vec],
        (total // ROWS,),
        [row_spec(width)] * 5 + [whole_spec(1, width)],
        [row_spec(width)] * 2 + [whole_spec(1, width)] * 3,
        [middle, part_own, part_other, part_pair, cot_rel, gain],
        name="middle_backward",
    )


def first_backward(x_rel, part_own, part_other, keyval_grad, w_keyval, dh, gain, ids, count):
    total, width = dh.shape
    part = width // count
    kv = keyval_grad.shape[1]

    def body(ids_ref, x_ref, a_ref, b_ref, kv_ref, w_ref, dh_ref, g_ref, t_out, gg_out, gc_out):
        unit, inv = norm_stats(x_ref[...].astype(f32))
        grad = (a_ref[...].astype(f32) + b_ref[...].astype(f32)) + lax.dot_general(
            kv_ref[...], w_ref[...], (((1,), (1,)), ((), ())), preferred_element_type=f32
        )
        scaled = grad * g_ref[...]
        value = dh_ref[...] + inv * (
            scaled
            - jnp.mean(scaled, axis=-1, keepdims=True)
            - unit * jnp.mean(scaled * unit, axis=-1, keepdims=True)
        )
        low = value.astype(bf16)
        if part % LANES:
            t_out[...] = low
        else:
            for o in range(count):
                t_out[:, columns_of(ids_ref[o], part)] = low[:, o * part : (o + 1) * part]
        add_rows(gg_out, grad * unit)
        add_rows(gc_out, grad)

    vec = shape((1, width), f32)
    result, gain_grad, bias_grad = call(
        body,
        [shape((total, width), bf16), vec, vec],
        (total // ROWS,),
        [row_spec(width)] * 3
        + [row_spec(kv), whole_spec(width, kv), row_spec(width), whole_spec(1, width)],
        [row_spec(width)] + [whole_spec(1, width)] * 2,
        [x_rel, part_own, part_other, keyval_grad, w_keyval, dh, gain],
        ids=[ids],
        flops=2 * total * width * kv,
        name="first_backward",
    )
    return put_back(result, ids, count), gain_grad, bias_grad


TILE = 256


def score_limits(lengths, token_count, first_place):
    doc_ends = jnp.cumsum(lengths)
    doc_starts = doc_ends - lengths
    places = (jnp.arange(token_count, dtype=jnp.int32) + first_place) % token_count
    doc_ids = jnp.sum((places[:, None] >= doc_ends[None, :]).astype(jnp.int32), axis=1)
    owners = doc_ids[:, None] == jnp.arange(lengths.shape[0], dtype=jnp.int32)[None, :]
    doc_begin = jnp.sum(jnp.where(owners, doc_starts[None, :], 0), axis=1)
    blocks = (places - doc_begin) // BLOCK
    seen = (doc_ids[:, None] == doc_ids[None, :]) & (blocks[None, :] <= blocks[:, None])
    seen_t = (doc_ids[None, :] == doc_ids[:, None]) & (blocks[:, None] <= blocks[None, :])
    pick = lambda s: jnp.where(s, shown_score, hidden_score).astype(f32)
    return pick(seen), pick(seen_t)


def attention_forward(queries, key_value, limits, heads):
    total = queries.shape[0]
    tiles = total // TILE
    c = score_scale * log2_e

    def body(q_ref, kv_ref, lim_ref, o_ref, lse_ref, top_ref):
        tile, head = pl.program_id(0), pl.program_id(1)
        k = kv_ref[:, :HD]
        v = kv_ref[:, HD:]
        s = lax.dot_general(
            q_ref[...], k, (((1,), (1,)), ((), ())), preferred_element_type=f32
        )
        s = jnp.minimum(s, lim_ref[...])
        m = jnp.max(s, axis=1, keepdims=True)
        p = jnp.exp2((s - m) * c)
        l = jnp.sum(p, axis=1, keepdims=True)
        o = jnp.dot(p.astype(bf16), v, preferred_element_type=f32)
        o_ref[...] = (o / l).astype(bf16)
        lane = lax.broadcasted_iota(jnp.int32, (TILE, LANES), 1)
        lse = m * c + jnp.log2(l)
        lse_ref[...] = jnp.where(lane == head, lse, lse_ref[...])

        @pl.when((tile == 0) & (head == 0))
        def _():
            top_ref[...] = jnp.full_like(top_ref, hidden_score)

        row = lax.broadcasted_iota(jnp.int32, (heads, LANES), 0)
        best = jnp.max(m, axis=0, keepdims=True) * score_scale
        top_ref[...] = jnp.where(row == head, jnp.maximum(top_ref[...], best), top_ref[...])

    return call(
        body,
        [shape((total, heads * HD), bf16), shape((total, LANES), f32), shape((heads, LANES), f32)],
        (tiles, heads),
        [
            pl.BlockSpec((TILE, HD), lambda i, h: (i, h)),
            pl.BlockSpec((total, 2 * HD), lambda i, h: (0, 0)),
            pl.BlockSpec((TILE, total), lambda i, h: (i, 0)),
        ],
        [
            pl.BlockSpec((TILE, HD), lambda i, h: (i, h)),
            pl.BlockSpec((TILE, LANES), lambda i, h: (i, 0)),
            pl.BlockSpec((heads, LANES), lambda i, h: (0, 0)),
        ],
        [queries, key_value, limits],
        flops=8 * total * total * HD * heads,
        name="attention_forward",
    )


def attention_backward(queries, grad_att, key_value, limits_t, lse_t, dot_t, heads):
    total = queries.shape[0]
    tiles = total // TILE
    c = score_scale * log2_e

    def body(q_ref, da_ref, kv_ref, lim_ref, lse_ref, dot_ref, dq_ref, dkv_ref):
        tile, head = pl.program_id(0), pl.program_id(1)
        k = kv_ref[:, :HD]
        v = kv_ref[:, HD:]
        q = q_ref[...]
        da = da_ref[...]
        nt = (((1,), (1,)), ((), ()))
        s = lax.dot_general(k, q, nt, preferred_element_type=f32)
        s = jnp.minimum(s, lim_ref[...])
        p = jnp.exp2(s * c - lse_ref[pl.ds(head, 1), :])
        dp = lax.dot_general(v, da, nt, preferred_element_type=f32)
        ds = (p * (dp - dot_ref[pl.ds(head, 1), :])).astype(bf16)
        dq = lax.dot_general(ds, k, (((0,), (0,)), ((), ())), preferred_element_type=f32)
        dq_ref[...] = (dq * score_scale).astype(bf16)

        @pl.when((tile == 0) & (head == 0))
        def _():
            dkv_ref[...] = jnp.zeros_like(dkv_ref)

        dkv_ref[:, :HD] += jnp.dot(ds, q, preferred_element_type=f32) * score_scale
        dkv_ref[:, HD:] += jnp.dot(p.astype(bf16), da, preferred_element_type=f32)

    return call(
        body,
        [shape((total, heads * HD), bf16), shape((total, 2 * HD), f32)],
        (tiles, heads),
        [
            pl.BlockSpec((TILE, HD), lambda i, h: (i, h)),
            pl.BlockSpec((TILE, HD), lambda i, h: (i, h)),
            pl.BlockSpec((total, 2 * HD), lambda i, h: (0, 0)),
            pl.BlockSpec((total, TILE), lambda i, h: (0, i)),
            pl.BlockSpec((heads, TILE), lambda i, h: (0, i)),
            pl.BlockSpec((heads, TILE), lambda i, h: (0, i)),
        ],
        [
            pl.BlockSpec((TILE, HD), lambda i, h: (i, h)),
            pl.BlockSpec((total, 2 * HD), lambda i, h: (0, 0)),
        ],
        [queries, grad_att, key_value, limits_t, lse_t, dot_t],
        flops=20 * total * total * HD * heads,
        name="attention_backward",
    )


def adam_values(gradient, weight, one, two, rate, decay):
    new_one = beta_one * one + (1.0 - beta_one) * gradient
    new_two = beta_two * two + (1.0 - beta_two) * gradient * gradient
    direction = (new_one * correct_one) / (jnp.sqrt(new_two * correct_two) + adam_eps)
    return new_one, new_two, weight - rate * (direction + decay * weight)


def to_tiles(flat, tiles_ref):
    for j in range(8):
        tiles_ref[:, j, :] = flat[:, j * LANES : (j + 1) * LANES]


def adam_in(gradient, weight, one, two, outer, start, full):
    rows, cols = gradient.shape
    step = 64
    base = (start // 1024).reshape(1)
    tall = pl.BlockSpec((step, 8, LANES), lambda i, j, b: (i, b[0] + j, 0))
    flat = pl.BlockSpec((step, 1024), lambda i, j, b: (i, j))
    args = [gradient, weight, one, two, outer]
    specs = [flat] + [tall] * 4
    aliases = {}
    if full is not None:
        aliases = {5: 0, 6: 1}
        args += list(full)
        specs += [pl.BlockSpec(memory_space=pl.ANY)] * 2

    def body(_, g_ref, w_ref, one_ref, two_ref, out_ref, *rest):
        one_out, two_out, delta_out, grad_tiles, delta_tiles = rest[-5:]
        to_tiles(g_ref[...].astype(f32), grad_tiles)
        new_one, new_two, stepped = adam_values(
            grad_tiles[...], w_ref[...], one_ref[...], two_ref[...], rate_matrix, weight_decay
        )
        one_out[...] = new_one
        two_out[...] = new_two
        delta_tiles[...] = out_ref[...] - stepped
        for j in range(8):
            delta_out[:, j * LANES : (j + 1) * LANES] = delta_tiles[:, j, :].astype(bf16)

    whole = shape(weight.shape, f32)
    return call(
        body,
        [whole, whole, shape((rows, cols), bf16)],
        (rows // step, cols // 1024),
        specs,
        [tall, tall, flat],
        args,
        ids=[base],
        scratch=[pltpu.VMEM((step, 8, LANES), f32)] * 2,
        aliases=aliases,
        name="adam_in",
        vmem=VMEM_MOST,
    )


def adam_out(gradient, weight, one, two, outer, start, full):
    rows, cols = gradient.shape
    step = 512
    base = (start // step).reshape(1)
    tall = pl.BlockSpec((step, cols), lambda i, b: (b[0] + i, 0))
    flat = pl.BlockSpec((step, cols), lambda i, b: (i, 0))
    args = [gradient, weight, one, two, outer]
    specs = [flat] + [tall] * 4
    aliases = {}
    if full is not None:
        aliases = {5: 0, 6: 1}
        args += list(full)
        specs += [pl.BlockSpec(memory_space=pl.ANY)] * 2

    def body(_, g_ref, w_ref, one_ref, two_ref, out_ref, *rest):
        one_out, two_out, delta_out = rest[-3:]
        new_one, new_two, stepped = adam_values(
            g_ref[...].astype(f32), w_ref[...], one_ref[...], two_ref[...], rate_matrix,
            weight_decay,
        )
        one_out[...] = new_one
        two_out[...] = new_two
        delta_out[...] = (out_ref[...] - stepped).astype(bf16)

    whole = shape(weight.shape, f32)
    return call(
        body,
        [whole, whole, shape((rows, cols), bf16)],
        (rows // step,),
        specs,
        [tall, tall, flat],
        args,
        ids=[base],
        aliases=aliases,
        name="adam_out",
        vmem=VMEM_MOST,
    )


def outer_values(mean, momentum, outer):
    velocity = outer_beta * momentum + mean
    return velocity, outer - outer_rate * (mean + outer_beta * velocity)


def outer_in(both, momentum, outer, factor, start, full):
    _, rows, cols = both.shape
    step = 64
    base = (start // 1024).reshape(1)
    tall = pl.BlockSpec((step, 8, LANES), lambda i, j, b: (i, b[0] + j, 0))
    flat = pl.BlockSpec((2, step, 1024), lambda i, j, b: (0, i, j))
    wide = pl.BlockSpec((step, 1024), lambda i, j, b: (i, b[0] + j))
    args = [both, momentum, outer]
    specs = [flat, tall, tall]
    if factor is not None:
        args.append(factor)
        specs.append(pl.BlockSpec((8, LANES), lambda i, j, b: (0, 0)))
    aliases = {}
    if full is not None:
        aliases = {len(args) + k: k for k in range(4)}
        args += list(full)
        specs += [pl.BlockSpec(memory_space=pl.ANY)] * 4

    def body(_, both_ref, mom_ref, out_ref, *rest):
        mean_out, vel_out, new_out, copy_out, mean_tiles, new_tiles = rest[-6:]
        to_tiles((both_ref[0].astype(f32) + both_ref[1].astype(f32)) * 0.5, mean_tiles)
        mean = mean_tiles[...]
        velocity, fresh = outer_values(mean, mom_ref[...], out_ref[...])
        if factor is not None:
            fresh = fresh * rest[0][...][None]
        mean_out[...] = mean
        vel_out[...] = velocity
        new_out[...] = fresh
        new_tiles[...] = fresh
        for j in range(8):
            copy_out[:, j * LANES : (j + 1) * LANES] = new_tiles[:, j, :].astype(bf16)

    whole = shape(outer.shape, f32)
    return call(
        body,
        [whole, whole, whole, shape((rows, outer.shape[1] * LANES), bf16)],
        (rows // step, cols // 1024),
        specs,
        [tall, tall, tall, wide],
        args,
        ids=[base],
        scratch=[pltpu.VMEM((step, 8, LANES), f32)] * 2,
        aliases=aliases,
        name="outer_in",
        vmem=VMEM_MOST,
    )


def outer_out(both, momentum, outer, start, full):
    _, rows, cols = both.shape
    step = 512
    base = (start // step).reshape(1)
    tall = pl.BlockSpec((step, cols), lambda i, b: (b[0] + i, 0))
    flat = pl.BlockSpec((2, step, cols), lambda i, b: (0, i, 0))
    args = [both, momentum, outer]
    specs = [flat, tall, tall]
    aliases = {}
    if full is not None:
        aliases = {3 + k: k for k in range(4)}
        args += list(full)
        specs += [pl.BlockSpec(memory_space=pl.ANY)] * 4

    def body(_, both_ref, mom_ref, out_ref, *rest):
        mean_out, vel_out, new_out, copy_out = rest[-4:]
        mean = (both_ref[0].astype(f32) + both_ref[1].astype(f32)) * 0.5
        velocity, fresh = outer_values(mean, mom_ref[...], out_ref[...])
        mean_out[...] = mean
        vel_out[...] = velocity
        new_out[...] = fresh
        copy_out[...] = fresh.astype(bf16)

    whole = shape(outer.shape, f32)
    return call(
        body,
        [whole, whole, whole, shape(outer.shape, bf16)],
        (rows // step,),
        specs,
        [tall] * 4,
        args,
        ids=[base],
        aliases=aliases,
        name="outer_out",
        vmem=VMEM_MOST,
    )


class Wire:
    def __init__(self, window):
        self.window, self.landed = window, []

    def send(self, block, axis, pairs):
        if len(self.landed) >= self.window:
            block, _ = lax.optimization_barrier((block, self.landed[-self.window]))
        arrived = lax.ppermute(block, axis, pairs)
        self.landed.append(arrived)
        return arrived


class Links:
    def __init__(self, count, splits, window):
        self.levels = count.bit_length() - 1
        self.far = ([1] + [1 << b for b in range(3, self.levels)])[: self.levels - 2]
        places = range(count)
        middle = [i for i in places if (i >> 1 ^ i >> 2) & 1]
        outer = [i for i in places if i not in middle]
        self.pair = [(i, i ^ 2) for i in places]
        self.inward = [(i, i ^ 2) for i in outer]
        self.outward = [(i, i ^ 2) for i in middle]
        self.between = [(i, i ^ 6) for i in middle]
        self.beside = [[(i, i ^ mask) for i in places] for mask in self.far]
        self.mirror = [(i, i ^ 6) for i in places]
        self.cores = [(i, (i + 1) % splits) for i in range(splits)]
        self.wire = Wire(window)

    def flips(self, across):
        masks = [2, across] + self.far
        table = []
        for o in range(1 << self.levels):
            flip = 0
            for level, mask in enumerate(masks):
                if o >> level & 1:
                    flip ^= mask
            table.append(flip)
        return table

    def to_side(self, block, pairs):
        return self.wire.send(block, "dp", pairs)

    def to_middle(self, block):
        return self.wire.send(block, "dp", self.between)

    def to_far(self, block, level):
        return self.wire.send(block, "dp", self.beside[level - 2])

    def to_pair(self, block):
        return self.wire.send(block, "dp", self.pair)

    def across(self, block):
        return lax.ppermute(block, "tensor", self.cores)

    def pair_now(self, block):
        return lax.ppermute(block, "dp", self.pair)


def after(value, *earlier):
    return lax.optimization_barrier((value, *earlier))[0]


class Gathered:
    def __init__(self, links, axis, mine, other=None):
        self.links, self.axis, self.mine, self.other = links, axis, mine, other
        self.held = {}

    def join(self, *blocks):
        return jnp.concatenate(blocks, axis=self.axis)

    def near(self):
        give = self.mine if self.other is None else self.other
        self.held[0] = self.join(self.mine, self.links.to_side(give, self.links.pair))

    def inward(self):
        if self.other is not None:
            self.passed = self.links.to_side(self.mine, self.links.inward)

    def middle(self):
        if self.other is None:
            self.relay = self.direct = self.links.to_middle(self.held[0])
        else:
            self.relay = self.links.to_middle(self.join(self.other, self.passed))

    def middle_rest(self):
        self.direct = self.links.to_middle(self.held[0])

    def outward(self):
        self.relayed = self.links.to_side(self.relay, self.links.outward)

    def join_far(self):
        self.held[2] = self.direct + self.relayed

    def far(self, level, o):
        self.held[o + (1 << level)] = self.links.to_far(self.held[o], level)

    def whole(self):
        for level in range(2, self.links.levels):
            for o in range(0, 1 << level, 2):
                if o + (1 << level) not in self.held:
                    self.far(level, o)
        return self.join(*[self.held[o] for o in sorted(self.held)])


class Reduced:
    def __init__(self, links, axis, size, halved, part):
        self.links, self.axis, self.size, self.halved, self.part = links, axis, size, halved, part
        self.landed = {}

    def pair_sum(self, o):
        total = self.part(o, 2)
        for block in self.landed.pop(o, []):
            total = total + block.astype(f32)
        return total.astype(bf16)

    def one(self, block, o):
        return lax.slice_in_dim(
            block, o * self.size, (o + 1) * self.size, axis=self.axis
        ).astype(f32)

    def far(self):
        sent = []
        for level in range(self.links.levels - 1, 1, -1):
            for o in reversed(range(1 << level, 2 << level, 2)):
                sent.append(self.pair_sum(o))
                arrived = self.links.to_far(sent[-1], level)
                self.landed.setdefault(o - (1 << level), []).append(arrived)
        return sent

    def inward(self):
        self.ahead = self.pair_sum(2)
        self.passed = self.links.to_side(self.ahead, self.links.inward)
        return self.ahead

    def middle(self):
        self.direct = self.links.to_middle(
            self.ahead if self.halved else self.ahead + self.passed
        )

    def middle_rest(self):
        self.relay = self.links.to_middle(self.passed)

    def single(self, o):
        total = self.part(o, 1)
        for block in self.landed[0] + [self.direct]:
            total = total + self.one(block, o)
        return total

    def near(self):
        value = self.single(1).astype(bf16)
        self.theirs = self.links.to_side(value, self.links.pair).astype(f32)
        return value

    def outward(self):
        value = self.one(self.relay, 1).astype(bf16)
        self.last = self.links.to_side(value, self.links.outward).astype(f32)

    def result(self):
        if not self.halved:
            return self.single(0) + self.theirs, None
        return self.single(0) + self.last, self.theirs + self.one(self.relay, 0)


def local(
    tokens,
    doc_lengths,
    cotangent,
    inner_in,
    inner_out,
    inner_shared,
    first_in,
    first_out,
    first_shared,
    second_in,
    second_out,
    second_shared,
    outer_in_w,
    outer_out_w,
    outer_shared,
    momentum_in,
    momentum_out,
    momentum_shared,
):
    splits = lax.axis_size("tensor")
    count = lax.axis_size("dp")
    split = lax.axis_index("tensor")
    place = lax.axis_index("dp")
    total, width = tokens.shape
    part = width // count
    local_cols = inner_in.shape[3]
    shared_cols = inner_shared.shape[2]
    heads = HEADS // splits
    qcols = heads * HD
    hidden = local_cols - qcols
    vec = 2 * HD
    own_cols = part // splits
    mine = total // 2

    links = Links(count, splits, 4)
    across = links.across
    levels = links.levels
    side = ((place >> 1) ^ (place >> 2)) & 1
    from_outer, from_middle = (jnp.array(links.flips(m), jnp.int32) for m in (4, 6))
    ids = (place ^ jnp.where(side == 0, from_outer, from_middle)).astype(jnp.int32)
    swap_group = [(0, 1), (1, 0)]
    split_id = split.astype(jnp.int32).reshape(1)

    def tall(array):
        return array.reshape(part, local_cols // LANES, LANES)

    w_in = tall(inner_in)
    w_out = inner_out.reshape(local_cols, part)
    everyone = ("dp", "tensor")
    keyval_rows = lax.all_gather(inner_shared[0, :, :vec].astype(bf16), everyone, axis=0, tiled=True)
    vector_rows = lax.all_gather(inner_shared[0, :, vec:], everyone, axis=0, tiled=True)

    half = hidden // 2
    flat_in = inner_in.reshape(part, local_cols)

    def sides(low, high):
        return (
            jnp.where(side == 0, low, high).astype(bf16),
            jnp.where(side == 0, high, low).astype(bf16),
        )

    block_q = flat_in[:, :qcols].astype(bf16)
    block_o = w_out[:qcols].astype(bf16)
    up_sides = sides(flat_in[:, qcols : qcols + half], flat_in[:, qcols + half :])
    down_sides = sides(w_out[qcols : qcols + half], w_out[qcols + half :])
    got_query = Gathered(links, 0, block_q)
    got_attn = Gathered(links, 1, block_o)
    got_up = Gathered(links, 0, *up_sides)
    got_down = Gathered(links, 1, *down_sides)
    w_keyval = order_rows(keyval_rows, ids, part, count)
    vectors_t = vector_rows.T
    vectors = pick_blocks(vectors_t, ids, part, count, False)
    gain_one, bias_one, gain_two, bias_two = (vectors[k : k + 1] for k in range(4))
    bias_out, bias_down = vectors[5:6], vectors[6:7]
    bias_query = lax.dynamic_slice_in_dim(vectors_t[4], split * qcols, qcols)
    bias_up = lax.dynamic_slice_in_dim(
        vectors_t[7:].reshape(FF), split * hidden + side * half, half
    )

    nt = (((1,), (1,)), ((), ()))
    tn = (((0,), (0,)), ((), ()))

    def mm(a, b, dims=(((1,), (0,)), ((), ()))):
        return lax.dot_general(a, b, dims, preferred_element_type=f32)

    def block(array, o, blocks):
        return array[:, o * part : (o + blocks) * part]

    def both_rows(rows):
        return lax.all_gather(rows, "tensor", axis=0, tiled=True)

    def far(weight, o):
        if levels == 3:
            weight.far(2, o)

    cot_own, cot_pair, grad_bias_down = cotangent_order(cotangent, ids, split_id, count)
    got_query.near()
    got_attn.near()
    got_query.middle()
    far(got_query, 0)
    got_down.near()
    got_down.inward()
    got_attn.middle()
    far(got_attn, 0)
    got_query.outward()
    got_query.join_far()
    far(got_query, 2)
    got_attn.outward()
    got_attn.join_far()
    got_down.middle()
    got_up.near()
    far(got_attn, 2)
    w_query = got_query.whole()
    w_attn = got_attn.whole()
    got_up.inward()
    far(got_down, 0)
    cot_theirs = links.to_pair(swap_small(cot_pair, part))
    got_down.outward()
    got_down.middle_rest()
    got_down.join_far()
    far(got_up, 0)
    got_up.middle()
    far(got_down, 2)
    w_down = got_down.whole()
    got_up.outward()
    got_up.middle_rest()
    got_up.join_far()

    x_rel, normed = first_norm(tokens, ids, split_id, gain_one, bias_one, count)
    limits, limits_t = score_limits(doc_lengths[0], total, split * mine)
    key_value = mm(normed, w_keyval).astype(bf16)
    queries = (mm(normed, w_query) + bias_query).astype(bf16)
    attended, log_totals, tops = attention_forward(queries, key_value, limits, heads)
    attn_give = mm(attended[mine:], w_attn).astype(bf16)
    attn_keep = mm(attended[:mine], w_attn).astype(bf16)
    attn_other = across(attn_give)
    middle, normed_two, normed_pair = middle_norm(
        x_rel, attn_keep, attn_other, bias_out, gain_two, bias_two, part
    )
    normed_theirs = links.to_pair(swap_small(normed_pair, part))
    far(got_up, 2)
    w_up = got_up.whole()
    normed_all = both_rows(jnp.concatenate([normed_two, normed_theirs], axis=0))
    cot_all = both_rows(jnp.concatenate([cot_own, cot_theirs], axis=0))
    hidden_grad = mm(cot_all, w_down, nt).astype(bf16)
    acts, grad_pre, grad_bias_up = hidden_units(normed_all, w_up, bias_up[None], hidden_grad)

    links.wire.window = 3
    sum_down = Reduced(
        links, 1, part, True, lambda o, b: mm(acts, block(cot_all, o, b), tn)
    )
    sum_up = Reduced(
        links, 0, part, True, lambda o, b: mm(block(normed_all, o, b), grad_pre, tn)
    )
    sent_down = sum_down.far()
    w_up_late = after(w_up, sent_down[0])
    pre_give = lax.dynamic_slice_in_dim(grad_pre, (1 - split) * 2 * mine, 2 * mine)
    pre_keep = lax.dynamic_slice_in_dim(grad_pre, split * 2 * mine, 2 * mine)
    two_give = mm(pre_give, w_up_late, nt).astype(bf16)
    two_other = across(two_give)
    two_keep = mm(pre_keep, after(w_up_late, two_give, *sent_down), nt).astype(bf16)
    two_theirs = two_keep[mine:].astype(f32) + two_other[mine:].astype(f32)
    two_pair = links.pair_now(swap_small(two_theirs.astype(bf16), part))
    sent_up = sum_up.far()
    ahead_down = sum_down.inward()
    sum_down.middle()
    dh, dh_mine, grad_gain_two, grad_bias_two, grad_bias_out = middle_backward(
        middle, two_keep, two_other, two_pair, cot_own, gain_two, part
    )
    dh_low = jnp.concatenate([dh_mine, across(dh_mine)], axis=0)

    grad_att = mm(dh_low, after(w_attn, *sent_up, ahead_down), nt).astype(bf16)
    dots = jnp.sum(
        (grad_att.astype(f32) * attended.astype(f32)).reshape(total, heads, HD), axis=2
    )
    grad_queries, kv_part = attention_backward(
        queries, grad_att, key_value, limits_t, log_totals.T[:heads], dots.T, heads
    )
    sum_down.middle_rest()
    sum_down.near()
    sum_down.outward()
    sum_attn = Reduced(
        links, 1, part, False, lambda o, b: mm(attended, block(dh_low, o, b), tn)
    )
    sent_attn = sum_attn.far()
    one_give = mm(grad_queries[mine:], w_query, nt).astype(bf16)
    one_other = across(one_give)
    one_keep = mm(grad_queries[:mine], w_query, nt).astype(bf16)
    kv_low = (kv_part[:mine] + across(kv_part[mine:])).astype(bf16)
    grad_keyval_t = mm(kv_low, normed[:mine], tn)
    sum_up.inward()
    sum_up.middle()
    sum_query = Reduced(
        links, 0, part, False, lambda o, b: mm(block(normed, o, b), grad_queries, tn)
    )
    sum_query.far()
    sum_up.middle_rest()
    grad_mine, grad_gain_one, grad_bias_one = first_backward(
        x_rel, one_keep, one_other, kv_low, w_keyval, dh, gain_one, ids, count
    )
    tokens_grad = both_rows(grad_mine)

    down_part = mm(after(acts, *sent_attn), w_down).astype(bf16)
    down_sum = lax.psum_scatter(down_part, "tensor", scatter_dimension=0, tiled=True)

    peers = across(after(tops, *sent_up))
    peak = jnp.where(
        split == 0, jnp.concatenate([tops, peers]), jnp.concatenate([peers, tops])
    )
    peak = jnp.maximum(peak, lax.ppermute(peak, "group", swap_group))
    for pairs in [links.pair, links.mirror] + links.beside:
        peak = jnp.maximum(peak, lax.ppermute(peak, "dp", pairs))
    clip_rows = clip_limit / jnp.maximum(peak, clip_limit)

    sum_up.near()
    sum_up.outward()
    sum_attn.inward()
    sum_attn.middle()
    sum_query.inward()
    down_pair = links.to_pair(swap_small(down_sum[mine:], part))
    block_out = both_rows(
        block_result(middle, down_sum, down_pair, bias_down, ids, count)
    )

    grad_bias_query = jnp.sum(grad_queries.astype(f32), axis=0)
    spread = jnp.concatenate(
        [
            lax.dynamic_update_slice_in_dim(
                jnp.zeros((width,), f32), grad_bias_query, split * qcols, 0
            ),
            lax.dynamic_update_slice_in_dim(
                jnp.zeros((FF,), f32), grad_bias_up[0], split * hidden + side * half, 0
            ),
        ]
    ).reshape(1 + FF // width, width)
    near = jnp.concatenate(
        [grad_keyval_t, grad_gain_one, grad_bias_one, grad_gain_two, grad_bias_two, grad_bias_out,
         grad_bias_down],
        axis=0,
    )
    steps = jnp.arange(count, dtype=jnp.int32)
    turned = jnp.where((side == 0) & ((steps & 2) != 0), steps ^ 1, steps)
    mirrored = (place ^ from_middle).astype(jnp.int32)

    def pieces(core):
        a = pick_blocks(near, turned * splits + core, own_cols, count, True)
        b = pick_blocks(spread, mirrored * splits + core, own_cols, count, True)
        return jnp.concatenate([a[:, : vec + 4], b[:, :1], a[:, vec + 4 :], b[:, 1:]], axis=1)

    red_shared = pieces(split) + across(pieces(1 - split))
    sum_query.middle()
    sum_attn.near()
    for pairs in reversed([links.pair, links.mirror] + links.beside):
        keep = red_shared.shape[0] // 2
        red_shared = red_shared[:keep] + links.to_side(red_shared[keep:], pairs)
    red_shared = red_shared[0]
    sum_query.near()
    red_down, red_up = sum_down.result(), sum_up.result()
    red_attn, red_query = sum_attn.result()[0], sum_query.result()[0]

    one_in, two_in = tall(first_in), tall(second_in)
    one_out, two_out = (a.reshape(local_cols, part) for a in (first_out, second_out))
    base_in, mom_in = tall(outer_in_w), tall(momentum_in)
    base_out, mom_out = (a.reshape(local_cols, part) for a in (outer_out_w, momentum_out))
    clip_own = lax.dynamic_slice_in_dim(clip_rows, split * heads, heads)

    starts = [qcols + side * half, qcols + (1 - side) * half]
    zero = jnp.zeros((), jnp.int32)
    gathered = []

    def groups(delta):
        both = lax.all_gather(after(delta, *gathered[-1:]), "group", axis=0)
        gathered.append(both)
        return both

    full_in = full_out = new_in = new_out = None
    for s, gradient in zip(starts, red_down):
        *full_out, delta = adam_out(gradient, w_out, one_out, two_out, base_out, s, full_out)
        new_out = outer_out(groups(delta), mom_out, base_out, s, new_out)
    for s, gradient in zip(starts, red_up):
        *full_in, delta = adam_in(gradient, w_in, one_in, two_in, base_in, s, full_in)
        new_in = outer_in(groups(delta), mom_in, base_in, None, s, new_in)
    *full_out, delta = adam_out(red_attn, w_out, one_out, two_out, base_out, zero, full_out)
    new_out = outer_out(groups(delta), mom_out, base_out, zero, new_out)
    *full_in, delta = adam_in(red_query, w_in, one_in, two_in, base_in, zero, full_in)
    both = jnp.stack([delta, lax.ppermute(delta, "group", swap_group)])
    new_in = outer_in(both, mom_in, base_in, clip_own, zero, new_in)

    ids_col = jnp.arange(shared_cols, dtype=jnp.int32)[:, None]
    one_sh, two_sh, stepped = adam_values(
        red_shared,
        inner_shared[0].T,
        first_shared[0].T,
        second_shared[0].T,
        jnp.where(ids_col < vec, rate_matrix, rate_vector),
        jnp.where(ids_col < vec, weight_decay, 0.0),
    )
    base_sh = outer_shared.T
    delta = (base_sh - stepped).astype(bf16)
    mean_sh = (delta.astype(f32) + lax.ppermute(delta, "group", swap_group).astype(f32)) * 0.5
    vel_sh, fresh_sh = outer_values(mean_sh, momentum_shared.T, base_sh)
    row_ids = (place * splits + split) * own_cols + jnp.arange(own_cols, dtype=jnp.int32)
    clip_vec = clip_rows[:, 0]
    row_clip = jnp.sum(
        jnp.where((row_ids // HD)[None, :] == jnp.arange(HEADS)[:, None], clip_vec[:, None], 0.0),
        axis=0,
    )
    fresh_sh = fresh_sh * jnp.where(ids_col == vec + 4, row_clip[None, :], 1.0)

    shape_in, shape_out = (part, 1, local_cols), (1, local_cols, part)
    mean_in, vel_in, fresh_in, copy_in = new_in
    mean_out, vel_out, fresh_out, copy_out = new_out
    return (
        block_out,
        tokens_grad,
        clip_vec,
        full_in[0].reshape((1,) + shape_in),
        full_out[0].reshape((1,) + shape_out),
        one_sh.T[None],
        full_in[1].reshape((1,) + shape_in),
        full_out[1].reshape((1,) + shape_out),
        two_sh.T[None],
        mean_in.reshape(shape_in),
        mean_out.reshape(shape_out),
        mean_sh.T,
        vel_in.reshape(shape_in),
        vel_out.reshape(shape_out),
        vel_sh.T,
        fresh_in.reshape(shape_in),
        fresh_out.reshape(shape_out),
        fresh_sh.T,
        copy_in.reshape(shape_in),
        copy_out.reshape(shape_out),
        fresh_sh.T.astype(bf16),
    )


def solution(mesh):
    rows = P(("group", "dp"), None)
    inner = [P("group", "dp", "tensor", None), P("group", "tensor", None, "dp"),
             P("group", ("dp", "tensor"), None)]
    outer = [P("dp", "tensor", None), P("tensor", None, "dp"), P(("dp", "tensor"), None)]
    in_specs = tuple([rows] * 3 + inner * 3 + outer * 2)
    out_specs = tuple([rows] * 2 + [P()] + inner * 2 + outer * 4)
    return jax.shard_map(local, mesh=mesh, in_specs=in_specs, out_specs=out_specs, check_vma=False)
```

```python
import jax
import jax.numpy as jnp
from jax import lax
from jax.experimental import pallas as pl
from jax.experimental.pallas import tpu as pltpu
from jax.sharding import PartitionSpec as P

HEADS = 16
HD = 128
FF = 8192
BLOCK = 256
STEP = 10

norm_eps = 1e-05
hidden_score = -1e30
shown_score = 3e38
beta_one = 0.9
beta_two = 0.95
adam_eps = 1e-08
rate_matrix = 0.02
rate_vector = 0.2
weight_decay = 0.1
outer_beta = 0.9
outer_rate = 0.7
clip_limit = 5.0
score_scale = HD ** (-0.5)
log2_e = 1.4426950408889634
correct_one = 1.0 / (1.0 - beta_one**STEP)
correct_two = 1.0 / (1.0 - beta_two**STEP)

f32 = jnp.float32
bf16 = jnp.bfloat16
ROWS = 128
LANES = 128
VMEM_LIMIT = 40 * 1024 * 1024
VMEM_MOST = 58 * 1024 * 1024


def shape(dims, dtype):
    return jax.ShapeDtypeStruct(dims, dtype)


def call(body, out_shape, grid, in_specs, out_specs, args, *, ids=(), scratch=(), aliases=None,
         flops=0, name=None, vmem=VMEM_LIMIT):
    outs = out_shape if isinstance(out_shape, (list, tuple)) else [out_shape]
    moved = sum(a.size * a.dtype.itemsize for a in args)
    moved += sum(o.size * o.dtype.itemsize for o in outs)
    return pl.pallas_call(
        body,
        out_shape=out_shape,
        grid_spec=pltpu.PrefetchScalarGridSpec(
            num_scalar_prefetch=len(ids),
            grid=grid,
            in_specs=in_specs,
            out_specs=out_specs,
            scratch_shapes=list(scratch),
        ),
        input_output_aliases={len(ids) + k: v for k, v in (aliases or {}).items()},
        compiler_params=pltpu.CompilerParams(vmem_limit_bytes=vmem),
        cost_estimate=pl.CostEstimate(flops=flops, bytes_accessed=moved, transcendentals=0),
        name=name,
    )(*ids, *args)


def pick_blocks(array, block_ids, width, count, stacked):
    rows = array.shape[0]
    if width % LANES:
        taken = jnp.take(array.reshape(rows, -1, width), block_ids, axis=1)
        return taken.transpose(1, 0, 2) if stacked else taken.reshape(rows, count * width)

    def body(ids_ref, in_ref, out_ref):
        if stacked:
            out_ref[0] = in_ref[...]
        else:
            out_ref[...] = in_ref[...]

    if stacked:
        out, spec = shape((count, rows, width), array.dtype), pl.BlockSpec(
            (1, rows, width), lambda j, ids: (j, 0, 0)
        )
    else:
        out, spec = shape((rows, count * width), array.dtype), pl.BlockSpec(
            (rows, width), lambda j, ids: (0, j)
        )
    return call(
        body, out, (count,), [pl.BlockSpec((rows, width), lambda j, ids: (0, ids[j]))], spec,
        [array], ids=[block_ids], name="pick_blocks",
    )


def columns_of(block_id, width):
    return pl.ds(pl.multiple_of(block_id * width, width), width)


def placing(array, ids, count):
    part = array.shape[1] // count
    if part % LANES == 0:
        return array, count, part
    return pick_blocks(array, ids, part, count, False), 0, part


def put_back(array, ids, count):
    part = array.shape[1] // count
    if part % LANES == 0:
        return array
    back = jnp.sum(
        jnp.where(ids[None, :] == jnp.arange(count)[:, None], jnp.arange(count)[None, :], 0), axis=1
    ).astype(jnp.int32)
    return pick_blocks(array, back, part, count, False)


def norm_stats(rows):
    mean = jnp.mean(rows, axis=-1, keepdims=True)
    centered = rows - mean
    inv = lax.rsqrt(jnp.mean(centered * centered, axis=-1, keepdims=True) + norm_eps)
    return centered * inv, inv


def row_spec(cols, rows=ROWS):
    return pl.BlockSpec((rows, cols), lambda i, *ids: (i, 0))


def turned_spec(cols, blocks):
    return pl.BlockSpec(
        (ROWS, cols), lambda i, ids, split: ((i + split[0] * (blocks // 2)) % blocks, 0)
    )


def whole_spec(rows, cols):
    return pl.BlockSpec((rows, cols), lambda i, *ids: (0, 0))


def first_norm(tokens, ids, split, gain, bias, count):
    total, width = tokens.shape
    tokens, moved, part = placing(tokens, ids, count)

    def body(ids_ref, split_ref, x_ref, g_ref, c_ref, x_out, n_out):
        for o in range(moved):
            x_out[:, o * part : (o + 1) * part] = x_ref[:, columns_of(ids_ref[o], part)]
        if not moved:
            x_out[...] = x_ref[...]
        unit, _ = norm_stats(x_out[...].astype(f32))
        n_out[...] = (unit * g_ref[...] + c_ref[...]).astype(bf16)

    return call(
        body,
        [shape((total, width), bf16)] * 2,
        (total // ROWS,),
        [turned_spec(width, total // ROWS), whole_spec(1, width), whole_spec(1, width)],
        [row_spec(width)] * 2,
        [tokens, gain, bias],
        ids=[ids, split],
        name="first_norm",
    )


def first_spec(cols, blocks):
    return pl.BlockSpec((ROWS, cols), lambda i, *ids: (jnp.minimum(i, blocks - 1), 0))


def swapped(values, part):
    if part % LANES:
        return values
    blocks = [values[:, o : o + part] for o in range(0, values.shape[1], part)]
    return jnp.concatenate([blocks[pair_of(o)] for o in range(len(blocks))], axis=1)


def pair_of(o):
    return o if o & 2 else o ^ 1


def swap_small(values, part):
    if part % LANES == 0:
        return values
    blocks = [values[:, o : o + part] for o in range(0, values.shape[1], part)]
    return jnp.concatenate([blocks[pair_of(o)] for o in range(len(blocks))], axis=1)


def cotangent_order(cotangent, ids, split, count):
    total, width = cotangent.shape
    cotangent, moved, part = placing(cotangent, ids, count)
    mine = total // ROWS // 2

    def body(ids_ref, split_ref, c_ref, c_out, pair_out, sum_out):
        for o in range(moved):
            c_out[:, o * part : (o + 1) * part] = c_ref[:, columns_of(ids_ref[o], part)]
        if not moved:
            c_out[...] = c_ref[...]
        pair_out[...] = swapped(c_out[...], part)
        add_rows(sum_out, c_out[...].astype(f32))

    return call(
        body,
        [shape((total // 2, width), bf16)] * 2 + [shape((1, width), f32)],
        (mine,),
        [turned_spec(width, total // ROWS)],
        [row_spec(width)] * 2 + [whole_spec(1, width)],
        [cotangent],
        ids=[ids, split],
        name="cotangent_order",
    )


def hidden_units(rows, weight, bias, hidden_grad):
    total, depth = rows.shape
    cols = weight.shape[1]
    high, wide, sub = 256, 1024, 256
    curve, cube = (2.0 / 3.141592653589793) ** 0.5, 0.044715

    def body(n_ref, w_ref, b_ref, dz_ref, z_out, du_out, sum_out):
        first = pl.program_id(1) == 0
        for c in range(0, wide, sub):
            at = slice(c, c + sub)
            u = jnp.dot(n_ref[...], w_ref[:, at], preferred_element_type=f32) + b_ref[:, at]
            square = u * u
            t = jnp.tanh(curve * u * (1.0 + cube * square))
            z_out[:, at] = (0.5 * u * (1.0 + t)).astype(bf16)
            slope = 0.5 * (1.0 + t) + (0.5 * curve) * u * (1.0 - t * t) * (
                1.0 + (3.0 * cube) * square
            )
            du = (slope * dz_ref[:, at].astype(f32)).astype(bf16)
            du_out[:, at] = du
            total_du = jnp.sum(du.astype(f32), axis=0, keepdims=True)
            sum_out[:, at] = jnp.where(first, total_du, sum_out[:, at] + total_du)

    tile = pl.BlockSpec((high, wide), lambda j, i: (i, j))
    line = pl.BlockSpec((1, wide), lambda j, i: (0, j))
    return call(
        body,
        [shape((total, cols), bf16)] * 2 + [shape((1, cols), f32)],
        (cols // wide, total // high),
        [
            pl.BlockSpec((high, depth), lambda j, i: (i, 0)),
            pl.BlockSpec((depth, wide), lambda j, i: (0, j)),
            line,
            tile,
        ],
        [tile, tile, line],
        [rows, weight, bias, hidden_grad],
        flops=2 * total * depth * cols,
        name="hidden_units",
    )


def add_rows(sum_ref, values):
    @pl.when(pl.program_id(0) == 0)
    def _():
        sum_ref[...] = jnp.zeros_like(sum_ref)

    sum_ref[...] += jnp.sum(values, axis=0, keepdims=True)


def middle_norm(x_rel, part_own, part_other, bias_out, gain, bias, part):
    total, width = part_other.shape

    def body(x_ref, a_ref, b_ref, bo_ref, g_ref, c_ref, h_out, n_out, pair_out):
        mid = x_ref[...].astype(f32) + (
            a_ref[...].astype(f32) + b_ref[...].astype(f32)
        ) + bo_ref[...]
        h_out[...] = mid
        unit, _ = norm_stats(mid)
        low = (unit * g_ref[...] + c_ref[...]).astype(bf16)
        n_out[...] = low
        pair_out[...] = swapped(low, part)

    return call(
        body,
        [shape((total, width), f32)] + [shape((total, width), bf16)] * 2,
        (total // ROWS,),
        [row_spec(width)] * 3 + [whole_spec(1, width)] * 3,
        [row_spec(width)] * 3,
        [x_rel, part_own, part_other, bias_out, gain, bias],
        name="middle_norm",
    )


def block_result(middle, part_own, part_pair, bias_down, ids, count):
    total, width = middle.shape
    part = width // count

    def body(ids_ref, h_ref, a_ref, p_ref, b2_ref, out_ref):
        value = a_ref[...].astype(f32) + swapped(p_ref[...], part).astype(f32)
        value = (h_ref[...] + value + b2_ref[...]).astype(bf16)
        if part % LANES:
            out_ref[...] = value
        else:
            for o in range(count):
                out_ref[:, columns_of(ids_ref[o], part)] = value[:, o * part : (o + 1) * part]

    result = call(
        body,
        shape((total, width), bf16),
        (total // ROWS,),
        [row_spec(width)] * 3 + [whole_spec(1, width)],
        row_spec(width),
        [middle, part_own, part_pair, bias_down],
        ids=[ids],
        name="block_result",
    )
    return put_back(result, ids, count)


def middle_backward(middle, part_own, part_other, part_pair, cot_rel, gain, part):
    total, width = middle.shape

    def body(h_ref, a_ref, b_ref, p_ref, dy_ref, g_ref, dh_out, low_out, gg_out, gc_out, gbo_out):
        unit, inv = norm_stats(h_ref[...])
        grad = a_ref[...].astype(f32) + b_ref[...].astype(f32)
        grad = grad + swapped(p_ref[...], part).astype(f32)
        scaled = grad * g_ref[...]
        dh = dy_ref[...].astype(f32) + inv * (
            scaled
            - jnp.mean(scaled, axis=-1, keepdims=True)
            - unit * jnp.mean(scaled * unit, axis=-1, keepdims=True)
        )
        dh_out[...] = dh
        low = dh.astype(bf16)
        low_out[...] = low
        add_rows(gg_out, grad * unit)
        add_rows(gc_out, grad)
        add_rows(gbo_out, low.astype(f32))

    vec = shape((1, width), f32)
    return call(
        body,
        [shape((total, width), f32), shape((total, width), bf16), vec, vec, vec],
        (total // ROWS,),
        [row_spec(width)] * 5 + [whole_spec(1, width)],
        [row_spec(width)] * 2 + [whole_spec(1, width)] * 3,
        [middle, part_own, part_other, part_pair, cot_rel, gain],
        name="middle_backward",
    )


def first_backward(x_rel, part_own, part_other, keyval_grad, w_keyval_t, dh, gain, ids, count):
    total, width = dh.shape
    part = width // count
    kv = keyval_grad.shape[1]

    def body(ids_ref, x_ref, a_ref, b_ref, kv_ref, w_ref, dh_ref, g_ref, t_out, gg_out, gc_out):
        unit, inv = norm_stats(x_ref[...].astype(f32))
        grad = (a_ref[...].astype(f32) + b_ref[...].astype(f32)) + jnp.dot(
            kv_ref[...], w_ref[...], preferred_element_type=f32
        )
        scaled = grad * g_ref[...]
        value = dh_ref[...] + inv * (
            scaled
            - jnp.mean(scaled, axis=-1, keepdims=True)
            - unit * jnp.mean(scaled * unit, axis=-1, keepdims=True)
        )
        low = value.astype(bf16)
        if part % LANES:
            t_out[...] = low
        else:
            for o in range(count):
                t_out[:, columns_of(ids_ref[o], part)] = low[:, o * part : (o + 1) * part]
        add_rows(gg_out, grad * unit)
        add_rows(gc_out, grad)

    vec = shape((1, width), f32)
    result, gain_grad, bias_grad = call(
        body,
        [shape((total, width), bf16), vec, vec],
        (total // ROWS,),
        [row_spec(width)] * 3
        + [row_spec(kv), whole_spec(kv, width), row_spec(width), whole_spec(1, width)],
        [row_spec(width)] + [whole_spec(1, width)] * 2,
        [x_rel, part_own, part_other, keyval_grad, w_keyval_t, dh, gain],
        ids=[ids],
        flops=2 * total * width * kv,
        name="first_backward",
    )
    return put_back(result, ids, count), gain_grad, bias_grad


TILE = 256


def score_limits(lengths, token_count, first_place):
    doc_ends = jnp.cumsum(lengths)
    doc_starts = doc_ends - lengths
    places = (jnp.arange(token_count, dtype=jnp.int32) + first_place) % token_count
    doc_ids = jnp.sum((places[:, None] >= doc_ends[None, :]).astype(jnp.int32), axis=1)
    owners = doc_ids[:, None] == jnp.arange(lengths.shape[0], dtype=jnp.int32)[None, :]
    doc_begin = jnp.sum(jnp.where(owners, doc_starts[None, :], 0), axis=1)
    blocks = (places - doc_begin) // BLOCK
    seen = (doc_ids[:, None] == doc_ids[None, :]) & (blocks[None, :] <= blocks[:, None])
    seen_t = (doc_ids[None, :] == doc_ids[:, None]) & (blocks[:, None] <= blocks[None, :])
    pick = lambda s: jnp.where(s, shown_score, hidden_score).astype(f32)
    return pick(seen), pick(seen_t)


def attention_forward(queries, key_value, limits, heads):
    total = queries.shape[0]
    tiles = total // TILE
    c = score_scale * log2_e

    def body(q_ref, kv_ref, lim_ref, o_ref, lse_ref, top_ref):
        tile, head = pl.program_id(0), pl.program_id(1)
        k = kv_ref[:, :HD]
        v = kv_ref[:, HD:]
        s = lax.dot_general(
            q_ref[...], k, (((1,), (1,)), ((), ())), preferred_element_type=f32
        )
        s = jnp.minimum(s, lim_ref[...])
        m = jnp.max(s, axis=1, keepdims=True)
        p = jnp.exp2((s - m) * c)
        l = jnp.sum(p, axis=1, keepdims=True)
        o = jnp.dot(p.astype(bf16), v, preferred_element_type=f32)
        o_ref[...] = (o / l).astype(bf16)
        lane = lax.broadcasted_iota(jnp.int32, (TILE, LANES), 1)
        lse = m * c + jnp.log2(l)
        lse_ref[...] = jnp.where(lane == head, lse, lse_ref[...])

        @pl.when((tile == 0) & (head == 0))
        def _():
            top_ref[...] = jnp.full_like(top_ref, hidden_score)

        row = lax.broadcasted_iota(jnp.int32, (heads, LANES), 0)
        best = jnp.max(m, axis=0, keepdims=True) * score_scale
        top_ref[...] = jnp.where(row == head, jnp.maximum(top_ref[...], best), top_ref[...])

    return call(
        body,
        [shape((total, heads * HD), bf16), shape((total, LANES), f32), shape((heads, LANES), f32)],
        (tiles, heads),
        [
            pl.BlockSpec((TILE, HD), lambda i, h: (i, h)),
            pl.BlockSpec((total, 2 * HD), lambda i, h: (0, 0)),
            pl.BlockSpec((TILE, total), lambda i, h: (i, 0)),
        ],
        [
            pl.BlockSpec((TILE, HD), lambda i, h: (i, h)),
            pl.BlockSpec((TILE, LANES), lambda i, h: (i, 0)),
            pl.BlockSpec((heads, LANES), lambda i, h: (0, 0)),
        ],
        [queries, key_value, limits],
        flops=8 * total * total * HD * heads,
        name="attention_forward",
    )


def attention_backward(queries, grad_att, key_value, limits_t, lse_t, dot_t, heads):
    total = queries.shape[0]
    tiles = total // TILE
    c = score_scale * log2_e

    def body(q_ref, da_ref, kv_ref, lim_ref, lse_ref, dot_ref, dq_ref, dkv_ref):
        tile, head = pl.program_id(0), pl.program_id(1)
        k = kv_ref[:, :HD]
        v = kv_ref[:, HD:]
        q = q_ref[...]
        da = da_ref[...]
        nt = (((1,), (1,)), ((), ()))
        s = lax.dot_general(k, q, nt, preferred_element_type=f32)
        s = jnp.minimum(s, lim_ref[...])
        p = jnp.exp2(s * c - lse_ref[pl.ds(head, 1), :])
        dp = lax.dot_general(v, da, nt, preferred_element_type=f32)
        ds = (p * (dp - dot_ref[pl.ds(head, 1), :])).astype(bf16)
        dq = lax.dot_general(ds, k, (((0,), (0,)), ((), ())), preferred_element_type=f32)
        dq_ref[...] = (dq * score_scale).astype(bf16)

        @pl.when((tile == 0) & (head == 0))
        def _():
            dkv_ref[...] = jnp.zeros_like(dkv_ref)

        dkv_ref[:, :HD] += jnp.dot(ds, q, preferred_element_type=f32) * score_scale
        dkv_ref[:, HD:] += jnp.dot(p.astype(bf16), da, preferred_element_type=f32)

    return call(
        body,
        [shape((total, heads * HD), bf16), shape((total, 2 * HD), f32)],
        (tiles, heads),
        [
            pl.BlockSpec((TILE, HD), lambda i, h: (i, h)),
            pl.BlockSpec((TILE, HD), lambda i, h: (i, h)),
            pl.BlockSpec((total, 2 * HD), lambda i, h: (0, 0)),
            pl.BlockSpec((total, TILE), lambda i, h: (0, i)),
            pl.BlockSpec((heads, TILE), lambda i, h: (0, i)),
            pl.BlockSpec((heads, TILE), lambda i, h: (0, i)),
        ],
        [
            pl.BlockSpec((TILE, HD), lambda i, h: (i, h)),
            pl.BlockSpec((total, 2 * HD), lambda i, h: (0, 0)),
        ],
        [queries, grad_att, key_value, limits_t, lse_t, dot_t],
        flops=20 * total * total * HD * heads,
        name="attention_backward",
    )


def adam_values(gradient, weight, one, two, rate, decay):
    new_one = beta_one * one + (1.0 - beta_one) * gradient
    new_two = beta_two * two + (1.0 - beta_two) * gradient * gradient
    direction = (new_one * correct_one) / (jnp.sqrt(new_two * correct_two) + adam_eps)
    return new_one, new_two, weight - rate * (direction + decay * weight)


def to_tiles(flat, tiles_ref):
    for j in range(8):
        tiles_ref[:, j, :] = flat[:, j * LANES : (j + 1) * LANES]


def adam_in(gradient, weight, one, two, outer, start, full):
    rows, cols = gradient.shape
    step = 64
    base = (start // 1024).reshape(1)
    tall = pl.BlockSpec((step, 8, LANES), lambda i, j, b: (i, b[0] + j, 0))
    flat = pl.BlockSpec((step, 1024), lambda i, j, b: (i, j))
    args = [gradient, weight, one, two, outer]
    specs = [flat] + [tall] * 4
    aliases = {}
    if full is not None:
        aliases = {5: 0, 6: 1}
        args += list(full)
        specs += [pl.BlockSpec(memory_space=pl.ANY)] * 2

    def body(_, g_ref, w_ref, one_ref, two_ref, out_ref, *rest):
        one_out, two_out, delta_out, grad_tiles, delta_tiles = rest[-5:]
        to_tiles(g_ref[...].astype(f32), grad_tiles)
        new_one, new_two, stepped = adam_values(
            grad_tiles[...], w_ref[...], one_ref[...], two_ref[...], rate_matrix, weight_decay
        )
        one_out[...] = new_one
        two_out[...] = new_two
        delta_tiles[...] = out_ref[...] - stepped
        for j in range(8):
            delta_out[:, j * LANES : (j + 1) * LANES] = delta_tiles[:, j, :].astype(bf16)

    whole = shape(weight.shape, f32)
    return call(
        body,
        [whole, whole, shape((rows, cols), bf16)],
        (rows // step, cols // 1024),
        specs,
        [tall, tall, flat],
        args,
        ids=[base],
        scratch=[pltpu.VMEM((step, 8, LANES), f32)] * 2,
        aliases=aliases,
        name="adam_in",
        vmem=VMEM_MOST,
    )


def adam_out(gradient, weight, one, two, outer, start, full):
    rows, cols = gradient.shape
    step = 512
    base = (start // step).reshape(1)
    tall = pl.BlockSpec((step, cols), lambda i, b: (b[0] + i, 0))
    flat = pl.BlockSpec((step, cols), lambda i, b: (i, 0))
    args = [gradient, weight, one, two, outer]
    specs = [flat] + [tall] * 4
    aliases = {}
    if full is not None:
        aliases = {5: 0, 6: 1}
        args += list(full)
        specs += [pl.BlockSpec(memory_space=pl.ANY)] * 2

    def body(_, g_ref, w_ref, one_ref, two_ref, out_ref, *rest):
        one_out, two_out, delta_out = rest[-3:]
        new_one, new_two, stepped = adam_values(
            g_ref[...].astype(f32), w_ref[...], one_ref[...], two_ref[...], rate_matrix,
            weight_decay,
        )
        one_out[...] = new_one
        two_out[...] = new_two
        delta_out[...] = (out_ref[...] - stepped).astype(bf16)

    whole = shape(weight.shape, f32)
    return call(
        body,
        [whole, whole, shape((rows, cols), bf16)],
        (rows // step,),
        specs,
        [tall, tall, flat],
        args,
        ids=[base],
        aliases=aliases,
        name="adam_out",
        vmem=VMEM_MOST,
    )


def outer_values(mean, momentum, outer):
    velocity = outer_beta * momentum + mean
    return velocity, outer - outer_rate * (mean + outer_beta * velocity)


def outer_in(both, momentum, outer, factor, start, full):
    _, rows, cols = both.shape
    step = 64
    base = (start // 1024).reshape(1)
    tall = pl.BlockSpec((step, 8, LANES), lambda i, j, b: (i, b[0] + j, 0))
    flat = pl.BlockSpec((2, step, 1024), lambda i, j, b: (0, i, j))
    wide = pl.BlockSpec((step, 1024), lambda i, j, b: (i, b[0] + j))
    args = [both, momentum, outer]
    specs = [flat, tall, tall]
    if factor is not None:
        args.append(factor)
        specs.append(pl.BlockSpec((8, LANES), lambda i, j, b: (0, 0)))
    aliases = {}
    if full is not None:
        aliases = {len(args) + k: k for k in range(4)}
        args += list(full)
        specs += [pl.BlockSpec(memory_space=pl.ANY)] * 4

    def body(_, both_ref, mom_ref, out_ref, *rest):
        mean_out, vel_out, new_out, copy_out, mean_tiles, new_tiles = rest[-6:]
        to_tiles((both_ref[0].astype(f32) + both_ref[1].astype(f32)) * 0.5, mean_tiles)
        mean = mean_tiles[...]
        velocity, fresh = outer_values(mean, mom_ref[...], out_ref[...])
        if factor is not None:
            fresh = fresh * rest[0][...][None]
        mean_out[...] = mean
        vel_out[...] = velocity
        new_out[...] = fresh
        new_tiles[...] = fresh
        for j in range(8):
            copy_out[:, j * LANES : (j + 1) * LANES] = new_tiles[:, j, :].astype(bf16)

    whole = shape(outer.shape, f32)
    return call(
        body,
        [whole, whole, whole, shape((rows, outer.shape[1] * LANES), bf16)],
        (rows // step, cols // 1024),
        specs,
        [tall, tall, tall, wide],
        args,
        ids=[base],
        scratch=[pltpu.VMEM((step, 8, LANES), f32)] * 2,
        aliases=aliases,
        name="outer_in",
        vmem=VMEM_MOST,
    )


def outer_out(both, momentum, outer, start, full):
    _, rows, cols = both.shape
    step = 512
    base = (start // step).reshape(1)
    tall = pl.BlockSpec((step, cols), lambda i, b: (b[0] + i, 0))
    flat = pl.BlockSpec((2, step, cols), lambda i, b: (0, i, 0))
    args = [both, momentum, outer]
    specs = [flat, tall, tall]
    aliases = {}
    if full is not None:
        aliases = {3 + k: k for k in range(4)}
        args += list(full)
        specs += [pl.BlockSpec(memory_space=pl.ANY)] * 4

    def body(_, both_ref, mom_ref, out_ref, *rest):
        mean_out, vel_out, new_out, copy_out = rest[-4:]
        mean = (both_ref[0].astype(f32) + both_ref[1].astype(f32)) * 0.5
        velocity, fresh = outer_values(mean, mom_ref[...], out_ref[...])
        mean_out[...] = mean
        vel_out[...] = velocity
        new_out[...] = fresh
        copy_out[...] = fresh.astype(bf16)

    whole = shape(outer.shape, f32)
    return call(
        body,
        [whole, whole, whole, shape(outer.shape, bf16)],
        (rows // step,),
        specs,
        [tall] * 4,
        args,
        ids=[base],
        aliases=aliases,
        name="outer_out",
        vmem=VMEM_MOST,
    )


class Wire:
    def __init__(self, window):
        self.window, self.landed = window, []

    def send(self, block, axis, pairs):
        if len(self.landed) >= self.window:
            block, _ = lax.optimization_barrier((block, self.landed[-self.window]))
        arrived = lax.ppermute(block, axis, pairs)
        self.landed.append(arrived)
        return arrived


class Links:
    def __init__(self, count, splits, window):
        self.levels = count.bit_length() - 1
        self.far = ([1] + [1 << b for b in range(3, self.levels)])[: self.levels - 2]
        places = range(count)
        middle = [i for i in places if (i >> 1 ^ i >> 2) & 1]
        outer = [i for i in places if i not in middle]
        self.pair = [(i, i ^ 2) for i in places]
        self.inward = [(i, i ^ 2) for i in outer]
        self.outward = [(i, i ^ 2) for i in middle]
        self.between = [(i, i ^ 6) for i in middle]
        self.beside = [[(i, i ^ mask) for i in places] for mask in self.far]
        self.mirror = [(i, i ^ 6) for i in places]
        self.cores = [(i, (i + 1) % splits) for i in range(splits)]
        self.wire = Wire(window)

    def flips(self, across):
        masks = [2, across] + self.far
        table = []
        for o in range(1 << self.levels):
            flip = 0
            for level, mask in enumerate(masks):
                if o >> level & 1:
                    flip ^= mask
            table.append(flip)
        return table

    def to_side(self, block, pairs):
        return self.wire.send(block, "dp", pairs)

    def to_middle(self, block):
        return self.wire.send(block, "dp", self.between)

    def to_far(self, block, level):
        return self.wire.send(block, "dp", self.beside[level - 2])

    def to_pair(self, block):
        return self.wire.send(block, "dp", self.pair)

    def across(self, block):
        return lax.ppermute(block, "tensor", self.cores)

    def pair_now(self, block):
        return lax.ppermute(block, "dp", self.pair)


def after(value, *earlier):
    return lax.optimization_barrier((value, *earlier))[0]


class Gathered:
    def __init__(self, links, axis, mine, other=None):
        self.links, self.axis, self.mine, self.other = links, axis, mine, other
        self.held = {}

    def join(self, *blocks):
        return jnp.concatenate(blocks, axis=self.axis)

    def near(self):
        give = self.mine if self.other is None else self.other
        self.held[0] = self.join(self.mine, self.links.to_side(give, self.links.pair))

    def inward(self):
        if self.other is not None:
            self.passed = self.links.to_side(self.mine, self.links.inward)

    def middle(self):
        if self.other is None:
            self.relay = self.direct = self.links.to_middle(self.held[0])
        else:
            self.relay = self.links.to_middle(self.join(self.other, self.passed))

    def middle_rest(self):
        self.direct = self.links.to_middle(self.held[0])

    def outward(self):
        self.relayed = self.links.to_side(self.relay, self.links.outward)

    def join_far(self):
        self.held[2] = self.direct + self.relayed

    def far(self, level, o):
        self.held[o + (1 << level)] = self.links.to_far(self.held[o], level)

    def whole(self):
        for level in range(2, self.links.levels):
            for o in range(0, 1 << level, 2):
                if o + (1 << level) not in self.held:
                    self.far(level, o)
        return self.join(*[self.held[o] for o in sorted(self.held)])


class Reduced:
    def __init__(self, links, axis, size, halved, part):
        self.links, self.axis, self.size, self.halved, self.part = links, axis, size, halved, part
        self.landed = {}

    def pair_sum(self, o):
        total = self.part(o, 2)
        for block in self.landed.pop(o, []):
            total = total + block.astype(f32)
        return total.astype(bf16)

    def one(self, block, o):
        return lax.slice_in_dim(
            block, o * self.size, (o + 1) * self.size, axis=self.axis
        ).astype(f32)

    def far(self):
        sent = []
        for level in range(self.links.levels - 1, 1, -1):
            for o in reversed(range(1 << level, 2 << level, 2)):
                sent.append(self.pair_sum(o))
                arrived = self.links.to_far(sent[-1], level)
                self.landed.setdefault(o - (1 << level), []).append(arrived)
        return sent

    def inward(self):
        self.ahead = self.pair_sum(2)
        self.passed = self.links.to_side(self.ahead, self.links.inward)
        return self.ahead

    def middle(self):
        self.direct = self.links.to_middle(
            self.ahead if self.halved else self.ahead + self.passed
        )

    def middle_rest(self):
        self.relay = self.links.to_middle(self.passed)

    def single(self, o):
        total = self.part(o, 1)
        for block in self.landed[0] + [self.direct]:
            total = total + self.one(block, o)
        return total

    def near(self):
        value = self.single(1).astype(bf16)
        self.theirs = self.links.to_side(value, self.links.pair).astype(f32)
        return value

    def outward(self):
        value = self.one(self.relay, 1).astype(bf16)
        self.last = self.links.to_side(value, self.links.outward).astype(f32)

    def result(self):
        if not self.halved:
            return self.single(0) + self.theirs, None
        return self.single(0) + self.last, self.theirs + self.one(self.relay, 0)


def local(
    tokens,
    doc_lengths,
    cotangent,
    inner_in,
    inner_out,
    inner_shared,
    first_in,
    first_out,
    first_shared,
    second_in,
    second_out,
    second_shared,
    outer_in_w,
    outer_out_w,
    outer_shared,
    momentum_in,
    momentum_out,
    momentum_shared,
):
    splits = lax.axis_size("tensor")
    count = lax.axis_size("dp")
    split = lax.axis_index("tensor")
    place = lax.axis_index("dp")
    total, width = tokens.shape
    part = width // count
    local_cols = inner_in.shape[3]
    shared_cols = inner_shared.shape[2]
    heads = HEADS // splits
    qcols = heads * HD
    hidden = local_cols - qcols
    vec = 2 * HD
    own_cols = part // splits
    mine = total // 2

    links = Links(count, splits, 4)
    across = links.across
    levels = links.levels
    side = ((place >> 1) ^ (place >> 2)) & 1
    from_outer, from_middle = (jnp.array(links.flips(m), jnp.int32) for m in (4, 6))
    ids = (place ^ jnp.where(side == 0, from_outer, from_middle)).astype(jnp.int32)
    swap_group = [(0, 1), (1, 0)]
    split_id = split.astype(jnp.int32).reshape(1)

    def tall(array):
        return array.reshape(part, local_cols // LANES, LANES)

    w_in = tall(inner_in)
    w_out = inner_out.reshape(local_cols, part)
    shared_rows = lax.all_gather(inner_shared[0], ("dp", "tensor"), axis=0, tiled=True)

    half = hidden // 2
    flat_in = inner_in.reshape(part, local_cols)

    def sides(low, high):
        return (
            jnp.where(side == 0, low, high).astype(bf16),
            jnp.where(side == 0, high, low).astype(bf16),
        )

    block_q = flat_in[:, :qcols].astype(bf16)
    block_o = w_out[:qcols].astype(bf16)
    up_sides = sides(flat_in[:, qcols : qcols + half], flat_in[:, qcols + half :])
    down_sides = sides(w_out[qcols : qcols + half], w_out[qcols + half :])
    got_query = Gathered(links, 0, block_q)
    got_attn = Gathered(links, 1, block_o)
    got_up = Gathered(links, 0, *up_sides)
    got_down = Gathered(links, 1, *down_sides)
    shared_t = shared_rows.T
    shared_rel = pick_blocks(shared_t, ids, part, count, False)
    w_keyval_t = shared_rel[:vec].astype(bf16)
    vectors_t, vectors = shared_t[vec:], shared_rel[vec:]
    gain_one, bias_one, gain_two, bias_two = (vectors[k : k + 1] for k in range(4))
    bias_out, bias_down = vectors[5:6], vectors[6:7]
    bias_query = lax.dynamic_slice_in_dim(vectors_t[4], split * qcols, qcols)
    bias_up = lax.dynamic_slice_in_dim(
        vectors_t[7:].reshape(FF), split * hidden + side * half, half
    )

    nt = (((1,), (1,)), ((), ()))
    tn = (((0,), (0,)), ((), ()))

    def mm(a, b, dims=(((1,), (0,)), ((), ()))):
        return lax.dot_general(a, b, dims, preferred_element_type=f32)

    def block(array, o, blocks):
        return array[:, o * part : (o + blocks) * part]

    def both_rows(rows):
        return lax.all_gather(rows, "tensor", axis=0, tiled=True)

    def far(weight, o):
        if levels == 3:
            weight.far(2, o)

    cot_own, cot_pair, grad_bias_down = cotangent_order(cotangent, ids, split_id, count)
    got_query.near()
    got_attn.near()
    got_query.middle()
    far(got_query, 0)
    got_down.near()
    got_down.inward()
    got_attn.middle()
    far(got_attn, 0)
    got_query.outward()
    got_query.join_far()
    far(got_query, 2)
    got_attn.outward()
    got_attn.join_far()
    got_down.middle()
    got_up.near()
    far(got_attn, 2)
    w_query = got_query.whole()
    w_attn = got_attn.whole()
    got_up.inward()
    far(got_down, 0)
    cot_theirs = links.to_pair(swap_small(cot_pair, part))
    got_down.outward()
    got_down.middle_rest()
    got_down.join_far()
    far(got_up, 0)
    got_up.middle()
    far(got_down, 2)
    w_down = got_down.whole()
    got_up.outward()
    got_up.middle_rest()
    got_up.join_far()

    x_rel, normed = first_norm(tokens, ids, split_id, gain_one, bias_one, count)
    limits, limits_t = score_limits(doc_lengths[0], total, split * mine)
    key_value = mm(normed, w_keyval_t, nt).astype(bf16)
    queries = (mm(normed, w_query) + bias_query).astype(bf16)
    attended, log_totals, tops = attention_forward(queries, key_value, limits, heads)
    attn_give = mm(attended[mine:], w_attn).astype(bf16)
    attn_keep = mm(attended[:mine], w_attn).astype(bf16)
    attn_other = across(attn_give)
    middle, normed_two, normed_pair = middle_norm(
        x_rel, attn_keep, attn_other, bias_out, gain_two, bias_two, part
    )
    normed_theirs = links.to_pair(swap_small(normed_pair, part))
    far(got_up, 2)
    w_up = got_up.whole()
    normed_all = both_rows(jnp.concatenate([normed_two, normed_theirs], axis=0))
    cot_all = both_rows(jnp.concatenate([cot_own, cot_theirs], axis=0))
    hidden_grad = mm(cot_all, w_down, nt).astype(bf16)
    acts, grad_pre, grad_bias_up = hidden_units(normed_all, w_up, bias_up[None], hidden_grad)

    links.wire.window = 1 << 30
    sum_down = Reduced(
        links, 1, part, True, lambda o, b: mm(acts, block(cot_all, o, b), tn)
    )
    sum_up = Reduced(
        links, 0, part, True, lambda o, b: mm(block(normed_all, o, b), grad_pre, tn)
    )
    sent_down = sum_down.far()
    w_up_late = after(w_up, *sent_down)
    pre_give = lax.dynamic_slice_in_dim(grad_pre, (1 - split) * 2 * mine, 2 * mine)
    pre_keep = lax.dynamic_slice_in_dim(grad_pre, split * 2 * mine, 2 * mine)
    two_give = mm(pre_give, w_up_late, nt).astype(bf16)
    two_other = across(two_give)
    two_keep = mm(pre_keep, after(w_up_late, two_give), nt).astype(bf16)
    two_theirs = two_keep[mine:].astype(f32) + two_other[mine:].astype(f32)
    two_pair = links.pair_now(swap_small(two_theirs.astype(bf16), part))
    sent_up = sum_up.far()
    sum_down.inward()
    sum_down.middle()
    dh, dh_mine, grad_gain_two, grad_bias_two, grad_bias_out = middle_backward(
        middle, two_keep, two_other, two_pair, cot_own, gain_two, part
    )
    dh_low = jnp.concatenate([dh_mine, across(dh_mine)], axis=0)

    grad_att = mm(dh_low, after(w_attn, *sent_up), nt).astype(bf16)
    dots = jnp.sum(
        (grad_att.astype(f32) * attended.astype(f32)).reshape(total, heads, HD), axis=2
    )
    grad_queries, kv_part = attention_backward(
        queries, grad_att, key_value, limits_t, log_totals.T[:heads], dots.T, heads
    )
    sum_down.middle_rest()
    sum_down.near()
    sum_down.outward()
    sum_attn = Reduced(
        links, 1, part, False, lambda o, b: mm(attended, block(dh_low, o, b), tn)
    )
    sent_attn = sum_attn.far()
    one_give = mm(grad_queries[mine:], w_query, nt).astype(bf16)
    one_other = across(one_give)
    one_keep = mm(grad_queries[:mine], w_query, nt).astype(bf16)
    kv_low = (kv_part[:mine] + across(kv_part[mine:])).astype(bf16)
    grad_keyval_t = mm(kv_low, normed[:mine], tn)
    sum_up.inward()
    sum_up.middle()
    sum_query = Reduced(
        links, 0, part, False, lambda o, b: mm(block(normed, o, b), grad_queries, tn)
    )
    sum_query.far()
    sum_up.middle_rest()
    grad_mine, grad_gain_one, grad_bias_one = first_backward(
        x_rel, one_keep, one_other, kv_low, w_keyval_t, dh, gain_one, ids, count
    )
    tokens_grad = both_rows(grad_mine)

    down_part = mm(after(acts, *sent_attn), w_down).astype(bf16)
    down_sum = lax.psum_scatter(down_part, "tensor", scatter_dimension=0, tiled=True)

    peers = across(after(tops, *sent_up))
    peak = jnp.where(
        split == 0, jnp.concatenate([tops, peers]), jnp.concatenate([peers, tops])
    )
    peak = jnp.maximum(peak, lax.ppermute(peak, "group", swap_group))
    for pairs in [links.pair, links.mirror] + links.beside:
        peak = jnp.maximum(peak, lax.ppermute(peak, "dp", pairs))
    clip_rows = clip_limit / jnp.maximum(peak, clip_limit)

    sum_up.near()
    sum_up.outward()
    sum_attn.inward()
    sum_attn.middle()
    sum_query.inward()
    down_pair = links.to_pair(swap_small(down_sum[mine:], part))
    block_out = both_rows(
        block_result(middle, down_sum, down_pair, bias_down, ids, count)
    )

    grad_bias_query = jnp.sum(grad_queries.astype(f32), axis=0)
    spread = jnp.concatenate(
        [
            lax.dynamic_update_slice_in_dim(
                jnp.zeros((width,), f32), grad_bias_query, split * qcols, 0
            ),
            lax.dynamic_update_slice_in_dim(
                jnp.zeros((FF,), f32), grad_bias_up[0], split * hidden + side * half, 0
            ),
        ]
    ).reshape(1 + FF // width, width)
    near = jnp.concatenate(
        [grad_keyval_t, grad_gain_one, grad_bias_one, grad_gain_two, grad_bias_two, grad_bias_out,
         grad_bias_down],
        axis=0,
    )
    steps = jnp.arange(count, dtype=jnp.int32)
    turned = jnp.where((side == 0) & ((steps & 2) != 0), steps ^ 1, steps)
    mirrored = (place ^ from_middle).astype(jnp.int32)

    def pieces(core):
        a = pick_blocks(near, turned * splits + core, own_cols, count, True)
        b = pick_blocks(spread, mirrored * splits + core, own_cols, count, True)
        return jnp.concatenate([a[:, : vec + 4], b[:, :1], a[:, vec + 4 :], b[:, 1:]], axis=1)

    red_shared = pieces(split) + across(pieces(1 - split))
    sum_query.middle()
    sum_attn.near()
    for pairs in reversed([links.pair, links.mirror] + links.beside):
        keep = red_shared.shape[0] // 2
        red_shared = red_shared[:keep] + links.to_side(red_shared[keep:], pairs)
    red_shared = red_shared[0]
    sum_query.near()
    red_down, red_up = sum_down.result(), sum_up.result()
    red_attn, red_query = sum_attn.result()[0], sum_query.result()[0]

    one_in, two_in = tall(first_in), tall(second_in)
    one_out, two_out = (a.reshape(local_cols, part) for a in (first_out, second_out))
    base_in, mom_in = tall(outer_in_w), tall(momentum_in)
    base_out, mom_out = (a.reshape(local_cols, part) for a in (outer_out_w, momentum_out))
    clip_own = lax.dynamic_slice_in_dim(clip_rows, split * heads, heads)

    starts = [qcols + side * half, qcols + (1 - side) * half]
    zero = jnp.zeros((), jnp.int32)
    gathered = []

    def groups(delta):
        both = lax.all_gather(after(delta, *gathered[-1:]), "group", axis=0)
        gathered.append(both)
        return both

    full_in = full_out = new_in = new_out = None
    for s, gradient in zip(starts, red_down):
        *full_out, delta = adam_out(gradient, w_out, one_out, two_out, base_out, s, full_out)
        new_out = outer_out(groups(delta), mom_out, base_out, s, new_out)
    for s, gradient in zip(starts, red_up):
        *full_in, delta = adam_in(gradient, w_in, one_in, two_in, base_in, s, full_in)
        new_in = outer_in(groups(delta), mom_in, base_in, None, s, new_in)
    red_query = after(red_query, new_in[0], new_out[0])
    *full_out, delta = adam_out(red_attn, w_out, one_out, two_out, base_out, zero, full_out)
    new_out = outer_out(groups(delta), mom_out, base_out, zero, new_out)
    *full_in, delta = adam_in(red_query, w_in, one_in, two_in, base_in, zero, full_in)
    both = jnp.stack([delta, lax.ppermute(delta, "group", swap_group)])
    new_in = outer_in(both, mom_in, base_in, clip_own, zero, new_in)

    ids_col = jnp.arange(shared_cols, dtype=jnp.int32)[:, None]
    one_sh, two_sh, stepped = adam_values(
        red_shared,
        inner_shared[0].T,
        first_shared[0].T,
        second_shared[0].T,
        jnp.where(ids_col < vec, rate_matrix, rate_vector),
        jnp.where(ids_col < vec, weight_decay, 0.0),
    )
    base_sh = outer_shared.T
    delta = (base_sh - stepped).astype(bf16)
    mean_sh = (delta.astype(f32) + lax.ppermute(delta, "group", swap_group).astype(f32)) * 0.5
    vel_sh, fresh_sh = outer_values(mean_sh, momentum_shared.T, base_sh)
    row_ids = (place * splits + split) * own_cols + jnp.arange(own_cols, dtype=jnp.int32)
    clip_vec = clip_rows[:, 0]
    row_clip = jnp.sum(
        jnp.where((row_ids // HD)[None, :] == jnp.arange(HEADS)[:, None], clip_vec[:, None], 0.0),
        axis=0,
    )
    fresh_sh = fresh_sh * jnp.where(ids_col == vec + 4, row_clip[None, :], 1.0)

    shape_in, shape_out = (part, 1, local_cols), (1, local_cols, part)
    mean_in, vel_in, fresh_in, copy_in = new_in
    mean_out, vel_out, fresh_out, copy_out = new_out
    return (
        block_out,
        tokens_grad,
        clip_vec,
        full_in[0].reshape((1,) + shape_in),
        full_out[0].reshape((1,) + shape_out),
        one_sh.T[None],
        full_in[1].reshape((1,) + shape_in),
        full_out[1].reshape((1,) + shape_out),
        two_sh.T[None],
        mean_in.reshape(shape_in),
        mean_out.reshape(shape_out),
        mean_sh.T,
        vel_in.reshape(shape_in),
        vel_out.reshape(shape_out),
        vel_sh.T,
        fresh_in.reshape(shape_in),
        fresh_out.reshape(shape_out),
        fresh_sh.T,
        copy_in.reshape(shape_in),
        copy_out.reshape(shape_out),
        fresh_sh.T.astype(bf16),
    )


def solution(mesh):
    rows = P(("group", "dp"), None)
    inner = [P("group", "dp", "tensor", None), P("group", "tensor", None, "dp"),
             P("group", ("dp", "tensor"), None)]
    outer = [P("dp", "tensor", None), P("tensor", None, "dp"), P(("dp", "tensor"), None)]
    in_specs = tuple([rows] * 3 + inner * 3 + outer * 2)
    out_specs = tuple([rows] * 2 + [P()] + inner * 2 + outer * 4)
    return jax.shard_map(local, mesh=mesh, in_specs=in_specs, out_specs=out_specs, check_vma=False)
```

```python
import jax
import jax.numpy as jnp
from jax import lax
from jax.experimental import pallas as pl
from jax.experimental.pallas import tpu as pltpu
from jax.sharding import PartitionSpec as P

HEADS = 16
HD = 128
FF = 8192
BLOCK = 256
STEP = 10

norm_eps = 1e-05
hidden_score = -1e30
shown_score = 3e38
beta_one = 0.9
beta_two = 0.95
adam_eps = 1e-08
rate_matrix = 0.02
rate_vector = 0.2
weight_decay = 0.1
outer_beta = 0.9
outer_rate = 0.7
clip_limit = 5.0
score_scale = HD ** (-0.5)
log2_e = 1.4426950408889634
correct_one = 1.0 / (1.0 - beta_one**STEP)
correct_two = 1.0 / (1.0 - beta_two**STEP)

f32 = jnp.float32
bf16 = jnp.bfloat16
ROWS = 128
LANES = 128
VMEM_LIMIT = 40 * 1024 * 1024
VMEM_MOST = 58 * 1024 * 1024


def shape(dims, dtype):
    return jax.ShapeDtypeStruct(dims, dtype)


def call(body, out_shape, grid, in_specs, out_specs, args, *, ids=(), scratch=(), aliases=None,
         flops=0, name=None, vmem=VMEM_LIMIT):
    outs = out_shape if isinstance(out_shape, (list, tuple)) else [out_shape]
    moved = sum(a.size * a.dtype.itemsize for a in args)
    moved += sum(o.size * o.dtype.itemsize for o in outs)
    return pl.pallas_call(
        body,
        out_shape=out_shape,
        grid_spec=pltpu.PrefetchScalarGridSpec(
            num_scalar_prefetch=len(ids),
            grid=grid,
            in_specs=in_specs,
            out_specs=out_specs,
            scratch_shapes=list(scratch),
        ),
        input_output_aliases={len(ids) + k: v for k, v in (aliases or {}).items()},
        compiler_params=pltpu.CompilerParams(vmem_limit_bytes=vmem),
        cost_estimate=pl.CostEstimate(flops=flops, bytes_accessed=moved, transcendentals=0),
        name=name,
    )(*ids, *args)


def pick_blocks(array, block_ids, width, count, stacked):
    rows = array.shape[0]
    if width % LANES:
        taken = jnp.take(array.reshape(rows, -1, width), block_ids, axis=1)
        return taken.transpose(1, 0, 2) if stacked else taken.reshape(rows, count * width)

    def body(ids_ref, in_ref, out_ref):
        if stacked:
            out_ref[0] = in_ref[...]
        else:
            out_ref[...] = in_ref[...]

    if stacked:
        out, spec = shape((count, rows, width), array.dtype), pl.BlockSpec(
            (1, rows, width), lambda j, ids: (j, 0, 0)
        )
    else:
        out, spec = shape((rows, count * width), array.dtype), pl.BlockSpec(
            (rows, width), lambda j, ids: (0, j)
        )
    return call(
        body, out, (count,), [pl.BlockSpec((rows, width), lambda j, ids: (0, ids[j]))], spec,
        [array], ids=[block_ids], name="pick_blocks",
    )


def columns_of(block_id, width):
    return pl.ds(pl.multiple_of(block_id * width, width), width)


def placing(array, ids, count):
    part = array.shape[1] // count
    if part % LANES == 0:
        return array, count, part
    return pick_blocks(array, ids, part, count, False), 0, part


def put_back(array, ids, count):
    part = array.shape[1] // count
    if part % LANES == 0:
        return array
    back = jnp.sum(
        jnp.where(ids[None, :] == jnp.arange(count)[:, None], jnp.arange(count)[None, :], 0), axis=1
    ).astype(jnp.int32)
    return pick_blocks(array, back, part, count, False)


def norm_stats(rows):
    mean = jnp.mean(rows, axis=-1, keepdims=True)
    centered = rows - mean
    inv = lax.rsqrt(jnp.mean(centered * centered, axis=-1, keepdims=True) + norm_eps)
    return centered * inv, inv


def row_spec(cols, rows=ROWS):
    return pl.BlockSpec((rows, cols), lambda i, *ids: (i, 0))


def turned_spec(cols, blocks):
    return pl.BlockSpec(
        (ROWS, cols), lambda i, ids, split: ((i + split[0] * (blocks // 2)) % blocks, 0)
    )


def whole_spec(rows, cols):
    return pl.BlockSpec((rows, cols), lambda i, *ids: (0, 0))


def first_norm(tokens, ids, split, gain, bias, count):
    total, width = tokens.shape
    tokens, moved, part = placing(tokens, ids, count)

    def body(ids_ref, split_ref, x_ref, g_ref, c_ref, x_out, n_out):
        for o in range(moved):
            x_out[:, o * part : (o + 1) * part] = x_ref[:, columns_of(ids_ref[o], part)]
        if not moved:
            x_out[...] = x_ref[...]
        unit, _ = norm_stats(x_out[...].astype(f32))
        n_out[...] = (unit * g_ref[...] + c_ref[...]).astype(bf16)

    return call(
        body,
        [shape((total, width), bf16)] * 2,
        (total // ROWS,),
        [turned_spec(width, total // ROWS), whole_spec(1, width), whole_spec(1, width)],
        [row_spec(width)] * 2,
        [tokens, gain, bias],
        ids=[ids, split],
        name="first_norm",
    )


def first_spec(cols, blocks):
    return pl.BlockSpec((ROWS, cols), lambda i, *ids: (jnp.minimum(i, blocks - 1), 0))


def swapped(values, part):
    if part % LANES:
        return values
    blocks = [values[:, o : o + part] for o in range(0, values.shape[1], part)]
    return jnp.concatenate([blocks[pair_of(o)] for o in range(len(blocks))], axis=1)


def pair_of(o):
    return o if o & 2 else o ^ 1


def swap_small(values, part):
    if part % LANES == 0:
        return values
    blocks = [values[:, o : o + part] for o in range(0, values.shape[1], part)]
    return jnp.concatenate([blocks[pair_of(o)] for o in range(len(blocks))], axis=1)


def cotangent_order(cotangent, ids, split, count):
    total, width = cotangent.shape
    cotangent, moved, part = placing(cotangent, ids, count)
    mine = total // ROWS // 2

    def body(ids_ref, split_ref, c_ref, c_out, pair_out, sum_out):
        for o in range(moved):
            c_out[:, o * part : (o + 1) * part] = c_ref[:, columns_of(ids_ref[o], part)]
        if not moved:
            c_out[...] = c_ref[...]
        pair_out[...] = swapped(c_out[...], part)
        add_rows(sum_out, c_out[...].astype(f32))

    return call(
        body,
        [shape((total // 2, width), bf16)] * 2 + [shape((1, width), f32)],
        (mine,),
        [turned_spec(width, total // ROWS)],
        [row_spec(width)] * 2 + [whole_spec(1, width)],
        [cotangent],
        ids=[ids, split],
        name="cotangent_order",
    )


def hidden_units(rows, weight, bias, hidden_grad):
    total, depth = rows.shape
    cols = weight.shape[1]
    high, wide, sub = 256, 1024, 256
    curve, cube = (2.0 / 3.141592653589793) ** 0.5, 0.044715

    def body(n_ref, w_ref, b_ref, dz_ref, z_out, du_out, sum_out):
        first = pl.program_id(1) == 0
        for c in range(0, wide, sub):
            at = slice(c, c + sub)
            u = jnp.dot(n_ref[...], w_ref[:, at], preferred_element_type=f32) + b_ref[:, at]
            square = u * u
            t = jnp.tanh(curve * u * (1.0 + cube * square))
            z_out[:, at] = (0.5 * u * (1.0 + t)).astype(bf16)
            slope = 0.5 * (1.0 + t) + (0.5 * curve) * u * (1.0 - t * t) * (
                1.0 + (3.0 * cube) * square
            )
            du = (slope * dz_ref[:, at].astype(f32)).astype(bf16)
            du_out[:, at] = du
            total_du = jnp.sum(du.astype(f32), axis=0, keepdims=True)
            sum_out[:, at] = jnp.where(first, total_du, sum_out[:, at] + total_du)

    tile = pl.BlockSpec((high, wide), lambda j, i: (i, j))
    line = pl.BlockSpec((1, wide), lambda j, i: (0, j))
    return call(
        body,
        [shape((total, cols), bf16)] * 2 + [shape((1, cols), f32)],
        (cols // wide, total // high),
        [
            pl.BlockSpec((high, depth), lambda j, i: (i, 0)),
            pl.BlockSpec((depth, wide), lambda j, i: (0, j)),
            line,
            tile,
        ],
        [tile, tile, line],
        [rows, weight, bias, hidden_grad],
        flops=2 * total * depth * cols,
        name="hidden_units",
    )


def add_rows(sum_ref, values):
    @pl.when(pl.program_id(0) == 0)
    def _():
        sum_ref[...] = jnp.zeros_like(sum_ref)

    sum_ref[...] += jnp.sum(values, axis=0, keepdims=True)


def middle_norm(x_rel, part_own, part_other, bias_out, gain, bias, part):
    total, width = part_other.shape

    def body(x_ref, a_ref, b_ref, bo_ref, g_ref, c_ref, h_out, n_out, pair_out):
        mid = x_ref[...].astype(f32) + (
            a_ref[...].astype(f32) + b_ref[...].astype(f32)
        ) + bo_ref[...]
        h_out[...] = mid
        unit, _ = norm_stats(mid)
        low = (unit * g_ref[...] + c_ref[...]).astype(bf16)
        n_out[...] = low
        pair_out[...] = swapped(low, part)

    return call(
        body,
        [shape((total, width), f32)] + [shape((total, width), bf16)] * 2,
        (total // ROWS,),
        [row_spec(width)] * 3 + [whole_spec(1, width)] * 3,
        [row_spec(width)] * 3,
        [x_rel, part_own, part_other, bias_out, gain, bias],
        name="middle_norm",
    )


def block_result(middle, part_own, part_pair, bias_down, ids, count):
    total, width = middle.shape
    part = width // count

    def body(ids_ref, h_ref, a_ref, p_ref, b2_ref, out_ref):
        value = a_ref[...].astype(f32) + swapped(p_ref[...], part).astype(f32)
        value = (h_ref[...] + value + b2_ref[...]).astype(bf16)
        if part % LANES:
            out_ref[...] = value
        else:
            for o in range(count):
                out_ref[:, columns_of(ids_ref[o], part)] = value[:, o * part : (o + 1) * part]

    result = call(
        body,
        shape((total, width), bf16),
        (total // ROWS,),
        [row_spec(width)] * 3 + [whole_spec(1, width)],
        row_spec(width),
        [middle, part_own, part_pair, bias_down],
        ids=[ids],
        name="block_result",
    )
    return put_back(result, ids, count)


def middle_backward(middle, part_own, part_other, part_pair, cot_rel, gain, part):
    total, width = middle.shape

    def body(h_ref, a_ref, b_ref, p_ref, dy_ref, g_ref, dh_out, low_out, gg_out, gc_out, gbo_out):
        unit, inv = norm_stats(h_ref[...])
        grad = a_ref[...].astype(f32) + b_ref[...].astype(f32)
        grad = grad + swapped(p_ref[...], part).astype(f32)
        scaled = grad * g_ref[...]
        dh = dy_ref[...].astype(f32) + inv * (
            scaled
            - jnp.mean(scaled, axis=-1, keepdims=True)
            - unit * jnp.mean(scaled * unit, axis=-1, keepdims=True)
        )
        dh_out[...] = dh
        low = dh.astype(bf16)
        low_out[...] = low
        add_rows(gg_out, grad * unit)
        add_rows(gc_out, grad)
        add_rows(gbo_out, low.astype(f32))

    vec = shape((1, width), f32)
    return call(
        body,
        [shape((total, width), f32), shape((total, width), bf16), vec, vec, vec],
        (total // ROWS,),
        [row_spec(width)] * 5 + [whole_spec(1, width)],
        [row_spec(width)] * 2 + [whole_spec(1, width)] * 3,
        [middle, part_own, part_other, part_pair, cot_rel, gain],
        name="middle_backward",
    )


def first_backward(x_rel, part_own, part_other, keyval_grad, w_keyval_t, dh, gain, ids, count):
    total, width = dh.shape
    part = width // count
    kv = keyval_grad.shape[1]

    def body(ids_ref, x_ref, a_ref, b_ref, kv_ref, w_ref, dh_ref, g_ref, t_out, gg_out, gc_out):
        unit, inv = norm_stats(x_ref[...].astype(f32))
        grad = (a_ref[...].astype(f32) + b_ref[...].astype(f32)) + jnp.dot(
            kv_ref[...], w_ref[...], preferred_element_type=f32
        )
        scaled = grad * g_ref[...]
        value = dh_ref[...] + inv * (
            scaled
            - jnp.mean(scaled, axis=-1, keepdims=True)
            - unit * jnp.mean(scaled * unit, axis=-1, keepdims=True)
        )
        low = value.astype(bf16)
        if part % LANES:
            t_out[...] = low
        else:
            for o in range(count):
                t_out[:, columns_of(ids_ref[o], part)] = low[:, o * part : (o + 1) * part]
        add_rows(gg_out, grad * unit)
        add_rows(gc_out, grad)

    vec = shape((1, width), f32)
    result, gain_grad, bias_grad = call(
        body,
        [shape((total, width), bf16), vec, vec],
        (total // ROWS,),
        [row_spec(width)] * 3
        + [row_spec(kv), whole_spec(kv, width), row_spec(width), whole_spec(1, width)],
        [row_spec(width)] + [whole_spec(1, width)] * 2,
        [x_rel, part_own, part_other, keyval_grad, w_keyval_t, dh, gain],
        ids=[ids],
        flops=2 * total * width * kv,
        name="first_backward",
    )
    return put_back(result, ids, count), gain_grad, bias_grad


TILE = 256


def score_limits(lengths, token_count, first_place):
    doc_ends = jnp.cumsum(lengths)
    doc_starts = doc_ends - lengths
    places = (jnp.arange(token_count, dtype=jnp.int32) + first_place) % token_count
    doc_ids = jnp.sum((places[:, None] >= doc_ends[None, :]).astype(jnp.int32), axis=1)
    owners = doc_ids[:, None] == jnp.arange(lengths.shape[0], dtype=jnp.int32)[None, :]
    doc_begin = jnp.sum(jnp.where(owners, doc_starts[None, :], 0), axis=1)
    blocks = (places - doc_begin) // BLOCK
    seen = (doc_ids[:, None] == doc_ids[None, :]) & (blocks[None, :] <= blocks[:, None])
    seen_t = (doc_ids[None, :] == doc_ids[:, None]) & (blocks[:, None] <= blocks[None, :])
    pick = lambda s: jnp.where(s, shown_score, hidden_score).astype(f32)
    return pick(seen), pick(seen_t)


def attention_forward(queries, key_value, limits, heads):
    total = queries.shape[0]
    tiles = total // TILE
    c = score_scale * log2_e

    def body(q_ref, kv_ref, lim_ref, o_ref, lse_ref, top_ref):
        tile, head = pl.program_id(0), pl.program_id(1)
        k = kv_ref[:, :HD]
        v = kv_ref[:, HD:]
        s = lax.dot_general(
            q_ref[...], k, (((1,), (1,)), ((), ())), preferred_element_type=f32
        )
        s = jnp.minimum(s, lim_ref[...])
        m = jnp.max(s, axis=1, keepdims=True)
        p = jnp.exp2((s - m) * c)
        l = jnp.sum(p, axis=1, keepdims=True)
        o = jnp.dot(p.astype(bf16), v, preferred_element_type=f32)
        o_ref[...] = (o / l).astype(bf16)
        lane = lax.broadcasted_iota(jnp.int32, (TILE, LANES), 1)
        lse = m * c + jnp.log2(l)
        lse_ref[...] = jnp.where(lane == head, lse, lse_ref[...])

        @pl.when((tile == 0) & (head == 0))
        def _():
            top_ref[...] = jnp.full_like(top_ref, hidden_score)

        row = lax.broadcasted_iota(jnp.int32, (heads, LANES), 0)
        best = jnp.max(m, axis=0, keepdims=True) * score_scale
        top_ref[...] = jnp.where(row == head, jnp.maximum(top_ref[...], best), top_ref[...])

    return call(
        body,
        [shape((total, heads * HD), bf16), shape((total, LANES), f32), shape((heads, LANES), f32)],
        (tiles, heads),
        [
            pl.BlockSpec((TILE, HD), lambda i, h: (i, h)),
            pl.BlockSpec((total, 2 * HD), lambda i, h: (0, 0)),
            pl.BlockSpec((TILE, total), lambda i, h: (i, 0)),
        ],
        [
            pl.BlockSpec((TILE, HD), lambda i, h: (i, h)),
            pl.BlockSpec((TILE, LANES), lambda i, h: (i, 0)),
            pl.BlockSpec((heads, LANES), lambda i, h: (0, 0)),
        ],
        [queries, key_value, limits],
        flops=8 * total * total * HD * heads,
        name="attention_forward",
    )


def attention_backward(queries, grad_att, key_value, limits_t, lse_t, dot_t, heads):
    total = queries.shape[0]
    tiles = total // TILE
    c = score_scale * log2_e

    def body(q_ref, da_ref, kv_ref, lim_ref, lse_ref, dot_ref, dq_ref, dkv_ref):
        tile, head = pl.program_id(0), pl.program_id(1)
        k = kv_ref[:, :HD]
        v = kv_ref[:, HD:]
        q = q_ref[...]
        da = da_ref[...]
        nt = (((1,), (1,)), ((), ()))
        s = lax.dot_general(k, q, nt, preferred_element_type=f32)
        s = jnp.minimum(s, lim_ref[...])
        p = jnp.exp2(s * c - lse_ref[pl.ds(head, 1), :])
        dp = lax.dot_general(v, da, nt, preferred_element_type=f32)
        ds = (p * (dp - dot_ref[pl.ds(head, 1), :])).astype(bf16)
        dq = lax.dot_general(ds, k, (((0,), (0,)), ((), ())), preferred_element_type=f32)
        dq_ref[...] = (dq * score_scale).astype(bf16)

        @pl.when((tile == 0) & (head == 0))
        def _():
            dkv_ref[...] = jnp.zeros_like(dkv_ref)

        dkv_ref[:, :HD] += jnp.dot(ds, q, preferred_element_type=f32) * score_scale
        dkv_ref[:, HD:] += jnp.dot(p.astype(bf16), da, preferred_element_type=f32)

    return call(
        body,
        [shape((total, heads * HD), bf16), shape((total, 2 * HD), f32)],
        (tiles, heads),
        [
            pl.BlockSpec((TILE, HD), lambda i, h: (i, h)),
            pl.BlockSpec((TILE, HD), lambda i, h: (i, h)),
            pl.BlockSpec((total, 2 * HD), lambda i, h: (0, 0)),
            pl.BlockSpec((total, TILE), lambda i, h: (0, i)),
            pl.BlockSpec((heads, TILE), lambda i, h: (0, i)),
            pl.BlockSpec((heads, TILE), lambda i, h: (0, i)),
        ],
        [
            pl.BlockSpec((TILE, HD), lambda i, h: (i, h)),
            pl.BlockSpec((total, 2 * HD), lambda i, h: (0, 0)),
        ],
        [queries, grad_att, key_value, limits_t, lse_t, dot_t],
        flops=20 * total * total * HD * heads,
        name="attention_backward",
    )


def adam_values(gradient, weight, one, two, rate, decay):
    new_one = beta_one * one + (1.0 - beta_one) * gradient
    new_two = beta_two * two + (1.0 - beta_two) * gradient * gradient
    direction = (new_one * correct_one) / (jnp.sqrt(new_two * correct_two) + adam_eps)
    return new_one, new_two, weight - rate * (direction + decay * weight)


def to_tiles(flat, tiles_ref):
    for j in range(8):
        tiles_ref[:, j, :] = flat[:, j * LANES : (j + 1) * LANES]


def adam_in(gradient, weight, one, two, outer, start, full):
    rows, cols = gradient.shape
    step = 64
    base = (start // 1024).reshape(1)
    tall = pl.BlockSpec((step, 8, LANES), lambda i, j, b: (i, b[0] + j, 0))
    flat = pl.BlockSpec((step, 1024), lambda i, j, b: (i, j))
    args = [gradient, weight, one, two, outer]
    specs = [flat] + [tall] * 4
    aliases = {}
    if full is not None:
        aliases = {5: 0, 6: 1}
        args += list(full)
        specs += [pl.BlockSpec(memory_space=pl.ANY)] * 2

    def body(_, g_ref, w_ref, one_ref, two_ref, out_ref, *rest):
        one_out, two_out, delta_out, grad_tiles, delta_tiles = rest[-5:]
        to_tiles(g_ref[...].astype(f32), grad_tiles)
        new_one, new_two, stepped = adam_values(
            grad_tiles[...], w_ref[...], one_ref[...], two_ref[...], rate_matrix, weight_decay
        )
        one_out[...] = new_one
        two_out[...] = new_two
        delta_tiles[...] = out_ref[...] - stepped
        for j in range(8):
            delta_out[:, j * LANES : (j + 1) * LANES] = delta_tiles[:, j, :].astype(bf16)

    whole = shape(weight.shape, f32)
    return call(
        body,
        [whole, whole, shape((rows, cols), bf16)],
        (rows // step, cols // 1024),
        specs,
        [tall, tall, flat],
        args,
        ids=[base],
        scratch=[pltpu.VMEM((step, 8, LANES), f32)] * 2,
        aliases=aliases,
        name="adam_in",
        vmem=VMEM_MOST,
    )


def adam_out(gradient, weight, one, two, outer, start, full):
    rows, cols = gradient.shape
    step = 512
    base = (start // step).reshape(1)
    tall = pl.BlockSpec((step, cols), lambda i, b: (b[0] + i, 0))
    flat = pl.BlockSpec((step, cols), lambda i, b: (i, 0))
    args = [gradient, weight, one, two, outer]
    specs = [flat] + [tall] * 4
    aliases = {}
    if full is not None:
        aliases = {5: 0, 6: 1}
        args += list(full)
        specs += [pl.BlockSpec(memory_space=pl.ANY)] * 2

    def body(_, g_ref, w_ref, one_ref, two_ref, out_ref, *rest):
        one_out, two_out, delta_out = rest[-3:]
        new_one, new_two, stepped = adam_values(
            g_ref[...].astype(f32), w_ref[...], one_ref[...], two_ref[...], rate_matrix,
            weight_decay,
        )
        one_out[...] = new_one
        two_out[...] = new_two
        delta_out[...] = (out_ref[...] - stepped).astype(bf16)

    whole = shape(weight.shape, f32)
    return call(
        body,
        [whole, whole, shape((rows, cols), bf16)],
        (rows // step,),
        specs,
        [tall, tall, flat],
        args,
        ids=[base],
        aliases=aliases,
        name="adam_out",
        vmem=VMEM_MOST,
    )


def outer_values(mean, momentum, outer):
    velocity = outer_beta * momentum + mean
    return velocity, outer - outer_rate * (mean + outer_beta * velocity)


def outer_in(both, momentum, outer, factor, start, full):
    _, rows, cols = both.shape
    step = 64
    base = (start // 1024).reshape(1)
    tall = pl.BlockSpec((step, 8, LANES), lambda i, j, b: (i, b[0] + j, 0))
    flat = pl.BlockSpec((2, step, 1024), lambda i, j, b: (0, i, j))
    wide = pl.BlockSpec((step, 1024), lambda i, j, b: (i, b[0] + j))
    args = [both, momentum, outer]
    specs = [flat, tall, tall]
    if factor is not None:
        args.append(factor)
        specs.append(pl.BlockSpec((8, LANES), lambda i, j, b: (0, 0)))
    aliases = {}
    if full is not None:
        aliases = {len(args) + k: k for k in range(4)}
        args += list(full)
        specs += [pl.BlockSpec(memory_space=pl.ANY)] * 4

    def body(_, both_ref, mom_ref, out_ref, *rest):
        mean_out, vel_out, new_out, copy_out, mean_tiles, new_tiles = rest[-6:]
        to_tiles((both_ref[0].astype(f32) + both_ref[1].astype(f32)) * 0.5, mean_tiles)
        mean = mean_tiles[...]
        velocity, fresh = outer_values(mean, mom_ref[...], out_ref[...])
        if factor is not None:
            fresh = fresh * rest[0][...][None]
        mean_out[...] = mean
        vel_out[...] = velocity
        new_out[...] = fresh
        new_tiles[...] = fresh
        for j in range(8):
            copy_out[:, j * LANES : (j + 1) * LANES] = new_tiles[:, j, :].astype(bf16)

    whole = shape(outer.shape, f32)
    return call(
        body,
        [whole, whole, whole, shape((rows, outer.shape[1] * LANES), bf16)],
        (rows // step, cols // 1024),
        specs,
        [tall, tall, tall, wide],
        args,
        ids=[base],
        scratch=[pltpu.VMEM((step, 8, LANES), f32)] * 2,
        aliases=aliases,
        name="outer_in",
        vmem=VMEM_MOST,
    )


def outer_out(both, momentum, outer, start, full):
    _, rows, cols = both.shape
    step = 512
    base = (start // step).reshape(1)
    tall = pl.BlockSpec((step, cols), lambda i, b: (b[0] + i, 0))
    flat = pl.BlockSpec((2, step, cols), lambda i, b: (0, i, 0))
    args = [both, momentum, outer]
    specs = [flat, tall, tall]
    aliases = {}
    if full is not None:
        aliases = {3 + k: k for k in range(4)}
        args += list(full)
        specs += [pl.BlockSpec(memory_space=pl.ANY)] * 4

    def body(_, both_ref, mom_ref, out_ref, *rest):
        mean_out, vel_out, new_out, copy_out = rest[-4:]
        mean = (both_ref[0].astype(f32) + both_ref[1].astype(f32)) * 0.5
        velocity, fresh = outer_values(mean, mom_ref[...], out_ref[...])
        mean_out[...] = mean
        vel_out[...] = velocity
        new_out[...] = fresh
        copy_out[...] = fresh.astype(bf16)

    whole = shape(outer.shape, f32)
    return call(
        body,
        [whole, whole, whole, shape(outer.shape, bf16)],
        (rows // step,),
        specs,
        [tall] * 4,
        args,
        ids=[base],
        aliases=aliases,
        name="outer_out",
        vmem=VMEM_MOST,
    )


class Wire:
    def __init__(self, window):
        self.window, self.landed = window, []

    def send(self, block, axis, pairs):
        if len(self.landed) >= self.window:
            block, _ = lax.optimization_barrier((block, self.landed[-self.window]))
        arrived = lax.ppermute(block, axis, pairs)
        self.landed.append(arrived)
        return arrived


class Links:
    def __init__(self, count, splits, window):
        self.levels = count.bit_length() - 1
        self.far = ([1] + [1 << b for b in range(3, self.levels)])[: self.levels - 2]
        places = range(count)
        middle = [i for i in places if (i >> 1 ^ i >> 2) & 1]
        outer = [i for i in places if i not in middle]
        self.pair = [(i, i ^ 2) for i in places]
        self.inward = [(i, i ^ 2) for i in outer]
        self.outward = [(i, i ^ 2) for i in middle]
        self.between = [(i, i ^ 6) for i in middle]
        self.beside = [[(i, i ^ mask) for i in places] for mask in self.far]
        self.mirror = [(i, i ^ 6) for i in places]
        self.cores = [(i, (i + 1) % splits) for i in range(splits)]
        self.wire = Wire(window)

    def flips(self, across):
        masks = [2, across] + self.far
        table = []
        for o in range(1 << self.levels):
            flip = 0
            for level, mask in enumerate(masks):
                if o >> level & 1:
                    flip ^= mask
            table.append(flip)
        return table

    def to_side(self, block, pairs):
        return self.wire.send(block, "dp", pairs)

    def to_middle(self, block):
        return self.wire.send(block, "dp", self.between)

    def to_far(self, block, level):
        return self.wire.send(block, "dp", self.beside[level - 2])

    def to_pair(self, block):
        return self.wire.send(block, "dp", self.pair)

    def across(self, block):
        return lax.ppermute(block, "tensor", self.cores)

    def pair_now(self, block):
        return lax.ppermute(block, "dp", self.pair)


def after(value, *earlier):
    return lax.optimization_barrier((value, *earlier))[0]


class Order:
    def __init__(self):
        self.last = ()

    def tie(self, value):
        return after(value, *self.last) if self.last else value

    def mark(self, *values):
        self.last = values
        return values[0]


class Gathered:
    def __init__(self, links, axis, mine, other=None):
        self.links, self.axis, self.mine, self.other = links, axis, mine, other
        self.held = {}

    def join(self, *blocks):
        return jnp.concatenate(blocks, axis=self.axis)

    def near(self):
        give = self.mine if self.other is None else self.other
        self.held[0] = self.join(self.mine, self.links.to_side(give, self.links.pair))

    def inward(self):
        if self.other is not None:
            self.passed = self.links.to_side(self.mine, self.links.inward)

    def middle(self):
        if self.other is None:
            self.relay = self.direct = self.links.to_middle(self.held[0])
        else:
            self.relay = self.links.to_middle(self.join(self.other, self.passed))

    def middle_rest(self):
        self.direct = self.links.to_middle(self.held[0])

    def outward(self):
        self.relayed = self.links.to_side(self.relay, self.links.outward)

    def join_far(self):
        self.held[2] = self.direct + self.relayed

    def far(self, level, o):
        self.held[o + (1 << level)] = self.links.to_far(self.held[o], level)

    def whole(self):
        for level in range(2, self.links.levels):
            for o in range(0, 1 << level, 2):
                if o + (1 << level) not in self.held:
                    self.far(level, o)
        return self.join(*[self.held[o] for o in sorted(self.held)])


class Reduced:
    def __init__(self, links, order, axis, size, halved, part):
        self.links, self.order, self.axis, self.size = links, order, axis, size
        self.halved, self.part = halved, part
        self.landed = {}

    def pair_sum(self, o):
        total = self.part(o, 2)
        for block in self.landed.pop(o, []):
            total = total + block.astype(f32)
        return self.order.mark(total.astype(bf16))

    def one(self, block, o):
        return lax.slice_in_dim(
            block, o * self.size, (o + 1) * self.size, axis=self.axis
        ).astype(f32)

    def far(self, level, o):
        arrived = self.links.to_far(self.pair_sum(o), level)
        self.landed.setdefault(o - (1 << level), []).append(arrived)
        return arrived

    def far_rest(self, done):
        arrived = None
        for level in range(self.links.levels - 1, 1, -1):
            for o in reversed(range(1 << level, 2 << level, 2)):
                if (level, o) not in done:
                    arrived = self.far(level, o)
        return arrived

    def inward(self):
        self.ahead = self.pair_sum(2)
        self.passed = self.links.to_side(self.ahead, self.links.inward)
        if self.halved:
            self.direct = self.links.to_middle(self.ahead)

    def middle(self):
        if self.halved:
            self.relay = self.links.to_middle(self.order.tie(self.passed))
        else:
            both = self.order.mark(self.order.tie(self.ahead) + self.passed)
            self.direct = self.links.to_middle(both)

    def single(self, o):
        total = self.part(o, 1)
        for block in self.landed[0] + [self.direct]:
            total = total + self.one(block, o)
        return total

    def near(self):
        value = self.order.mark(self.single(1).astype(bf16))
        self.theirs = self.links.to_side(value, self.links.pair).astype(f32)

    def outward(self):
        value = self.one(self.order.tie(self.relay), 1).astype(bf16)
        self.last = self.links.to_side(value, self.links.outward).astype(f32)

    def result(self):
        if not self.halved:
            return self.order.mark(self.single(0) + self.theirs), None
        own = self.order.mark(self.single(0) + self.last)
        return own, self.theirs + self.one(self.relay, 0)


def local(
    tokens,
    doc_lengths,
    cotangent,
    inner_in,
    inner_out,
    inner_shared,
    first_in,
    first_out,
    first_shared,
    second_in,
    second_out,
    second_shared,
    outer_in_w,
    outer_out_w,
    outer_shared,
    momentum_in,
    momentum_out,
    momentum_shared,
):
    splits = lax.axis_size("tensor")
    count = lax.axis_size("dp")
    split = lax.axis_index("tensor")
    place = lax.axis_index("dp")
    total, width = tokens.shape
    part = width // count
    local_cols = inner_in.shape[3]
    shared_cols = inner_shared.shape[2]
    heads = HEADS // splits
    qcols = heads * HD
    hidden = local_cols - qcols
    vec = 2 * HD
    own_cols = part // splits
    mine = total // 2

    links = Links(count, splits, 4)
    across = links.across
    levels = links.levels
    side = ((place >> 1) ^ (place >> 2)) & 1
    from_outer, from_middle = (jnp.array(links.flips(m), jnp.int32) for m in (4, 6))
    ids = (place ^ jnp.where(side == 0, from_outer, from_middle)).astype(jnp.int32)
    swap_group = [(0, 1), (1, 0)]
    split_id = split.astype(jnp.int32).reshape(1)

    def tall(array):
        return array.reshape(part, local_cols // LANES, LANES)

    w_in = tall(inner_in)
    w_out = inner_out.reshape(local_cols, part)
    shared_rows = lax.all_gather(inner_shared[0], ("dp", "tensor"), axis=0, tiled=True)

    half = hidden // 2
    flat_in = inner_in.reshape(part, local_cols)

    def sides(low, high):
        return (
            jnp.where(side == 0, low, high).astype(bf16),
            jnp.where(side == 0, high, low).astype(bf16),
        )

    block_q = flat_in[:, :qcols].astype(bf16)
    block_o = w_out[:qcols].astype(bf16)
    up_sides = sides(flat_in[:, qcols : qcols + half], flat_in[:, qcols + half :])
    down_sides = sides(w_out[qcols : qcols + half], w_out[qcols + half :])
    got_query = Gathered(links, 0, block_q)
    got_attn = Gathered(links, 1, block_o)
    got_up = Gathered(links, 0, *up_sides)
    got_down = Gathered(links, 1, *down_sides)
    shared_t = shared_rows.T
    shared_rel = pick_blocks(shared_t, ids, part, count, False)
    w_keyval_t = shared_rel[:vec].astype(bf16)
    vectors_t, vectors = shared_t[vec:], shared_rel[vec:]
    gain_one, bias_one, gain_two, bias_two = (vectors[k : k + 1] for k in range(4))
    bias_out, bias_down = vectors[5:6], vectors[6:7]
    bias_query = lax.dynamic_slice_in_dim(vectors_t[4], split * qcols, qcols)
    bias_up = lax.dynamic_slice_in_dim(
        vectors_t[7:].reshape(FF), split * hidden + side * half, half
    )

    nt = (((1,), (1,)), ((), ()))
    tn = (((0,), (0,)), ((), ()))

    def mm(a, b, dims=(((1,), (0,)), ((), ()))):
        return lax.dot_general(a, b, dims, preferred_element_type=f32)

    def block(array, o, blocks):
        return array[:, o * part : (o + blocks) * part]

    def both_rows(rows):
        return lax.all_gather(rows, "tensor", axis=0, tiled=True)

    def far(weight, o):
        if levels == 3:
            weight.far(2, o)

    cot_own, cot_pair, grad_bias_down = cotangent_order(cotangent, ids, split_id, count)
    got_query.near()
    got_attn.near()
    got_query.middle()
    far(got_query, 0)
    got_down.near()
    got_down.inward()
    got_attn.middle()
    far(got_attn, 0)
    got_query.outward()
    got_query.join_far()
    far(got_query, 2)
    got_attn.outward()
    got_attn.join_far()
    got_down.middle()
    got_up.near()
    far(got_attn, 2)
    w_query = got_query.whole()
    w_attn = got_attn.whole()
    got_up.inward()
    far(got_down, 0)
    cot_theirs = links.to_pair(swap_small(cot_pair, part))
    got_down.outward()
    got_down.middle_rest()
    got_down.join_far()
    far(got_up, 0)
    got_up.middle()
    far(got_down, 2)
    w_down = got_down.whole()
    got_up.outward()
    got_up.middle_rest()
    got_up.join_far()

    x_rel, normed = first_norm(tokens, ids, split_id, gain_one, bias_one, count)
    limits, limits_t = score_limits(doc_lengths[0], total, split * mine)
    key_value = mm(normed, w_keyval_t, nt).astype(bf16)
    queries = (mm(normed, w_query) + bias_query).astype(bf16)
    attended, log_totals, tops = attention_forward(queries, key_value, limits, heads)
    attn_give = mm(attended[mine:], w_attn).astype(bf16)
    attn_keep = mm(attended[:mine], w_attn).astype(bf16)
    attn_other = across(attn_give)
    middle, normed_two, normed_pair = middle_norm(
        x_rel, attn_keep, attn_other, bias_out, gain_two, bias_two, part
    )
    normed_theirs = links.to_pair(swap_small(normed_pair, part))
    far(got_up, 2)
    w_up = got_up.whole()
    normed_all = both_rows(jnp.concatenate([normed_two, normed_theirs], axis=0))
    cot_all = both_rows(jnp.concatenate([cot_own, cot_theirs], axis=0))
    hidden_grad = mm(cot_all, w_down, nt).astype(bf16)
    acts, grad_pre, grad_bias_up = hidden_units(normed_all, w_up, bias_up[None], hidden_grad)

    links.wire.window = 1 << 30
    order = Order()
    tie, mark = order.tie, order.mark
    sum_down = Reduced(
        links, order, 1, part, True, lambda o, b: mm(tie(acts), block(cot_all, o, b), tn)
    )
    sum_up = Reduced(
        links, order, 0, part, True, lambda o, b: mm(block(normed_all, o, b), tie(grad_pre), tn)
    )
    early = [(2, 6)] if levels == 3 else []
    for level, o in early:
        sum_down.far(level, o)
    pre_give = lax.dynamic_slice_in_dim(grad_pre, (1 - split) * 2 * mine, 2 * mine)
    pre_keep = lax.dynamic_slice_in_dim(grad_pre, split * 2 * mine, 2 * mine)
    two_give = mark(mm(pre_give, tie(w_up), nt).astype(bf16))
    two_other = across(two_give)
    down_landed = sum_down.far_rest(early)
    two_keep = mark(mm(pre_keep, tie(w_up), nt).astype(bf16))
    two_theirs = two_keep[mine:].astype(f32) + two_other[mine:].astype(f32)
    two_theirs = mark(swap_small(two_theirs.astype(bf16), part))
    two_pair = links.pair_now(two_theirs)
    up_landed = sum_up.far_rest([])
    sum_down.inward()
    dh, dh_mine, grad_gain_two, grad_bias_two, grad_bias_out = middle_backward(
        middle, tie(two_keep), two_other, two_pair, cot_own, gain_two, part
    )
    mark(dh_mine)
    dh_low = jnp.concatenate([dh_mine, across(dh_mine)], axis=0)
    grad_att = mark(mm(dh_low, w_attn, nt).astype(bf16))
    dots = jnp.sum(
        (grad_att.astype(f32) * attended.astype(f32)).reshape(total, heads, HD), axis=2
    )
    grad_queries, kv_part = attention_backward(
        queries, after(grad_att, down_landed), key_value, limits_t, log_totals.T[:heads], dots.T,
        heads,
    )
    mark(grad_queries)
    sum_down.middle()
    one_give = mark(mm(grad_queries[mine:], w_query, nt).astype(bf16))
    one_other = across(one_give)
    kv_other = across(kv_part[mine:])
    sum_down.near()
    sum_up.inward()
    sum_attn = Reduced(
        links, order, 1, part, False, lambda o, b: mm(tie(attended), block(dh_low, o, b), tn)
    )
    sum_attn.far_rest([])
    one_keep = mark(mm(grad_queries[:mine], tie(w_query), nt).astype(bf16))
    kv_low = (kv_part[:mine] + kv_other).astype(bf16)
    grad_mine, grad_gain_one, grad_bias_one = first_backward(
        x_rel, after(one_keep, up_landed), one_other, kv_low, w_keyval_t, dh, gain_one, ids, count
    )
    mark(grad_mine)
    tokens_grad = both_rows(grad_mine)
    sum_query = Reduced(
        links, order, 0, part, False, lambda o, b: mm(block(normed, o, b), tie(grad_queries), tn)
    )
    sum_query.far_rest([])
    sum_up.middle()
    sum_down.outward()

    grad_keyval_t = mm(tie(kv_low), normed[:mine], tn)
    grad_bias_query = jnp.sum(grad_queries.astype(f32), axis=0)
    spread = jnp.concatenate(
        [
            lax.dynamic_update_slice_in_dim(
                jnp.zeros((width,), f32), grad_bias_query, split * qcols, 0
            ),
            lax.dynamic_update_slice_in_dim(
                jnp.zeros((FF,), f32), grad_bias_up[0], split * hidden + side * half, 0
            ),
        ]
    ).reshape(1 + FF // width, width)
    near = jnp.concatenate(
        [grad_keyval_t, grad_gain_one, grad_bias_one, grad_gain_two, grad_bias_two, grad_bias_out,
         grad_bias_down],
        axis=0,
    )
    steps = jnp.arange(count, dtype=jnp.int32)
    turned = jnp.where((side == 0) & ((steps & 2) != 0), steps ^ 1, steps)
    mirrored = (place ^ from_middle).astype(jnp.int32)

    def pieces(core):
        a = pick_blocks(near, turned * splits + core, own_cols, count, True)
        b = pick_blocks(spread, mirrored * splits + core, own_cols, count, True)
        return jnp.concatenate([a[:, : vec + 4], b[:, :1], a[:, vec + 4 :], b[:, 1:]], axis=1)

    shared_give = mark(pieces(1 - split))
    shared_other = across(shared_give)
    red_down = sum_down.result()

    down_part = mark(mm(tie(acts), w_down).astype(bf16))
    down_sum = lax.psum_scatter(down_part, "tensor", scatter_dimension=0, tiled=True)
    sum_up.near()
    sum_attn.inward()

    red_shared = pieces(split) + shared_other
    keep = red_shared.shape[0] // 2
    cube = list(reversed([links.pair, links.mirror] + links.beside))
    for pairs in cube[:-2]:
        keep = red_shared.shape[0] // 2
        red_shared = red_shared[:keep] + lax.ppermute(red_shared[keep:], "dp", pairs)
    sum_query.inward()
    sum_attn.middle()
    sum_up.outward()
    down_pair = links.to_pair(swap_small(tie(down_sum)[mine:], part))

    peers = across(tie(tops))
    peak = jnp.where(
        split == 0, jnp.concatenate([tops, peers]), jnp.concatenate([peers, tops])
    )
    peak = jnp.maximum(peak, lax.ppermute(peak, "group", swap_group))
    for pairs in [links.pair, links.mirror] + links.beside:
        peak = jnp.maximum(peak, lax.ppermute(peak, "dp", pairs))
    clip_rows = clip_limit / jnp.maximum(peak, clip_limit)

    sum_query.middle()
    red_up = sum_up.result()
    sum_attn.near()
    for pairs in cube[-2:]:
        keep = red_shared.shape[0] // 2
        red_shared = red_shared[:keep] + lax.ppermute(red_shared[keep:], "dp", pairs)
    red_shared = red_shared[0]
    block_out = both_rows(
        block_result(middle, down_sum, down_pair, bias_down, ids, count)
    )
    sum_query.near()
    red_attn, red_query = sum_attn.result()[0], sum_query.result()[0]

    one_in, two_in = tall(first_in), tall(second_in)
    one_out, two_out = (a.reshape(local_cols, part) for a in (first_out, second_out))
    base_in, mom_in = tall(outer_in_w), tall(momentum_in)
    base_out, mom_out = (a.reshape(local_cols, part) for a in (outer_out_w, momentum_out))
    clip_own = lax.dynamic_slice_in_dim(clip_rows, split * heads, heads)

    starts = [qcols + side * half, qcols + (1 - side) * half]
    zero = jnp.zeros((), jnp.int32)
    gathered = []

    def groups(delta):
        both = lax.all_gather(after(delta, *gathered[-1:]), "group", axis=0)
        gathered.append(both)
        return both

    full_in = full_out = new_in = new_out = None
    for s, gradient in zip(starts, red_down):
        *full_out, delta = adam_out(gradient, w_out, one_out, two_out, base_out, s, full_out)
        new_out = outer_out(groups(delta), mom_out, base_out, s, new_out)
    for s, gradient in zip(starts, red_up):
        *full_in, delta = adam_in(gradient, w_in, one_in, two_in, base_in, s, full_in)
        new_in = outer_in(groups(delta), mom_in, base_in, None, s, new_in)
    red_query = after(red_query, new_in[0], new_out[0])
    *full_out, delta = adam_out(red_attn, w_out, one_out, two_out, base_out, zero, full_out)
    new_out = outer_out(groups(delta), mom_out, base_out, zero, new_out)
    *full_in, delta = adam_in(red_query, w_in, one_in, two_in, base_in, zero, full_in)
    both = jnp.stack([delta, lax.ppermute(delta, "group", swap_group)])
    new_in = outer_in(both, mom_in, base_in, clip_own, zero, new_in)

    ids_col = jnp.arange(shared_cols, dtype=jnp.int32)[:, None]
    one_sh, two_sh, stepped = adam_values(
        red_shared,
        inner_shared[0].T,
        first_shared[0].T,
        second_shared[0].T,
        jnp.where(ids_col < vec, rate_matrix, rate_vector),
        jnp.where(ids_col < vec, weight_decay, 0.0),
    )
    base_sh = outer_shared.T
    delta = (base_sh - stepped).astype(bf16)
    mean_sh = (delta.astype(f32) + lax.ppermute(delta, "group", swap_group).astype(f32)) * 0.5
    vel_sh, fresh_sh = outer_values(mean_sh, momentum_shared.T, base_sh)
    row_ids = (place * splits + split) * own_cols + jnp.arange(own_cols, dtype=jnp.int32)
    clip_vec = clip_rows[:, 0]
    row_clip = jnp.sum(
        jnp.where((row_ids // HD)[None, :] == jnp.arange(HEADS)[:, None], clip_vec[:, None], 0.0),
        axis=0,
    )
    fresh_sh = fresh_sh * jnp.where(ids_col == vec + 4, row_clip[None, :], 1.0)

    shape_in, shape_out = (part, 1, local_cols), (1, local_cols, part)
    mean_in, vel_in, fresh_in, copy_in = new_in
    mean_out, vel_out, fresh_out, copy_out = new_out
    return (
        block_out,
        tokens_grad,
        clip_vec,
        full_in[0].reshape((1,) + shape_in),
        full_out[0].reshape((1,) + shape_out),
        one_sh.T[None],
        full_in[1].reshape((1,) + shape_in),
        full_out[1].reshape((1,) + shape_out),
        two_sh.T[None],
        mean_in.reshape(shape_in),
        mean_out.reshape(shape_out),
        mean_sh.T,
        vel_in.reshape(shape_in),
        vel_out.reshape(shape_out),
        vel_sh.T,
        fresh_in.reshape(shape_in),
        fresh_out.reshape(shape_out),
        fresh_sh.T,
        copy_in.reshape(shape_in),
        copy_out.reshape(shape_out),
        fresh_sh.T.astype(bf16),
    )


def solution(mesh):
    rows = P(("group", "dp"), None)
    inner = [P("group", "dp", "tensor", None), P("group", "tensor", None, "dp"),
             P("group", ("dp", "tensor"), None)]
    outer = [P("dp", "tensor", None), P("tensor", None, "dp"), P(("dp", "tensor"), None)]
    in_specs = tuple([rows] * 3 + inner * 3 + outer * 2)
    out_specs = tuple([rows] * 2 + [P()] + inner * 2 + outer * 4)
    return jax.shard_map(local, mesh=mesh, in_specs=in_specs, out_specs=out_specs, check_vma=False)
```

```python
import jax
import jax.numpy as jnp
from jax import lax
from jax.experimental import pallas as pl
from jax.experimental.pallas import tpu as pltpu
from jax.sharding import PartitionSpec as P

HEADS = 16
HD = 128
FF = 8192
BLOCK = 256
STEP = 10

norm_eps = 1e-05
hidden_score = -1e30
shown_score = 3e38
beta_one = 0.9
beta_two = 0.95
adam_eps = 1e-08
rate_matrix = 0.02
rate_vector = 0.2
weight_decay = 0.1
outer_beta = 0.9
outer_rate = 0.7
clip_limit = 5.0
score_scale = HD ** (-0.5)
log2_e = 1.4426950408889634
correct_one = 1.0 / (1.0 - beta_one**STEP)
correct_two = 1.0 / (1.0 - beta_two**STEP)

f32 = jnp.float32
bf16 = jnp.bfloat16
ROWS = 128
LANES = 128
VMEM_LIMIT = 40 * 1024 * 1024
VMEM_MOST = 58 * 1024 * 1024


def shape(dims, dtype):
    return jax.ShapeDtypeStruct(dims, dtype)


def call(body, out_shape, grid, in_specs, out_specs, args, *, ids=(), scratch=(), aliases=None,
         flops=0, name=None, vmem=VMEM_LIMIT):
    outs = out_shape if isinstance(out_shape, (list, tuple)) else [out_shape]
    moved = sum(a.size * a.dtype.itemsize for a in args)
    moved += sum(o.size * o.dtype.itemsize for o in outs)
    return pl.pallas_call(
        body,
        out_shape=out_shape,
        grid_spec=pltpu.PrefetchScalarGridSpec(
            num_scalar_prefetch=len(ids),
            grid=grid,
            in_specs=in_specs,
            out_specs=out_specs,
            scratch_shapes=list(scratch),
        ),
        input_output_aliases={len(ids) + k: v for k, v in (aliases or {}).items()},
        compiler_params=pltpu.CompilerParams(vmem_limit_bytes=vmem),
        cost_estimate=pl.CostEstimate(flops=flops, bytes_accessed=moved, transcendentals=0),
        name=name,
    )(*ids, *args)


def pick_blocks(array, block_ids, width, count, stacked):
    rows = array.shape[0]
    if width % LANES:
        taken = jnp.take(array.reshape(rows, -1, width), block_ids, axis=1)
        return taken.transpose(1, 0, 2) if stacked else taken.reshape(rows, count * width)

    def body(ids_ref, in_ref, out_ref):
        if stacked:
            out_ref[0] = in_ref[...]
        else:
            out_ref[...] = in_ref[...]

    if stacked:
        out, spec = shape((count, rows, width), array.dtype), pl.BlockSpec(
            (1, rows, width), lambda j, ids: (j, 0, 0)
        )
    else:
        out, spec = shape((rows, count * width), array.dtype), pl.BlockSpec(
            (rows, width), lambda j, ids: (0, j)
        )
    return call(
        body, out, (count,), [pl.BlockSpec((rows, width), lambda j, ids: (0, ids[j]))], spec,
        [array], ids=[block_ids], name="pick_blocks",
    )


def columns_of(block_id, width):
    return pl.ds(pl.multiple_of(block_id * width, width), width)


def placing(array, ids, count):
    part = array.shape[1] // count
    if part % LANES == 0:
        return array, count, part
    return pick_blocks(array, ids, part, count, False), 0, part


def put_back(array, ids, count):
    part = array.shape[1] // count
    if part % LANES == 0:
        return array
    back = jnp.sum(
        jnp.where(ids[None, :] == jnp.arange(count)[:, None], jnp.arange(count)[None, :], 0), axis=1
    ).astype(jnp.int32)
    return pick_blocks(array, back, part, count, False)


def norm_stats(rows):
    mean = jnp.mean(rows, axis=-1, keepdims=True)
    centered = rows - mean
    inv = lax.rsqrt(jnp.mean(centered * centered, axis=-1, keepdims=True) + norm_eps)
    return centered * inv, inv


def row_spec(cols, rows=ROWS):
    return pl.BlockSpec((rows, cols), lambda i, *ids: (i, 0))


def turned_spec(cols, blocks):
    return pl.BlockSpec(
        (ROWS, cols), lambda i, ids, split: ((i + split[0] * (blocks // 2)) % blocks, 0)
    )


def whole_spec(rows, cols):
    return pl.BlockSpec((rows, cols), lambda i, *ids: (0, 0))


def first_norm(tokens, ids, split, gain, bias, count):
    total, width = tokens.shape
    tokens, moved, part = placing(tokens, ids, count)

    def body(ids_ref, split_ref, x_ref, g_ref, c_ref, x_out, n_out):
        for o in range(moved):
            x_out[:, o * part : (o + 1) * part] = x_ref[:, columns_of(ids_ref[o], part)]
        if not moved:
            x_out[...] = x_ref[...]
        unit, _ = norm_stats(x_out[...].astype(f32))
        n_out[...] = (unit * g_ref[...] + c_ref[...]).astype(bf16)

    return call(
        body,
        [shape((total, width), bf16)] * 2,
        (total // ROWS,),
        [turned_spec(width, total // ROWS), whole_spec(1, width), whole_spec(1, width)],
        [row_spec(width)] * 2,
        [tokens, gain, bias],
        ids=[ids, split],
        name="first_norm",
    )


def first_spec(cols, blocks):
    return pl.BlockSpec((ROWS, cols), lambda i, *ids: (jnp.minimum(i, blocks - 1), 0))


def swapped(values, part):
    if part % LANES:
        return values
    blocks = [values[:, o : o + part] for o in range(0, values.shape[1], part)]
    return jnp.concatenate([blocks[pair_of(o)] for o in range(len(blocks))], axis=1)


def pair_of(o):
    return o if o & 2 else o ^ 1


def swap_small(values, part):
    if part % LANES == 0:
        return values
    blocks = [values[:, o : o + part] for o in range(0, values.shape[1], part)]
    return jnp.concatenate([blocks[pair_of(o)] for o in range(len(blocks))], axis=1)


def cotangent_order(cotangent, ids, split, count):
    total, width = cotangent.shape
    cotangent, moved, part = placing(cotangent, ids, count)
    mine = total // ROWS // 2

    def body(ids_ref, split_ref, c_ref, c_out, pair_out, sum_out):
        for o in range(moved):
            c_out[:, o * part : (o + 1) * part] = c_ref[:, columns_of(ids_ref[o], part)]
        if not moved:
            c_out[...] = c_ref[...]
        pair_out[...] = swapped(c_out[...], part)
        add_rows(sum_out, c_out[...].astype(f32))

    return call(
        body,
        [shape((total // 2, width), bf16)] * 2 + [shape((1, width), f32)],
        (mine,),
        [turned_spec(width, total // ROWS)],
        [row_spec(width)] * 2 + [whole_spec(1, width)],
        [cotangent],
        ids=[ids, split],
        name="cotangent_order",
    )


def hidden_units(rows, weight, bias, hidden_grad):
    total, depth = rows.shape
    cols = weight.shape[1]
    high, wide, sub = 256, 1024, 256
    curve, cube = (2.0 / 3.141592653589793) ** 0.5, 0.044715

    def body(n_ref, w_ref, b_ref, dz_ref, z_out, du_out, sum_out):
        first = pl.program_id(1) == 0
        for c in range(0, wide, sub):
            at = slice(c, c + sub)
            u = jnp.dot(n_ref[...], w_ref[:, at], preferred_element_type=f32) + b_ref[:, at]
            square = u * u
            t = jnp.tanh(curve * u * (1.0 + cube * square))
            z_out[:, at] = (0.5 * u * (1.0 + t)).astype(bf16)
            slope = 0.5 * (1.0 + t) + (0.5 * curve) * u * (1.0 - t * t) * (
                1.0 + (3.0 * cube) * square
            )
            du = (slope * dz_ref[:, at].astype(f32)).astype(bf16)
            du_out[:, at] = du
            total_du = jnp.sum(du.astype(f32), axis=0, keepdims=True)
            sum_out[:, at] = jnp.where(first, total_du, sum_out[:, at] + total_du)

    tile = pl.BlockSpec((high, wide), lambda j, i: (i, j))
    line = pl.BlockSpec((1, wide), lambda j, i: (0, j))
    return call(
        body,
        [shape((total, cols), bf16)] * 2 + [shape((1, cols), f32)],
        (cols // wide, total // high),
        [
            pl.BlockSpec((high, depth), lambda j, i: (i, 0)),
            pl.BlockSpec((depth, wide), lambda j, i: (0, j)),
            line,
            tile,
        ],
        [tile, tile, line],
        [rows, weight, bias, hidden_grad],
        flops=2 * total * depth * cols,
        name="hidden_units",
    )


def add_rows(sum_ref, values):
    @pl.when(pl.program_id(0) == 0)
    def _():
        sum_ref[...] = jnp.zeros_like(sum_ref)

    sum_ref[...] += jnp.sum(values, axis=0, keepdims=True)


def middle_norm(x_rel, part_own, part_other, bias_out, gain, bias, part):
    total, width = part_other.shape

    def body(x_ref, a_ref, b_ref, bo_ref, g_ref, c_ref, h_out, n_out, pair_out):
        mid = x_ref[...].astype(f32) + (
            a_ref[...].astype(f32) + b_ref[...].astype(f32)
        ) + bo_ref[...]
        h_out[...] = mid
        unit, _ = norm_stats(mid)
        low = (unit * g_ref[...] + c_ref[...]).astype(bf16)
        n_out[...] = low
        pair_out[...] = swapped(low, part)

    return call(
        body,
        [shape((total, width), f32)] + [shape((total, width), bf16)] * 2,
        (total // ROWS,),
        [row_spec(width)] * 3 + [whole_spec(1, width)] * 3,
        [row_spec(width)] * 3,
        [x_rel, part_own, part_other, bias_out, gain, bias],
        name="middle_norm",
    )


def block_result(middle, part_own, part_pair, bias_down, ids, count):
    total, width = middle.shape
    part = width // count

    def body(ids_ref, h_ref, a_ref, p_ref, b2_ref, out_ref):
        value = a_ref[...].astype(f32) + swapped(p_ref[...], part).astype(f32)
        value = (h_ref[...] + value + b2_ref[...]).astype(bf16)
        if part % LANES:
            out_ref[...] = value
        else:
            for o in range(count):
                out_ref[:, columns_of(ids_ref[o], part)] = value[:, o * part : (o + 1) * part]

    result = call(
        body,
        shape((total, width), bf16),
        (total // ROWS,),
        [row_spec(width)] * 3 + [whole_spec(1, width)],
        row_spec(width),
        [middle, part_own, part_pair, bias_down],
        ids=[ids],
        name="block_result",
    )
    return put_back(result, ids, count)


def middle_backward(middle, part_own, part_other, part_pair, cot_rel, gain, part):
    total, width = middle.shape

    def body(h_ref, a_ref, b_ref, p_ref, dy_ref, g_ref, dh_out, low_out, gg_out, gc_out, gbo_out):
        unit, inv = norm_stats(h_ref[...])
        grad = a_ref[...].astype(f32) + b_ref[...].astype(f32)
        grad = grad + swapped(p_ref[...], part).astype(f32)
        scaled = grad * g_ref[...]
        dh = dy_ref[...].astype(f32) + inv * (
            scaled
            - jnp.mean(scaled, axis=-1, keepdims=True)
            - unit * jnp.mean(scaled * unit, axis=-1, keepdims=True)
        )
        dh_out[...] = dh
        low = dh.astype(bf16)
        low_out[...] = low
        add_rows(gg_out, grad * unit)
        add_rows(gc_out, grad)
        add_rows(gbo_out, low.astype(f32))

    vec = shape((1, width), f32)
    return call(
        body,
        [shape((total, width), f32), shape((total, width), bf16), vec, vec, vec],
        (total // ROWS,),
        [row_spec(width)] * 5 + [whole_spec(1, width)],
        [row_spec(width)] * 2 + [whole_spec(1, width)] * 3,
        [middle, part_own, part_other, part_pair, cot_rel, gain],
        name="middle_backward",
    )


def first_backward(x_rel, part_own, part_other, keyval_grad, w_keyval_t, dh, gain, ids, count):
    total, width = dh.shape
    part = width // count
    kv = keyval_grad.shape[1]

    def body(ids_ref, x_ref, a_ref, b_ref, kv_ref, w_ref, dh_ref, g_ref, t_out, gg_out, gc_out):
        unit, inv = norm_stats(x_ref[...].astype(f32))
        grad = (a_ref[...].astype(f32) + b_ref[...].astype(f32)) + jnp.dot(
            kv_ref[...], w_ref[...], preferred_element_type=f32
        )
        scaled = grad * g_ref[...]
        value = dh_ref[...] + inv * (
            scaled
            - jnp.mean(scaled, axis=-1, keepdims=True)
            - unit * jnp.mean(scaled * unit, axis=-1, keepdims=True)
        )
        low = value.astype(bf16)
        if part % LANES:
            t_out[...] = low
        else:
            for o in range(count):
                t_out[:, columns_of(ids_ref[o], part)] = low[:, o * part : (o + 1) * part]
        add_rows(gg_out, grad * unit)
        add_rows(gc_out, grad)

    vec = shape((1, width), f32)
    result, gain_grad, bias_grad = call(
        body,
        [shape((total, width), bf16), vec, vec],
        (total // ROWS,),
        [row_spec(width)] * 3
        + [row_spec(kv), whole_spec(kv, width), row_spec(width), whole_spec(1, width)],
        [row_spec(width)] + [whole_spec(1, width)] * 2,
        [x_rel, part_own, part_other, keyval_grad, w_keyval_t, dh, gain],
        ids=[ids],
        flops=2 * total * width * kv,
        name="first_backward",
    )
    return put_back(result, ids, count), gain_grad, bias_grad


TILE = 256


def score_limits(lengths, token_count, first_place):
    doc_ends = jnp.cumsum(lengths)
    doc_starts = doc_ends - lengths
    places = (jnp.arange(token_count, dtype=jnp.int32) + first_place) % token_count
    doc_ids = jnp.sum((places[:, None] >= doc_ends[None, :]).astype(jnp.int32), axis=1)
    owners = doc_ids[:, None] == jnp.arange(lengths.shape[0], dtype=jnp.int32)[None, :]
    doc_begin = jnp.sum(jnp.where(owners, doc_starts[None, :], 0), axis=1)
    blocks = (places - doc_begin) // BLOCK
    seen = (doc_ids[:, None] == doc_ids[None, :]) & (blocks[None, :] <= blocks[:, None])
    seen_t = (doc_ids[None, :] == doc_ids[:, None]) & (blocks[:, None] <= blocks[None, :])
    pick = lambda s: jnp.where(s, shown_score, hidden_score).astype(f32)
    return pick(seen), pick(seen_t)


def attention_forward(queries, key_value, limits, heads):
    total = queries.shape[0]
    tiles = total // TILE
    c = score_scale * log2_e

    def body(q_ref, kv_ref, lim_ref, o_ref, lse_ref, top_ref):
        tile, head = pl.program_id(0), pl.program_id(1)
        k = kv_ref[:, :HD]
        v = kv_ref[:, HD:]
        s = lax.dot_general(
            q_ref[...], k, (((1,), (1,)), ((), ())), preferred_element_type=f32
        )
        s = jnp.minimum(s, lim_ref[...])
        m = jnp.max(s, axis=1, keepdims=True)
        p = jnp.exp2((s - m) * c)
        l = jnp.sum(p, axis=1, keepdims=True)
        o = jnp.dot(p.astype(bf16), v, preferred_element_type=f32)
        o_ref[...] = (o / l).astype(bf16)
        lane = lax.broadcasted_iota(jnp.int32, (TILE, LANES), 1)
        lse = m * c + jnp.log2(l)
        lse_ref[...] = jnp.where(lane == head, lse, lse_ref[...])

        @pl.when((tile == 0) & (head == 0))
        def _():
            top_ref[...] = jnp.full_like(top_ref, hidden_score)

        row = lax.broadcasted_iota(jnp.int32, (heads, LANES), 0)
        best = jnp.max(m, axis=0, keepdims=True) * score_scale
        top_ref[...] = jnp.where(row == head, jnp.maximum(top_ref[...], best), top_ref[...])

    return call(
        body,
        [shape((total, heads * HD), bf16), shape((total, LANES), f32), shape((heads, LANES), f32)],
        (tiles, heads),
        [
            pl.BlockSpec((TILE, HD), lambda i, h: (i, h)),
            pl.BlockSpec((total, 2 * HD), lambda i, h: (0, 0)),
            pl.BlockSpec((TILE, total), lambda i, h: (i, 0)),
        ],
        [
            pl.BlockSpec((TILE, HD), lambda i, h: (i, h)),
            pl.BlockSpec((TILE, LANES), lambda i, h: (i, 0)),
            pl.BlockSpec((heads, LANES), lambda i, h: (0, 0)),
        ],
        [queries, key_value, limits],
        flops=8 * total * total * HD * heads,
        name="attention_forward",
    )


def attention_backward(queries, grad_att, key_value, limits_t, lse_t, dot_t, heads):
    total = queries.shape[0]
    tiles = total // TILE
    c = score_scale * log2_e

    def body(q_ref, da_ref, kv_ref, lim_ref, lse_ref, dot_ref, dq_ref, dkv_ref):
        tile, head = pl.program_id(0), pl.program_id(1)
        k = kv_ref[:, :HD]
        v = kv_ref[:, HD:]
        q = q_ref[...]
        da = da_ref[...]
        nt = (((1,), (1,)), ((), ()))
        s = lax.dot_general(k, q, nt, preferred_element_type=f32)
        s = jnp.minimum(s, lim_ref[...])
        p = jnp.exp2(s * c - lse_ref[pl.ds(head, 1), :])
        dp = lax.dot_general(v, da, nt, preferred_element_type=f32)
        ds = (p * (dp - dot_ref[pl.ds(head, 1), :])).astype(bf16)
        dq = lax.dot_general(ds, k, (((0,), (0,)), ((), ())), preferred_element_type=f32)
        dq_ref[...] = (dq * score_scale).astype(bf16)

        @pl.when((tile == 0) & (head == 0))
        def _():
            dkv_ref[...] = jnp.zeros_like(dkv_ref)

        dkv_ref[:, :HD] += jnp.dot(ds, q, preferred_element_type=f32) * score_scale
        dkv_ref[:, HD:] += jnp.dot(p.astype(bf16), da, preferred_element_type=f32)

    return call(
        body,
        [shape((total, heads * HD), bf16), shape((total, 2 * HD), f32)],
        (tiles, heads),
        [
            pl.BlockSpec((TILE, HD), lambda i, h: (i, h)),
            pl.BlockSpec((TILE, HD), lambda i, h: (i, h)),
            pl.BlockSpec((total, 2 * HD), lambda i, h: (0, 0)),
            pl.BlockSpec((total, TILE), lambda i, h: (0, i)),
            pl.BlockSpec((heads, TILE), lambda i, h: (0, i)),
            pl.BlockSpec((heads, TILE), lambda i, h: (0, i)),
        ],
        [
            pl.BlockSpec((TILE, HD), lambda i, h: (i, h)),
            pl.BlockSpec((total, 2 * HD), lambda i, h: (0, 0)),
        ],
        [queries, grad_att, key_value, limits_t, lse_t, dot_t],
        flops=20 * total * total * HD * heads,
        name="attention_backward",
    )


def adam_values(gradient, weight, one, two, rate, decay):
    new_one = beta_one * one + (1.0 - beta_one) * gradient
    new_two = beta_two * two + (1.0 - beta_two) * gradient * gradient
    direction = (new_one * correct_one) / (jnp.sqrt(new_two * correct_two) + adam_eps)
    return new_one, new_two, weight - rate * (direction + decay * weight)


def to_tiles(flat, tiles_ref):
    for j in range(8):
        tiles_ref[:, j, :] = flat[:, j * LANES : (j + 1) * LANES]


def adam_in(gradient, weight, one, two, outer, start, full):
    rows, cols = gradient.shape
    step = 64
    base = (start // 1024).reshape(1)
    tall = pl.BlockSpec((step, 8, LANES), lambda i, j, b: (i, b[0] + j, 0))
    flat = pl.BlockSpec((step, 1024), lambda i, j, b: (i, j))
    args = [gradient, weight, one, two, outer]
    specs = [flat] + [tall] * 4
    aliases = {}
    if full is not None:
        aliases = {5: 0, 6: 1}
        args += list(full)
        specs += [pl.BlockSpec(memory_space=pl.ANY)] * 2

    def body(_, g_ref, w_ref, one_ref, two_ref, out_ref, *rest):
        one_out, two_out, delta_out, grad_tiles, delta_tiles = rest[-5:]
        to_tiles(g_ref[...].astype(f32), grad_tiles)
        new_one, new_two, stepped = adam_values(
            grad_tiles[...], w_ref[...], one_ref[...], two_ref[...], rate_matrix, weight_decay
        )
        one_out[...] = new_one
        two_out[...] = new_two
        delta_tiles[...] = out_ref[...] - stepped
        for j in range(8):
            delta_out[:, j * LANES : (j + 1) * LANES] = delta_tiles[:, j, :].astype(bf16)

    whole = shape(weight.shape, f32)
    return call(
        body,
        [whole, whole, shape((rows, cols), bf16)],
        (rows // step, cols // 1024),
        specs,
        [tall, tall, flat],
        args,
        ids=[base],
        scratch=[pltpu.VMEM((step, 8, LANES), f32)] * 2,
        aliases=aliases,
        name="adam_in",
        vmem=VMEM_MOST,
    )


def adam_out(gradient, weight, one, two, outer, start, full):
    rows, cols = gradient.shape
    step = 512
    base = (start // step).reshape(1)
    tall = pl.BlockSpec((step, cols), lambda i, b: (b[0] + i, 0))
    flat = pl.BlockSpec((step, cols), lambda i, b: (i, 0))
    args = [gradient, weight, one, two, outer]
    specs = [flat] + [tall] * 4
    aliases = {}
    if full is not None:
        aliases = {5: 0, 6: 1}
        args += list(full)
        specs += [pl.BlockSpec(memory_space=pl.ANY)] * 2

    def body(_, g_ref, w_ref, one_ref, two_ref, out_ref, *rest):
        one_out, two_out, delta_out = rest[-3:]
        new_one, new_two, stepped = adam_values(
            g_ref[...].astype(f32), w_ref[...], one_ref[...], two_ref[...], rate_matrix,
            weight_decay,
        )
        one_out[...] = new_one
        two_out[...] = new_two
        delta_out[...] = (out_ref[...] - stepped).astype(bf16)

    whole = shape(weight.shape, f32)
    return call(
        body,
        [whole, whole, shape((rows, cols), bf16)],
        (rows // step,),
        specs,
        [tall, tall, flat],
        args,
        ids=[base],
        aliases=aliases,
        name="adam_out",
        vmem=VMEM_MOST,
    )


def outer_values(mean, momentum, outer):
    velocity = outer_beta * momentum + mean
    return velocity, outer - outer_rate * (mean + outer_beta * velocity)


def outer_in(both, momentum, outer, factor, start, full):
    _, rows, cols = both.shape
    step = 64
    base = (start // 1024).reshape(1)
    tall = pl.BlockSpec((step, 8, LANES), lambda i, j, b: (i, b[0] + j, 0))
    flat = pl.BlockSpec((2, step, 1024), lambda i, j, b: (0, i, j))
    wide = pl.BlockSpec((step, 1024), lambda i, j, b: (i, b[0] + j))
    args = [both, momentum, outer]
    specs = [flat, tall, tall]
    if factor is not None:
        args.append(factor)
        specs.append(pl.BlockSpec((8, LANES), lambda i, j, b: (0, 0)))
    aliases = {}
    if full is not None:
        aliases = {len(args) + k: k for k in range(4)}
        args += list(full)
        specs += [pl.BlockSpec(memory_space=pl.ANY)] * 4

    def body(_, both_ref, mom_ref, out_ref, *rest):
        mean_out, vel_out, new_out, copy_out, mean_tiles, new_tiles = rest[-6:]
        to_tiles((both_ref[0].astype(f32) + both_ref[1].astype(f32)) * 0.5, mean_tiles)
        mean = mean_tiles[...]
        velocity, fresh = outer_values(mean, mom_ref[...], out_ref[...])
        if factor is not None:
            fresh = fresh * rest[0][...][None]
        mean_out[...] = mean
        vel_out[...] = velocity
        new_out[...] = fresh
        new_tiles[...] = fresh
        for j in range(8):
            copy_out[:, j * LANES : (j + 1) * LANES] = new_tiles[:, j, :].astype(bf16)

    whole = shape(outer.shape, f32)
    return call(
        body,
        [whole, whole, whole, shape((rows, outer.shape[1] * LANES), bf16)],
        (rows // step, cols // 1024),
        specs,
        [tall, tall, tall, wide],
        args,
        ids=[base],
        scratch=[pltpu.VMEM((step, 8, LANES), f32)] * 2,
        aliases=aliases,
        name="outer_in",
        vmem=VMEM_MOST,
    )


def outer_out(both, momentum, outer, start, full):
    _, rows, cols = both.shape
    step = 512
    base = (start // step).reshape(1)
    tall = pl.BlockSpec((step, cols), lambda i, b: (b[0] + i, 0))
    flat = pl.BlockSpec((2, step, cols), lambda i, b: (0, i, 0))
    args = [both, momentum, outer]
    specs = [flat, tall, tall]
    aliases = {}
    if full is not None:
        aliases = {3 + k: k for k in range(4)}
        args += list(full)
        specs += [pl.BlockSpec(memory_space=pl.ANY)] * 4

    def body(_, both_ref, mom_ref, out_ref, *rest):
        mean_out, vel_out, new_out, copy_out = rest[-4:]
        mean = (both_ref[0].astype(f32) + both_ref[1].astype(f32)) * 0.5
        velocity, fresh = outer_values(mean, mom_ref[...], out_ref[...])
        mean_out[...] = mean
        vel_out[...] = velocity
        new_out[...] = fresh
        copy_out[...] = fresh.astype(bf16)

    whole = shape(outer.shape, f32)
    return call(
        body,
        [whole, whole, whole, shape(outer.shape, bf16)],
        (rows // step,),
        specs,
        [tall] * 4,
        args,
        ids=[base],
        aliases=aliases,
        name="outer_out",
        vmem=VMEM_MOST,
    )


class Wire:
    def __init__(self, window):
        self.window, self.landed = window, []

    def send(self, block, axis, pairs):
        if len(self.landed) >= self.window:
            block, _ = lax.optimization_barrier((block, self.landed[-self.window]))
        arrived = lax.ppermute(block, axis, pairs)
        self.landed.append(arrived)
        return arrived


class Links:
    def __init__(self, count, splits, window):
        self.levels = count.bit_length() - 1
        self.far = ([1] + [1 << b for b in range(3, self.levels)])[: self.levels - 2]
        places = range(count)
        middle = [i for i in places if (i >> 1 ^ i >> 2) & 1]
        outer = [i for i in places if i not in middle]
        self.pair = [(i, i ^ 2) for i in places]
        self.inward = [(i, i ^ 2) for i in outer]
        self.outward = [(i, i ^ 2) for i in middle]
        self.between = [(i, i ^ 6) for i in middle]
        self.beside = [[(i, i ^ mask) for i in places] for mask in self.far]
        self.mirror = [(i, i ^ 6) for i in places]
        self.cores = [(i, (i + 1) % splits) for i in range(splits)]
        self.wire = Wire(window)

    def flips(self, across):
        masks = [2, across] + self.far
        table = []
        for o in range(1 << self.levels):
            flip = 0
            for level, mask in enumerate(masks):
                if o >> level & 1:
                    flip ^= mask
            table.append(flip)
        return table

    def to_side(self, block, pairs):
        return self.wire.send(block, "dp", pairs)

    def to_middle(self, block):
        return self.wire.send(block, "dp", self.between)

    def to_far(self, block, level):
        return self.wire.send(block, "dp", self.beside[level - 2])

    def to_pair(self, block):
        return self.wire.send(block, "dp", self.pair)

    def across(self, block):
        return lax.ppermute(block, "tensor", self.cores)

    def pair_now(self, block):
        return lax.ppermute(block, "dp", self.pair)


def after(value, *earlier):
    return lax.optimization_barrier((value, *earlier))[0]


class Order:
    def __init__(self):
        self.last = ()

    def tie(self, value):
        return after(value, *self.last) if self.last else value

    def mark(self, *values):
        self.last = values
        return values[0]


class Gathered:
    def __init__(self, links, axis, mine, other=None):
        self.links, self.axis, self.mine, self.other = links, axis, mine, other
        self.held = {}

    def join(self, *blocks):
        return jnp.concatenate(blocks, axis=self.axis)

    def near(self):
        give = self.mine if self.other is None else self.other
        self.held[0] = self.join(self.mine, self.links.to_side(give, self.links.pair))

    def inward(self):
        if self.other is not None:
            self.passed = self.links.to_side(self.mine, self.links.inward)

    def middle(self):
        if self.other is None:
            self.relay = self.direct = self.links.to_middle(self.held[0])
        else:
            self.relay = self.links.to_middle(self.join(self.other, self.passed))

    def middle_rest(self):
        self.direct = self.links.to_middle(self.held[0])

    def outward(self):
        self.relayed = self.links.to_side(self.relay, self.links.outward)

    def join_far(self):
        self.held[2] = self.direct + self.relayed

    def far(self, level, o):
        self.held[o + (1 << level)] = self.links.to_far(self.held[o], level)

    def whole(self):
        for level in range(2, self.links.levels):
            for o in range(0, 1 << level, 2):
                if o + (1 << level) not in self.held:
                    self.far(level, o)
        return self.join(*[self.held[o] for o in sorted(self.held)])


class Reduced:
    def __init__(self, links, order, axis, size, halved, part):
        self.links, self.order, self.axis, self.size = links, order, axis, size
        self.halved, self.part = halved, part
        self.landed = {}

    def pair_sum(self, o):
        total = self.part(o, 2)
        for block in self.landed.pop(o, []):
            total = total + block.astype(f32)
        return self.order.mark(total.astype(bf16))

    def one(self, block, o):
        return lax.slice_in_dim(
            block, o * self.size, (o + 1) * self.size, axis=self.axis
        ).astype(f32)

    def far(self, level, o):
        arrived = self.links.to_far(self.pair_sum(o), level)
        self.landed.setdefault(o - (1 << level), []).append(arrived)
        return arrived

    def far_rest(self, done):
        arrived = None
        for level in range(self.links.levels - 1, 1, -1):
            for o in reversed(range(1 << level, 2 << level, 2)):
                if (level, o) not in done:
                    arrived = self.far(level, o)
        return arrived

    def inward(self):
        self.ahead = self.pair_sum(2)
        self.passed = self.links.to_side(self.ahead, self.links.inward)
        if self.halved:
            self.direct = self.links.to_middle(self.ahead)

    def middle(self):
        if self.halved:
            self.relay = self.links.to_middle(self.order.tie(self.passed))
        else:
            both = self.order.mark(self.order.tie(self.ahead) + self.passed)
            self.direct = self.links.to_middle(both)

    def single(self, o):
        total = self.part(o, 1)
        for block in self.landed[0] + [self.direct]:
            total = total + self.one(block, o)
        return total

    def near(self):
        value = self.order.mark(self.single(1).astype(bf16))
        self.theirs = self.links.to_side(value, self.links.pair).astype(f32)

    def outward(self):
        value = self.one(self.order.tie(self.relay), 1).astype(bf16)
        self.last = self.links.to_side(value, self.links.outward).astype(f32)

    def result(self):
        if not self.halved:
            return self.order.mark(self.single(0) + self.theirs), None
        own = self.order.mark(self.single(0) + self.last)
        return own, self.theirs + self.one(self.relay, 0)


def local(
    tokens,
    doc_lengths,
    cotangent,
    inner_in,
    inner_out,
    inner_shared,
    first_in,
    first_out,
    first_shared,
    second_in,
    second_out,
    second_shared,
    outer_in_w,
    outer_out_w,
    outer_shared,
    momentum_in,
    momentum_out,
    momentum_shared,
):
    splits = lax.axis_size("tensor")
    count = lax.axis_size("dp")
    split = lax.axis_index("tensor")
    place = lax.axis_index("dp")
    total, width = tokens.shape
    part = width // count
    local_cols = inner_in.shape[3]
    shared_cols = inner_shared.shape[2]
    heads = HEADS // splits
    qcols = heads * HD
    hidden = local_cols - qcols
    vec = 2 * HD
    own_cols = part // splits
    mine = total // 2

    links = Links(count, splits, 4)
    across = links.across
    levels = links.levels
    side = ((place >> 1) ^ (place >> 2)) & 1
    from_outer, from_middle = (jnp.array(links.flips(m), jnp.int32) for m in (4, 6))
    ids = (place ^ jnp.where(side == 0, from_outer, from_middle)).astype(jnp.int32)
    swap_group = [(0, 1), (1, 0)]
    split_id = split.astype(jnp.int32).reshape(1)

    def tall(array):
        return array.reshape(part, local_cols // LANES, LANES)

    w_in = tall(inner_in)
    w_out = inner_out.reshape(local_cols, part)
    shared_rows = lax.all_gather(inner_shared[0], ("dp", "tensor"), axis=0, tiled=True)

    half = hidden // 2
    flat_in = inner_in.reshape(part, local_cols)

    def sides(low, high):
        return (
            jnp.where(side == 0, low, high).astype(bf16),
            jnp.where(side == 0, high, low).astype(bf16),
        )

    block_q = flat_in[:, :qcols].astype(bf16)
    block_o = w_out[:qcols].astype(bf16)
    up_sides = sides(flat_in[:, qcols : qcols + half], flat_in[:, qcols + half :])
    down_sides = sides(w_out[qcols : qcols + half], w_out[qcols + half :])
    got_query = Gathered(links, 0, block_q)
    got_attn = Gathered(links, 1, block_o)
    got_up = Gathered(links, 0, *up_sides)
    got_down = Gathered(links, 1, *down_sides)
    shared_t = shared_rows.T
    shared_rel = pick_blocks(shared_t, ids, part, count, False)
    w_keyval_t = shared_rel[:vec].astype(bf16)
    vectors_t, vectors = shared_t[vec:], shared_rel[vec:]
    gain_one, bias_one, gain_two, bias_two = (vectors[k : k + 1] for k in range(4))
    bias_out, bias_down = vectors[5:6], vectors[6:7]
    bias_query = lax.dynamic_slice_in_dim(vectors_t[4], split * qcols, qcols)
    bias_up = lax.dynamic_slice_in_dim(
        vectors_t[7:].reshape(FF), split * hidden + side * half, half
    )

    nt = (((1,), (1,)), ((), ()))
    tn = (((0,), (0,)), ((), ()))

    def mm(a, b, dims=(((1,), (0,)), ((), ()))):
        return lax.dot_general(a, b, dims, preferred_element_type=f32)

    def block(array, o, blocks):
        return array[:, o * part : (o + blocks) * part]

    def both_rows(rows):
        return lax.all_gather(rows, "tensor", axis=0, tiled=True)

    def far(weight, o):
        if levels == 3:
            weight.far(2, o)

    cot_own, cot_pair, grad_bias_down = cotangent_order(cotangent, ids, split_id, count)
    got_query.near()
    got_query.middle()
    far(got_query, 0)
    got_attn.near()
    got_down.near()
    got_down.inward()
    got_attn.middle()
    far(got_attn, 0)
    got_query.outward()
    got_query.join_far()
    far(got_query, 2)
    far(got_down, 0)
    got_attn.outward()
    got_attn.join_far()
    got_down.middle()
    got_up.near()
    far(got_attn, 2)
    w_query = got_query.whole()
    w_attn = got_attn.whole()
    got_up.inward()
    got_down.outward()
    got_down.middle_rest()
    got_down.join_far()
    far(got_up, 0)
    cot_theirs = links.to_pair(swap_small(cot_pair, part))
    got_up.middle()
    far(got_down, 2)
    w_down = got_down.whole()
    got_up.outward()
    got_up.middle_rest()
    got_up.join_far()

    x_rel, normed = first_norm(tokens, ids, split_id, gain_one, bias_one, count)
    limits, limits_t = score_limits(doc_lengths[0], total, split * mine)
    key_value = mm(normed, w_keyval_t, nt).astype(bf16)
    queries = (mm(normed, w_query) + bias_query).astype(bf16)
    attended, log_totals, tops = attention_forward(queries, key_value, limits, heads)
    attn_give = mm(attended[mine:], w_attn).astype(bf16)
    attn_keep = mm(attended[:mine], w_attn).astype(bf16)
    attn_other = across(attn_give)
    middle, normed_two, normed_pair = middle_norm(
        x_rel, attn_keep, attn_other, bias_out, gain_two, bias_two, part
    )
    normed_theirs = links.to_pair(swap_small(normed_pair, part))
    far(got_up, 2)
    w_up = got_up.whole()
    normed_all = both_rows(jnp.concatenate([normed_two, normed_theirs], axis=0))
    cot_all = both_rows(jnp.concatenate([cot_own, cot_theirs], axis=0))
    hidden_grad = mm(cot_all, w_down, nt).astype(bf16)
    acts, grad_pre, grad_bias_up = hidden_units(normed_all, w_up, bias_up[None], hidden_grad)

    links.wire.window = 1 << 30
    order = Order()
    tie, mark = order.tie, order.mark
    sum_down = Reduced(
        links, order, 1, part, True, lambda o, b: mm(tie(acts), block(cot_all, o, b), tn)
    )
    sum_up = Reduced(
        links, order, 0, part, True, lambda o, b: mm(block(normed_all, o, b), tie(grad_pre), tn)
    )
    early = [(2, 6)] if levels == 3 else []
    for level, o in early:
        sum_down.far(level, o)
    pre_give = lax.dynamic_slice_in_dim(grad_pre, (1 - split) * 2 * mine, 2 * mine)
    pre_keep = lax.dynamic_slice_in_dim(grad_pre, split * 2 * mine, 2 * mine)
    two_give = mark(mm(pre_give, tie(w_up), nt).astype(bf16))
    two_other = across(two_give)
    down_landed = sum_down.far_rest(early)
    two_keep = mark(mm(pre_keep, tie(w_up), nt).astype(bf16))
    two_theirs = two_keep[mine:].astype(f32) + two_other[mine:].astype(f32)
    two_theirs = mark(swap_small(two_theirs.astype(bf16), part))
    two_pair = links.pair_now(two_theirs)
    for level, o in early:
        sum_up.far(level, o)
    sum_down.inward()
    dh, dh_mine, grad_gain_two, grad_bias_two, grad_bias_out = middle_backward(
        middle, tie(two_keep), two_other, two_pair, cot_own, gain_two, part
    )
    mark(dh_mine)
    dh_low = jnp.concatenate([dh_mine, across(dh_mine)], axis=0)
    grad_att = mark(mm(dh_low, w_attn, nt).astype(bf16))
    dots = jnp.sum(
        (grad_att.astype(f32) * attended.astype(f32)).reshape(total, heads, HD), axis=2
    )
    grad_queries, kv_part = attention_backward(
        queries, after(grad_att, down_landed), key_value, limits_t, log_totals.T[:heads], dots.T,
        heads,
    )
    mark(grad_queries)
    up_landed = sum_up.far_rest(early)
    one_give = mark(mm(grad_queries[mine:], tie(w_query), nt).astype(bf16))
    one_other = across(one_give)
    kv_other = across(kv_part[mine:])
    sum_down.middle()
    sum_down.near()
    sum_up.inward()
    sum_attn = Reduced(
        links, order, 1, part, False, lambda o, b: mm(tie(attended), block(dh_low, o, b), tn)
    )
    sum_attn.far_rest([])
    one_keep = mark(mm(grad_queries[:mine], tie(w_query), nt).astype(bf16))
    kv_low = (kv_part[:mine] + kv_other).astype(bf16)
    grad_mine, grad_gain_one, grad_bias_one = first_backward(
        x_rel, after(one_keep, up_landed), one_other, kv_low, w_keyval_t, dh, gain_one, ids, count
    )
    mark(grad_mine)
    tokens_grad = both_rows(grad_mine)
    sum_query = Reduced(
        links, order, 0, part, False, lambda o, b: mm(block(normed, o, b), tie(grad_queries), tn)
    )
    sum_query.far_rest([])
    sum_up.middle()
    sum_down.outward()

    grad_keyval_t = mm(tie(kv_low), normed[:mine], tn)
    grad_bias_query = jnp.sum(grad_queries.astype(f32), axis=0)
    spread = jnp.concatenate(
        [
            lax.dynamic_update_slice_in_dim(
                jnp.zeros((width,), f32), grad_bias_query, split * qcols, 0
            ),
            lax.dynamic_update_slice_in_dim(
                jnp.zeros((FF,), f32), grad_bias_up[0], split * hidden + side * half, 0
            ),
        ]
    ).reshape(1 + FF // width, width)
    near = jnp.concatenate(
        [grad_keyval_t, grad_gain_one, grad_bias_one, grad_gain_two, grad_bias_two, grad_bias_out,
         grad_bias_down],
        axis=0,
    )
    steps = jnp.arange(count, dtype=jnp.int32)
    turned = jnp.where((side == 0) & ((steps & 2) != 0), steps ^ 1, steps)
    mirrored = (place ^ from_middle).astype(jnp.int32)

    def pieces(core):
        a = pick_blocks(near, turned * splits + core, own_cols, count, True)
        b = pick_blocks(spread, mirrored * splits + core, own_cols, count, True)
        return jnp.concatenate([a[:, : vec + 4], b[:, :1], a[:, vec + 4 :], b[:, 1:]], axis=1)

    shared_give = mark(pieces(1 - split))
    shared_other = across(shared_give)

    one_in, two_in = tall(first_in), tall(second_in)
    one_out, two_out = (a.reshape(local_cols, part) for a in (first_out, second_out))
    base_in, mom_in = tall(outer_in_w), tall(momentum_in)
    base_out, mom_out = (a.reshape(local_cols, part) for a in (outer_out_w, momentum_out))
    starts = [qcols + side * half, qcols + (1 - side) * half]
    zero = jnp.zeros((), jnp.int32)
    gathered = []

    def groups(delta):
        both = lax.all_gather(after(delta, *gathered[-1:]), "group", axis=0)
        gathered.append(both)
        return both

    def adam_down(gradient, start, full):
        *full, delta = adam_out(tie(gradient), w_out, one_out, two_out, base_out, start, full)
        mark(delta)
        return full, delta

    def adam_up(gradient, start, full):
        *full, delta = adam_in(tie(gradient), w_in, one_in, two_in, base_in, start, full)
        mark(delta)
        return full, delta

    red_down = sum_down.result()
    full_out, delta_down = adam_down(red_down[0], starts[0], None)
    both_down = [groups(delta_down)]
    sum_attn.inward()
    full_out, delta_down = adam_down(red_down[1], starts[1], full_out)
    both_down.append(groups(delta_down))
    sum_up.near()
    sum_query.inward()

    peers = across(tie(tops))
    peak = jnp.where(
        split == 0, jnp.concatenate([tops, peers]), jnp.concatenate([peers, tops])
    )
    peak = jnp.maximum(peak, lax.ppermute(peak, "group", swap_group))
    for pairs in [links.pair, links.mirror] + links.beside:
        peak = jnp.maximum(peak, lax.ppermute(peak, "dp", pairs))
    clip_rows = clip_limit / jnp.maximum(peak, clip_limit)
    clip_own = lax.dynamic_slice_in_dim(clip_rows, split * heads, heads)

    down_part = mark(mm(tie(acts), w_down).astype(bf16))
    down_sum = lax.psum_scatter(down_part, "tensor", scatter_dimension=0, tiled=True)
    sum_attn.middle()
    sum_up.outward()
    red_shared = pieces(split) + shared_other
    cube = list(reversed([links.pair, links.mirror] + links.beside))
    for pairs in cube[:-2]:
        keep = red_shared.shape[0] // 2
        red_shared = red_shared[:keep] + lax.ppermute(red_shared[keep:], "dp", pairs)
    sum_query.middle()
    new_out = outer_out(both_down[0], mom_out, after(base_out, *order.last), starts[0], None)
    mark(new_out[0])
    red_up = sum_up.result()
    full_in, delta_up = adam_up(red_up[0], starts[0], None)
    both_up = [groups(delta_up)]
    down_pair = links.to_pair(swap_small(down_sum[mine:], part))
    last_middle = after(red_up[1], sum_attn.direct, sum_query.direct, clip_rows)
    full_in, delta_up = adam_up(last_middle, starts[1], full_in)
    both_up.append(groups(delta_up))
    sum_query.near()
    sum_attn.near()
    for pairs in cube[-2:]:
        keep = red_shared.shape[0] // 2
        red_shared = red_shared[:keep] + lax.ppermute(red_shared[keep:], "dp", pairs)
    red_shared = red_shared[0]
    new_out = outer_out(both_down[1], mom_out, tie(base_out), starts[1], new_out)
    mark(new_out[0])
    block_out = both_rows(
        block_result(middle, down_sum, down_pair, bias_down, ids, count)
    )
    red_query = sum_query.result()[0]
    full_in, delta_query = adam_up(red_query, zero, full_in)
    other_query = lax.ppermute(delta_query, "group", swap_group)
    red_attn = sum_attn.result()[0]
    full_out, delta_attn = adam_down(red_attn, zero, full_out)
    other_attn = lax.ppermute(delta_attn, "group", swap_group)
    new_in = outer_in(both_up[0], mom_in, tie(base_in), None, starts[0], None)
    new_in = outer_in(both_up[1], mom_in, base_in, None, starts[1], new_in)
    both = jnp.stack([delta_attn, other_attn])
    new_out = outer_out(both, mom_out, base_out, zero, new_out)
    both = jnp.stack([delta_query, other_query])
    new_in = outer_in(both, mom_in, base_in, clip_own, zero, new_in)

    ids_col = jnp.arange(shared_cols, dtype=jnp.int32)[:, None]
    one_sh, two_sh, stepped = adam_values(
        red_shared,
        inner_shared[0].T,
        first_shared[0].T,
        second_shared[0].T,
        jnp.where(ids_col < vec, rate_matrix, rate_vector),
        jnp.where(ids_col < vec, weight_decay, 0.0),
    )
    base_sh = outer_shared.T
    delta = (base_sh - stepped).astype(bf16)
    mean_sh = (delta.astype(f32) + lax.ppermute(delta, "group", swap_group).astype(f32)) * 0.5
    vel_sh, fresh_sh = outer_values(mean_sh, momentum_shared.T, base_sh)
    row_ids = (place * splits + split) * own_cols + jnp.arange(own_cols, dtype=jnp.int32)
    clip_vec = clip_rows[:, 0]
    row_clip = jnp.sum(
        jnp.where((row_ids // HD)[None, :] == jnp.arange(HEADS)[:, None], clip_vec[:, None], 0.0),
        axis=0,
    )
    fresh_sh = fresh_sh * jnp.where(ids_col == vec + 4, row_clip[None, :], 1.0)

    shape_in, shape_out = (part, 1, local_cols), (1, local_cols, part)
    mean_in, vel_in, fresh_in, copy_in = new_in
    mean_out, vel_out, fresh_out, copy_out = new_out
    return (
        block_out,
        tokens_grad,
        clip_vec,
        full_in[0].reshape((1,) + shape_in),
        full_out[0].reshape((1,) + shape_out),
        one_sh.T[None],
        full_in[1].reshape((1,) + shape_in),
        full_out[1].reshape((1,) + shape_out),
        two_sh.T[None],
        mean_in.reshape(shape_in),
        mean_out.reshape(shape_out),
        mean_sh.T,
        vel_in.reshape(shape_in),
        vel_out.reshape(shape_out),
        vel_sh.T,
        fresh_in.reshape(shape_in),
        fresh_out.reshape(shape_out),
        fresh_sh.T,
        copy_in.reshape(shape_in),
        copy_out.reshape(shape_out),
        fresh_sh.T.astype(bf16),
    )


def solution(mesh):
    rows = P(("group", "dp"), None)
    inner = [P("group", "dp", "tensor", None), P("group", "tensor", None, "dp"),
             P("group", ("dp", "tensor"), None)]
    outer = [P("dp", "tensor", None), P("tensor", None, "dp"), P(("dp", "tensor"), None)]
    in_specs = tuple([rows] * 3 + inner * 3 + outer * 2)
    out_specs = tuple([rows] * 2 + [P()] + inner * 2 + outer * 4)
    return jax.shard_map(local, mesh=mesh, in_specs=in_specs, out_specs=out_specs, check_vma=False)
```

```python
import jax
import jax.numpy as jnp
from jax import lax
from jax.experimental import pallas as pl
from jax.experimental.pallas import tpu as pltpu
from jax.sharding import PartitionSpec as P

HEADS = 16
HD = 128
FF = 8192
BLOCK = 256
STEP = 10

norm_eps = 1e-05
hidden_score = -1e30
shown_score = 3e38
beta_one = 0.9
beta_two = 0.95
adam_eps = 1e-08
rate_matrix = 0.02
rate_vector = 0.2
weight_decay = 0.1
outer_beta = 0.9
outer_rate = 0.7
clip_limit = 5.0
score_scale = HD ** (-0.5)
log2_e = 1.4426950408889634
correct_one = 1.0 / (1.0 - beta_one**STEP)
correct_two = 1.0 / (1.0 - beta_two**STEP)

f32 = jnp.float32
bf16 = jnp.bfloat16
ROWS = 128
LANES = 128
VMEM_LIMIT = 40 * 1024 * 1024
VMEM_MOST = 58 * 1024 * 1024


def shape(dims, dtype):
    return jax.ShapeDtypeStruct(dims, dtype)


def call(body, out_shape, grid, in_specs, out_specs, args, *, ids=(), scratch=(), aliases=None,
         flops=0, name=None, vmem=VMEM_LIMIT):
    outs = out_shape if isinstance(out_shape, (list, tuple)) else [out_shape]
    moved = sum(a.size * a.dtype.itemsize for a in args)
    moved += sum(o.size * o.dtype.itemsize for o in outs)
    return pl.pallas_call(
        body,
        out_shape=out_shape,
        grid_spec=pltpu.PrefetchScalarGridSpec(
            num_scalar_prefetch=len(ids),
            grid=grid,
            in_specs=in_specs,
            out_specs=out_specs,
            scratch_shapes=list(scratch),
        ),
        input_output_aliases={len(ids) + k: v for k, v in (aliases or {}).items()},
        compiler_params=pltpu.CompilerParams(vmem_limit_bytes=vmem),
        cost_estimate=pl.CostEstimate(flops=flops, bytes_accessed=moved, transcendentals=0),
        name=name,
    )(*ids, *args)


def pick_blocks(array, block_ids, width, count, stacked):
    rows = array.shape[0]
    if width % LANES:
        taken = jnp.take(array.reshape(rows, -1, width), block_ids, axis=1)
        return taken.transpose(1, 0, 2) if stacked else taken.reshape(rows, count * width)

    def body(ids_ref, in_ref, out_ref):
        if stacked:
            out_ref[0] = in_ref[...]
        else:
            out_ref[...] = in_ref[...]

    if stacked:
        out, spec = shape((count, rows, width), array.dtype), pl.BlockSpec(
            (1, rows, width), lambda j, ids: (j, 0, 0)
        )
    else:
        out, spec = shape((rows, count * width), array.dtype), pl.BlockSpec(
            (rows, width), lambda j, ids: (0, j)
        )
    return call(
        body, out, (count,), [pl.BlockSpec((rows, width), lambda j, ids: (0, ids[j]))], spec,
        [array], ids=[block_ids], name="pick_blocks",
    )


def columns_of(block_id, width):
    return pl.ds(pl.multiple_of(block_id * width, width), width)


def placing(array, ids, count):
    part = array.shape[1] // count
    if part % LANES == 0:
        return array, count, part
    return pick_blocks(array, ids, part, count, False), 0, part


def put_back(array, ids, count):
    part = array.shape[1] // count
    if part % LANES == 0:
        return array
    back = jnp.sum(
        jnp.where(ids[None, :] == jnp.arange(count)[:, None], jnp.arange(count)[None, :], 0), axis=1
    ).astype(jnp.int32)
    return pick_blocks(array, back, part, count, False)


def norm_stats(rows):
    mean = jnp.mean(rows, axis=-1, keepdims=True)
    centered = rows - mean
    inv = lax.rsqrt(jnp.mean(centered * centered, axis=-1, keepdims=True) + norm_eps)
    return centered * inv, inv


def row_spec(cols, rows=ROWS):
    return pl.BlockSpec((rows, cols), lambda i, *ids: (i, 0))


def turned_spec(cols, blocks):
    return pl.BlockSpec(
        (ROWS, cols), lambda i, ids, split: ((i + split[0] * (blocks // 2)) % blocks, 0)
    )


def whole_spec(rows, cols):
    return pl.BlockSpec((rows, cols), lambda i, *ids: (0, 0))


def first_norm(tokens, ids, split, gain, bias, count):
    total, width = tokens.shape
    tokens, moved, part = placing(tokens, ids, count)

    def body(ids_ref, split_ref, x_ref, g_ref, c_ref, x_out, n_out):
        for o in range(moved):
            x_out[:, o * part : (o + 1) * part] = x_ref[:, columns_of(ids_ref[o], part)]
        if not moved:
            x_out[...] = x_ref[...]
        unit, _ = norm_stats(x_out[...].astype(f32))
        n_out[...] = (unit * g_ref[...] + c_ref[...]).astype(bf16)

    return call(
        body,
        [shape((total, width), bf16)] * 2,
        (total // ROWS,),
        [turned_spec(width, total // ROWS), whole_spec(1, width), whole_spec(1, width)],
        [row_spec(width)] * 2,
        [tokens, gain, bias],
        ids=[ids, split],
        name="first_norm",
    )


def first_spec(cols, blocks):
    return pl.BlockSpec((ROWS, cols), lambda i, *ids: (jnp.minimum(i, blocks - 1), 0))


def swapped(values, part):
    if part % LANES:
        return values
    blocks = [values[:, o : o + part] for o in range(0, values.shape[1], part)]
    return jnp.concatenate([blocks[pair_of(o)] for o in range(len(blocks))], axis=1)


def pair_of(o):
    return o if o & 2 else o ^ 1


def swap_small(values, part):
    if part % LANES == 0:
        return values
    blocks = [values[:, o : o + part] for o in range(0, values.shape[1], part)]
    return jnp.concatenate([blocks[pair_of(o)] for o in range(len(blocks))], axis=1)


def cotangent_order(cotangent, ids, split, count):
    total, width = cotangent.shape
    cotangent, moved, part = placing(cotangent, ids, count)
    mine = total // ROWS // 2

    def body(ids_ref, split_ref, c_ref, c_out, pair_out, sum_out):
        for o in range(moved):
            c_out[:, o * part : (o + 1) * part] = c_ref[:, columns_of(ids_ref[o], part)]
        if not moved:
            c_out[...] = c_ref[...]
        pair_out[...] = swapped(c_out[...], part)
        add_rows(sum_out, c_out[...].astype(f32))

    return call(
        body,
        [shape((total // 2, width), bf16)] * 2 + [shape((1, width), f32)],
        (mine,),
        [turned_spec(width, total // ROWS)],
        [row_spec(width)] * 2 + [whole_spec(1, width)],
        [cotangent],
        ids=[ids, split],
        name="cotangent_order",
    )


def hidden_units(rows, weight, bias, hidden_grad):
    total, depth = rows.shape
    cols = weight.shape[1]
    high, wide, sub = 256, 1024, 256
    curve, cube = (2.0 / 3.141592653589793) ** 0.5, 0.044715

    def body(n_ref, w_ref, b_ref, dz_ref, z_out, du_out, sum_out):
        first = pl.program_id(1) == 0
        for c in range(0, wide, sub):
            at = slice(c, c + sub)
            u = jnp.dot(n_ref[...], w_ref[:, at], preferred_element_type=f32) + b_ref[:, at]
            square = u * u
            t = jnp.tanh(curve * u * (1.0 + cube * square))
            z_out[:, at] = (0.5 * u * (1.0 + t)).astype(bf16)
            slope = 0.5 * (1.0 + t) + (0.5 * curve) * u * (1.0 - t * t) * (
                1.0 + (3.0 * cube) * square
            )
            du = (slope * dz_ref[:, at].astype(f32)).astype(bf16)
            du_out[:, at] = du
            total_du = jnp.sum(du.astype(f32), axis=0, keepdims=True)
            sum_out[:, at] = jnp.where(first, total_du, sum_out[:, at] + total_du)

    tile = pl.BlockSpec((high, wide), lambda j, i: (i, j))
    line = pl.BlockSpec((1, wide), lambda j, i: (0, j))
    return call(
        body,
        [shape((total, cols), bf16)] * 2 + [shape((1, cols), f32)],
        (cols // wide, total // high),
        [
            pl.BlockSpec((high, depth), lambda j, i: (i, 0)),
            pl.BlockSpec((depth, wide), lambda j, i: (0, j)),
            line,
            tile,
        ],
        [tile, tile, line],
        [rows, weight, bias, hidden_grad],
        flops=2 * total * depth * cols,
        name="hidden_units",
    )


def add_rows(sum_ref, values):
    @pl.when(pl.program_id(0) == 0)
    def _():
        sum_ref[...] = jnp.zeros_like(sum_ref)

    sum_ref[...] += jnp.sum(values, axis=0, keepdims=True)


def middle_norm(x_rel, part_own, part_other, bias_out, gain, bias, part):
    total, width = part_other.shape

    def body(x_ref, a_ref, b_ref, bo_ref, g_ref, c_ref, h_out, n_out, pair_out):
        mid = x_ref[...].astype(f32) + (
            a_ref[...].astype(f32) + b_ref[...].astype(f32)
        ) + bo_ref[...]
        h_out[...] = mid
        unit, _ = norm_stats(mid)
        low = (unit * g_ref[...] + c_ref[...]).astype(bf16)
        n_out[...] = low
        pair_out[...] = swapped(low, part)

    return call(
        body,
        [shape((total, width), f32)] + [shape((total, width), bf16)] * 2,
        (total // ROWS,),
        [row_spec(width)] * 3 + [whole_spec(1, width)] * 3,
        [row_spec(width)] * 3,
        [x_rel, part_own, part_other, bias_out, gain, bias],
        name="middle_norm",
    )


def block_result(middle, part_own, part_pair, bias_down, ids, count):
    total, width = middle.shape
    part = width // count

    def body(ids_ref, h_ref, a_ref, p_ref, b2_ref, out_ref):
        value = a_ref[...].astype(f32) + swapped(p_ref[...], part).astype(f32)
        value = (h_ref[...] + value + b2_ref[...]).astype(bf16)
        if part % LANES:
            out_ref[...] = value
        else:
            for o in range(count):
                out_ref[:, columns_of(ids_ref[o], part)] = value[:, o * part : (o + 1) * part]

    result = call(
        body,
        shape((total, width), bf16),
        (total // ROWS,),
        [row_spec(width)] * 3 + [whole_spec(1, width)],
        row_spec(width),
        [middle, part_own, part_pair, bias_down],
        ids=[ids],
        name="block_result",
    )
    return put_back(result, ids, count)


def middle_backward(middle, part_own, part_other, part_pair, cot_rel, gain, part):
    total, width = middle.shape

    def body(h_ref, a_ref, b_ref, p_ref, dy_ref, g_ref, dh_out, low_out, gg_out, gc_out, gbo_out):
        unit, inv = norm_stats(h_ref[...])
        grad = a_ref[...].astype(f32) + b_ref[...].astype(f32)
        grad = grad + swapped(p_ref[...], part).astype(f32)
        scaled = grad * g_ref[...]
        dh = dy_ref[...].astype(f32) + inv * (
            scaled
            - jnp.mean(scaled, axis=-1, keepdims=True)
            - unit * jnp.mean(scaled * unit, axis=-1, keepdims=True)
        )
        dh_out[...] = dh
        low = dh.astype(bf16)
        low_out[...] = low
        add_rows(gg_out, grad * unit)
        add_rows(gc_out, grad)
        add_rows(gbo_out, low.astype(f32))

    vec = shape((1, width), f32)
    return call(
        body,
        [shape((total, width), f32), shape((total, width), bf16), vec, vec, vec],
        (total // ROWS,),
        [row_spec(width)] * 5 + [whole_spec(1, width)],
        [row_spec(width)] * 2 + [whole_spec(1, width)] * 3,
        [middle, part_own, part_other, part_pair, cot_rel, gain],
        name="middle_backward",
    )


def first_backward(x_rel, part_own, part_other, keyval_grad, w_keyval_t, dh, gain, ids, count):
    total, width = dh.shape
    part = width // count
    kv = keyval_grad.shape[1]

    def body(ids_ref, x_ref, a_ref, b_ref, kv_ref, w_ref, dh_ref, g_ref, t_out, gg_out, gc_out):
        unit, inv = norm_stats(x_ref[...].astype(f32))
        grad = (a_ref[...].astype(f32) + b_ref[...].astype(f32)) + jnp.dot(
            kv_ref[...], w_ref[...], preferred_element_type=f32
        )
        scaled = grad * g_ref[...]
        value = dh_ref[...] + inv * (
            scaled
            - jnp.mean(scaled, axis=-1, keepdims=True)
            - unit * jnp.mean(scaled * unit, axis=-1, keepdims=True)
        )
        low = value.astype(bf16)
        if part % LANES:
            t_out[...] = low
        else:
            for o in range(count):
                t_out[:, columns_of(ids_ref[o], part)] = low[:, o * part : (o + 1) * part]
        add_rows(gg_out, grad * unit)
        add_rows(gc_out, grad)

    vec = shape((1, width), f32)
    result, gain_grad, bias_grad = call(
        body,
        [shape((total, width), bf16), vec, vec],
        (total // ROWS,),
        [row_spec(width)] * 3
        + [row_spec(kv), whole_spec(kv, width), row_spec(width), whole_spec(1, width)],
        [row_spec(width)] + [whole_spec(1, width)] * 2,
        [x_rel, part_own, part_other, keyval_grad, w_keyval_t, dh, gain],
        ids=[ids],
        flops=2 * total * width * kv,
        name="first_backward",
    )
    return put_back(result, ids, count), gain_grad, bias_grad


TILE = 256


def score_limits(lengths, token_count, first_place):
    doc_ends = jnp.cumsum(lengths)
    doc_starts = doc_ends - lengths
    places = (jnp.arange(token_count, dtype=jnp.int32) + first_place) % token_count
    doc_ids = jnp.sum((places[:, None] >= doc_ends[None, :]).astype(jnp.int32), axis=1)
    owners = doc_ids[:, None] == jnp.arange(lengths.shape[0], dtype=jnp.int32)[None, :]
    doc_begin = jnp.sum(jnp.where(owners, doc_starts[None, :], 0), axis=1)
    blocks = (places - doc_begin) // BLOCK
    seen = (doc_ids[:, None] == doc_ids[None, :]) & (blocks[None, :] <= blocks[:, None])
    seen_t = (doc_ids[None, :] == doc_ids[:, None]) & (blocks[:, None] <= blocks[None, :])
    pick = lambda s: jnp.where(s, shown_score, hidden_score).astype(f32)
    return pick(seen), pick(seen_t)


def attention_forward(queries, key_value, limits, heads):
    total = queries.shape[0]
    tiles = total // TILE
    c = score_scale * log2_e

    def body(q_ref, kv_ref, lim_ref, o_ref, lse_ref, top_ref):
        tile, head = pl.program_id(0), pl.program_id(1)
        k = kv_ref[:, :HD]
        v = kv_ref[:, HD:]
        s = lax.dot_general(
            q_ref[...], k, (((1,), (1,)), ((), ())), preferred_element_type=f32
        )
        s = jnp.minimum(s, lim_ref[...])
        m = jnp.max(s, axis=1, keepdims=True)
        p = jnp.exp2((s - m) * c)
        l = jnp.sum(p, axis=1, keepdims=True)
        o = jnp.dot(p.astype(bf16), v, preferred_element_type=f32)
        o_ref[...] = (o / l).astype(bf16)
        lane = lax.broadcasted_iota(jnp.int32, (TILE, LANES), 1)
        lse = m * c + jnp.log2(l)
        lse_ref[...] = jnp.where(lane == head, lse, lse_ref[...])

        @pl.when((tile == 0) & (head == 0))
        def _():
            top_ref[...] = jnp.full_like(top_ref, hidden_score)

        row = lax.broadcasted_iota(jnp.int32, (heads, LANES), 0)
        best = jnp.max(m, axis=0, keepdims=True) * score_scale
        top_ref[...] = jnp.where(row == head, jnp.maximum(top_ref[...], best), top_ref[...])

    return call(
        body,
        [shape((total, heads * HD), bf16), shape((total, LANES), f32), shape((heads, LANES), f32)],
        (tiles, heads),
        [
            pl.BlockSpec((TILE, HD), lambda i, h: (i, h)),
            pl.BlockSpec((total, 2 * HD), lambda i, h: (0, 0)),
            pl.BlockSpec((TILE, total), lambda i, h: (i, 0)),
        ],
        [
            pl.BlockSpec((TILE, HD), lambda i, h: (i, h)),
            pl.BlockSpec((TILE, LANES), lambda i, h: (i, 0)),
            pl.BlockSpec((heads, LANES), lambda i, h: (0, 0)),
        ],
        [queries, key_value, limits],
        flops=8 * total * total * HD * heads,
        name="attention_forward",
    )


def attention_backward(queries, grad_att, key_value, limits_t, lse_t, dot_t, heads):
    total = queries.shape[0]
    tiles = total // TILE
    c = score_scale * log2_e

    def body(q_ref, da_ref, kv_ref, lim_ref, lse_ref, dot_ref, dq_ref, dkv_ref):
        tile, head = pl.program_id(0), pl.program_id(1)
        k = kv_ref[:, :HD]
        v = kv_ref[:, HD:]
        q = q_ref[...]
        da = da_ref[...]
        nt = (((1,), (1,)), ((), ()))
        s = lax.dot_general(k, q, nt, preferred_element_type=f32)
        s = jnp.minimum(s, lim_ref[...])
        p = jnp.exp2(s * c - lse_ref[pl.ds(head, 1), :])
        dp = lax.dot_general(v, da, nt, preferred_element_type=f32)
        ds = (p * (dp - dot_ref[pl.ds(head, 1), :])).astype(bf16)
        dq = lax.dot_general(ds, k, (((0,), (0,)), ((), ())), preferred_element_type=f32)
        dq_ref[...] = (dq * score_scale).astype(bf16)

        @pl.when((tile == 0) & (head == 0))
        def _():
            dkv_ref[...] = jnp.zeros_like(dkv_ref)

        dkv_ref[:, :HD] += jnp.dot(ds, q, preferred_element_type=f32) * score_scale
        dkv_ref[:, HD:] += jnp.dot(p.astype(bf16), da, preferred_element_type=f32)

    return call(
        body,
        [shape((total, heads * HD), bf16), shape((total, 2 * HD), f32)],
        (tiles, heads),
        [
            pl.BlockSpec((TILE, HD), lambda i, h: (i, h)),
            pl.BlockSpec((TILE, HD), lambda i, h: (i, h)),
            pl.BlockSpec((total, 2 * HD), lambda i, h: (0, 0)),
            pl.BlockSpec((total, TILE), lambda i, h: (0, i)),
            pl.BlockSpec((heads, TILE), lambda i, h: (0, i)),
            pl.BlockSpec((heads, TILE), lambda i, h: (0, i)),
        ],
        [
            pl.BlockSpec((TILE, HD), lambda i, h: (i, h)),
            pl.BlockSpec((total, 2 * HD), lambda i, h: (0, 0)),
        ],
        [queries, grad_att, key_value, limits_t, lse_t, dot_t],
        flops=20 * total * total * HD * heads,
        name="attention_backward",
    )


def adam_values(gradient, weight, one, two, rate, decay):
    new_one = beta_one * one + (1.0 - beta_one) * gradient
    new_two = beta_two * two + (1.0 - beta_two) * gradient * gradient
    direction = (new_one * correct_one) / (jnp.sqrt(new_two * correct_two) + adam_eps)
    return new_one, new_two, weight - rate * (direction + decay * weight)


def to_tiles(flat, tiles_ref):
    for j in range(8):
        tiles_ref[:, j, :] = flat[:, j * LANES : (j + 1) * LANES]


def adam_in(gradient, weight, one, two, outer, start, full):
    rows, cols = gradient.shape
    step = 64
    base = (start // 1024).reshape(1)
    tall = pl.BlockSpec((step, 8, LANES), lambda i, j, b: (i, b[0] + j, 0))
    flat = pl.BlockSpec((step, 1024), lambda i, j, b: (i, j))
    args = [gradient, weight, one, two, outer]
    specs = [flat] + [tall] * 4
    aliases = {}
    if full is not None:
        aliases = {5: 0, 6: 1}
        args += list(full)
        specs += [pl.BlockSpec(memory_space=pl.ANY)] * 2

    def body(_, g_ref, w_ref, one_ref, two_ref, out_ref, *rest):
        one_out, two_out, delta_out, grad_tiles, delta_tiles = rest[-5:]
        to_tiles(g_ref[...].astype(f32), grad_tiles)
        new_one, new_two, stepped = adam_values(
            grad_tiles[...], w_ref[...], one_ref[...], two_ref[...], rate_matrix, weight_decay
        )
        one_out[...] = new_one
        two_out[...] = new_two
        delta_tiles[...] = out_ref[...] - stepped
        for j in range(8):
            delta_out[:, j * LANES : (j + 1) * LANES] = delta_tiles[:, j, :].astype(bf16)

    whole = shape(weight.shape, f32)
    return call(
        body,
        [whole, whole, shape((rows, cols), bf16)],
        (rows // step, cols // 1024),
        specs,
        [tall, tall, flat],
        args,
        ids=[base],
        scratch=[pltpu.VMEM((step, 8, LANES), f32)] * 2,
        aliases=aliases,
        name="adam_in",
        vmem=VMEM_MOST,
    )


def adam_out(gradient, weight, one, two, outer, start, full):
    rows, cols = gradient.shape
    step = 512
    base = (start // step).reshape(1)
    tall = pl.BlockSpec((step, cols), lambda i, b: (b[0] + i, 0))
    flat = pl.BlockSpec((step, cols), lambda i, b: (i, 0))
    args = [gradient, weight, one, two, outer]
    specs = [flat] + [tall] * 4
    aliases = {}
    if full is not None:
        aliases = {5: 0, 6: 1}
        args += list(full)
        specs += [pl.BlockSpec(memory_space=pl.ANY)] * 2

    def body(_, g_ref, w_ref, one_ref, two_ref, out_ref, *rest):
        one_out, two_out, delta_out = rest[-3:]
        new_one, new_two, stepped = adam_values(
            g_ref[...].astype(f32), w_ref[...], one_ref[...], two_ref[...], rate_matrix,
            weight_decay,
        )
        one_out[...] = new_one
        two_out[...] = new_two
        delta_out[...] = (out_ref[...] - stepped).astype(bf16)

    whole = shape(weight.shape, f32)
    return call(
        body,
        [whole, whole, shape((rows, cols), bf16)],
        (rows // step,),
        specs,
        [tall, tall, flat],
        args,
        ids=[base],
        aliases=aliases,
        name="adam_out",
        vmem=VMEM_MOST,
    )


def outer_values(mean, momentum, outer):
    velocity = outer_beta * momentum + mean
    return velocity, outer - outer_rate * (mean + outer_beta * velocity)


def outer_in(both, momentum, outer, factor, start, full):
    _, rows, cols = both.shape
    step = 64
    base = (start // 1024).reshape(1)
    tall = pl.BlockSpec((step, 8, LANES), lambda i, j, b: (i, b[0] + j, 0))
    flat = pl.BlockSpec((2, step, 1024), lambda i, j, b: (0, i, j))
    wide = pl.BlockSpec((step, 1024), lambda i, j, b: (i, b[0] + j))
    args = [both, momentum, outer]
    specs = [flat, tall, tall]
    if factor is not None:
        args.append(factor)
        specs.append(pl.BlockSpec((8, LANES), lambda i, j, b: (0, 0)))
    aliases = {}
    if full is not None:
        aliases = {len(args) + k: k for k in range(4)}
        args += list(full)
        specs += [pl.BlockSpec(memory_space=pl.ANY)] * 4

    def body(_, both_ref, mom_ref, out_ref, *rest):
        mean_out, vel_out, new_out, copy_out, mean_tiles, new_tiles = rest[-6:]
        to_tiles((both_ref[0].astype(f32) + both_ref[1].astype(f32)) * 0.5, mean_tiles)
        mean = mean_tiles[...]
        velocity, fresh = outer_values(mean, mom_ref[...], out_ref[...])
        if factor is not None:
            fresh = fresh * rest[0][...][None]
        mean_out[...] = mean
        vel_out[...] = velocity
        new_out[...] = fresh
        new_tiles[...] = fresh
        for j in range(8):
            copy_out[:, j * LANES : (j + 1) * LANES] = new_tiles[:, j, :].astype(bf16)

    whole = shape(outer.shape, f32)
    return call(
        body,
        [whole, whole, whole, shape((rows, outer.shape[1] * LANES), bf16)],
        (rows // step, cols // 1024),
        specs,
        [tall, tall, tall, wide],
        args,
        ids=[base],
        scratch=[pltpu.VMEM((step, 8, LANES), f32)] * 2,
        aliases=aliases,
        name="outer_in",
        vmem=VMEM_MOST,
    )


def outer_out(both, momentum, outer, start, full):
    _, rows, cols = both.shape
    step = 512
    base = (start // step).reshape(1)
    tall = pl.BlockSpec((step, cols), lambda i, b: (b[0] + i, 0))
    flat = pl.BlockSpec((2, step, cols), lambda i, b: (0, i, 0))
    args = [both, momentum, outer]
    specs = [flat, tall, tall]
    aliases = {}
    if full is not None:
        aliases = {3 + k: k for k in range(4)}
        args += list(full)
        specs += [pl.BlockSpec(memory_space=pl.ANY)] * 4

    def body(_, both_ref, mom_ref, out_ref, *rest):
        mean_out, vel_out, new_out, copy_out = rest[-4:]
        mean = (both_ref[0].astype(f32) + both_ref[1].astype(f32)) * 0.5
        velocity, fresh = outer_values(mean, mom_ref[...], out_ref[...])
        mean_out[...] = mean
        vel_out[...] = velocity
        new_out[...] = fresh
        copy_out[...] = fresh.astype(bf16)

    whole = shape(outer.shape, f32)
    return call(
        body,
        [whole, whole, whole, shape(outer.shape, bf16)],
        (rows // step,),
        specs,
        [tall] * 4,
        args,
        ids=[base],
        aliases=aliases,
        name="outer_out",
        vmem=VMEM_MOST,
    )


class Wire:
    def __init__(self, window):
        self.window, self.landed = window, []

    def send(self, block, axis, pairs):
        if len(self.landed) >= self.window:
            block, _ = lax.optimization_barrier((block, self.landed[-self.window]))
        arrived = lax.ppermute(block, axis, pairs)
        self.landed.append(arrived)
        return arrived


class Links:
    def __init__(self, count, splits, window):
        self.levels = count.bit_length() - 1
        self.far = ([1] + [1 << b for b in range(3, self.levels)])[: self.levels - 2]
        places = range(count)
        middle = [i for i in places if (i >> 1 ^ i >> 2) & 1]
        outer = [i for i in places if i not in middle]
        self.pair = [(i, i ^ 2) for i in places]
        self.inward = [(i, i ^ 2) for i in outer]
        self.outward = [(i, i ^ 2) for i in middle]
        self.between = [(i, i ^ 6) for i in middle]
        self.beside = [[(i, i ^ mask) for i in places] for mask in self.far]
        self.mirror = [(i, i ^ 6) for i in places]
        self.cores = [(i, (i + 1) % splits) for i in range(splits)]
        self.wire = Wire(window)

    def flips(self, across):
        masks = [2, across] + self.far
        table = []
        for o in range(1 << self.levels):
            flip = 0
            for level, mask in enumerate(masks):
                if o >> level & 1:
                    flip ^= mask
            table.append(flip)
        return table

    def to_side(self, block, pairs):
        return self.wire.send(block, "dp", pairs)

    def to_middle(self, block):
        return self.wire.send(block, "dp", self.between)

    def to_far(self, block, level):
        return self.wire.send(block, "dp", self.beside[level - 2])

    def to_pair(self, block):
        return self.wire.send(block, "dp", self.pair)

    def across(self, block):
        return lax.ppermute(block, "tensor", self.cores)

    def pair_now(self, block):
        return lax.ppermute(block, "dp", self.pair)


def after(value, *earlier):
    return lax.optimization_barrier((value, *earlier))[0]


class Order:
    def __init__(self):
        self.last = ()

    def tie(self, value):
        return after(value, *self.last) if self.last else value

    def mark(self, *values):
        self.last = values
        return values[0]

    def landed(self, *arrivals):
        self.last = tuple(self.last) + arrivals


class Gathered:
    def __init__(self, links, axis, mine, other=None):
        self.links, self.axis, self.mine, self.other = links, axis, mine, other
        self.held = {}

    def join(self, *blocks):
        return jnp.concatenate(blocks, axis=self.axis)

    def near(self):
        give = self.mine if self.other is None else self.other
        self.held[0] = self.join(self.mine, self.links.to_side(give, self.links.pair))

    def inward(self):
        if self.other is not None:
            self.passed = self.links.to_side(self.mine, self.links.inward)

    def middle(self):
        if self.other is None:
            self.relay = self.direct = self.links.to_middle(self.held[0])
        else:
            self.relay = self.links.to_middle(self.join(self.other, self.passed))

    def middle_rest(self):
        self.direct = self.links.to_middle(self.held[0])

    def outward(self):
        self.relayed = self.links.to_side(self.relay, self.links.outward)

    def join_far(self):
        self.held[2] = self.direct + self.relayed

    def far(self, level, o):
        self.held[o + (1 << level)] = self.links.to_far(self.held[o], level)

    def whole(self):
        for level in range(2, self.links.levels):
            for o in range(0, 1 << level, 2):
                if o + (1 << level) not in self.held:
                    self.far(level, o)
        return self.join(*[self.held[o] for o in sorted(self.held)])


class Reduced:
    def __init__(self, links, order, axis, size, halved, part):
        self.links, self.order, self.axis, self.size = links, order, axis, size
        self.halved, self.part = halved, part
        self.landed = {}

    def pair_sum(self, o):
        total = self.part(o, 2)
        for block in self.landed.pop(o, []):
            total = total + block.astype(f32)
        return self.order.mark(total.astype(bf16))

    def one(self, block, o):
        return lax.slice_in_dim(
            block, o * self.size, (o + 1) * self.size, axis=self.axis
        ).astype(f32)

    def far(self, level, o):
        arrived = self.links.to_far(self.pair_sum(o), level)
        self.landed.setdefault(o - (1 << level), []).append(arrived)
        return arrived

    def far_rest(self, done):
        arrived = None
        for level in range(self.links.levels - 1, 1, -1):
            for o in reversed(range(1 << level, 2 << level, 2)):
                if (level, o) not in done:
                    arrived = self.far(level, o)
        return arrived

    def inward(self):
        self.ahead = self.pair_sum(2)
        self.passed = self.links.to_side(self.ahead, self.links.inward)
        if self.halved:
            self.direct = self.links.to_middle(self.ahead)

    def middle(self):
        if self.halved:
            self.relay = self.links.to_middle(self.order.tie(self.passed))
        else:
            both = self.order.mark(self.order.tie(self.ahead) + self.passed)
            self.direct = self.links.to_middle(both)

    def single(self, o):
        total = self.part(o, 1)
        for block in self.landed[0] + [self.direct]:
            total = total + self.one(block, o)
        return total

    def near(self):
        value = self.order.mark(self.single(1).astype(bf16))
        self.theirs = self.links.to_side(value, self.links.pair).astype(f32)

    def outward(self):
        value = self.one(self.order.tie(self.relay), 1).astype(bf16)
        self.last = self.links.to_side(value, self.links.outward).astype(f32)

    def result(self):
        if not self.halved:
            return self.order.mark(self.single(0) + self.theirs), None
        own = self.order.mark(self.single(0) + self.last)
        return own, self.theirs + self.one(self.relay, 0)


def local(
    tokens,
    doc_lengths,
    cotangent,
    inner_in,
    inner_out,
    inner_shared,
    first_in,
    first_out,
    first_shared,
    second_in,
    second_out,
    second_shared,
    outer_in_w,
    outer_out_w,
    outer_shared,
    momentum_in,
    momentum_out,
    momentum_shared,
):
    splits = lax.axis_size("tensor")
    count = lax.axis_size("dp")
    split = lax.axis_index("tensor")
    place = lax.axis_index("dp")
    total, width = tokens.shape
    part = width // count
    local_cols = inner_in.shape[3]
    shared_cols = inner_shared.shape[2]
    heads = HEADS // splits
    qcols = heads * HD
    hidden = local_cols - qcols
    vec = 2 * HD
    own_cols = part // splits
    mine = total // 2

    links = Links(count, splits, 4)
    across = links.across
    levels = links.levels
    side = ((place >> 1) ^ (place >> 2)) & 1
    from_outer, from_middle = (jnp.array(links.flips(m), jnp.int32) for m in (4, 6))
    ids = (place ^ jnp.where(side == 0, from_outer, from_middle)).astype(jnp.int32)
    swap_group = [(0, 1), (1, 0)]
    split_id = split.astype(jnp.int32).reshape(1)

    def tall(array):
        return array.reshape(part, local_cols // LANES, LANES)

    w_in = tall(inner_in)
    w_out = inner_out.reshape(local_cols, part)
    shared_rows = lax.all_gather(inner_shared[0], ("dp", "tensor"), axis=0, tiled=True)

    half = hidden // 2
    flat_in = inner_in.reshape(part, local_cols)

    def sides(low, high):
        return (
            jnp.where(side == 0, low, high).astype(bf16),
            jnp.where(side == 0, high, low).astype(bf16),
        )

    block_q = flat_in[:, :qcols].astype(bf16)
    block_o = w_out[:qcols].astype(bf16)
    up_sides = sides(flat_in[:, qcols : qcols + half], flat_in[:, qcols + half :])
    down_sides = sides(w_out[qcols : qcols + half], w_out[qcols + half :])
    got_query = Gathered(links, 0, block_q)
    got_attn = Gathered(links, 1, block_o)
    got_up = Gathered(links, 0, *up_sides)
    got_down = Gathered(links, 1, *down_sides)
    shared_t = shared_rows.T
    shared_rel = pick_blocks(shared_t, ids, part, count, False)
    w_keyval_t = shared_rel[:vec].astype(bf16)
    vectors_t, vectors = shared_t[vec:], shared_rel[vec:]
    gain_one, bias_one, gain_two, bias_two = (vectors[k : k + 1] for k in range(4))
    bias_out, bias_down = vectors[5:6], vectors[6:7]
    bias_query = lax.dynamic_slice_in_dim(vectors_t[4], split * qcols, qcols)
    bias_up = lax.dynamic_slice_in_dim(
        vectors_t[7:].reshape(FF), split * hidden + side * half, half
    )

    nt = (((1,), (1,)), ((), ()))
    tn = (((0,), (0,)), ((), ()))

    def mm(a, b, dims=(((1,), (0,)), ((), ()))):
        return lax.dot_general(a, b, dims, preferred_element_type=f32)

    def block(array, o, blocks):
        return array[:, o * part : (o + blocks) * part]

    def both_rows(rows):
        return lax.all_gather(rows, "tensor", axis=0, tiled=True)

    def far(weight, o):
        if levels == 3:
            weight.far(2, o)

    cot_own, cot_pair, grad_bias_down = cotangent_order(cotangent, ids, split_id, count)
    got_query.near()
    got_attn.near()
    got_query.middle()
    far(got_query, 0)
    got_down.near()
    got_down.inward()
    got_attn.middle()
    far(got_attn, 0)
    got_query.outward()
    got_query.join_far()
    far(got_query, 2)
    got_attn.outward()
    got_attn.join_far()
    got_down.middle()
    got_up.near()
    far(got_attn, 2)
    w_query = got_query.whole()
    w_attn = got_attn.whole()
    got_up.inward()
    far(got_down, 0)
    cot_theirs = links.to_pair(swap_small(cot_pair, part))
    got_down.outward()
    got_down.middle_rest()
    got_down.join_far()
    far(got_up, 0)
    got_up.middle()
    far(got_down, 2)
    w_down = got_down.whole()
    got_up.outward()
    got_up.middle_rest()
    got_up.join_far()

    x_rel, normed = first_norm(tokens, ids, split_id, gain_one, bias_one, count)
    limits, limits_t = score_limits(doc_lengths[0], total, split * mine)
    key_value = mm(normed, w_keyval_t, nt).astype(bf16)
    queries = (mm(normed, w_query) + bias_query).astype(bf16)
    attended, log_totals, tops = attention_forward(queries, key_value, limits, heads)
    attn_give = mm(attended[mine:], w_attn).astype(bf16)
    attn_keep = mm(attended[:mine], w_attn).astype(bf16)
    attn_other = across(attn_give)
    middle, normed_two, normed_pair = middle_norm(
        x_rel, attn_keep, attn_other, bias_out, gain_two, bias_two, part
    )
    normed_theirs = links.to_pair(swap_small(normed_pair, part))
    far(got_up, 2)
    w_up = got_up.whole()
    normed_all = both_rows(jnp.concatenate([normed_two, normed_theirs], axis=0))
    cot_all = both_rows(jnp.concatenate([cot_own, cot_theirs], axis=0))
    hidden_grad = mm(cot_all, w_down, nt).astype(bf16)
    acts, grad_pre, grad_bias_up = hidden_units(normed_all, w_up, bias_up[None], hidden_grad)

    links.wire.window = 1 << 30
    order = Order()
    tie, mark = order.tie, order.mark
    sum_down = Reduced(
        links, order, 1, part, True, lambda o, b: mm(tie(acts), block(cot_all, o, b), tn)
    )
    sum_up = Reduced(
        links, order, 0, part, True, lambda o, b: mm(block(normed_all, o, b), tie(grad_pre), tn)
    )
    early = [(2, 6)] if levels == 3 else []
    for level, o in early:
        sum_down.far(level, o)
    pre_give = lax.dynamic_slice_in_dim(grad_pre, (1 - split) * 2 * mine, 2 * mine)
    pre_keep = lax.dynamic_slice_in_dim(grad_pre, split * 2 * mine, 2 * mine)
    two_give = mark(mm(pre_give, tie(w_up), nt).astype(bf16))
    two_other = across(two_give)
    down_landed = sum_down.far_rest(early)
    two_keep = mark(mm(pre_keep, tie(w_up), nt).astype(bf16))
    two_theirs = two_keep[mine:].astype(f32) + two_other[mine:].astype(f32)
    two_theirs = mark(swap_small(two_theirs.astype(bf16), part))
    two_pair = links.pair_now(two_theirs)
    for level, o in early:
        sum_up.far(level, o)
    sum_down.inward()
    dh, dh_mine, grad_gain_two, grad_bias_two, grad_bias_out = middle_backward(
        middle, tie(two_keep), two_other, two_pair, cot_own, gain_two, part
    )
    mark(dh_mine)
    dh_low = jnp.concatenate([dh_mine, across(dh_mine)], axis=0)
    grad_att = mark(mm(dh_low, w_attn, nt).astype(bf16))
    dots = jnp.sum(
        (grad_att.astype(f32) * attended.astype(f32)).reshape(total, heads, HD), axis=2
    )
    grad_queries, kv_part = attention_backward(
        queries, after(grad_att, down_landed), key_value, limits_t, log_totals.T[:heads], dots.T,
        heads,
    )
    mark(grad_queries)
    up_landed = sum_up.far_rest(early)
    one_give = mark(mm(grad_queries[mine:], tie(w_query), nt).astype(bf16))
    one_other = across(one_give)
    kv_other = across(kv_part[mine:])
    sum_down.middle()
    sum_down.near()
    sum_up.inward()
    sum_attn = Reduced(
        links, order, 1, part, False, lambda o, b: mm(tie(attended), block(dh_low, o, b), tn)
    )
    sum_attn.far_rest([])
    one_keep = mark(mm(grad_queries[:mine], tie(w_query), nt).astype(bf16))
    kv_low = (kv_part[:mine] + kv_other).astype(bf16)
    grad_mine, grad_gain_one, grad_bias_one = first_backward(
        x_rel, after(one_keep, up_landed), one_other, kv_low, w_keyval_t, dh, gain_one, ids, count
    )
    mark(grad_mine)
    tokens_grad = both_rows(grad_mine)
    sum_query = Reduced(
        links, order, 0, part, False, lambda o, b: mm(block(normed, o, b), tie(grad_queries), tn)
    )
    sum_query.far_rest([])
    order.landed(sum_up.passed)
    sum_up.middle()
    sum_down.outward()

    peers = across(tie(tops))
    peak = jnp.where(
        split == 0, jnp.concatenate([tops, peers]), jnp.concatenate([peers, tops])
    )
    peak = jnp.maximum(peak, lax.ppermute(peak, "group", swap_group))
    for pairs in [links.pair, links.mirror] + links.beside:
        peak = jnp.maximum(peak, lax.ppermute(peak, "dp", pairs))
    clip_rows = clip_limit / jnp.maximum(peak, clip_limit)
    clip_own = lax.dynamic_slice_in_dim(clip_rows, split * heads, heads)

    grad_keyval_t = mm(tie(kv_low), normed[:mine], tn)
    grad_bias_query = jnp.sum(grad_queries.astype(f32), axis=0)
    spread = jnp.concatenate(
        [
            lax.dynamic_update_slice_in_dim(
                jnp.zeros((width,), f32), grad_bias_query, split * qcols, 0
            ),
            lax.dynamic_update_slice_in_dim(
                jnp.zeros((FF,), f32), grad_bias_up[0], split * hidden + side * half, 0
            ),
        ]
    ).reshape(1 + FF // width, width)
    near = jnp.concatenate(
        [grad_keyval_t, grad_gain_one, grad_bias_one, grad_gain_two, grad_bias_two, grad_bias_out,
         grad_bias_down],
        axis=0,
    )
    steps = jnp.arange(count, dtype=jnp.int32)
    turned = jnp.where((side == 0) & ((steps & 2) != 0), steps ^ 1, steps)
    mirrored = (place ^ from_middle).astype(jnp.int32)

    def pieces(core):
        a = pick_blocks(near, turned * splits + core, own_cols, count, True)
        b = pick_blocks(spread, mirrored * splits + core, own_cols, count, True)
        return jnp.concatenate([a[:, : vec + 4], b[:, :1], a[:, vec + 4 :], b[:, 1:]], axis=1)

    shared_give = mark(pieces(1 - split))
    shared_other = across(shared_give)

    one_in, two_in = tall(first_in), tall(second_in)
    one_out, two_out = (a.reshape(local_cols, part) for a in (first_out, second_out))
    base_in, mom_in = tall(outer_in_w), tall(momentum_in)
    base_out, mom_out = (a.reshape(local_cols, part) for a in (outer_out_w, momentum_out))
    starts = [qcols + side * half, qcols + (1 - side) * half]
    zero = jnp.zeros((), jnp.int32)
    gathered = []

    def groups(delta):
        both = lax.all_gather(after(delta, *gathered[-1:]), "group", axis=0)
        gathered.append(both)
        return both

    def adam_down(gradient, start, full):
        *full, delta = adam_out(tie(gradient), w_out, one_out, two_out, base_out, start, full)
        mark(delta)
        return full, delta

    def adam_up(gradient, start, full):
        *full, delta = adam_in(tie(gradient), w_in, one_in, two_in, base_in, start, full)
        mark(delta)
        return full, delta

    red_down = sum_down.result()
    full_out, delta_down = adam_down(red_down[0], starts[0], None)
    both_down = [groups(delta_down)]
    sum_attn.inward()
    order.landed(sum_up.relay, clip_rows)
    full_out, delta_down = adam_down(red_down[1], starts[1], full_out)
    both_down.append(groups(delta_down))
    sum_up.outward()
    sum_up.near()
    sum_query.inward()
    order.landed(sum_attn.passed)
    sum_attn.middle()

    down_part = mark(mm(tie(acts), w_down).astype(bf16))
    down_sum = lax.psum_scatter(down_part, "tensor", scatter_dimension=0, tiled=True)
    order.landed(sum_query.passed)
    sum_query.middle()
    new_out = outer_out(both_down[0], mom_out, tie(base_out), starts[0], None)
    mark(new_out[0], sum_attn.direct)
    red_up = sum_up.result()
    full_in, delta_up = adam_up(red_up[0], starts[0], None)
    both_up = [groups(delta_up)]
    down_pair = links.to_pair(swap_small(down_sum[mine:], part))
    red_shared = pieces(split) + shared_other
    cube = list(reversed([links.pair, links.mirror] + links.beside))
    for pairs in cube[:-2]:
        keep = red_shared.shape[0] // 2
        red_shared = red_shared[:keep] + lax.ppermute(red_shared[keep:], "dp", pairs)
    sum_query.near()
    sum_attn.near()
    for pairs in cube[-2:]:
        keep = red_shared.shape[0] // 2
        red_shared = red_shared[:keep] + lax.ppermute(red_shared[keep:], "dp", pairs)
    red_shared = red_shared[0]
    full_in, delta_up = adam_up(red_up[1], starts[1], full_in)
    both_up.append(groups(delta_up))
    new_out = outer_out(both_down[1], mom_out, tie(base_out), starts[1], new_out)
    mark(new_out[0])
    result = mark(block_result(tie(middle), down_sum, down_pair, bias_down, ids, count))
    block_out = both_rows(result)
    red_query = sum_query.result()[0]
    full_in, delta_query = adam_up(red_query, zero, full_in)
    other_query = lax.ppermute(delta_query, "group", swap_group)
    red_attn = sum_attn.result()[0]
    full_out, delta_attn = adam_down(red_attn, zero, full_out)
    other_attn = lax.ppermute(delta_attn, "group", swap_group)
    new_in = outer_in(both_up[0], mom_in, tie(base_in), None, starts[0], None)
    new_in = outer_in(both_up[1], mom_in, base_in, None, starts[1], new_in)
    both = jnp.stack([delta_attn, other_attn])
    new_out = outer_out(both, mom_out, base_out, zero, new_out)
    both = jnp.stack([delta_query, other_query])
    new_in = outer_in(both, mom_in, base_in, clip_own, zero, new_in)

    ids_col = jnp.arange(shared_cols, dtype=jnp.int32)[:, None]
    one_sh, two_sh, stepped = adam_values(
        red_shared,
        inner_shared[0].T,
        first_shared[0].T,
        second_shared[0].T,
        jnp.where(ids_col < vec, rate_matrix, rate_vector),
        jnp.where(ids_col < vec, weight_decay, 0.0),
    )
    base_sh = outer_shared.T
    delta = (base_sh - stepped).astype(bf16)
    mean_sh = (delta.astype(f32) + lax.ppermute(delta, "group", swap_group).astype(f32)) * 0.5
    vel_sh, fresh_sh = outer_values(mean_sh, momentum_shared.T, base_sh)
    row_ids = (place * splits + split) * own_cols + jnp.arange(own_cols, dtype=jnp.int32)
    clip_vec = clip_rows[:, 0]
    row_clip = jnp.sum(
        jnp.where((row_ids // HD)[None, :] == jnp.arange(HEADS)[:, None], clip_vec[:, None], 0.0),
        axis=0,
    )
    fresh_sh = fresh_sh * jnp.where(ids_col == vec + 4, row_clip[None, :], 1.0)

    shape_in, shape_out = (part, 1, local_cols), (1, local_cols, part)
    mean_in, vel_in, fresh_in, copy_in = new_in
    mean_out, vel_out, fresh_out, copy_out = new_out
    return (
        block_out,
        tokens_grad,
        clip_vec,
        full_in[0].reshape((1,) + shape_in),
        full_out[0].reshape((1,) + shape_out),
        one_sh.T[None],
        full_in[1].reshape((1,) + shape_in),
        full_out[1].reshape((1,) + shape_out),
        two_sh.T[None],
        mean_in.reshape(shape_in),
        mean_out.reshape(shape_out),
        mean_sh.T,
        vel_in.reshape(shape_in),
        vel_out.reshape(shape_out),
        vel_sh.T,
        fresh_in.reshape(shape_in),
        fresh_out.reshape(shape_out),
        fresh_sh.T,
        copy_in.reshape(shape_in),
        copy_out.reshape(shape_out),
        fresh_sh.T.astype(bf16),
    )


def solution(mesh):
    rows = P(("group", "dp"), None)
    inner = [P("group", "dp", "tensor", None), P("group", "tensor", None, "dp"),
             P("group", ("dp", "tensor"), None)]
    outer = [P("dp", "tensor", None), P("tensor", None, "dp"), P(("dp", "tensor"), None)]
    in_specs = tuple([rows] * 3 + inner * 3 + outer * 2)
    out_specs = tuple([rows] * 2 + [P()] + inner * 2 + outer * 4)
    return jax.shard_map(local, mesh=mesh, in_specs=in_specs, out_specs=out_specs, check_vma=False)
```

```python
import jax
import jax.numpy as jnp
from jax import lax
from jax.experimental import pallas as pl
from jax.experimental.pallas import tpu as pltpu
from jax.sharding import PartitionSpec as P

HEADS = 16
HD = 128
FF = 8192
BLOCK = 256
STEP = 10

norm_eps = 1e-05
hidden_score = -1e30
shown_score = 3e38
beta_one = 0.9
beta_two = 0.95
adam_eps = 1e-08
rate_matrix = 0.02
rate_vector = 0.2
weight_decay = 0.1
outer_beta = 0.9
outer_rate = 0.7
clip_limit = 5.0
score_scale = HD ** (-0.5)
log2_e = 1.4426950408889634
correct_one = 1.0 / (1.0 - beta_one**STEP)
correct_two = 1.0 / (1.0 - beta_two**STEP)

f32 = jnp.float32
bf16 = jnp.bfloat16
ROWS = 128
LANES = 128
VMEM_LIMIT = 40 * 1024 * 1024
VMEM_MOST = 58 * 1024 * 1024


def shape(dims, dtype):
    return jax.ShapeDtypeStruct(dims, dtype)


def call(body, out_shape, grid, in_specs, out_specs, args, *, ids=(), scratch=(), aliases=None,
         flops=0, name=None, vmem=VMEM_LIMIT):
    outs = out_shape if isinstance(out_shape, (list, tuple)) else [out_shape]
    moved = sum(a.size * a.dtype.itemsize for a in args)
    moved += sum(o.size * o.dtype.itemsize for o in outs)
    return pl.pallas_call(
        body,
        out_shape=out_shape,
        grid_spec=pltpu.PrefetchScalarGridSpec(
            num_scalar_prefetch=len(ids),
            grid=grid,
            in_specs=in_specs,
            out_specs=out_specs,
            scratch_shapes=list(scratch),
        ),
        input_output_aliases={len(ids) + k: v for k, v in (aliases or {}).items()},
        compiler_params=pltpu.CompilerParams(vmem_limit_bytes=vmem),
        cost_estimate=pl.CostEstimate(flops=flops, bytes_accessed=moved, transcendentals=0),
        name=name,
    )(*ids, *args)


def pick_blocks(array, block_ids, width, count, stacked):
    rows = array.shape[0]
    if width % LANES:
        taken = jnp.take(array.reshape(rows, -1, width), block_ids, axis=1)
        return taken.transpose(1, 0, 2) if stacked else taken.reshape(rows, count * width)

    def body(ids_ref, in_ref, out_ref):
        if stacked:
            out_ref[0] = in_ref[...]
        else:
            out_ref[...] = in_ref[...]

    if stacked:
        out, spec = shape((count, rows, width), array.dtype), pl.BlockSpec(
            (1, rows, width), lambda j, ids: (j, 0, 0)
        )
    else:
        out, spec = shape((rows, count * width), array.dtype), pl.BlockSpec(
            (rows, width), lambda j, ids: (0, j)
        )
    return call(
        body, out, (count,), [pl.BlockSpec((rows, width), lambda j, ids: (0, ids[j]))], spec,
        [array], ids=[block_ids], name="pick_blocks",
    )


def columns_of(block_id, width):
    return pl.ds(pl.multiple_of(block_id * width, width), width)


def placing(array, ids, count):
    part = array.shape[1] // count
    if part % LANES == 0:
        return array, count, part
    return pick_blocks(array, ids, part, count, False), 0, part


def put_back(array, ids, count):
    part = array.shape[1] // count
    if part % LANES == 0:
        return array
    back = jnp.sum(
        jnp.where(ids[None, :] == jnp.arange(count)[:, None], jnp.arange(count)[None, :], 0), axis=1
    ).astype(jnp.int32)
    return pick_blocks(array, back, part, count, False)


def norm_stats(rows):
    mean = jnp.mean(rows, axis=-1, keepdims=True)
    centered = rows - mean
    inv = lax.rsqrt(jnp.mean(centered * centered, axis=-1, keepdims=True) + norm_eps)
    return centered * inv, inv


def row_spec(cols, rows=ROWS):
    return pl.BlockSpec((rows, cols), lambda i, *ids: (i, 0))


def turned_spec(cols, blocks):
    return pl.BlockSpec(
        (ROWS, cols), lambda i, ids, split: ((i + split[0] * (blocks // 2)) % blocks, 0)
    )


def whole_spec(rows, cols):
    return pl.BlockSpec((rows, cols), lambda i, *ids: (0, 0))


def first_norm(tokens, ids, split, gain, bias, count):
    total, width = tokens.shape
    tokens, moved, part = placing(tokens, ids, count)

    def body(ids_ref, split_ref, x_ref, g_ref, c_ref, x_out, n_out):
        for o in range(moved):
            x_out[:, o * part : (o + 1) * part] = x_ref[:, columns_of(ids_ref[o], part)]
        if not moved:
            x_out[...] = x_ref[...]
        unit, _ = norm_stats(x_out[...].astype(f32))
        n_out[...] = (unit * g_ref[...] + c_ref[...]).astype(bf16)

    return call(
        body,
        [shape((total, width), bf16)] * 2,
        (total // ROWS,),
        [turned_spec(width, total // ROWS), whole_spec(1, width), whole_spec(1, width)],
        [row_spec(width)] * 2,
        [tokens, gain, bias],
        ids=[ids, split],
        name="first_norm",
    )


def first_spec(cols, blocks):
    return pl.BlockSpec((ROWS, cols), lambda i, *ids: (jnp.minimum(i, blocks - 1), 0))


def swapped(values, part):
    if part % LANES:
        return values
    blocks = [values[:, o : o + part] for o in range(0, values.shape[1], part)]
    return jnp.concatenate([blocks[pair_of(o)] for o in range(len(blocks))], axis=1)


def pair_of(o):
    return o if o & 2 else o ^ 1


def swap_small(values, part):
    if part % LANES == 0:
        return values
    blocks = [values[:, o : o + part] for o in range(0, values.shape[1], part)]
    return jnp.concatenate([blocks[pair_of(o)] for o in range(len(blocks))], axis=1)


def cotangent_order(cotangent, ids, split, count):
    total, width = cotangent.shape
    cotangent, moved, part = placing(cotangent, ids, count)
    mine = total // ROWS // 2

    def body(ids_ref, split_ref, c_ref, c_out, pair_out, sum_out):
        for o in range(moved):
            c_out[:, o * part : (o + 1) * part] = c_ref[:, columns_of(ids_ref[o], part)]
        if not moved:
            c_out[...] = c_ref[...]
        pair_out[...] = swapped(c_out[...], part)
        add_rows(sum_out, c_out[...].astype(f32))

    return call(
        body,
        [shape((total // 2, width), bf16)] * 2 + [shape((1, width), f32)],
        (mine,),
        [turned_spec(width, total // ROWS)],
        [row_spec(width)] * 2 + [whole_spec(1, width)],
        [cotangent],
        ids=[ids, split],
        name="cotangent_order",
    )


def hidden_units(rows, weight, bias, hidden_grad):
    total, depth = rows.shape
    cols = weight.shape[1]
    high, wide, sub = 256, 1024, 256
    curve, cube = (2.0 / 3.141592653589793) ** 0.5, 0.044715

    def body(n_ref, w_ref, b_ref, dz_ref, z_out, du_out, sum_out):
        first = pl.program_id(1) == 0
        for c in range(0, wide, sub):
            at = slice(c, c + sub)
            u = jnp.dot(n_ref[...], w_ref[:, at], preferred_element_type=f32) + b_ref[:, at]
            square = u * u
            t = jnp.tanh(curve * u * (1.0 + cube * square))
            z_out[:, at] = (0.5 * u * (1.0 + t)).astype(bf16)
            slope = 0.5 * (1.0 + t) + (0.5 * curve) * u * (1.0 - t * t) * (
                1.0 + (3.0 * cube) * square
            )
            du = (slope * dz_ref[:, at].astype(f32)).astype(bf16)
            du_out[:, at] = du
            total_du = jnp.sum(du.astype(f32), axis=0, keepdims=True)
            sum_out[:, at] = jnp.where(first, total_du, sum_out[:, at] + total_du)

    tile = pl.BlockSpec((high, wide), lambda j, i: (i, j))
    line = pl.BlockSpec((1, wide), lambda j, i: (0, j))
    return call(
        body,
        [shape((total, cols), bf16)] * 2 + [shape((1, cols), f32)],
        (cols // wide, total // high),
        [
            pl.BlockSpec((high, depth), lambda j, i: (i, 0)),
            pl.BlockSpec((depth, wide), lambda j, i: (0, j)),
            line,
            tile,
        ],
        [tile, tile, line],
        [rows, weight, bias, hidden_grad],
        flops=2 * total * depth * cols,
        name="hidden_units",
    )


def add_rows(sum_ref, values):
    @pl.when(pl.program_id(0) == 0)
    def _():
        sum_ref[...] = jnp.zeros_like(sum_ref)

    sum_ref[...] += jnp.sum(values, axis=0, keepdims=True)


def middle_norm(x_rel, part_own, part_other, bias_out, gain, bias, part):
    total, width = part_other.shape

    def body(x_ref, a_ref, b_ref, bo_ref, g_ref, c_ref, h_out, n_out, pair_out):
        mid = x_ref[...].astype(f32) + (
            a_ref[...].astype(f32) + b_ref[...].astype(f32)
        ) + bo_ref[...]
        h_out[...] = mid
        unit, _ = norm_stats(mid)
        low = (unit * g_ref[...] + c_ref[...]).astype(bf16)
        n_out[...] = low
        pair_out[...] = swapped(low, part)

    return call(
        body,
        [shape((total, width), f32)] + [shape((total, width), bf16)] * 2,
        (total // ROWS,),
        [row_spec(width)] * 3 + [whole_spec(1, width)] * 3,
        [row_spec(width)] * 3,
        [x_rel, part_own, part_other, bias_out, gain, bias],
        name="middle_norm",
    )


def block_result(middle, part_own, part_pair, bias_down, ids, count):
    total, width = middle.shape
    part = width // count

    def body(ids_ref, h_ref, a_ref, p_ref, b2_ref, out_ref):
        value = a_ref[...].astype(f32) + swapped(p_ref[...], part).astype(f32)
        value = (h_ref[...] + value + b2_ref[...]).astype(bf16)
        if part % LANES:
            out_ref[...] = value
        else:
            for o in range(count):
                out_ref[:, columns_of(ids_ref[o], part)] = value[:, o * part : (o + 1) * part]

    result = call(
        body,
        shape((total, width), bf16),
        (total // ROWS,),
        [row_spec(width)] * 3 + [whole_spec(1, width)],
        row_spec(width),
        [middle, part_own, part_pair, bias_down],
        ids=[ids],
        name="block_result",
    )
    return put_back(result, ids, count)


def middle_backward(middle, part_own, part_other, part_pair, cot_rel, gain, part):
    total, width = middle.shape

    def body(h_ref, a_ref, b_ref, p_ref, dy_ref, g_ref, dh_out, low_out, gg_out, gc_out, gbo_out):
        unit, inv = norm_stats(h_ref[...])
        grad = a_ref[...].astype(f32) + b_ref[...].astype(f32)
        grad = grad + swapped(p_ref[...], part).astype(f32)
        scaled = grad * g_ref[...]
        dh = dy_ref[...].astype(f32) + inv * (
            scaled
            - jnp.mean(scaled, axis=-1, keepdims=True)
            - unit * jnp.mean(scaled * unit, axis=-1, keepdims=True)
        )
        dh_out[...] = dh
        low = dh.astype(bf16)
        low_out[...] = low
        add_rows(gg_out, grad * unit)
        add_rows(gc_out, grad)
        add_rows(gbo_out, low.astype(f32))

    vec = shape((1, width), f32)
    return call(
        body,
        [shape((total, width), f32), shape((total, width), bf16), vec, vec, vec],
        (total // ROWS,),
        [row_spec(width)] * 5 + [whole_spec(1, width)],
        [row_spec(width)] * 2 + [whole_spec(1, width)] * 3,
        [middle, part_own, part_other, part_pair, cot_rel, gain],
        name="middle_backward",
    )


def first_backward(x_rel, part_own, part_other, keyval_grad, w_keyval_t, dh, gain, ids, count):
    total, width = dh.shape
    part = width // count
    kv = keyval_grad.shape[1]

    def body(ids_ref, x_ref, a_ref, b_ref, kv_ref, w_ref, dh_ref, g_ref, t_out, gg_out, gc_out):
        unit, inv = norm_stats(x_ref[...].astype(f32))
        grad = (a_ref[...].astype(f32) + b_ref[...].astype(f32)) + jnp.dot(
            kv_ref[...], w_ref[...], preferred_element_type=f32
        )
        scaled = grad * g_ref[...]
        value = dh_ref[...] + inv * (
            scaled
            - jnp.mean(scaled, axis=-1, keepdims=True)
            - unit * jnp.mean(scaled * unit, axis=-1, keepdims=True)
        )
        low = value.astype(bf16)
        if part % LANES:
            t_out[...] = low
        else:
            for o in range(count):
                t_out[:, columns_of(ids_ref[o], part)] = low[:, o * part : (o + 1) * part]
        add_rows(gg_out, grad * unit)
        add_rows(gc_out, grad)

    vec = shape((1, width), f32)
    result, gain_grad, bias_grad = call(
        body,
        [shape((total, width), bf16), vec, vec],
        (total // ROWS,),
        [row_spec(width)] * 3
        + [row_spec(kv), whole_spec(kv, width), row_spec(width), whole_spec(1, width)],
        [row_spec(width)] + [whole_spec(1, width)] * 2,
        [x_rel, part_own, part_other, keyval_grad, w_keyval_t, dh, gain],
        ids=[ids],
        flops=2 * total * width * kv,
        name="first_backward",
    )
    return put_back(result, ids, count), gain_grad, bias_grad


TILE = 256


def score_limits(lengths, token_count, first_place):
    doc_ends = jnp.cumsum(lengths)
    doc_starts = doc_ends - lengths
    places = (jnp.arange(token_count, dtype=jnp.int32) + first_place) % token_count
    doc_ids = jnp.sum((places[:, None] >= doc_ends[None, :]).astype(jnp.int32), axis=1)
    owners = doc_ids[:, None] == jnp.arange(lengths.shape[0], dtype=jnp.int32)[None, :]
    doc_begin = jnp.sum(jnp.where(owners, doc_starts[None, :], 0), axis=1)
    blocks = (places - doc_begin) // BLOCK
    seen = (doc_ids[:, None] == doc_ids[None, :]) & (blocks[None, :] <= blocks[:, None])
    seen_t = (doc_ids[None, :] == doc_ids[:, None]) & (blocks[:, None] <= blocks[None, :])
    pick = lambda s: jnp.where(s, shown_score, hidden_score).astype(f32)
    return pick(seen), pick(seen_t)


def attention_forward(queries, key_value, limits, heads):
    total = queries.shape[0]
    tiles = total // TILE
    c = score_scale * log2_e

    def body(q_ref, kv_ref, lim_ref, o_ref, lse_ref, top_ref):
        tile, head = pl.program_id(0), pl.program_id(1)
        k = kv_ref[:, :HD]
        v = kv_ref[:, HD:]
        s = lax.dot_general(
            q_ref[...], k, (((1,), (1,)), ((), ())), preferred_element_type=f32
        )
        s = jnp.minimum(s, lim_ref[...])
        m = jnp.max(s, axis=1, keepdims=True)
        p = jnp.exp2((s - m) * c)
        l = jnp.sum(p, axis=1, keepdims=True)
        o = jnp.dot(p.astype(bf16), v, preferred_element_type=f32)
        o_ref[...] = (o / l).astype(bf16)
        lane = lax.broadcasted_iota(jnp.int32, (TILE, LANES), 1)
        lse = m * c + jnp.log2(l)
        lse_ref[...] = jnp.where(lane == head, lse, lse_ref[...])

        @pl.when((tile == 0) & (head == 0))
        def _():
            top_ref[...] = jnp.full_like(top_ref, hidden_score)

        row = lax.broadcasted_iota(jnp.int32, (heads, LANES), 0)
        best = jnp.max(m, axis=0, keepdims=True) * score_scale
        top_ref[...] = jnp.where(row == head, jnp.maximum(top_ref[...], best), top_ref[...])

    return call(
        body,
        [shape((total, heads * HD), bf16), shape((total, LANES), f32), shape((heads, LANES), f32)],
        (tiles, heads),
        [
            pl.BlockSpec((TILE, HD), lambda i, h: (i, h)),
            pl.BlockSpec((total, 2 * HD), lambda i, h: (0, 0)),
            pl.BlockSpec((TILE, total), lambda i, h: (i, 0)),
        ],
        [
            pl.BlockSpec((TILE, HD), lambda i, h: (i, h)),
            pl.BlockSpec((TILE, LANES), lambda i, h: (i, 0)),
            pl.BlockSpec((heads, LANES), lambda i, h: (0, 0)),
        ],
        [queries, key_value, limits],
        flops=8 * total * total * HD * heads,
        name="attention_forward",
    )


def attention_backward(queries, grad_att, key_value, limits_t, lse_t, dot_t, heads):
    total = queries.shape[0]
    tiles = total // TILE
    c = score_scale * log2_e

    def body(q_ref, da_ref, kv_ref, lim_ref, lse_ref, dot_ref, dq_ref, dkv_ref):
        tile, head = pl.program_id(0), pl.program_id(1)
        k = kv_ref[:, :HD]
        v = kv_ref[:, HD:]
        q = q_ref[...]
        da = da_ref[...]
        nt = (((1,), (1,)), ((), ()))
        s = lax.dot_general(k, q, nt, preferred_element_type=f32)
        s = jnp.minimum(s, lim_ref[...])
        p = jnp.exp2(s * c - lse_ref[pl.ds(head, 1), :])
        dp = lax.dot_general(v, da, nt, preferred_element_type=f32)
        ds = (p * (dp - dot_ref[pl.ds(head, 1), :])).astype(bf16)
        dq = lax.dot_general(ds, k, (((0,), (0,)), ((), ())), preferred_element_type=f32)
        dq_ref[...] = (dq * score_scale).astype(bf16)

        @pl.when((tile == 0) & (head == 0))
        def _():
            dkv_ref[...] = jnp.zeros_like(dkv_ref)

        dkv_ref[:, :HD] += jnp.dot(ds, q, preferred_element_type=f32) * score_scale
        dkv_ref[:, HD:] += jnp.dot(p.astype(bf16), da, preferred_element_type=f32)

    return call(
        body,
        [shape((total, heads * HD), bf16), shape((total, 2 * HD), f32)],
        (tiles, heads),
        [
            pl.BlockSpec((TILE, HD), lambda i, h: (i, h)),
            pl.BlockSpec((TILE, HD), lambda i, h: (i, h)),
            pl.BlockSpec((total, 2 * HD), lambda i, h: (0, 0)),
            pl.BlockSpec((total, TILE), lambda i, h: (0, i)),
            pl.BlockSpec((heads, TILE), lambda i, h: (0, i)),
            pl.BlockSpec((heads, TILE), lambda i, h: (0, i)),
        ],
        [
            pl.BlockSpec((TILE, HD), lambda i, h: (i, h)),
            pl.BlockSpec((total, 2 * HD), lambda i, h: (0, 0)),
        ],
        [queries, grad_att, key_value, limits_t, lse_t, dot_t],
        flops=20 * total * total * HD * heads,
        name="attention_backward",
    )


def adam_values(gradient, weight, one, two, rate, decay):
    new_one = beta_one * one + (1.0 - beta_one) * gradient
    new_two = beta_two * two + (1.0 - beta_two) * gradient * gradient
    direction = (new_one * correct_one) / (jnp.sqrt(new_two * correct_two) + adam_eps)
    return new_one, new_two, weight - rate * (direction + decay * weight)


def to_tiles(flat, tiles_ref):
    for j in range(8):
        tiles_ref[:, j, :] = flat[:, j * LANES : (j + 1) * LANES]


def adam_in(gradient, weight, one, two, outer, start, full):
    rows, cols = gradient.shape
    step = 64
    base = (start // 1024).reshape(1)
    tall = pl.BlockSpec((step, 8, LANES), lambda i, j, b: (i, b[0] + j, 0))
    flat = pl.BlockSpec((step, 1024), lambda i, j, b: (i, j))
    args = [gradient, weight, one, two, outer]
    specs = [flat] + [tall] * 4
    aliases = {}
    if full is not None:
        aliases = {5: 0, 6: 1}
        args += list(full)
        specs += [pl.BlockSpec(memory_space=pl.ANY)] * 2

    def body(_, g_ref, w_ref, one_ref, two_ref, out_ref, *rest):
        one_out, two_out, delta_out, grad_tiles, delta_tiles = rest[-5:]
        to_tiles(g_ref[...].astype(f32), grad_tiles)
        new_one, new_two, stepped = adam_values(
            grad_tiles[...], w_ref[...], one_ref[...], two_ref[...], rate_matrix, weight_decay
        )
        one_out[...] = new_one
        two_out[...] = new_two
        delta_tiles[...] = out_ref[...] - stepped
        for j in range(8):
            delta_out[:, j * LANES : (j + 1) * LANES] = delta_tiles[:, j, :].astype(bf16)

    whole = shape(weight.shape, f32)
    return call(
        body,
        [whole, whole, shape((rows, cols), bf16)],
        (rows // step, cols // 1024),
        specs,
        [tall, tall, flat],
        args,
        ids=[base],
        scratch=[pltpu.VMEM((step, 8, LANES), f32)] * 2,
        aliases=aliases,
        name="adam_in",
        vmem=VMEM_MOST,
    )


def adam_out(gradient, weight, one, two, outer, start, full):
    rows, cols = gradient.shape
    step = 512
    base = (start // step).reshape(1)
    tall = pl.BlockSpec((step, cols), lambda i, b: (b[0] + i, 0))
    flat = pl.BlockSpec((step, cols), lambda i, b: (i, 0))
    args = [gradient, weight, one, two, outer]
    specs = [flat] + [tall] * 4
    aliases = {}
    if full is not None:
        aliases = {5: 0, 6: 1}
        args += list(full)
        specs += [pl.BlockSpec(memory_space=pl.ANY)] * 2

    def body(_, g_ref, w_ref, one_ref, two_ref, out_ref, *rest):
        one_out, two_out, delta_out = rest[-3:]
        new_one, new_two, stepped = adam_values(
            g_ref[...].astype(f32), w_ref[...], one_ref[...], two_ref[...], rate_matrix,
            weight_decay,
        )
        one_out[...] = new_one
        two_out[...] = new_two
        delta_out[...] = (out_ref[...] - stepped).astype(bf16)

    whole = shape(weight.shape, f32)
    return call(
        body,
        [whole, whole, shape((rows, cols), bf16)],
        (rows // step,),
        specs,
        [tall, tall, flat],
        args,
        ids=[base],
        aliases=aliases,
        name="adam_out",
        vmem=VMEM_MOST,
    )


def outer_values(mean, momentum, outer):
    velocity = outer_beta * momentum + mean
    return velocity, outer - outer_rate * (mean + outer_beta * velocity)


def outer_in(both, momentum, outer, factor, start, full):
    _, rows, cols = both.shape
    step = 64
    base = (start // 1024).reshape(1)
    tall = pl.BlockSpec((step, 8, LANES), lambda i, j, b: (i, b[0] + j, 0))
    flat = pl.BlockSpec((2, step, 1024), lambda i, j, b: (0, i, j))
    wide = pl.BlockSpec((step, 1024), lambda i, j, b: (i, b[0] + j))
    args = [both, momentum, outer]
    specs = [flat, tall, tall]
    if factor is not None:
        args.append(factor)
        specs.append(pl.BlockSpec((8, LANES), lambda i, j, b: (0, 0)))
    aliases = {}
    if full is not None:
        aliases = {len(args) + k: k for k in range(4)}
        args += list(full)
        specs += [pl.BlockSpec(memory_space=pl.ANY)] * 4

    def body(_, both_ref, mom_ref, out_ref, *rest):
        mean_out, vel_out, new_out, copy_out, mean_tiles, new_tiles = rest[-6:]
        to_tiles((both_ref[0].astype(f32) + both_ref[1].astype(f32)) * 0.5, mean_tiles)
        mean = mean_tiles[...]
        velocity, fresh = outer_values(mean, mom_ref[...], out_ref[...])
        if factor is not None:
            fresh = fresh * rest[0][...][None]
        mean_out[...] = mean
        vel_out[...] = velocity
        new_out[...] = fresh
        new_tiles[...] = fresh
        for j in range(8):
            copy_out[:, j * LANES : (j + 1) * LANES] = new_tiles[:, j, :].astype(bf16)

    whole = shape(outer.shape, f32)
    return call(
        body,
        [whole, whole, whole, shape((rows, outer.shape[1] * LANES), bf16)],
        (rows // step, cols // 1024),
        specs,
        [tall, tall, tall, wide],
        args,
        ids=[base],
        scratch=[pltpu.VMEM((step, 8, LANES), f32)] * 2,
        aliases=aliases,
        name="outer_in",
        vmem=VMEM_MOST,
    )


def outer_out(both, momentum, outer, start, full):
    _, rows, cols = both.shape
    step = 512
    base = (start // step).reshape(1)
    tall = pl.BlockSpec((step, cols), lambda i, b: (b[0] + i, 0))
    flat = pl.BlockSpec((2, step, cols), lambda i, b: (0, i, 0))
    args = [both, momentum, outer]
    specs = [flat, tall, tall]
    aliases = {}
    if full is not None:
        aliases = {3 + k: k for k in range(4)}
        args += list(full)
        specs += [pl.BlockSpec(memory_space=pl.ANY)] * 4

    def body(_, both_ref, mom_ref, out_ref, *rest):
        mean_out, vel_out, new_out, copy_out = rest[-4:]
        mean = (both_ref[0].astype(f32) + both_ref[1].astype(f32)) * 0.5
        velocity, fresh = outer_values(mean, mom_ref[...], out_ref[...])
        mean_out[...] = mean
        vel_out[...] = velocity
        new_out[...] = fresh
        copy_out[...] = fresh.astype(bf16)

    whole = shape(outer.shape, f32)
    return call(
        body,
        [whole, whole, whole, shape(outer.shape, bf16)],
        (rows // step,),
        specs,
        [tall] * 4,
        args,
        ids=[base],
        aliases=aliases,
        name="outer_out",
        vmem=VMEM_MOST,
    )


class Wire:
    def __init__(self, window):
        self.window, self.landed = window, []

    def send(self, block, axis, pairs):
        if len(self.landed) >= self.window:
            block, _ = lax.optimization_barrier((block, self.landed[-self.window]))
        arrived = lax.ppermute(block, axis, pairs)
        self.landed.append(arrived)
        return arrived


class Links:
    def __init__(self, count, splits, window):
        self.levels = count.bit_length() - 1
        self.far = ([1] + [1 << b for b in range(3, self.levels)])[: self.levels - 2]
        places = range(count)
        middle = [i for i in places if (i >> 1 ^ i >> 2) & 1]
        outer = [i for i in places if i not in middle]
        self.pair = [(i, i ^ 2) for i in places]
        self.inward = [(i, i ^ 2) for i in outer]
        self.outward = [(i, i ^ 2) for i in middle]
        self.between = [(i, i ^ 6) for i in middle]
        self.beside = [[(i, i ^ mask) for i in places] for mask in self.far]
        self.mirror = [(i, i ^ 6) for i in places]
        self.cores = [(i, (i + 1) % splits) for i in range(splits)]
        self.wire = Wire(window)

    def flips(self, across):
        masks = [2, across] + self.far
        table = []
        for o in range(1 << self.levels):
            flip = 0
            for level, mask in enumerate(masks):
                if o >> level & 1:
                    flip ^= mask
            table.append(flip)
        return table

    def to_side(self, block, pairs):
        return self.wire.send(block, "dp", pairs)

    def to_middle(self, block):
        return self.wire.send(block, "dp", self.between)

    def to_far(self, block, level):
        return self.wire.send(block, "dp", self.beside[level - 2])

    def to_pair(self, block):
        return self.wire.send(block, "dp", self.pair)

    def across(self, block):
        return lax.ppermute(block, "tensor", self.cores)

    def pair_now(self, block):
        return lax.ppermute(block, "dp", self.pair)


def after(value, *earlier):
    return lax.optimization_barrier((value, *earlier))[0]


class Order:
    def __init__(self):
        self.last = ()

    def tie(self, value):
        return after(value, *self.last) if self.last else value

    def mark(self, *values):
        self.last = values
        return values[0]

    def landed(self, *arrivals):
        self.last = tuple(self.last) + arrivals


class Gathered:
    def __init__(self, links, axis, mine, other=None):
        self.links, self.axis, self.mine, self.other = links, axis, mine, other
        self.held = {}

    def join(self, *blocks):
        return jnp.concatenate(blocks, axis=self.axis)

    def near(self):
        give = self.mine if self.other is None else self.other
        self.held[0] = self.join(self.mine, self.links.to_side(give, self.links.pair))

    def inward(self):
        if self.other is not None:
            self.passed = self.links.to_side(self.mine, self.links.inward)

    def middle(self):
        if self.other is None:
            self.relay = self.direct = self.links.to_middle(self.held[0])
        else:
            self.relay = self.links.to_middle(self.join(self.other, self.passed))

    def middle_rest(self):
        self.direct = self.links.to_middle(self.held[0])

    def outward(self):
        self.relayed = self.links.to_side(self.relay, self.links.outward)

    def join_far(self):
        self.held[2] = self.direct + self.relayed

    def far(self, level, o):
        self.held[o + (1 << level)] = self.links.to_far(self.held[o], level)

    def whole(self):
        for level in range(2, self.links.levels):
            for o in range(0, 1 << level, 2):
                if o + (1 << level) not in self.held:
                    self.far(level, o)
        return self.join(*[self.held[o] for o in sorted(self.held)])


class Reduced:
    def __init__(self, links, order, axis, size, halved, part):
        self.links, self.order, self.axis, self.size = links, order, axis, size
        self.halved, self.part = halved, part
        self.landed = {}

    def pair_sum(self, o):
        total = self.part(o, 2)
        for block in self.landed.pop(o, []):
            total = total + block.astype(f32)
        return self.order.mark(total.astype(bf16))

    def one(self, block, o):
        return lax.slice_in_dim(
            block, o * self.size, (o + 1) * self.size, axis=self.axis
        ).astype(f32)

    def far(self, level, o):
        arrived = self.links.to_far(self.pair_sum(o), level)
        self.landed.setdefault(o - (1 << level), []).append(arrived)
        return arrived

    def far_rest(self, done):
        arrived = None
        for level in range(self.links.levels - 1, 1, -1):
            for o in reversed(range(1 << level, 2 << level, 2)):
                if (level, o) not in done:
                    arrived = self.far(level, o)
        return arrived

    def inward(self):
        self.ahead = self.pair_sum(2)
        self.passed = self.links.to_side(self.ahead, self.links.inward)
        if self.halved:
            self.direct = self.links.to_middle(self.ahead)

    def middle(self):
        if self.halved:
            self.relay = self.links.to_middle(self.order.tie(self.passed))
        else:
            both = self.order.mark(self.order.tie(self.ahead) + self.passed)
            self.direct = self.links.to_middle(both)

    def single(self, o):
        total = self.part(o, 1)
        for block in self.landed[0] + [self.direct]:
            total = total + self.one(block, o)
        return total

    def near(self):
        value = self.order.mark(self.single(1).astype(bf16))
        self.beside = self.links.to_side(value, self.links.pair)
        self.theirs = self.beside.astype(f32)

    def outward(self):
        value = self.one(self.order.tie(self.relay), 1).astype(bf16)
        self.last = self.links.to_side(value, self.links.outward).astype(f32)

    def result(self):
        if not self.halved:
            return self.order.mark(self.single(0) + self.theirs), None
        own = self.order.mark(self.single(0) + self.last)
        return own, self.theirs + self.one(self.relay, 0)


def local(
    tokens,
    doc_lengths,
    cotangent,
    inner_in,
    inner_out,
    inner_shared,
    first_in,
    first_out,
    first_shared,
    second_in,
    second_out,
    second_shared,
    outer_in_w,
    outer_out_w,
    outer_shared,
    momentum_in,
    momentum_out,
    momentum_shared,
):
    splits = lax.axis_size("tensor")
    count = lax.axis_size("dp")
    split = lax.axis_index("tensor")
    place = lax.axis_index("dp")
    total, width = tokens.shape
    part = width // count
    local_cols = inner_in.shape[3]
    shared_cols = inner_shared.shape[2]
    heads = HEADS // splits
    qcols = heads * HD
    hidden = local_cols - qcols
    vec = 2 * HD
    own_cols = part // splits
    mine = total // 2

    links = Links(count, splits, 4)
    across = links.across
    levels = links.levels
    side = ((place >> 1) ^ (place >> 2)) & 1
    from_outer, from_middle = (jnp.array(links.flips(m), jnp.int32) for m in (4, 6))
    ids = (place ^ jnp.where(side == 0, from_outer, from_middle)).astype(jnp.int32)
    swap_group = [(0, 1), (1, 0)]
    split_id = split.astype(jnp.int32).reshape(1)

    def tall(array):
        return array.reshape(part, local_cols // LANES, LANES)

    w_in = tall(inner_in)
    w_out = inner_out.reshape(local_cols, part)
    shared_rows = lax.all_gather(inner_shared[0], ("dp", "tensor"), axis=0, tiled=True)

    half = hidden // 2
    flat_in = inner_in.reshape(part, local_cols)

    def sides(low, high):
        return (
            jnp.where(side == 0, low, high).astype(bf16),
            jnp.where(side == 0, high, low).astype(bf16),
        )

    block_q = flat_in[:, :qcols].astype(bf16)
    block_o = w_out[:qcols].astype(bf16)
    up_sides = sides(flat_in[:, qcols : qcols + half], flat_in[:, qcols + half :])
    down_sides = sides(w_out[qcols : qcols + half], w_out[qcols + half :])
    got_query = Gathered(links, 0, block_q)
    got_attn = Gathered(links, 1, block_o)
    got_up = Gathered(links, 0, *up_sides)
    got_down = Gathered(links, 1, *down_sides)
    shared_t = shared_rows.T
    shared_rel = pick_blocks(shared_t, ids, part, count, False)
    w_keyval_t = shared_rel[:vec].astype(bf16)
    vectors_t, vectors = shared_t[vec:], shared_rel[vec:]
    gain_one, bias_one, gain_two, bias_two = (vectors[k : k + 1] for k in range(4))
    bias_out, bias_down = vectors[5:6], vectors[6:7]
    bias_query = lax.dynamic_slice_in_dim(vectors_t[4], split * qcols, qcols)
    bias_up = lax.dynamic_slice_in_dim(
        vectors_t[7:].reshape(FF), split * hidden + side * half, half
    )

    nt = (((1,), (1,)), ((), ()))
    tn = (((0,), (0,)), ((), ()))

    def mm(a, b, dims=(((1,), (0,)), ((), ()))):
        return lax.dot_general(a, b, dims, preferred_element_type=f32)

    def block(array, o, blocks):
        return array[:, o * part : (o + blocks) * part]

    def both_rows(rows):
        return lax.all_gather(rows, "tensor", axis=0, tiled=True)

    def far(weight, o):
        if levels == 3:
            weight.far(2, o)

    cot_own, cot_pair, grad_bias_down = cotangent_order(cotangent, ids, split_id, count)
    got_query.near()
    got_attn.near()
    got_query.middle()
    far(got_query, 0)
    got_down.near()
    got_down.inward()
    got_attn.middle()
    far(got_attn, 0)
    got_query.outward()
    got_query.join_far()
    far(got_query, 2)
    got_attn.outward()
    got_attn.join_far()
    got_down.middle()
    got_up.near()
    far(got_attn, 2)
    w_query = got_query.whole()
    w_attn = got_attn.whole()
    got_up.inward()
    far(got_down, 0)
    cot_theirs = links.to_pair(swap_small(cot_pair, part))
    got_down.outward()
    got_down.middle_rest()
    got_down.join_far()
    far(got_up, 0)
    got_up.middle()
    far(got_down, 2)
    w_down = got_down.whole()
    got_up.outward()
    got_up.middle_rest()
    got_up.join_far()

    x_rel, normed = first_norm(tokens, ids, split_id, gain_one, bias_one, count)
    limits, limits_t = score_limits(doc_lengths[0], total, split * mine)
    key_value = mm(normed, w_keyval_t, nt).astype(bf16)
    queries = (mm(normed, w_query) + bias_query).astype(bf16)
    attended, log_totals, tops = attention_forward(queries, key_value, limits, heads)
    attn_give = mm(attended[mine:], w_attn).astype(bf16)
    attn_keep = mm(attended[:mine], w_attn).astype(bf16)
    attn_other = across(attn_give)
    middle, normed_two, normed_pair = middle_norm(
        x_rel, attn_keep, attn_other, bias_out, gain_two, bias_two, part
    )
    normed_theirs = links.to_pair(swap_small(normed_pair, part))
    far(got_up, 2)
    w_up = got_up.whole()
    normed_all = both_rows(jnp.concatenate([normed_two, normed_theirs], axis=0))
    cot_all = both_rows(jnp.concatenate([cot_own, cot_theirs], axis=0))
    hidden_grad = mm(cot_all, w_down, nt).astype(bf16)
    acts, grad_pre, grad_bias_up = hidden_units(normed_all, w_up, bias_up[None], hidden_grad)

    links.wire.window = 1 << 30
    order = Order()
    tie, mark = order.tie, order.mark
    sum_down = Reduced(
        links, order, 1, part, True, lambda o, b: mm(tie(acts), block(cot_all, o, b), tn)
    )
    sum_up = Reduced(
        links, order, 0, part, True, lambda o, b: mm(block(normed_all, o, b), tie(grad_pre), tn)
    )
    early = [(2, 6)] if levels == 3 else []
    for level, o in early:
        sum_down.far(level, o)
    pre_give = lax.dynamic_slice_in_dim(grad_pre, (1 - split) * 2 * mine, 2 * mine)
    pre_keep = lax.dynamic_slice_in_dim(grad_pre, split * 2 * mine, 2 * mine)
    two_give = mark(mm(pre_give, tie(w_up), nt).astype(bf16))
    two_other = across(two_give)
    down_landed = sum_down.far_rest(early)
    two_keep = mark(mm(pre_keep, tie(w_up), nt).astype(bf16))
    two_theirs = two_keep[mine:].astype(f32) + two_other[mine:].astype(f32)
    two_theirs = mark(swap_small(two_theirs.astype(bf16), part))
    two_pair = links.pair_now(two_theirs)
    for level, o in early:
        sum_up.far(level, o)
    sum_down.inward()
    dh, dh_mine, grad_gain_two, grad_bias_two, grad_bias_out = middle_backward(
        middle, tie(two_keep), two_other, two_pair, cot_own, gain_two, part
    )
    mark(dh_mine)
    dh_low = jnp.concatenate([dh_mine, across(dh_mine)], axis=0)
    grad_att = mark(mm(dh_low, w_attn, nt).astype(bf16))
    dots = jnp.sum(
        (grad_att.astype(f32) * attended.astype(f32)).reshape(total, heads, HD), axis=2
    )
    grad_queries, kv_part = attention_backward(
        queries, after(grad_att, down_landed), key_value, limits_t, log_totals.T[:heads], dots.T,
        heads,
    )
    mark(grad_queries)
    up_landed = sum_up.far_rest(early)
    one_give = mark(mm(grad_queries[mine:], tie(w_query), nt).astype(bf16))
    one_other = across(one_give)
    kv_other = across(kv_part[mine:])
    sum_down.middle()
    sum_down.near()
    sum_up.inward()
    sum_attn = Reduced(
        links, order, 1, part, False, lambda o, b: mm(tie(attended), block(dh_low, o, b), tn)
    )
    sum_attn.far_rest([])
    one_keep = mark(mm(grad_queries[:mine], tie(w_query), nt).astype(bf16))
    kv_low = (kv_part[:mine] + kv_other).astype(bf16)
    grad_mine, grad_gain_one, grad_bias_one = first_backward(
        x_rel, after(one_keep, up_landed), one_other, kv_low, w_keyval_t, dh, gain_one, ids, count
    )
    mark(grad_mine)
    tokens_grad = both_rows(grad_mine)
    sum_query = Reduced(
        links, order, 0, part, False, lambda o, b: mm(block(normed, o, b), tie(grad_queries), tn)
    )
    sum_query.far_rest([])
    order.landed(sum_up.passed, sum_up.direct)
    sum_up.middle()
    sum_down.outward()

    grad_keyval_t = mm(tie(kv_low), normed[:mine], tn)
    grad_bias_query = jnp.sum(grad_queries.astype(f32), axis=0)
    spread = jnp.concatenate(
        [
            lax.dynamic_update_slice_in_dim(
                jnp.zeros((width,), f32), grad_bias_query, split * qcols, 0
            ),
            lax.dynamic_update_slice_in_dim(
                jnp.zeros((FF,), f32), grad_bias_up[0], split * hidden + side * half, 0
            ),
        ]
    ).reshape(1 + FF // width, width)
    near = jnp.concatenate(
        [grad_keyval_t, grad_gain_one, grad_bias_one, grad_gain_two, grad_bias_two, grad_bias_out,
         grad_bias_down],
        axis=0,
    )
    steps = jnp.arange(count, dtype=jnp.int32)
    turned = jnp.where((side == 0) & ((steps & 2) != 0), steps ^ 1, steps)
    mirrored = (place ^ from_middle).astype(jnp.int32)

    def pieces(core):
        a = pick_blocks(near, turned * splits + core, own_cols, count, True)
        b = pick_blocks(spread, mirrored * splits + core, own_cols, count, True)
        return jnp.concatenate([a[:, : vec + 4], b[:, :1], a[:, vec + 4 :], b[:, 1:]], axis=1)

    shared_give = mark(pieces(1 - split))
    shared_other = across(shared_give)

    one_in, two_in = tall(first_in), tall(second_in)
    one_out, two_out = (a.reshape(local_cols, part) for a in (first_out, second_out))
    base_in, mom_in = tall(outer_in_w), tall(momentum_in)
    base_out, mom_out = (a.reshape(local_cols, part) for a in (outer_out_w, momentum_out))
    starts = [qcols + side * half, qcols + (1 - side) * half]
    zero = jnp.zeros((), jnp.int32)
    gathered = []

    def groups(delta):
        both = lax.all_gather(after(delta, *gathered[-1:]), "group", axis=0)
        gathered.append(both)
        return both

    def adam_down(gradient, start, full):
        *full, delta = adam_out(tie(gradient), w_out, one_out, two_out, base_out, start, full)
        mark(delta)
        return full, delta

    def adam_up(gradient, start, full):
        *full, delta = adam_in(tie(gradient), w_in, one_in, two_in, base_in, start, full)
        mark(delta)
        return full, delta

    red_down = sum_down.result()
    full_out, delta_down = adam_down(red_down[0], starts[0], None)
    both_down = [groups(delta_down)]
    sum_attn.inward()
    order.landed(sum_up.relay)
    full_out, delta_down = adam_down(red_down[1], starts[1], full_out)
    both_down.append(groups(delta_down))
    sum_up.outward()
    sum_up.near()
    sum_query.inward()
    order.landed(sum_attn.passed)
    sum_attn.middle()

    down_part = mark(mm(tie(acts), w_down).astype(bf16))
    down_sum = lax.psum_scatter(down_part, "tensor", scatter_dimension=0, tiled=True)
    order.landed(sum_query.passed)
    sum_query.middle()
    new_out = outer_out(both_down[0], mom_out, tie(base_out), starts[0], None)
    mark(new_out[0], sum_attn.direct)
    red_up = sum_up.result()
    full_in, delta_up = adam_up(red_up[0], starts[0], None)
    both_up = [groups(delta_up)]
    down_pair = links.to_pair(swap_small(down_sum[mine:], part))
    red_shared = pieces(split) + shared_other
    cube = list(reversed([links.pair, links.mirror] + links.beside))
    for pairs in cube[:-2]:
        keep = red_shared.shape[0] // 2
        red_shared = red_shared[:keep] + lax.ppermute(red_shared[keep:], "dp", pairs)
    peers = across(tie(tops))
    peak = jnp.where(
        split == 0, jnp.concatenate([tops, peers]), jnp.concatenate([peers, tops])
    )
    peak = jnp.maximum(peak, lax.ppermute(peak, "group", swap_group))
    for pairs in [links.pair, links.mirror] + links.beside:
        peak = jnp.maximum(peak, lax.ppermute(peak, "dp", pairs))
    clip_rows = clip_limit / jnp.maximum(peak, clip_limit)
    clip_own = lax.dynamic_slice_in_dim(clip_rows, split * heads, heads)

    sum_query.near()
    sum_attn.near()
    for pairs in cube[-2:]:
        keep = red_shared.shape[0] // 2
        red_shared = red_shared[:keep] + lax.ppermute(red_shared[keep:], "dp", pairs)
    red_shared = red_shared[0]
    order.landed(down_pair)
    full_in, delta_up = adam_up(red_up[1], starts[1], full_in)
    order.landed(sum_query.beside, sum_attn.beside)
    both_up.append(groups(delta_up))
    new_out = outer_out(both_down[1], mom_out, tie(base_out), starts[1], new_out)
    mark(new_out[0])
    block_out = both_rows(block_result(middle, down_sum, down_pair, bias_down, ids, count))
    red_query = sum_query.result()[0]
    full_in, delta_query = adam_up(red_query, zero, full_in)
    other_query = lax.ppermute(delta_query, "group", swap_group)
    red_attn = sum_attn.result()[0]
    full_out, delta_attn = adam_down(red_attn, zero, full_out)
    other_attn = lax.ppermute(delta_attn, "group", swap_group)
    new_in = outer_in(both_up[0], mom_in, tie(base_in), None, starts[0], None)
    new_in = outer_in(both_up[1], mom_in, base_in, None, starts[1], new_in)
    both = jnp.stack([delta_attn, other_attn])
    new_out = outer_out(both, mom_out, base_out, zero, new_out)
    both = jnp.stack([delta_query, other_query])
    new_in = outer_in(both, mom_in, base_in, clip_own, zero, new_in)

    ids_col = jnp.arange(shared_cols, dtype=jnp.int32)[:, None]
    one_sh, two_sh, stepped = adam_values(
        red_shared,
        inner_shared[0].T,
        first_shared[0].T,
        second_shared[0].T,
        jnp.where(ids_col < vec, rate_matrix, rate_vector),
        jnp.where(ids_col < vec, weight_decay, 0.0),
    )
    base_sh = outer_shared.T
    delta = (base_sh - stepped).astype(bf16)
    mean_sh = (delta.astype(f32) + lax.ppermute(delta, "group", swap_group).astype(f32)) * 0.5
    vel_sh, fresh_sh = outer_values(mean_sh, momentum_shared.T, base_sh)
    row_ids = (place * splits + split) * own_cols + jnp.arange(own_cols, dtype=jnp.int32)
    clip_vec = clip_rows[:, 0]
    row_clip = jnp.sum(
        jnp.where((row_ids // HD)[None, :] == jnp.arange(HEADS)[:, None], clip_vec[:, None], 0.0),
        axis=0,
    )
    fresh_sh = fresh_sh * jnp.where(ids_col == vec + 4, row_clip[None, :], 1.0)

    shape_in, shape_out = (part, 1, local_cols), (1, local_cols, part)
    mean_in, vel_in, fresh_in, copy_in = new_in
    mean_out, vel_out, fresh_out, copy_out = new_out
    return (
        block_out,
        tokens_grad,
        clip_vec,
        full_in[0].reshape((1,) + shape_in),
        full_out[0].reshape((1,) + shape_out),
        one_sh.T[None],
        full_in[1].reshape((1,) + shape_in),
        full_out[1].reshape((1,) + shape_out),
        two_sh.T[None],
        mean_in.reshape(shape_in),
        mean_out.reshape(shape_out),
        mean_sh.T,
        vel_in.reshape(shape_in),
        vel_out.reshape(shape_out),
        vel_sh.T,
        fresh_in.reshape(shape_in),
        fresh_out.reshape(shape_out),
        fresh_sh.T,
        copy_in.reshape(shape_in),
        copy_out.reshape(shape_out),
        fresh_sh.T.astype(bf16),
    )


def solution(mesh):
    rows = P(("group", "dp"), None)
    inner = [P("group", "dp", "tensor", None), P("group", "tensor", None, "dp"),
             P("group", ("dp", "tensor"), None)]
    outer = [P("dp", "tensor", None), P("tensor", None, "dp"), P(("dp", "tensor"), None)]
    in_specs = tuple([rows] * 3 + inner * 3 + outer * 2)
    out_specs = tuple([rows] * 2 + [P()] + inner * 2 + outer * 4)
    return jax.shard_map(local, mesh=mesh, in_specs=in_specs, out_specs=out_specs, check_vma=False)
```
